32 devices in a mesh: seq: 8 (over y, x, core), stream: 4 (over z).
Axes of the slice: x: 2, y: 2, z: 4, core: 2. Of those that a mesh axis runs over, the one named last changes fastest.
Arguments:
- tokens: bfloat16 [4, 1024, 1024], P('stream', 'seq'), may hold values from -6 to 6
- grad_out: bfloat16 [4, 1024, 1024], P('stream', 'seq'), may hold values from -6 to 6
- doc_lengths: int32 [4, 8], P('stream'), may hold values from 1 to 512, 1024 in all within a row
- gain_in: float32 [1024], replicated, may hold values from 0.5 to 1.5
- in_weight: bfloat16 [1024, 6144], replicated, may hold values from -0.1875 to 0.1875
- small_weight: float32 [1024, 24], replicated, may hold values from -0.1875 to 0.1875
- gate_bias: float32 [8], replicated, may hold values from -1 to 1
- decay_rate: float32 [8], replicated, may hold values from 0.0009765625 to 0.1
- conv_weight: float32 [4, 5120], replicated, may hold values from -3 to 3
- gain_head: float32 [128], replicated, may hold values from 0.5 to 1.5
- out_weight: bfloat16 [1024, 1024], replicated, may hold values from -0.1875 to 0.1875
- gain_mid: float32 [1024], replicated, may hold values from 0.5 to 1.5
- gate_up_weight: bfloat16 [1024, 5632], replicated, may hold values from -0.1875 to 0.1875
- down_weight: bfloat16 [2816, 1024], replicated, may hold values from -0.109375 to 0.109375
Outputs:
- output: bfloat16 [4, 1024, 1024], P('stream', 'seq')
- grad_input: float32 [4, 1024, 1024], P('stream', 'seq')
- grad_gain_in: float32 [1024], replicated
- grad_in_weight: float32 [1024, 6144], P(('seq', 'stream'))
- grad_small_weight: float32 [1024, 24], replicated
- grad_gate_bias: float32 [8], replicated
- grad_decay_rate: float32 [8], replicated
- grad_conv_weight: float32 [4, 5120], replicated
- grad_gain_head: float32 [128], replicated
- grad_out_weight: float32 [1024, 1024], P(('seq', 'stream'))
- grad_gain_mid: float32 [1024], replicated
- grad_gate_up_weight: float32 [1024, 5632], P(('seq', 'stream'))
- grad_down_weight: float32 [2816, 1024], P(('seq', 'stream'))
The draws below stay inside these ranges and needn't reach their ends.
Inputs may be any that keep to these rules, and one draw needn't show every extreme that they name: `doc_lengths`: each row holds the lengths of the 8 consecutive documents of one domain sequence, 1 or more each, summing to 1024; the longest is exactly 512.
All inputs are finite; a program needn't handle non-finite values.
Results may differ from the reference program's by a relative error of at most 0.014.
The reference program's roundings to bfloat16 on the way count: a program that leaves them out, or rounds other values in their place, can miss the bound.
Values may be sent and summed in bfloat16 or wider, within the bound.
A program may use at most 256 MiB of HBM per device.

```python
import math
import jax
import jax.numpy as jnp
import numpy as np
from jax import lax

D = 1024
H = 8
HD = 128
FF = 2816
NH = 2
CONV = 4
SPAN = 64
DOCS = 8
LENGTH = 1024
SEQS = 4


def block_levels(own_key, dims, split, low, top_value):
    def one(axis_at, parts):
        draws = jax.random.uniform(jax.random.fold_in(jax.random.fold_in(own_key, 6), axis_at), (parts,), jnp.float32, low / len(split), top_value / len(split))
        return jnp.repeat(jnp.exp(draws), dims[axis_at] // parts).reshape((-1,) + (1,) * (len(dims) - axis_at - 1))

    loudness = one(*split[0])
    for cut in split[1:]:
        loudness = loudness * one(*cut)
    return loudness


def profile(number_of, total, most, slope):
    weights = [(1 << 20) // math.isqrt(rank ** slope) + 1 for rank in range(2, number_of + 1)]
    surplus, given = total - most - (number_of - 1), [1] * (number_of - 1)
    while surplus > 0:
        movable = [i for i in range(number_of - 1) if given[i] < most]
        whole, budget = sum([weights[i] for i in movable]), surplus
        for i in movable:
            addition = min(most - given[i], max(1, budget * weights[i] // whole), surplus)
            given[i] = given[i] + addition
            surplus = surplus - addition
    return np.array([most] + given)


def uneven_parts(stream_key, amount, total, bound, lean):
    if amount == 2:
        one = jax.random.randint(stream_key, (), max(1, total - bound), min(bound, total - 1) + 1)
        return jnp.stack([one, total - one])
    sizes = jnp.asarray(profile(amount, total, bound, lean), jnp.int32)
    pairs = (amount - 1) // 2
    donor, taker = sizes[1:1 + 2 * pairs:2], sizes[2:2 + 2 * pairs:2]
    margin = jnp.minimum(donor - 1, bound - taker)
    shifted = jax.random.randint(jax.random.fold_in(stream_key, 1), (pairs,), 0, 1 << 20) % (margin + 1)
    sizes = sizes.at[1:1 + 2 * pairs:2].set(donor - shifted).at[2:2 + 2 * pairs:2].set(taker + shifted)
    return sizes[jax.random.permutation(jax.random.fold_in(stream_key, 2), amount)]


def noise(key, dims, scale, most, shards=(), kind=jnp.bfloat16):
    level = block_levels(key, dims, shards, -0.22, 0.18) if shards else 1.0
    array = jax.random.normal(key, dims, jnp.float32) * scale * level
    return jnp.minimum(jnp.maximum(array, -most), most).astype(kind)


def setup_inputs(seed: int = 0) -> dict:
    keys = jax.random.split(jax.random.key(seed), 15)
    return {
        "tokens": noise(keys[0], (SEQS, LENGTH, D), 1.0, 6.0, ((0, 4), (1, 8))),
        "grad_out": noise(keys[1], (SEQS, LENGTH, D), 1.0, 6.0, ((0, 4), (1, 8))),
        "doc_lengths": jax.vmap(lambda own: uneven_parts(own, DOCS, LENGTH, LENGTH // 2, 2))(jax.random.split(keys[2], SEQS)).reshape((SEQS, DOCS)).astype(jnp.int32),
        "gain_in": jnp.clip(1.0 + 0.1 * jax.random.normal(keys[3], (D,), jnp.float32), 0.5, 1.5),
        "in_weight": noise(keys[4], (D, (2 + 2 * NH) * D), D ** -0.5, 0.1875),
        "small_weight": noise(keys[5], (D, (NH + 1) * H), D ** -0.5, 0.1875, (), jnp.float32),
        "gate_bias": jnp.clip(jax.random.uniform(keys[6], (H,), jnp.float32, -1.0, 1.0), -1.0, 1.0),
        "decay_rate": jnp.clip(jnp.exp(jax.random.uniform(keys[7], (H,), jnp.float32, math.log(0.0009765625), math.log(0.1))), 0.0009765625, 0.1),
        "conv_weight": noise(keys[8], (CONV, (1 + 2 * NH) * D), 0.5, 3.0, (), jnp.float32),
        "gain_head": jnp.clip(1.0 + 0.1 * jax.random.normal(keys[9], (HD,), jnp.float32), 0.5, 1.5),
        "out_weight": noise(keys[10], (D, D), D ** -0.5, 0.1875),
        "gain_mid": jnp.clip(1.0 + 0.1 * jax.random.normal(keys[11], (D,), jnp.float32), 0.5, 1.5),
        "gate_up_weight": noise(keys[12], (D, 2 * FF), D ** -0.5, 0.1875),
        "down_weight": noise(keys[13], (FF, D), FF ** -0.5, 0.109375),
    }


highest = lax.Precision.HIGHEST

@jax.custom_vjp
def low(v):
    return lax.optimization_barrier(v.astype(jnp.bfloat16)).astype(jnp.float32)

@jax.custom_vjp
def low_back(v):
    return v

def low_keep(v):
    return (low(v), None)

def low_pass(kept, grad):
    return (grad,)

def back_keep(v):
    return (v, None)

def back_low(kept, grad):
    return (low(grad),)
low.defvjp(low_keep, low_pass)
low_back.defvjp(back_keep, back_low)

def rms_scale(values, gain):
    return values * lax.rsqrt(lax.optimization_barrier(jnp.mean(values * values, axis=-1, keepdims=True)) + 1e-06) * gain

def solve_lower(matrix, target):
    return jax.scipy.linalg.solve_triangular(matrix, target, lower=True, unit_diagonal=True)

def block_core(state, key_rows, value_rows, betas, log_gates, resets):
    width = resets.shape[0]
    places = jnp.arange(width, dtype=jnp.int32)
    counted = jnp.cumsum(resets)
    joined = (counted[:, None] == counted[None, :]) & (places[None, :] <= places[:, None])
    before = (joined & (places[None, :] < places[:, None])).astype(jnp.float32)
    cumul = jnp.cumsum(log_gates, axis=0).T
    decays = jnp.exp(jnp.where(joined[None], cumul[:, :, None] - cumul[:, None, :], 0.0)) * joined.astype(jnp.float32)[None]
    head_decay = jnp.exp(cumul) * (counted == 0).astype(jnp.float32)[None, :]
    products = jnp.einsum('ihk,jhk->hij', key_rows, key_rows, precision=highest)
    beta_heads = betas.T
    strict_lower = beta_heads[:, :, None] * decays * products * before[None]
    from_state = jnp.einsum('hvk,ihk->hiv', state, key_rows, precision=highest)
    target = beta_heads[:, :, None] * (jnp.transpose(value_rows, (1, 0, 2)) - head_decay[:, :, None] * from_state)
    new_values = jax.vmap(solve_lower)(strict_lower, target)
    return (new_values, decays, head_decay)

def block_end(state, key_rows, new_values, decays, head_decay):
    carried = head_decay[:, -1][:, None, None] * state
    return carried + jnp.einsum('hj,hjv,jhk->hvk', decays[:, -1, :], new_values, key_rows, precision=highest)

def block_out(state, queries, key_rows, new_values, decays, head_decay):
    chosen = decays[:, NH - 1::NH, :]
    head_chosen = head_decay[:, NH - 1::NH]
    scores = jnp.einsum('rhk,jhk->hrj', queries, key_rows, precision=highest) * chosen
    from_state = jnp.einsum('hvk,rhk->rhv', state, queries, precision=highest)
    return head_chosen.T[:, :, None] * from_state + jnp.einsum('hrj,hjv->rhv', scores, new_values, precision=highest)

def run_outputs(start_state, prepared, resets):

    def advance(state, block):
        queries, key_rows, value_rows, betas, log_gates, reset_flags = block
        new_values, decays, head_decay = block_core(state, key_rows, value_rows, betas, log_gates, reset_flags)
        return (block_end(state, key_rows, new_values, decays, head_decay), block_out(state, queries, key_rows, new_values, decays, head_decay))
    end_state, outputs = lax.scan(jax.checkpoint(advance), start_state, prepared + (resets,))
    return (outputs.reshape(-1, H, HD), end_state)

def doc_masks(lengths, first_position, count_tokens):
    offsets = jnp.cumsum(lengths) - lengths
    positions = first_position - (CONV - 1) + jnp.arange(count_tokens + CONV - 1, dtype=jnp.int32)
    doc_ids = lax.optimization_barrier(jnp.sum((offsets[None, :] <= positions[:, None]).astype(jnp.int32), axis=1)) - 1
    current = doc_ids[CONV - 1:]
    same_doc = jnp.stack([(doc_ids[CONV - 1 - lag_step:CONV - 1 - lag_step + count_tokens] == current).astype(jnp.float32) for lag_step in range(CONV)])
    starts = jnp.any(offsets[None, :] == positions[CONV - 1:, None], axis=1).astype(jnp.int32)
    flags = jnp.concatenate([starts[:, None], jnp.zeros((count_tokens, NH - 1), jnp.int32)], axis=1)
    return (same_doc, flags.reshape(count_tokens // SPAN, NH * SPAN))

def mix_inputs(extended, small, conv_weight, gate_bias, decay_rate, same_doc):
    count_tokens = extended.shape[0] - (CONV - 1)
    mixed = extended[CONV - 1:] * conv_weight[CONV - 1]
    for lag_step in range(1, CONV):
        earlier = extended[CONV - 1 - lag_step:CONV - 1 - lag_step + count_tokens]
        mixed = mixed + earlier * conv_weight[CONV - 1 - lag_step] * same_doc[lag_step][:, None]
    active = jax.nn.silu(mixed)
    queries = active[:, :D].reshape(count_tokens, H, HD)
    key_rows = active[:, D:D + NH * D].reshape(count_tokens * NH, H, HD)
    key_rows = key_rows * lax.rsqrt(lax.optimization_barrier(jnp.sum(key_rows * key_rows, axis=-1, keepdims=True)) + 1e-06)
    value_rows = active[:, D + NH * D:].reshape(count_tokens * NH, H, HD)
    betas = (2.0 * jax.nn.sigmoid(small[:, :NH * H])).reshape(count_tokens * NH, H)
    log_first = -decay_rate * jax.nn.softplus(small[:, NH * H:] + gate_bias)
    log_gates = jnp.concatenate([log_first[:, None, :], jnp.zeros((count_tokens, NH - 1, H), jnp.float32)], axis=1)
    blocks = count_tokens // SPAN
    return (queries.reshape(blocks, SPAN, H, HD), key_rows.reshape(blocks, NH * SPAN, H, HD), value_rows.reshape(blocks, NH * SPAN, H, HD), betas.reshape(blocks, NH * SPAN, H), log_gates.reshape(blocks, NH * SPAN, H))

def gate_piece(outputs, gate_raw, gain_head):
    count_tokens = outputs.shape[0]
    scaled = outputs * lax.rsqrt(lax.optimization_barrier(jnp.mean(outputs * outputs, axis=-1, keepdims=True)) + 1e-06) * gain_head
    return (scaled * jax.nn.silu(gate_raw.reshape(count_tokens, H, HD))).reshape(count_tokens, H * HD)

def layer_forward(params, tokens, lengths):
    gain_in, in_weight, small_weight, gate_bias, decay_rate, conv_weight, gain_head, out_weight, gain_mid, gate_up_weight, down_weight = params
    count_tokens = tokens.shape[0]
    channels = (1 + 2 * NH) * D
    same_doc, reset_flags = doc_masks(lengths, 0, count_tokens)
    normed = low(rms_scale(tokens, gain_in))
    projected = low_back(low(jnp.dot(normed, in_weight, precision=highest)))
    small = jnp.dot(normed, small_weight, precision=highest)
    extended = jnp.concatenate([jnp.zeros((CONV - 1, channels), jnp.float32), projected[:, :channels]], axis=0)
    prepared = mix_inputs(extended, small, conv_weight, gate_bias, decay_rate, same_doc)
    outputs = run_outputs(jnp.zeros((H, HD, HD), jnp.float32), prepared, reset_flags)[0]
    gated = low(gate_piece(outputs, projected[:, channels:], gain_head))
    attention = low_back(jnp.dot(gated, out_weight, precision=highest))
    residual = tokens + attention
    normed_mid = low(rms_scale(residual, gain_mid))
    gate_up = low_back(jnp.dot(normed_mid, gate_up_weight, precision=highest))
    hidden = low(jax.nn.silu(gate_up[:, :FF]) * gate_up[:, FF:])
    return residual + jnp.dot(hidden, down_weight, precision=highest)

def reference(tokens, grad_out, doc_lengths, gain_in, in_weight, small_weight, gate_bias, decay_rate, conv_weight, gain_head, out_weight, gain_mid, gate_up_weight, down_weight):
    params = (gain_in.astype(jnp.float32), in_weight.astype(jnp.float32), small_weight.astype(jnp.float32), gate_bias.astype(jnp.float32), decay_rate.astype(jnp.float32), conv_weight.astype(jnp.float32), gain_head.astype(jnp.float32), out_weight.astype(jnp.float32), gain_mid.astype(jnp.float32), gate_up_weight.astype(jnp.float32), down_weight.astype(jnp.float32))

    def one_domain(totals, inputs):
        domain_rows, cotangent, lengths = inputs

        def forward(weights, values):
            return layer_forward(weights, values, lengths)
        result, pullback = jax.vjp(forward, params, domain_rows.astype(jnp.float32))
        weight_grads, row_grads = pullback(cotangent.astype(jnp.float32))
        totals = jax.tree.map(lambda first, second: first + second, totals, weight_grads)
        return (totals, (result.astype(jnp.bfloat16), row_grads))
    zeros = jax.tree.map(jnp.zeros_like, params)
    totals, (outputs, input_grads) = lax.scan(one_domain, zeros, (tokens, grad_out, doc_lengths))
    return (outputs, input_grads, totals[0], totals[1], totals[2], totals[3], totals[4], totals[5], totals[6], totals[7], totals[8], totals[9], totals[10])
```

```python
import functools

import jax
import jax.numpy as jnp
from jax import lax
from jax.experimental import pallas as pl
from jax.experimental.pallas import tpu as pltpu
from jax.sharding import PartitionSpec as P

D = 1024
H = 8
HD = 128
FF = 2816
NH = 2
CONV = 4
GROUPS = 2 + 2 * NH
MIXED = GROUPS - 1
DOCS = 8
EPS = 1e-06

f32 = jnp.float32
bf16 = jnp.bfloat16


def dot(a, b, dims):
    return lax.dot_general(
        a.astype(bf16), b.astype(bf16), ((dims[:1], dims[1:]), ((), ())), preferred_element_type=f32
    )


def nn(a, b):
    return dot(a, b, (1, 0))


def nt(a, b):
    return dot(a, b, (1, 1))


def tn(a, b):
    return dot(a, b, (0, 0))


def halves(x):
    high = x.astype(bf16)
    return high, (x - high.astype(f32)).astype(bf16)


def nt_fine(a, b):
    (a_high, a_low), (b_high, b_low) = halves(a), halves(b)
    return nt(a_high, b_high) + (nt(a_high, b_low) + nt(a_low, b_high))


def nn_exact(ones, x):
    high, low = halves(x)
    lowest = (x - high.astype(f32) - low.astype(f32)).astype(bf16)
    return nn(ones, high) + (nn(ones, low) + nn(ones, lowest))


def sigmoid(x):
    return 1.0 / (1.0 + jnp.exp(-x))


def softplus(x):
    return jnp.maximum(x, 0.0) + jnp.log(1.0 + jnp.exp(-jnp.abs(x)))


def doc_at(starts, positions):
    total = jnp.full(positions.shape, -1, jnp.int32)
    for start in starts:
        total = total + (start <= positions).astype(jnp.int32)
    return total


def doc_starts(lengths_ref):
    starts, at = [], jnp.int32(0)
    for j in range(DOCS):
        starts.append(at)
        at = at + lengths_ref[0, j]
    return starts


def stack2(a, b):
    return jnp.concatenate([a, b], axis=0)


def beside(a, b):
    return jnp.concatenate([a, b], axis=1)


def quad(a, b, c, d):
    return stack2(beside(a, b), beside(c, d))


def conv_of(block, taps, docs, T):
    total = block[8:] * taps[CONV - 1 : CONV]
    for lag in range(1, CONV):
        same = (docs[0] == docs[lag]).astype(f32)
        total = total + block[8 - lag : 8 - lag + T] * (taps[CONV - 1 - lag : CONV - lag] * same)
    return total


def chunk_gates(raw, consts, starts, first, T):
    lane = lax.broadcasted_iota(jnp.int32, (T, HD), 1)
    row = lax.broadcasted_iota(jnp.int32, (T, HD), 0)
    logits = raw + (pltpu.roll(raw, HD - 3, 1) + pltpu.roll(raw, HD - 6, 1))
    bias, rate = consts[0:1], consts[1:2]
    shifted = logits + bias
    gate = -rate * softplus(shifted)
    lower = (lax.broadcasted_iota(jnp.int32, (T, T), 1) <= lax.broadcasted_iota(jnp.int32, (T, T), 0))
    cumul = nn_exact(lower.astype(bf16), jnp.where(lane == 2, gate, 0.0))
    beta = 2.0 * sigmoid(logits)
    b0, b1 = beta[:, 0:1], beta[:, 1:2]
    g = cumul[:, 2:3]
    g_row = jnp.transpose(cumul)[2:3, :]
    g_last = cumul[T - 1 : T, 2:3]
    position = first + row[:, 0:1]
    docs = [doc_at(starts, position - lag) for lag in range(CONV)]
    doc = docs[0]
    doc_row = doc_at(starts, first + lax.broadcasted_iota(jnp.int32, (1, T), 1))
    doc_before = doc_at(starts, jnp.full((1, 1), first - 1, jnp.int32))
    doc_last = doc_at(starts, jnp.full((1, 1), first + (T - 1), jnp.int32))
    joined = lower & (doc == doc_row)
    decay = jnp.where(joined, jnp.exp(jnp.where(joined, g - g_row, 0.0)), 0.0)
    place_i = lax.broadcasted_iota(jnp.int32, (T, T), 0)
    place_j = lax.broadcasted_iota(jnp.int32, (T, T), 1)
    strict = jnp.where(place_i == place_j, 0.0, decay)
    from_start = jnp.exp(g) * (doc == doc_before).astype(f32)
    to_end = jnp.exp(jnp.minimum(g_last - g, 0.0)) * (doc == doc_last).astype(f32)
    whole = jnp.exp(g_last) * (doc_last == doc_before).astype(f32)
    return dict(
        logits=logits, shifted=shifted, gate=gate, beta=beta, b=stack2(b0, b1), docs=docs,
        decay=decay, decays=quad(strict, strict, decay, strict), hd=from_start,
        hd2=stack2(from_start, from_start), to_end=stack2(to_end, to_end), whole=whole,
    )


def key_scale(raw):
    return lax.rsqrt(jnp.sum(raw * raw, axis=-1, keepdims=True) + EPS)


def chunk_inputs(block, taps, docs, T):
    conv = conv_of(block, taps, docs, T)
    sig = sigmoid(conv)
    active = conv * sig
    cut = [active[:, i * HD : (i + 1) * HD] for i in range(MIXED)]
    scales = (key_scale(cut[1]), key_scale(cut[2]))
    keys = stack2(cut[1] * scales[0], cut[2] * scales[1])
    values = stack2(cut[3], cut[4])
    return conv, sig, cut[0], keys, values, stack2(*scales)


def inverses(lowers, T):
    size = NH * T
    row = lax.broadcasted_iota(jnp.int32, (size, size), 0)
    col = lax.broadcasted_iota(jnp.int32, (size, size), 1)
    token_i, token_j = row & (T - 1), col & (T - 1)
    differ = token_i ^ token_j
    eye = (row == col).astype(f32)
    found = [jnp.where(row == col, 1.0, jnp.where(differ == 0, -a, 0.0)) for a in lowers]
    step = 1
    while step < T:
        level = (differ >= step) & (differ < 2 * step)
        parts = [nn(jnp.where(level, a, 0.0), x) for a, x in zip(lowers, found)]
        found = [x - nn(x, part) for x, part in zip(found, parts)]
        step *= 2
    a_cut = [halves(a) for a in lowers]
    x_cut = [halves(x) for x in found]
    errors = [
        eye - x - (nn(a[0], xc[0]) + (nn(a[0], xc[1]) + nn(a[1], xc[0])))
        for a, x, xc in zip(a_cut, found, x_cut)
    ]
    return [x + nn(xc[0], e) for x, xc, e in zip(found, x_cut, errors)]


def head_gate(mixed, raw, gain):
    scale = lax.rsqrt(jnp.mean(mixed * mixed, axis=-1, keepdims=True) + EPS)
    return mixed * scale, scale, sigmoid(raw)


def forward_kernel(T, per, lengths, proj, small, taps_ref, consts, gain, gated, mixed_out, states, news, invs,
                   xbuf, ubuf, wbuf, qbuf, pbuf, dbuf, gates):
    count = proj.shape[0] // T
    width = MIXED * HD
    starts = doc_starts(lengths)
    taps = taps_ref[...]
    xbuf[0:8, :] = jnp.zeros((8, width), f32)

    def fill(c, _):
        xbuf[pl.ds(pl.multiple_of(8 + c * T, 8), T), :] = proj[pl.ds(pl.multiple_of(c * T, T), T), :width].astype(f32)
        return 0

    lax.fori_loop(0, count, fill, 0)

    def intra(turn, _):
        kept, lowers = [], []
        for i in range(per):
            c = turn * per + i
            first = pl.multiple_of(c * T, T)
            gate = chunk_gates(small[pl.ds(first, T), :], consts, starts, first, T)
            block = xbuf[pl.ds(first, T + 8), :]
            conv, sig, query, keys, values, scales = chunk_inputs(block, taps, gate["docs"], T)
            keys_low = keys.astype(bf16)
            lowers.append(gate["b"] * (nt(keys_low, keys_low) * gate["decays"]))
            kept.append((c, first, gate, query, keys, keys_low, values))
        found = inverses(lowers, T)
        for (c, first, gate, query, keys, keys_low, values), inverse in zip(kept, found):
            two = pl.multiple_of(c * (NH * T), NH * T)
            low = inverse.astype(bf16)
            invs[c] = low
            right = gate["b"] * beside(values, gate["hd2"] * keys)
            both = nn(low, right)
            ubuf[pl.ds(two, NH * T), :] = both[:, :HD]
            wbuf[pl.ds(two, NH * T), :] = both[:, HD:].astype(bf16)
            query_low = query.astype(bf16)
            qbuf[pl.ds(first, T), :] = query_low
            pbuf[pl.ds(first, T), :] = (nt_fine(query, keys) * beside(gate["decay"], gate["decay"])).astype(bf16)
            dbuf[pl.ds(two, NH * T), :] = (gate["to_end"] * keys).astype(bf16)
            lane = lax.broadcasted_iota(jnp.int32, (T, HD), 1)
            gates[pl.ds(first, T), :] = jnp.where(lane == 0, gate["hd"], gate["whole"])
        return 0

    lax.fori_loop(0, count // per, intra, 0)

    def across(c, state):
        first = pl.multiple_of(c * T, T)
        two = pl.multiple_of(c * (NH * T), NH * T)
        state_low = state.astype(bf16)
        states[c] = state_low
        new = ubuf[pl.ds(two, NH * T), :] - nn(wbuf[pl.ds(two, NH * T), :], state_low)
        new_low = new.astype(bf16)
        news[pl.ds(two, NH * T), :] = new_low
        gate = gates[pl.ds(first, T), :]
        mixed = gate[:, 0:1] * nn(qbuf[pl.ds(first, T), :], state_low) + nn(pbuf[pl.ds(first, T), :], new_low)
        mixed_out[pl.ds(first, T), :] = mixed
        raw = proj[pl.ds(first, T), width:].astype(f32)
        normal, _, sig = head_gate(mixed, raw, None)
        gated[pl.ds(first, T), :] = ((normal * gain[0:1]) * (raw * sig)).astype(bf16)
        return gate[0:1, 1:2] * state + tn(dbuf[pl.ds(two, NH * T), :], new_low)

    lax.fori_loop(0, count, across, jnp.zeros((HD, HD), f32))


def backward_kernel(T, lengths, proj, small, taps_ref, consts, gain, mixed_in, states, news, invs, grad_gated,
                    gp, gconv_w, sums, xbuf, gbuf):
    count = proj.shape[0] // T
    width = MIXED * HD
    starts = doc_starts(lengths)
    taps = taps_ref[...]
    xbuf[0:8, :] = jnp.zeros((8, width), f32)
    gbuf[...] = jnp.zeros((8, width), f32)

    def fill(c, _):
        xbuf[pl.ds(pl.multiple_of(8 + c * T, 8), T), :] = proj[pl.ds(pl.multiple_of(c * T, T), T), :width].astype(f32)
        return 0

    lax.fori_loop(0, count, fill, 0)
    lane = lax.broadcasted_iota(jnp.int32, (T, HD), 1)
    place_i = lax.broadcasted_iota(jnp.int32, (T, T), 0)
    place_j = lax.broadcasted_iota(jnp.int32, (T, T), 1)
    upper = (place_j >= place_i).astype(bf16)
    under = (place_j < place_i)

    def turn(k, carry):
        state_grad, gain_grad, gate_sums = carry
        c = count - 1 - k
        first = pl.multiple_of(c * T, T)
        two = pl.multiple_of(c * (NH * T), NH * T)
        gate = chunk_gates(small[pl.ds(first, T), :], consts, starts, first, T)
        block = xbuf[pl.ds(first, T + 8), :]
        conv, sig, query, keys, values, scales = chunk_inputs(block, taps, gate["docs"], T)
        keys_low, query_low = keys.astype(bf16), query.astype(bf16)
        b, hd, hd2, to_end = gate["b"], gate["hd"], gate["hd2"], gate["to_end"]
        decay2 = beside(gate["decay"], gate["decay"])
        pairs = nt(keys_low, keys_low) * gate["decays"]
        scores = nt_fine(query, keys) * decay2
        state = states[c]
        new = news[pl.ds(two, NH * T), :]
        inverse = invs[c]
        mixed = mixed_in[pl.ds(first, T), :]
        raw = proj[pl.ds(first, T), width:].astype(f32)
        normal, scale, zsig = head_gate(mixed, raw, None)
        incoming = grad_gated[pl.ds(first, T), :]
        passed = incoming * (raw * zsig)
        gain_grad = gain_grad + jnp.sum(passed * normal, axis=0, keepdims=True)
        grad_z = incoming * (normal * gain[0:1]) * (zsig * (1.0 + raw * (1.0 - zsig)))
        e = passed * gain[0:1]
        grad_mixed = scale * (e - normal * jnp.mean(e * normal, axis=-1, keepdims=True))
        gm = grad_mixed.astype(bf16)
        ended = (to_end * keys).astype(bf16)
        grad_low = state_grad.astype(bf16)
        grad_new = tn(scores, gm) + nn(ended, grad_low)
        grad_right = tn(inverse, grad_new)
        moved = b * grad_right
        next_grad = gate["whole"] * state_grad + tn(hd * query, gm) - tn(hd2 * keys, moved)
        grad_right_low, moved_low = grad_right.astype(bf16), moved.astype(bf16)
        grad_ended = nt(new, grad_low)
        grad_scores = nt(gm, new)
        grad_lower = jnp.where(gate["decays"] != 0.0, -nt(grad_right_low, new), 0.0)
        from_grad = nt(gm, state)
        scored = grad_scores * decay2
        grad_query = hd * from_grad + nn(scored, keys_low)
        paired = (b * grad_lower) * gate["decays"]
        keyed = nn(keys_low, state)
        grad_keys = (
            tn(scored, query_low) + to_end * grad_ended - hd2 * nt(moved_low, state)
            + nn(paired, keys_low) + tn(paired, keys_low)
        )
        lower_pairs = grad_lower * pairs
        grad_b = jnp.sum(grad_right * (values - hd2 * keyed), axis=-1, keepdims=True) + jnp.sum(
            lower_pairs, axis=-1, keepdims=True
        )
        four = b * lower_pairs
        both = grad_scores * scores
        joint = (four[:T, :T] + four[:T, T:]) + (four[T:, :T] + four[T:, T:]) + (both[:, :T] + both[:, T:])
        crossing = jnp.sum(jnp.where(under, nn_exact(upper, joint), 0.0), axis=-1, keepdims=True)
        start_part = -hd2 * jnp.sum(moved * keyed, axis=-1, keepdims=True)
        start_part = start_part[:T] + start_part[T:] + hd * jnp.sum(query * from_grad, axis=-1, keepdims=True)
        end_part = to_end * jnp.sum(grad_ended * keys, axis=-1, keepdims=True)
        end_part = end_part[:T] + end_part[T:]
        sums_in = jnp.where(lane == 0, start_part, jnp.where(lane == 1, end_part, 0.0))
        after = nn_exact(upper, sums_in)
        before = nn_exact(under.astype(bf16), sums_in)
        whole_part = gate["whole"] * jnp.sum(state_grad * state.astype(f32), keepdims=True)
        grad_gate = crossing + after[:, 0:1] + before[:, 1:2] + whole_part
        beta = gate["beta"]
        grad_beta = jnp.where(lane == 0, grad_b[:T], grad_b[T:]) * (beta * (1.0 - 0.5 * beta))
        grad_decay = -grad_gate * consts[1:2] * sigmoid(gate["shifted"])
        grad_small = jnp.where(lane < 2, grad_beta, jnp.where(lane == 2, grad_decay, 0.0))
        gate_sums = gate_sums + stack2(
            jnp.sum(grad_small, axis=0, keepdims=True),
            jnp.sum(jnp.where(lane == 2, grad_gate * -softplus(gate["shifted"]), 0.0), axis=0, keepdims=True),
        )
        high, low = halves(grad_small)
        gp[pl.ds(first, T), GROUPS * HD :] = (high.astype(f32) + pltpu.roll(low.astype(f32), 3, 1)).astype(bf16)
        gp[pl.ds(first, T), width : GROUPS * HD] = grad_z.astype(bf16)
        projected_out = jnp.sum(keys * grad_keys, axis=-1, keepdims=True)
        grad_raw = (grad_keys - keys * projected_out) * scales
        slope = sig * (1.0 + conv * (1.0 - sig))
        grad_active = jnp.concatenate([grad_query, grad_raw[:T], grad_raw[T:], moved[:T], moved[T:]], axis=1)
        grad_conv = grad_active * slope
        after_block = stack2(grad_conv, gbuf[...])
        gbuf[...] = grad_conv[:8]
        position = first + lax.broadcasted_iota(jnp.int32, (T, 1), 0)
        total = grad_conv * taps[CONV - 1 : CONV]
        taps_grads = [None] * CONV
        taps_grads[CONV - 1] = jnp.sum(grad_conv * block[8:], axis=0, keepdims=True)
        for lag in range(1, CONV):
            same = (doc_at(starts, position + lag) == gate["docs"][0]).astype(f32)
            total = total + after_block[lag : lag + T] * (taps[CONV - 1 - lag : CONV - lag] * same)
            same = (gate["docs"][lag] == gate["docs"][0]).astype(f32)
            taps_grads[CONV - 1 - lag] = jnp.sum(
                grad_conv * (block[8 - lag : 8 - lag + T] * same), axis=0, keepdims=True
            )
        gp[pl.ds(first, T), :width] = total.astype(bf16)
        gconv_w[...] += jnp.concatenate(taps_grads, axis=0)
        return next_grad, gain_grad, gate_sums

    gconv_w[...] = jnp.zeros(gconv_w.shape, f32)
    _, gain_grad, gate_sums = lax.fori_loop(
        0, count, turn, (jnp.zeros((HD, HD), f32), jnp.zeros((1, HD), f32), jnp.zeros((2, HD), f32))
    )
    sums[...] = jnp.concatenate([gain_grad, gate_sums, jnp.zeros((5, HD), f32)], axis=0)


VMEM = pl.BlockSpec(memory_space=pltpu.VMEM)
SMEM = pl.BlockSpec(memory_space=pltpu.SMEM)
LIMIT = 56 * 1024 * 1024


def run_forward(T, lengths, proj, small, taps, consts, gain):
    rows = proj.shape[0]
    count = rows // T
    shape = jax.ShapeDtypeStruct
    return pl.pallas_call(
        functools.partial(forward_kernel, T, 4 if count % 4 == 0 else 1),
        out_shape=(
            shape((rows, HD), bf16), shape((rows, HD), f32), shape((count, HD, HD), bf16),
            shape((NH * rows, HD), bf16), shape((count, NH * T, NH * T), bf16),
        ),
        in_specs=[SMEM] + [VMEM] * 5,
        out_specs=[VMEM] * 5,
        scratch_shapes=[
            pltpu.VMEM((rows + 8, MIXED * HD), f32), pltpu.VMEM((NH * rows, HD), f32),
            pltpu.VMEM((NH * rows, HD), bf16), pltpu.VMEM((rows, HD), bf16), pltpu.VMEM((rows, NH * T), bf16),
            pltpu.VMEM((NH * rows, HD), bf16), pltpu.VMEM((rows, HD), f32),
        ],
        compiler_params=pltpu.CompilerParams(vmem_limit_bytes=LIMIT),
        name="mixer_forward",
    )(lengths, proj, small, taps, consts, gain)


def run_backward(T, lengths, proj, small, taps, consts, gain, mixed, states, news, invs, grad_gated):
    rows = proj.shape[0]
    shape = jax.ShapeDtypeStruct
    return pl.pallas_call(
        functools.partial(backward_kernel, T),
        out_shape=(
            shape((rows, (GROUPS + 1) * HD), bf16), shape((CONV, MIXED * HD), f32), shape((8, HD), f32),
        ),
        in_specs=[SMEM] + [VMEM] * 10,
        out_specs=[VMEM] * 3,
        scratch_shapes=[
            pltpu.VMEM((rows + 8, MIXED * HD), f32), pltpu.VMEM((8, MIXED * HD), f32),
        ],
        compiler_params=pltpu.CompilerParams(vmem_limit_bytes=LIMIT),
        name="mixer_backward",
    )(lengths, proj, small, taps, consts, gain, mixed, states, news, invs, grad_gated)


def norm_scale(values):
    return lax.rsqrt(jnp.mean(values * values, axis=-1, keepdims=True) + EPS)


def norm_back(values, scale, gain, grad):
    normal = values * scale
    e = grad * gain
    return scale * (e - normal * jnp.mean(e * normal, axis=-1, keepdims=True)), jnp.sum(grad * normal, axis=0)


def take(array, start, size, axis):
    return lax.dynamic_slice_in_dim(array, start, size, axis)


def mm(a, b, dims="ij,jk->ik"):
    return jnp.einsum(dims, a, b, preferred_element_type=f32)


def on_device(tokens, grad_out, doc_lengths, gain_in, in_weight, small_weight, gate_bias, decay_rate, conv_weight,
              gain_head, out_weight, gain_mid, gate_up_weight, down_weight):
    seq, stream = lax.axis_size("seq"), lax.axis_size("stream")
    s = lax.axis_index("seq")
    rep = max(1, seq // H)
    head, part = s // rep, s % rep
    T = tokens.shape[1]
    rows = D // seq
    piece = D // (seq * stream)
    shard = FF // seq

    values = tokens[0].astype(f32)
    scale_in = norm_scale(values)
    normed = (values * scale_in * gain_in).astype(bf16)
    normed_all = lax.all_gather(normed, "seq", tiled=True)
    out_all = lax.all_gather(grad_out[0], "seq", tiled=True)

    w_head = take(in_weight.reshape(D, GROUPS, H, HD), head, 1, 2).reshape(D, GROUPS * HD)
    s_head = take(small_weight.reshape(D, NH + 1, H), head, 1, 2).reshape(D, NH + 1)
    s_high, s_low = halves(s_head)
    s_lowest = (s_head - s_high.astype(f32) - s_low.astype(f32)).astype(bf16)
    s_wide = jnp.pad(jnp.concatenate([s_high, s_low, s_lowest], axis=1), ((0, 0), (0, HD - 3 * (NH + 1))))
    taps = take(conv_weight.reshape(CONV, MIXED, H, HD), head, 1, 2).reshape(CONV, MIXED * HD)
    consts = jnp.zeros((8, HD), f32).at[0, 2].set(gate_bias[head]).at[1, 2].set(decay_rate[head])
    gain = gain_head.reshape(1, HD)

    proj = mm(normed_all, w_head).astype(bf16)
    small = mm(normed_all, s_wide)
    gated_h, mixed, states, news, invs = run_forward(T, doc_lengths, proj, small, taps, consts, gain)

    gated = lax.all_to_all(gated_h.reshape(seq, T, HD), "seq", 0, 0)[::rep]
    gated = jnp.transpose(gated, (1, 0, 2)).reshape(T, D)
    residual = values + mm(gated, out_weight)
    scale_mid = norm_scale(residual)
    normed_mid = (residual * scale_mid * gain_mid).astype(bf16)
    mid_all = lax.all_gather(normed_mid, "seq", tiled=True)

    def feed(rows_in, cotangent, w_gate, w_up, w_down):
        gate, up = mm(rows_in, w_gate), mm(rows_in, w_up)
        sig = jax.nn.sigmoid(gate)
        hidden = (gate * sig * up).astype(bf16)
        grad_hidden = mm(cotangent, w_down, "ij,kj->ik")
        grad_gate = (grad_hidden * up * (sig * (1.0 + gate * (1.0 - sig)))).astype(bf16)
        return hidden, grad_gate, (grad_hidden * (gate * sig)).astype(bf16)

    hidden, g_gate, g_up = feed(normed_mid, grad_out[0], gate_up_weight[:, :FF], gate_up_weight[:, FF:], down_weight)
    result = (residual + mm(hidden, down_weight)).astype(bf16)
    grad_mid = mm(g_gate, gate_up_weight[:, :FF], "ij,kj->ik") + mm(g_up, gate_up_weight[:, FF:], "ij,kj->ik")
    back_mid, grad_gain_mid = norm_back(residual, scale_mid, gain_mid, grad_mid)
    grad_residual = grad_out[0].astype(f32) + back_mid
    low_all = lax.all_gather(grad_residual.astype(bf16), "seq", tiled=True)

    at = s * shard
    w_down = take(down_weight, at, shard, 0)
    hidden_s, g_gate_s, g_up_s = feed(
        mid_all, out_all, take(gate_up_weight, at, shard, 1), take(gate_up_weight, FF + at, shard, 1), w_down
    )
    grad_down = lax.psum_scatter(
        mm(hidden_s, out_all, "ji,jk->ik").astype(bf16), "stream", scatter_dimension=0, tiled=True
    )
    up_part = jnp.stack([mm(mid_all, g_gate_s, "ji,jk->ik"), mm(mid_all, g_up_s, "ji,jk->ik")], axis=1).astype(bf16)
    up_part = jnp.swapaxes(up_part.reshape(seq, stream, piece, 2 * shard), 0, 1)
    up_part = lax.psum_scatter(up_part, "stream", scatter_dimension=0, tiled=False)
    up_part = lax.all_to_all(up_part, "seq", 0, 0)
    grad_gate_up = jnp.transpose(up_part.reshape(seq, piece, 2, shard), (1, 2, 0, 3)).reshape(piece, 2 * FF)

    w_out = take(out_weight, head * HD, HD, 0)
    grad_gated = mm(low_all, w_out, "ij,kj->ik")
    mine = take(gated_h, part * rows, rows, 1) if rep > 1 else gated_h
    grad_out_weight = lax.psum_scatter(
        mm(mine, low_all, "ji,jk->ik").astype(bf16), "stream", scatter_dimension=0, tiled=True
    )
    gp, grad_taps, sums = run_backward(
        T, doc_lengths, proj, small, taps, consts, gain, mixed, states, news, invs, grad_gated
    )
    back = lax.all_to_all(gp.reshape(seq, T, (GROUPS + 1) * HD), "seq", 0, 0)[::rep]
    in_part = mm(normed_all, gp, "ji,jk->ik")
    tail = in_part[:, GROUPS * HD :]
    grad_small_h = tail[:, : NH + 1] + tail[:, NH + 1 : 2 * (NH + 1)]
    in_part = jnp.swapaxes(in_part[:, : GROUPS * HD].astype(bf16).reshape(seq, stream, piece, GROUPS * HD), 0, 1)
    in_part = lax.psum_scatter(in_part, "stream", scatter_dimension=0, tiled=False)
    in_part = lax.all_to_all(in_part, "seq", 0, 0)[::rep]
    grad_in_weight = jnp.transpose(in_part.reshape(H, piece, GROUPS, HD), (1, 2, 0, 3)).reshape(piece, GROUPS * D)

    grad_proj = jnp.transpose(back[:, :, : GROUPS * HD].reshape(H, T, GROUPS, HD), (1, 2, 0, 3)).reshape(T, GROUPS * D)
    grad_logits = back[:, :, GROUPS * HD :].astype(f32)
    grad_logits = grad_logits[:, :, : NH + 1] + grad_logits[:, :, NH + 1 : 2 * (NH + 1)]
    grad_logits = jnp.transpose(grad_logits, (1, 2, 0)).reshape(T, (NH + 1) * H)
    grad_normed = mm(grad_proj, in_weight, "ij,kj->ik") + jnp.einsum(
        "ij,kj->ik", grad_logits, small_weight, precision=lax.Precision.HIGHEST
    )
    back_in, grad_gain_in = norm_back(values, scale_in, gain_in, grad_normed)
    grad_input = grad_residual + back_in

    own = (part == 0).astype(f32)
    flat = jnp.concatenate(
        [
            grad_gain_in, grad_gain_mid,
            own * jnp.concatenate([sums[0], sums[1], sums[2], grad_small_h.T.reshape(-1), grad_taps.reshape(-1)]),
        ]
    )
    every = lax.all_gather(flat, ("seq", "stream"))
    lanes = [jnp.sum(every[:, i : i + D], axis=0) for i in (0, D)]
    every = jnp.sum(every[:, 2 * D :].reshape(seq, stream, -1), axis=1).reshape(H, rep, -1).sum(axis=1)
    heads = every[:, : 3 * HD].reshape(H, 3, HD)
    at = 3 * HD
    grad_small = jnp.transpose(every[:, at : at + 3 * D].reshape(H, NH + 1, D), (2, 1, 0)).reshape(D, (NH + 1) * H)
    at += 3 * D
    grad_conv = jnp.transpose(every[:, at:].reshape(H, CONV, MIXED, HD), (1, 2, 0, 3)).reshape(CONV, MIXED * D)
    return (
        result[None], grad_input[None], lanes[0], grad_in_weight.astype(f32), grad_small, heads[:, 1, 2],
        heads[:, 2, 2], grad_conv, jnp.sum(heads[:, 0], axis=0), grad_out_weight.astype(f32), lanes[1],
        grad_gate_up.astype(f32), grad_down.astype(f32),
    )


def solution(mesh):
    rows, whole, split = P("stream", "seq", None), P(), P(("seq", "stream"), None)
    return jax.shard_map(
        on_device,
        mesh=mesh,
        in_specs=(rows, rows, P("stream", None)) + (whole,) * 11,
        out_specs=(rows, rows, whole, split, whole, whole, whole, whole, whole, split, whole, split, split),
        check_vma=False,
    )
```

```python
import functools

import jax
import jax.numpy as jnp
from jax import lax
from jax.experimental import pallas as pl
from jax.experimental.pallas import tpu as pltpu
from jax.sharding import PartitionSpec as P

D = 1024
H = 8
HD = 128
FF = 2816
NH = 2
CONV = 4
GROUPS = 2 + 2 * NH
MIXED = GROUPS - 1
SMALL = NH + 1
DOCS = 8
TILE = 256
EPS = 1e-06

f32 = jnp.float32
bf16 = jnp.bfloat16
MESH = pl.DeviceIdType.MESH
DMA = pltpu.SemaphoreType.DMA
VMEM = pl.BlockSpec(memory_space=pltpu.VMEM)
SMEM = pl.BlockSpec(memory_space=pltpu.SMEM)
ANY = pl.BlockSpec(memory_space=pl.ANY)
LIMIT = 56 * 1024 * 1024
shape = jax.ShapeDtypeStruct


def dot(a, b, dims):
    if isinstance(a, tuple) and isinstance(b, tuple):
        return dot(a[0], b[0], dims) + (dot(a[0], b[1], dims) + dot(a[1], b[0], dims))
    if isinstance(a, tuple):
        return dot(a[0], b, dims) + dot(a[1], b, dims)
    if isinstance(b, tuple):
        return dot(a, b[0], dims) + dot(a, b[1], dims)
    return lax.dot_general(
        a.astype(bf16), b.astype(bf16), ((dims[:1], dims[1:]), ((), ())), preferred_element_type=f32
    )


def nn(a, b):
    return dot(a, b, (1, 0))


def nt(a, b):
    return dot(a, b, (1, 1))


def tn(a, b):
    return dot(a, b, (0, 0))


def halves(x):
    high = x.astype(bf16)
    return high, (x - high.astype(f32)).astype(bf16)


def thirds(x):
    high, low = halves(x)
    return high, low, (x - high.astype(f32) - low.astype(f32)).astype(bf16)


def keep(ref, at, x):
    ref[0, at], ref[1, at] = halves(x)


def kept(ref, at):
    return ref[0, at], ref[1, at]


def nn_exact(ones, x):
    high, low, lowest = thirds(x)
    return nn(ones, high) + (nn(ones, low) + nn(ones, lowest))


def sigmoid(x):
    return 1.0 / (1.0 + jnp.exp(-x))


def softplus(x):
    return jnp.maximum(x, 0.0) + jnp.log(1.0 + jnp.exp(-jnp.abs(x)))


def norm_scale(values):
    return lax.rsqrt(jnp.mean(values * values, axis=-1, keepdims=True) + EPS)


def norm_back(values, scale, gain, grad):
    normal = values * scale
    e = grad * gain
    back = scale * (e - normal * jnp.mean(e * normal, axis=-1, keepdims=True))
    return back, jnp.sum(grad * normal, axis=0, keepdims=True)


def iota(dims, axis):
    return lax.broadcasted_iota(jnp.int32, dims, axis)


def doc_at(starts, positions):
    total = jnp.full(positions.shape, -1, jnp.int32)
    for start in starts:
        total = total + (start <= positions).astype(jnp.int32)
    return total


def doc_starts(lengths_ref):
    starts, at = [], jnp.int32(0)
    for j in range(DOCS):
        starts.append(at)
        at = at + lengths_ref[0, j]
    return starts


def stack2(a, b):
    return jnp.concatenate([a, b], axis=0)


def beside(a, b):
    return jnp.concatenate([a, b], axis=1)


def quad(a, b, c, d):
    return stack2(beside(a, b), beside(c, d))


def rows_of(i, size):
    return pl.ds(pl.multiple_of(i * size, size), size)


def greet(axis, peers):
    barrier = pltpu.get_barrier_semaphore()
    for peer in peers:
        pl.semaphore_signal(barrier, inc=1, device_id={axis: peer}, device_id_type=MESH)
    return lambda: pl.semaphore_wait(barrier, len(peers))


def remote(src, dst, send, receive, axis, peer):
    return pltpu.make_async_remote_copy(src, dst, send, receive, device_id={axis: peer}, device_id_type=MESH)


class Gather:
    def __init__(self, n, T, src, dst, sems):
        self.n, self.T, self.src, self.dst = n, T, src, dst
        self.ss, self.rs, self.fs, self.fr = sems
        self.me = lax.axis_index("seq")
        self.sib = self.me + 1 - 2 * lax.rem(self.me, 2)

    def at(self, device):
        return self.dst.at[rows_of(device, self.T)]

    def direct(self, k):
        peer = self.sib if k == 0 else lax.rem(self.me + 2 * k, self.n)
        return remote(self.src, self.at(self.me), self.ss.at[k], self.rs.at[k], "seq", peer)

    def passed(self, k):
        block = self.at(lax.rem(self.me - 2 * k + self.n, self.n))
        return remote(block, block, self.fs.at[k], self.fr.at[k], "seq", self.sib)

    def start(self):
        for k in (*range(1, self.n // 2), 0):
            self.direct(k).start()

    def forward(self):
        for k in range(1, self.n // 2):
            self.direct(k).wait_recv()
            self.passed(k).start()

    def finish(self):
        for k in range(self.n // 2):
            self.direct(k).wait_send()
            if k:
                self.passed(k).wait_send()


def gather_sems(n):
    return [DMA((n // 2,)) for _ in range(4)]


def conv_of(block, taps, docs, T):
    total = block[8:] * taps[CONV - 1 : CONV]
    for lag in range(1, CONV):
        same = (docs[0] == docs[lag]).astype(f32)
        total = total + block[8 - lag : 8 - lag + T] * (taps[CONV - 1 - lag : CONV - lag] * same)
    return total


def chunk_gates(logits, bias, rate, starts, first, T):
    lane = iota((T, HD), 1)
    shifted = logits + bias
    gate = -rate * softplus(shifted)
    place_i, place_j = iota((T, T), 0), iota((T, T), 1)
    lower = place_j <= place_i
    cumul = nn_exact(lower.astype(bf16), jnp.where(lane == NH, gate, 0.0))
    beta = 2.0 * sigmoid(logits)
    b0, b1 = beta[:, 0:1], beta[:, 1:2]
    g = cumul[:, NH : NH + 1]
    g_row = jnp.transpose(cumul)[NH : NH + 1, :]
    g_last = cumul[T - 1 : T, NH : NH + 1]
    position = first + iota((T, 1), 0)
    docs = [doc_at(starts, position - lag) for lag in range(CONV)]
    doc = docs[0]
    doc_row = doc_at(starts, first + iota((1, T), 1))
    doc_before = doc_at(starts, jnp.full((1, 1), first - 1, jnp.int32))
    doc_last = doc_at(starts, jnp.full((1, 1), first + (T - 1), jnp.int32))
    joined = lower & (doc == doc_row)
    decay = jnp.where(joined, jnp.exp(jnp.where(joined, g - g_row, 0.0)), 0.0)
    strict = jnp.where(place_i == place_j, 0.0, decay)
    from_start = jnp.exp(g) * (doc == doc_before).astype(f32)
    to_end = jnp.exp(jnp.minimum(g_last - g, 0.0)) * (doc == doc_last).astype(f32)
    whole = jnp.exp(g_last) * (doc_last == doc_before).astype(f32)
    return dict(
        shifted=shifted, beta=beta, b=stack2(b0, b1), docs=docs, decay=decay,
        decays=quad(strict, strict, decay, strict), hd=from_start, hd2=stack2(from_start, from_start),
        to_end=stack2(to_end, to_end), whole=whole,
    )


def key_scale(raw):
    return lax.rsqrt(jnp.sum(raw * raw, axis=-1, keepdims=True) + EPS)


def chunk_inputs(block, taps, docs, T):
    conv = conv_of(block, taps, docs, T)
    sig = sigmoid(conv)
    active = conv * sig
    cut = [active[:, i * HD : (i + 1) * HD] for i in range(MIXED)]
    scales = (key_scale(cut[1]), key_scale(cut[2]))
    keys = stack2(cut[1] * scales[0], cut[2] * scales[1])
    values = stack2(cut[3], cut[4])
    return conv, sig, cut[0], keys, values, stack2(*scales)


def inverses(lowers, T):
    size = NH * T
    row, col = iota((size, size), 0), iota((size, size), 1)
    differ = (row & (T - 1)) ^ (col & (T - 1))
    eye = (row == col).astype(f32)
    found = [jnp.where(row == col, 1.0, jnp.where(differ == 0, -a, 0.0)) for a in lowers]
    step = 1
    while step < T:
        level = (differ >= step) & (differ < 2 * step)
        parts = [nn(jnp.where(level, a, 0.0), x) for a, x in zip(lowers, found)]
        found = [x - nn(x, part) for x, part in zip(found, parts)]
        step *= 2
    a_cut = [halves(a) for a in lowers]
    x_cut = [halves(x) for x in found]
    errors = [
        eye - x - (nn(a[0], xc[0]) + (nn(a[0], xc[1]) + nn(a[1], xc[0])))
        for a, x, xc in zip(a_cut, found, x_cut)
    ]
    return [x + nn(xc[0], e) for x, xc, e in zip(found, x_cut, errors)]


def head_gate(mixed, raw):
    scale = norm_scale(mixed)
    return mixed * scale, scale, sigmoid(raw)


def head_taps(taps_ref, head):
    cuts = [taps_ref[:, pl.ds(pl.multiple_of(i * D + head * HD, HD), HD)] for i in range(MIXED)]
    return jnp.concatenate(cuts, axis=1)


def intra_turn(T, per, starts, bias, rate, taps, small, xbuf, invs, ubuf, wbuf, qbuf, pbuf, dbuf, gates, turn, _):
    held, lowers = [], []
    for i in range(per):
        c = turn * per + i
        first = pl.multiple_of(c * T, T)
        gate = chunk_gates(small[pl.ds(first, T), :], bias, rate, starts, first, T)
        block = xbuf[pl.ds(first, T + 8), :]
        conv, sig, query, keys, values, scales = chunk_inputs(block, taps, gate["docs"], T)
        key_pair = halves(keys)
        lowers.append(gate["b"] * (nt(key_pair, key_pair) * gate["decays"]))
        held.append((c, gate, query, keys, key_pair, values))
    found = inverses(lowers, T)
    for (c, gate, query, keys, key_pair, values), inverse in zip(held, found):
        at, two = rows_of(c, T), rows_of(c, NH * T)
        pair = halves(inverse)
        invs[0, c], invs[1, c] = pair
        both = nn(pair, halves(gate["b"] * beside(values, gate["hd2"] * keys)))
        ubuf[two, :] = both[:, :HD]
        keep(wbuf, two, both[:, HD:])
        query_pair = halves(query)
        qbuf[0, at], qbuf[1, at] = query_pair
        keep(pbuf, at, nt(query_pair, key_pair) * beside(gate["decay"], gate["decay"]))
        keep(dbuf, two, gate["to_end"] * keys)
        gates[at, :] = jnp.where(iota((T, HD), 1) == 0, gate["hd"], gate["whole"])
    return 0


def across_turn(T, gain, proj, mixed_out, states, news, head_rows, ubuf, wbuf, qbuf, pbuf, dbuf, gates, done, c, state):
    at, two = rows_of(c, T), rows_of(c, NH * T)
    state_pair = halves(state)
    states[0, c], states[1, c] = state_pair
    new = ubuf[two, :] - nn(kept(wbuf, two), state_pair)
    new_pair = halves(new)
    news[0, two], news[1, two] = new_pair
    gate = gates[at, :]
    mixed = gate[:, 0:1] * nn(kept(qbuf, at), state_pair) + nn(kept(pbuf, at), new_pair)
    mixed_out[at, :] = mixed
    raw = proj[at, MIXED * HD :].astype(f32)
    normal, _, sig = head_gate(mixed, raw)
    head_rows[at, :] = ((normal * gain[...]) * (raw * sig)).astype(bf16)
    done(c)
    return gate[0:1, 1:2] * state + tn(kept(dbuf, two), new_pair)


def forward_kernel(
    n, rep, T, per, lengths, bias_ref, rate_ref, tokens, cotangent, gain_in, w_in, w_small, taps_ref, gain,
    gated, normed, out_all, proj, small, mixed_out, states, news, invs, head_rows,
    own, w_head, w_wide, xbuf, ubuf, wbuf, qbuf, pbuf, dbuf, gates,
    w_sems, own_sem, a_ss, a_rs, *sems,
):
    me = lax.axis_index("seq")
    head = me // rep
    wait_for_all = greet("seq", [lax.rem(me + k, n) for k in range(1, n)])
    width = MIXED * HD
    loads = [
        pltpu.make_async_copy(
            w_in.at[:, pl.ds(pl.multiple_of(i * D + head * HD, HD), HD)], w_head.at[:, i * HD : (i + 1) * HD], w_sems.at[i]
        )
        for i in range(GROUPS)
    ]
    for load in loads:
        load.start()
    values = tokens[...].astype(f32)
    own[...] = (values * norm_scale(values) * gain_in[...]).astype(bf16)
    local = pltpu.make_async_copy(own, normed.at[rows_of(me, T)], own_sem)
    local.start()
    wait_for_all()
    first_gather = Gather(n, T, own, normed, sems[:4])
    first_gather.start()
    second_gather = Gather(n, T, cotangent, out_all, sems[4:8])

    starts = doc_starts(lengths)
    bias, rate = bias_ref[head], rate_ref[head]
    taps = head_taps(taps_ref, head)
    xbuf[0:8, :] = jnp.zeros((8, width), f32)
    w_wide[...] = jnp.zeros((D, HD), bf16)
    chosen = jnp.where((iota((D, SMALL * H), 1) & (H - 1)) == head, w_small[...], 0.0)
    for i, piece in enumerate(thirds(chosen)):
        w_wide[:, i * SMALL * H : (i + 1) * SMALL * H] = piece
    group = iota((HD, HD), 0) >> 3
    lane = iota((HD, HD), 1)
    picks = ((group == lane) | (group == lane + SMALL) | (group == lane + 2 * SMALL)) & (lane < SMALL)
    picks = picks.astype(bf16)
    for load in loads:
        load.wait()
    local.wait()
    for k in range(n // 2):
        if k == 1:
            first_gather.forward()
        if k:
            first_gather.passed(k).wait_recv()
        else:
            first_gather.direct(0).wait_recv()
        at = rows_of(lax.rem(me // 2 - k + n // 2, n // 2), 2 * T)
        block = normed[at, :]
        result = nn(block, w_head[...]).astype(bf16)
        proj[at, :] = result
        xbuf[pl.ds(pl.multiple_of(8 + lax.rem(me // 2 - k + n // 2, n // 2) * (2 * T), 8), 2 * T), :] = result[:, :width].astype(f32)
        raw = thirds(nn(block, w_wide[...]))
        small[at, :] = nn(raw[0], picks) + (nn(raw[1], picks) + nn(raw[2], picks))
    first_gather.finish()
    keep = pltpu.make_async_copy(cotangent, out_all.at[rows_of(me, T)], own_sem)
    keep.start()
    second_gather.start()

    intra = functools.partial(
        intra_turn, T, per, starts, bias, rate, taps, small, xbuf, invs, ubuf, wbuf, qbuf, pbuf, dbuf, gates
    )
    lax.fori_loop(0, n // per, intra, 0)
    second_gather.forward()
    column = pl.ds(pl.multiple_of(head * HD, HD), HD)

    def row_copy(c):
        return remote(head_rows.at[rows_of(c, T)], gated.at[:, column], a_ss.at[c], a_rs.at[head], "seq", c)

    def send_rows(c):
        @pl.when((c != me) & (lax.rem(me, rep) == 0))
        def _():
            row_copy(c).start()

    across = functools.partial(
        across_turn, T, gain, proj, mixed_out, states, news, head_rows, ubuf, wbuf, qbuf, pbuf, dbuf, gates, send_rows
    )
    lax.fori_loop(0, n, across, jnp.zeros((HD, HD), f32))

    @pl.when(lax.rem(me, rep) == 0)
    def _():
        mine = pltpu.make_async_copy(head_rows.at[rows_of(me, T)], gated.at[:, column], own_sem)
        keep.wait()
        mine.start()
        mine.wait()

    @pl.when(lax.rem(me, rep) != 0)
    def _():
        keep.wait()

    def settle(k, _):
        peer = lax.rem(me + k, n)

        @pl.when(lax.rem(me, rep) == 0)
        def _():
            row_copy(peer).wait_send()

        @pl.when(lax.rem(peer, rep) == 0)
        def _():
            source = peer // rep
            remote(
                head_rows.at[rows_of(me, T)], gated.at[:, pl.ds(pl.multiple_of(source * HD, HD), HD)],
                a_ss.at[peer], a_rs.at[source], "seq", peer,
            ).wait_recv()

        return 0

    lax.fori_loop(1, n, settle, 0)
    second_gather.direct(0).wait_recv()
    for k in range(1, n // 2):
        second_gather.passed(k).wait_recv()
    second_gather.finish()


def forward_scratch(n, T):
    rows = n * T
    return [
        pltpu.VMEM((rows + 8, MIXED * HD), f32), pltpu.VMEM((NH * rows, HD), f32),
        pltpu.VMEM((2, NH * rows, HD), bf16), pltpu.VMEM((2, rows, HD), bf16), pltpu.VMEM((2, rows, NH * T), bf16),
        pltpu.VMEM((2, NH * rows, HD), bf16), pltpu.VMEM((rows, HD), f32),
    ]


def run_forward(n, rep, T, lengths, bias, rate, tokens, cotangent, gain_in, w_in, w_small, taps, gain):
    rows = n * T
    return pl.pallas_call(
        functools.partial(forward_kernel, n, rep, T, 4),
        out_shape=(
            shape((T, D), bf16), shape((rows, D), bf16), shape((rows, D), bf16), shape((rows, GROUPS * HD), bf16),
            shape((rows, HD), f32), shape((rows, HD), f32), shape((2, n, HD, HD), bf16), shape((2, NH * rows, HD), bf16),
            shape((2, n, NH * T, NH * T), bf16), shape((rows, HD), bf16),
        ),
        in_specs=[SMEM] * 3 + [VMEM, ANY, VMEM, ANY, VMEM, VMEM, VMEM],
        out_specs=[VMEM, VMEM, ANY] + [VMEM] * 7,
        scratch_shapes=[
            pltpu.VMEM((T, D), bf16), pltpu.VMEM((D, GROUPS * HD), bf16), pltpu.VMEM((D, HD), bf16),
            *forward_scratch(n, T),
            DMA((GROUPS,)), DMA, DMA((n,)), DMA((H,)), *gather_sems(n), *gather_sems(n),
        ],
        compiler_params=pltpu.CompilerParams(vmem_limit_bytes=LIMIT, collective_id=1, has_side_effects=True),
        name="mixer_forward",
    )(lengths, bias, rate, tokens, cotangent, gain_in, w_in, w_small, taps, gain)


def feed_kernel(
    n, T, steps, tokens, gated, cotangent, w_out, gain_mid, w_gate, w_up, w_down,
    result, grad_residual, mid_all, gain_grad, residual, middle, total, grad_mid, own_sem, *sems,
):
    step = pl.program_id(0)
    me = lax.axis_index("seq")
    gather = Gather(n, T, middle, mid_all, sems)
    local = pltpu.make_async_copy(middle, mid_all.at[rows_of(me, T)], own_sem)

    @pl.when(step == 0)
    def _():
        peers = [gather.sib] + [lax.rem(me + 2 * k, n) for k in range(1, n // 2)]
        wait_for_all = greet("seq", peers)
        found = tokens[...].astype(f32) + nn(gated[...], w_out[...])
        residual[...] = found
        middle[...] = (found * norm_scale(found) * gain_mid[...]).astype(bf16)
        total[...] = found
        grad_mid[...] = jnp.zeros((T, D), f32)
        wait_for_all()
        gather.start()
        local.start()

    gate, up = nn(middle[...], w_gate[...]), nn(middle[...], w_up[...])
    sig = sigmoid(gate)
    silu = gate * sig
    hidden = (silu * up).astype(bf16)
    total[...] += nn(hidden, w_down[...])
    grad_hidden = nt(cotangent[...], w_down[...])
    grad_gate = (grad_hidden * up * (sig * (1.0 + gate * (1.0 - sig)))).astype(bf16)
    grad_up = (grad_hidden * silu).astype(bf16)
    grad_mid[...] += nt(grad_gate, w_gate[...]) + nt(grad_up, w_up[...])

    @pl.when(step == steps - 2)
    def _():
        gather.forward()

    @pl.when(step == steps - 1)
    def _():
        result[...] = total[...].astype(bf16)
        values = residual[...]
        back, gain_part = norm_back(values, norm_scale(values), gain_mid[...], grad_mid[...])
        gain_grad[...] = gain_part
        grad_residual[...] = cotangent[...].astype(f32) + back
        gather.direct(0).wait_recv()
        for k in range(1, n // 2):
            gather.passed(k).wait_recv()
        gather.finish()
        local.wait()


def run_feed(n, T, tokens, gated, cotangent, w_out, gain_mid, w_gate_up, w_down):
    steps = FF // TILE
    fixed = lambda *dims: pl.BlockSpec(dims, lambda i: (0, 0))
    return pl.pallas_call(
        functools.partial(feed_kernel, n, T, steps),
        grid=(steps,),
        out_shape=(shape((T, D), bf16), shape((T, D), f32), shape((n * T, D), bf16), shape((1, D), f32)),
        in_specs=[
            fixed(T, D), fixed(T, D), fixed(T, D), fixed(D, D), fixed(1, D),
            pl.BlockSpec((D, TILE), lambda i: (0, i)), pl.BlockSpec((D, TILE), lambda i: (0, i + FF // TILE)),
            pl.BlockSpec((TILE, D), lambda i: (i, 0)),
        ],
        out_specs=[fixed(T, D), fixed(T, D), ANY, fixed(1, D)],
        scratch_shapes=[
            pltpu.VMEM((T, D), f32), pltpu.VMEM((T, D), bf16), pltpu.VMEM((T, D), f32), pltpu.VMEM((T, D), f32),
            DMA, *gather_sems(n),
        ],
        compiler_params=pltpu.CompilerParams(vmem_limit_bytes=LIMIT, collective_id=2, has_side_effects=True),
        name="feed_forward",
    )(tokens, gated, cotangent, w_out, gain_mid, w_gate_up, w_gate_up, w_down)


def store_pieces(out, part, first, stream, piece):
    for i in range(part.shape[0] // piece):
        at = first // piece + i
        out[at % stream, at // stream] = part[i * piece : (i + 1) * piece].astype(bf16)


def backward_turn(
    n, T, starts, bias, rate, taps, gain, incoming_of, proj, small, mixed_in, states, news, invs,
    gp, grad_small, gconv_w, staged, xbuf, halo, gates_sum, grad_state, done, k, _,
):
    width = MIXED * HD
    lane = iota((T, HD), 1)
    place_i, place_j = iota((T, T), 0), iota((T, T), 1)
    upper = (place_j >= place_i).astype(bf16)
    under = place_j < place_i
    c = n - 1 - k
    first = pl.multiple_of(c * T, T)
    at, two = rows_of(c, T), rows_of(c, NH * T)
    gate = chunk_gates(small[at, :], bias, rate, starts, first, T)
    block = xbuf[pl.ds(first, T + 8), :]
    conv, sig, query, keys, values, scales = chunk_inputs(block, taps, gate["docs"], T)
    key_pair, query_pair = halves(keys), halves(query)
    b, hd, hd2, to_end = gate["b"], gate["hd"], gate["hd2"], gate["to_end"]
    decay2 = beside(gate["decay"], gate["decay"])
    pairs = nt(key_pair, key_pair) * gate["decays"]
    scores = nt(query_pair, key_pair) * decay2
    state = (states[0, c], states[1, c])
    state_grad = grad_state[...]
    new = kept(news, two)
    inverse = (invs[0, c], invs[1, c])
    mixed = mixed_in[at, :]
    raw = proj[at, width:].astype(f32)
    normal, scale, zsig = head_gate(mixed, raw)
    incoming = incoming_of(at)
    passed = incoming * (raw * zsig)
    gates_sum[0:1, :] += jnp.sum(passed * normal, axis=0, keepdims=True)
    grad_z = incoming * (normal * gain[...]) * (zsig * (1.0 + raw * (1.0 - zsig)))
    e = passed * gain[...]
    grad_mixed = scale * (e - normal * jnp.mean(e * normal, axis=-1, keepdims=True))
    gm = halves(grad_mixed)
    ended = halves(to_end * keys)
    grad_pair = halves(state_grad)
    grad_new = tn(halves(scores), gm) + nn(ended, grad_pair)
    grad_right = tn(inverse, halves(grad_new))
    moved = b * grad_right
    grad_state[...] = gate["whole"] * state_grad + tn(halves(hd * query), gm) - tn(halves(hd2 * keys), halves(moved))
    grad_ended = nt(new, grad_pair)
    grad_scores = nt(gm, new)
    grad_lower = jnp.where(gate["decays"] != 0.0, -nt(halves(grad_right), new), 0.0)
    from_grad = nt(gm, state)
    scored = grad_scores * decay2
    grad_query = hd * from_grad + nn(scored, key_pair[0])
    paired = (b * grad_lower) * gate["decays"]
    keyed = nn(key_pair, state)
    grad_keys = (
        tn(scored, query_pair[0]) + to_end * grad_ended - hd2 * nt(moved, state[0])
        + nn(paired, key_pair[0]) + tn(paired, key_pair[0])
    )
    lower_pairs = grad_lower * pairs
    grad_b = jnp.sum(grad_right * (values - hd2 * keyed), axis=-1, keepdims=True) + jnp.sum(
        lower_pairs, axis=-1, keepdims=True
    )
    four = b * lower_pairs
    both = grad_scores * scores
    joint = (four[:T, :T] + four[:T, T:]) + (four[T:, :T] + four[T:, T:]) + (both[:, :T] + both[:, T:])
    crossing = jnp.sum(jnp.where(under, nn_exact(upper, joint), 0.0), axis=-1, keepdims=True)
    start_part = -hd2 * jnp.sum(moved * keyed, axis=-1, keepdims=True)
    start_part = start_part[:T] + start_part[T:] + hd * jnp.sum(query * from_grad, axis=-1, keepdims=True)
    end_part = to_end * jnp.sum(grad_ended * keys, axis=-1, keepdims=True)
    end_part = end_part[:T] + end_part[T:]
    sums_in = jnp.where(lane == 0, start_part, jnp.where(lane == 1, end_part, 0.0))
    after = nn_exact(upper, sums_in)
    before = nn_exact(under.astype(bf16), sums_in)
    whole_part = gate["whole"] * jnp.sum(state_grad * (state[0].astype(f32) + state[1].astype(f32)), keepdims=True)
    grad_gate = crossing + after[:, 0:1] + before[:, 1:2] + whole_part
    beta = gate["beta"]
    grad_beta = jnp.where(lane == 0, grad_b[:T], grad_b[T:]) * (beta * (1.0 - 0.5 * beta))
    grad_decay = -grad_gate * rate * sigmoid(gate["shifted"])
    grad_logits = jnp.where(lane < NH, grad_beta, jnp.where(lane == NH, grad_decay, 0.0))
    gates_sum[1:2, :] += jnp.sum(grad_logits, axis=0, keepdims=True)
    gates_sum[2:3, :] += jnp.sum(
        jnp.where(lane == NH, grad_gate * -softplus(gate["shifted"]), 0.0), axis=0, keepdims=True
    )
    high, low_part = halves(grad_logits)
    grad_small[at, :] = (high.astype(f32) + pltpu.roll(low_part.astype(f32), SMALL, 1)).astype(bf16)
    projected_out = jnp.sum(keys * grad_keys, axis=-1, keepdims=True)
    grad_raw = (grad_keys - keys * projected_out) * scales
    slope = sig * (1.0 + conv * (1.0 - sig))
    grad_active = jnp.concatenate([grad_query, grad_raw[:T], grad_raw[T:], moved[:T], moved[T:]], axis=1)
    grad_conv = grad_active * slope
    after_block = stack2(grad_conv, halo[...])
    halo[...] = grad_conv[:8]
    position = first + iota((T, 1), 0)
    total = grad_conv * taps[CONV - 1 : CONV]
    taps_grads = [None] * CONV
    taps_grads[CONV - 1] = jnp.sum(grad_conv * block[8:], axis=0, keepdims=True)
    for lag in range(1, CONV):
        same = (doc_at(starts, position + lag) == gate["docs"][0]).astype(f32)
        total = total + after_block[lag : lag + T] * (taps[CONV - 1 - lag : CONV - lag] * same)
        same = (gate["docs"][lag] == gate["docs"][0]).astype(f32)
        taps_grads[CONV - 1 - lag] = jnp.sum(
            grad_conv * (block[8 - lag : 8 - lag + T] * same), axis=0, keepdims=True
        )
    everything = beside(total, grad_z).astype(bf16)
    gp[at, :] = everything
    for i in range(GROUPS):
        staged[c, i] = everything[:, i * HD : (i + 1) * HD]
    gconv_w[...] += jnp.concatenate(taps_grads, axis=0)
    done(c)
    return 0


def exchange(own, arrived, k, send, receive, axis, me, size):
    peer = lax.rem(me + k, size)
    return remote(own.at[peer], arrived.at[k - 1], send.at[k - 1], receive.at[k - 1], axis, peer)


def scatter_to(own, arrived, k, send, receive, me, size):
    peer = lax.rem(me + k, size)
    return remote(own.at[peer], arrived.at[me], send.at[k - 1], receive.at[k - 1], "seq", peer)


def back_kernel(
    n, m, rep, T, piece, shard, wide,
    lengths, bias_ref, rate_ref, tokens, grad_residual, gain_in, gain_mid_grad, w_small, taps_ref, gain,
    mid_any, out_any, w_gate_up, w_down, w_out, proj_any, small_any, mixed_any, states_any, news_any, invs_any,
    normed_any, rows_any, w_in_any,
    grad_input, g_in, g_out, g_gate_up, g_down, g_gain_in, g_gain_mid, g_small, g_bias, g_rate, g_taps, g_gain_head,
    mid, cot, w_gate, w_up, w_hid, w_head, proj, small, mixed, states, news, invs, normed, head_rows, w_in,
    low_all, hidden, grad_gate, grad_up, gp, grad_small, staged, back, back_small, gconv_w, xbuf, halo, gates_sum, grad_state,
    z_gu, z_gu_in, z_down, z_down_in, z_out, z_out_in, z_w, z_w_in, z_sum, z_sum_in, q_gu, q_gu_in, q_w, q_w_in, q_sum,
    l_sems, own_sems, gu_ss, gu_rs, down_ss, down_rs, out_ss, out_rs, w_ss, w_rs, sum_ss, sum_rs,
    qgu_ss, qgu_rs, qw_ss, qw_rs, qsum_ss, qsum_rs, p_ss, p_rs, s_ss, s_rs, *sems,
):
    me, my = lax.axis_index("seq"), lax.axis_index("stream")
    head = me // rep
    barrier = pltpu.get_barrier_semaphore()
    for k in range(1, n):
        pl.semaphore_signal(barrier, inc=1, device_id={"seq": lax.rem(me + k, n)}, device_id_type=MESH)
    for k in range(1, m):
        pl.semaphore_signal(barrier, inc=1, device_id={"stream": lax.rem(my + k, m)}, device_id_type=MESH)
    first_unit = me * shard
    base = (first_unit // HD - me // (n - 1)) * HD
    offset = first_unit - base
    sources = [
        mid_any, out_any, w_gate_up.at[:, pl.ds(pl.multiple_of(base, HD), wide)],
        w_gate_up.at[:, pl.ds(pl.multiple_of(FF + base, HD), wide)], w_down.at[pl.ds(pl.multiple_of(base, HD), wide)],
        w_out.at[rows_of(head, HD)], rows_any, proj_any, small_any, mixed_any, states_any, news_any, invs_any, normed_any, w_in_any,
    ]
    places = [mid, cot, w_gate, w_up, w_hid, w_head, head_rows, proj, small, mixed, states, news, invs, normed, w_in]
    roomy = len(w_in.shape) == 2
    loads = [pltpu.make_async_copy(a, b, l_sems.at[i]) for i, (a, b) in enumerate(zip(sources, places)) if i < 13 or roomy]
    for load in loads:
        load.start()
    low_all[rows_of(me, T), :] = grad_residual[...].astype(bf16)
    pl.semaphore_wait(barrier, n + m - 2)
    gather = Gather(n, T, low_all.at[rows_of(me, T)], low_all, sems)
    gather.start()

    for load in loads[:5]:
        load.wait()

    def feed_turn(i, _):
        at = rows_of(i, TILE)
        block = mid[at, :]
        gate, up = nn(block, w_gate[...]), nn(block, w_up[...])
        sig = sigmoid(gate)
        silu = gate * sig
        grad_hidden = nt(cot[at, :], w_hid[...])
        own = lambda x: pltpu.roll(x, wide - offset, 1)[:, :shard].astype(bf16)
        hidden[at, :] = own(silu * up)
        grad_gate[at, :] = own(grad_hidden * up * (sig * (1.0 + gate * (1.0 - sig))))
        grad_up[at, :] = own(grad_hidden * silu)
        return 0

    lax.fori_loop(0, n * T // TILE, feed_turn, 0)
    part = tn(hidden[...], cot[...])
    for d in range(m):
        z_down[d] = part[d * (shard // m) : (d + 1) * (shard // m)].astype(bf16)
    downs = [exchange(z_down, z_down_in, k, down_ss, down_rs, "stream", my, m) for k in range(1, m)]
    for copy in downs:
        copy.start()
    gather.forward()
    for first in range(0, D, TILE):
        block = mid[:, first : first + TILE]
        store_pieces(z_gu.at[0], tn(block, grad_gate[...]), first, m, piece)
        store_pieces(z_gu.at[1], tn(block, grad_up[...]), first, m, piece)
    ups = [exchange(z_gu.at[i], z_gu_in.at[i], k, gu_ss.at[i], gu_rs.at[i], "stream", my, m) for i in range(2) for k in range(1, m)]
    for copy in ups:
        copy.start()
    gather.direct(0).wait_recv()
    for k in range(1, n // 2):
        gather.passed(k).wait_recv()
    gather.finish()
    for load in loads[5:]:
        load.wait()
    rows = tn(head_rows[...], low_all[...])
    for share in range(rep):

        @pl.when(lax.rem(me, rep) == share)
        def _():
            for d in range(m):
                at = share * (HD // rep) + d * piece
                z_out[d] = rows[at : at + piece].astype(bf16)

    if not roomy:
        normed = mid
        late = pltpu.make_async_copy(normed_any, normed, l_sems.at[13])
        late.start()
        late.wait()
    outs = [exchange(z_out, z_out_in, k, out_ss, out_rs, "stream", my, m) for k in range(1, m)]
    for copy in outs:
        copy.start()

    width = MIXED * HD
    starts = doc_starts(lengths)
    bias, rate = bias_ref[head], rate_ref[head]
    taps = head_taps(taps_ref, head)
    xbuf[0:8, :] = jnp.zeros((8, width), f32)
    halo[...] = jnp.zeros((8, width), f32)
    gconv_w[...] = jnp.zeros(gconv_w.shape, f32)
    gates_sum[...] = jnp.zeros((8, HD), f32)
    grad_state[...] = jnp.zeros((HD, HD), f32)

    def fill(c, _):
        xbuf[pl.ds(pl.multiple_of(8 + c * T, 8), T), :] = proj[rows_of(c, T), :width].astype(f32)
        return 0

    lax.fori_loop(0, n, fill, 0)
    turn = functools.partial(
        backward_turn, n, T, starts, bias, rate, taps, gain, lambda at: nt(low_all[at, :], w_head[...]),
        proj, small, mixed, states, news, invs, gp, grad_small, gconv_w, staged, xbuf, halo, gates_sum, grad_state,
        lambda c: None,
    )
    lax.fori_loop(0, n, turn, 0)

    column = pl.ds(pl.multiple_of(head * HD, HD), HD)

    def big_copy(c):
        return remote(staged.at[c], back.at[:, :, column], p_ss.at[c], p_rs.at[head], "seq", c)

    def small_copy(c):
        return remote(grad_small.at[rows_of(c, T)], back_small.at[head], s_ss.at[c], s_rs.at[head], "seq", c)

    mine = pltpu.make_async_copy(staged.at[me], back.at[:, :, column], own_sems.at[0])
    also = pltpu.make_async_copy(grad_small.at[rows_of(me, T)], back_small.at[head], own_sems.at[1])

    @pl.when(lax.rem(me, rep) == 0)
    def _():
        for k in range(1, n):
            peer = lax.rem(me + k, n)
            big_copy(peer).start()
            small_copy(peer).start()
        mine.start()
        also.start()

    units = TILE // (piece * m)
    ins = []
    for i, first in enumerate(range(0, D, TILE)):
        store_pieces(z_w, tn(normed[:, first : first + TILE], gp[...]), first, m, piece)
        for k in range(1, m):
            peer = lax.rem(my + k, m)
            at = pl.ds(i * units, units)
            ins.append(remote(z_w.at[peer, at], z_w_in.at[k - 1, at], w_ss.at[i, k - 1], w_rs.at[i, k - 1], "stream", peer))
            ins[-1].start()
    small_t = tn(grad_small[...], normed[...])
    small_t = small_t[:SMALL] + small_t[SMALL : 2 * SMALL]

    @pl.when(lax.rem(me, rep) == 0)
    def _():
        mine.wait()
        also.wait()

    for k in range(1, n):
        peer = lax.rem(me + k, n)

        @pl.when(lax.rem(me, rep) == 0)
        def _():
            big_copy(peer).wait_send()
            small_copy(peer).wait_send()

        @pl.when(lax.rem(peer, rep) == 0)
        def _():
            source = peer // rep
            there = pl.ds(pl.multiple_of(source * HD, HD), HD)
            remote(staged.at[me], back.at[:, :, there], p_ss.at[peer], p_rs.at[source], "seq", peer).wait_recv()
            remote(
                grad_small.at[rows_of(me, T)], back_small.at[source], s_ss.at[peer], s_rs.at[source], "seq", peer
            ).wait_recv()

    lane, place = iota((HD, SMALL * H), 0), iota((HD, SMALL * H), 1)
    logits = jnp.zeros((T, SMALL * H), f32)
    for h in range(H):
        picks = ((place >> 3) == jnp.where(lane < SMALL, lane, lane - SMALL)) & (lane < 2 * SMALL) & ((place & (H - 1)) == h)
        logits = logits + nn(back_small[h], picks.astype(bf16))
    total = nt(halves(logits), halves(w_small[...]))
    for i in range(GROUPS):
        if roomy:
            block = w_in[:, i * D : (i + 1) * D]
        else:
            late = pltpu.make_async_copy(w_in_any.at[:, i * D : (i + 1) * D], w_in.at[0], l_sems.at[14])
            late.start()
            late.wait()
            block = w_in[0]
        total = total + nt(back[i], block)
    values = tokens[...].astype(f32)
    part, gain_part = norm_back(values, norm_scale(values), gain_in[...], total)
    grad_input[...] = grad_residual[...] + part

    z_sum[...] = jnp.zeros(z_sum.shape, f32)
    z_sum[0:1, :] = gain_part
    z_sum[1:2, :] = gain_mid_grad[...]
    z_sum[2 : 2 + SMALL, :] = small_t
    z_sum[5 : 5 + CONV, :width] = gconv_w[...]
    z_sum[9:12, :HD] = gates_sum[0:3, :]

    def sum_copy(k):
        peer = lax.rem(my + k, m)
        return remote(z_sum, z_sum_in.at[k - 1], sum_ss.at[k - 1], sum_rs.at[k - 1], "stream", peer)

    for k in range(1, m):
        sum_copy(k).start()

    def added(own, arrived):
        found = own[my].astype(f32)
        for k in range(1, m):
            found = found + arrived[k - 1].astype(f32)
        return found

    for copy in downs:
        copy.wait()
    g_down[...] = added(z_down, z_down_in)
    for copy in ups:
        copy.wait()
    for i in range(2):
        q_gu[i] = added(z_gu.at[i], z_gu_in.at[i]).astype(bf16)
    q_ups = [scatter_to(q_gu.at[i], q_gu_in.at[i], k, qgu_ss.at[i], qgu_rs.at[i], me, n) for i in range(2) for k in range(1, n)]
    for copy in q_ups:
        copy.start()
    for i in range(2):
        q_gu_in[i, me] = q_gu[i, me]
    for copy in outs:
        copy.wait()
    g_out[...] = added(z_out, z_out_in)
    for k in range(1, m):
        sum_copy(k).wait()
    found = z_sum[...]
    for k in range(1, m):
        found = found + z_sum_in[k - 1]
    q_sum[me] = found
    q_sums = [
        remote(q_sum.at[me], q_sum.at[me], qsum_ss.at[k - 1], qsum_rs.at[k - 1], "seq", lax.rem(me + k, n)) for k in range(1, n)
    ]
    for copy in q_sums:
        copy.start()
    for copy in ins:
        copy.wait()
    q_w[...] = added(z_w, z_w_in).astype(bf16)
    q_ins = [scatter_to(q_w, q_w_in, k, qw_ss, qw_rs, me, n) for k in range(1, n)]
    for copy in q_ins:
        copy.start()
    q_w_in[me] = q_w[me]
    for copy in q_ups:
        copy.wait()
    for i in range(2):
        for source in range(n):
            at = i * FF + source * shard
            g_gate_up[:, at : at + shard] = q_gu_in[i, source].astype(f32)
    for copy in q_sums:
        copy.wait()
    g_gain_in[...] = jnp.sum(q_sum[:, 0:1, :], axis=0)
    g_gain_mid[...] = jnp.sum(q_sum[:, 1:2, :], axis=0)
    gain_total = jnp.zeros((1, HD), f32)
    for h in range(H):
        found = q_sum[h * rep]
        for j in range(SMALL):
            g_small[j * H + h : j * H + h + 1, :] = found[2 + j : 3 + j, :]
        for i in range(MIXED):
            g_taps[:, i * D + h * HD : i * D + (h + 1) * HD] = found[5 : 5 + CONV, i * HD : (i + 1) * HD]
        gain_total = gain_total + found[9:10, :HD]
        g_bias[h] = found[10, NH]
        g_rate[h] = found[11, NH]
    g_gain_head[...] = gain_total
    for copy in q_ins:
        copy.wait()
    for h in range(H):
        found = q_w_in[h * rep].astype(f32)
        for i in range(GROUPS):
            g_in[:, i * D + h * HD : i * D + (h + 1) * HD] = found[:, i * HD : (i + 1) * HD]


def run_back(n, m, rep, T, lengths, bias, rate, tokens, grad_residual, gain_in, gain_mid_grad, w_small, taps, gain,
             mid, cot, w_gate_up, w_down, w_out, proj, small, mixed, states, news, invs, normed, head_rows, w_in):
    rows, piece, shard = n * T, D // (n * m), FF // n
    wide = -(-(shard + HD - 1) // HD) * HD
    vm, roomy = pltpu.VMEM, rows <= 1024
    return pl.pallas_call(
        functools.partial(back_kernel, n, m, rep, T, piece, shard, wide),
        out_shape=(
            shape((T, D), f32), shape((piece, GROUPS * D), f32), shape((piece, D), f32), shape((piece, 2 * FF), f32),
            shape((shard // m, D), f32), shape((1, D), f32), shape((1, D), f32), shape((SMALL * H, D), f32),
            shape((H,), f32), shape((H,), f32), shape((CONV, MIXED * D), f32), shape((1, HD), f32),
        ),
        in_specs=[SMEM] * 3 + [VMEM] * 7 + [ANY] * 14,
        out_specs=[VMEM] * 8 + [SMEM] * 2 + [VMEM] * 2,
        scratch_shapes=[
            vm((rows, D), bf16), vm((rows, D), bf16), vm((D, wide), bf16), vm((D, wide), bf16), vm((wide, D), bf16),
            vm((HD, D), bf16), vm((rows, GROUPS * HD), bf16), vm((rows, HD), f32), vm((rows, HD), f32), vm((2, n, HD, HD), bf16),
            vm((2, NH * rows, HD), bf16), vm((2, n, NH * T, NH * T), bf16), vm((rows if roomy else 16, D), bf16),
            vm((rows, HD), bf16), vm((D, GROUPS * D) if roomy else (1, D, D), bf16),
            vm((rows, D), bf16), vm((rows, shard), bf16), vm((rows, shard), bf16), vm((rows, shard), bf16),
            vm((rows, GROUPS * HD), bf16), vm((rows, HD), bf16), vm((n, GROUPS, T, HD), bf16), vm((GROUPS, T, D), bf16),
            vm((H, T, HD), bf16), vm((CONV, MIXED * HD), f32), vm((rows + 8, MIXED * HD), f32), vm((8, MIXED * HD), f32),
            vm((8, HD), f32), vm((HD, HD), f32),
            vm((2, m, n, piece, shard), bf16), vm((2, m - 1, n, piece, shard), bf16),
            vm((m, shard // m, D), bf16), vm((m - 1, shard // m, D), bf16),
            vm((m, piece, D), bf16), vm((m - 1, piece, D), bf16),
            vm((m, n, piece, GROUPS * HD), bf16), vm((m - 1, n, piece, GROUPS * HD), bf16),
            vm((16, D), f32), vm((m - 1, 16, D), f32),
            vm((2, n, piece, shard), bf16), vm((2, n, piece, shard), bf16),
            vm((n, piece, GROUPS * HD), bf16), vm((n, piece, GROUPS * HD), bf16), vm((n, 16, D), f32),
            DMA((15,)), DMA((2,)), DMA((2, m - 1)), DMA((2, m - 1)), DMA((m - 1,)), DMA((m - 1,)), DMA((m - 1,)), DMA((m - 1,)),
            DMA((D // TILE, m - 1)), DMA((D // TILE, m - 1)), DMA((m - 1,)), DMA((m - 1,)),
            DMA((2, n - 1)), DMA((2, n - 1)), DMA((n - 1,)), DMA((n - 1,)), DMA((n - 1,)), DMA((n - 1,)),
            DMA((n,)), DMA((H,)), DMA((n,)), DMA((H,)), *gather_sems(n),
        ],
        compiler_params=pltpu.CompilerParams(vmem_limit_bytes=(60 if roomy else 62) * 1024 * 1024, collective_id=3, has_side_effects=True),
        name="backward",
    )(lengths, bias, rate, tokens, grad_residual, gain_in, gain_mid_grad, w_small, taps, gain,
      mid, cot, w_gate_up, w_down, w_out, proj, small, mixed, states, news, invs, normed, head_rows, w_in)


def on_device(tokens, grad_out, doc_lengths, gain_in, in_weight, small_weight, gate_bias, decay_rate, conv_weight,
              gain_head, out_weight, gain_mid, gate_up_weight, down_weight):
    seq, stream = lax.axis_size("seq"), lax.axis_size("stream")
    rep = seq // H
    T = tokens.shape[1]
    gain = gain_head.reshape(1, HD)
    gain_in, gain_mid = gain_in.reshape(1, D), gain_mid.reshape(1, D)
    rows, cotangent = tokens[0], grad_out[0]
    gated, normed, out_all, proj, small, mixed, states, news, invs, head_rows = run_forward(
        seq, rep, T, doc_lengths, gate_bias, decay_rate, rows, cotangent, gain_in, in_weight, small_weight, conv_weight, gain
    )
    result, grad_residual, mid_all, grad_gain_mid = run_feed(
        seq, T, rows, gated, cotangent, out_weight, gain_mid, gate_up_weight, down_weight
    )
    grad_input, g_in, g_out, g_gate_up, g_down, g_gain_in, g_gain_mid, g_small, g_bias, g_rate, g_taps, g_gain_head = run_back(
        seq, stream, rep, T, doc_lengths, gate_bias, decay_rate, rows, grad_residual, gain_in, grad_gain_mid, small_weight,
        conv_weight, gain, mid_all, out_all, gate_up_weight, down_weight, out_weight, proj, small, mixed, states, news, invs,
        normed, head_rows, in_weight,
    )
    return (
        result[None], grad_input[None], g_gain_in.reshape(D), g_in, g_small.T, g_bias, g_rate, g_taps,
        g_gain_head.reshape(HD), g_out, g_gain_mid.reshape(D), g_gate_up, g_down,
    )


def solution(mesh):
    rows, whole, split = P("stream", "seq", None), P(), P(("seq", "stream"), None)
    return jax.shard_map(
        on_device,
        mesh=mesh,
        in_specs=(rows, rows, P("stream", None)) + (whole,) * 11,
        out_specs=(rows, rows, whole, split, whole, whole, whole, whole, whole, split, whole, split, split),
        check_vma=False,
    )
```

```python
import functools

import jax
import jax.numpy as jnp
from jax import lax
from jax.experimental import pallas as pl
from jax.experimental.pallas import tpu as pltpu
from jax.sharding import PartitionSpec as P

D = 1024
H = 8
HD = 128
FF = 2816
NH = 2
CONV = 4
GROUPS = 2 + 2 * NH
MIXED = GROUPS - 1
SMALL = NH + 1
DOCS = 8
TILE = 256
EPS = 1e-06

f32 = jnp.float32
bf16 = jnp.bfloat16
MESH = pl.DeviceIdType.MESH
DMA = pltpu.SemaphoreType.DMA
VMEM = pl.BlockSpec(memory_space=pltpu.VMEM)
SMEM = pl.BlockSpec(memory_space=pltpu.SMEM)
ANY = pl.BlockSpec(memory_space=pl.ANY)
LIMIT = 56 * 1024 * 1024
shape = jax.ShapeDtypeStruct


def dot(a, b, dims):
    if isinstance(a, tuple) and isinstance(b, tuple):
        return dot(a[0], b[0], dims) + (dot(a[0], b[1], dims) + dot(a[1], b[0], dims))
    if isinstance(a, tuple):
        return dot(a[0], b, dims) + dot(a[1], b, dims)
    if isinstance(b, tuple):
        return dot(a, b[0], dims) + dot(a, b[1], dims)
    return lax.dot_general(
        a.astype(bf16), b.astype(bf16), ((dims[:1], dims[1:]), ((), ())), preferred_element_type=f32
    )


def nn(a, b):
    return dot(a, b, (1, 0))


def nt(a, b):
    return dot(a, b, (1, 1))


def tn(a, b):
    return dot(a, b, (0, 0))


def halves(x):
    high = x.astype(bf16)
    return high, (x - high.astype(f32)).astype(bf16)


def thirds(x):
    high, low = halves(x)
    return high, low, (x - high.astype(f32) - low.astype(f32)).astype(bf16)


def keep(ref, at, x):
    ref[0, at], ref[1, at] = halves(x)


def kept(ref, at):
    return ref[0, at], ref[1, at]


def nn_exact(ones, x):
    high, low, lowest = thirds(x)
    return nn(ones, high) + (nn(ones, low) + nn(ones, lowest))


def sigmoid(x):
    return 1.0 / (1.0 + jnp.exp(-x))


def softplus(x):
    return jnp.maximum(x, 0.0) + jnp.log(1.0 + jnp.exp(-jnp.abs(x)))


def norm_scale(values):
    return lax.rsqrt(jnp.mean(values * values, axis=-1, keepdims=True) + EPS)


def norm_back(values, scale, gain, grad):
    normal = values * scale
    e = grad * gain
    back = scale * (e - normal * jnp.mean(e * normal, axis=-1, keepdims=True))
    return back, jnp.sum(grad * normal, axis=0, keepdims=True)


def iota(dims, axis):
    return lax.broadcasted_iota(jnp.int32, dims, axis)


def doc_at(starts, positions):
    total = jnp.full(positions.shape, -1, jnp.int32)
    for start in starts:
        total = total + (start <= positions).astype(jnp.int32)
    return total


def doc_starts(lengths_ref):
    starts, at = [], jnp.int32(0)
    for j in range(DOCS):
        starts.append(at)
        at = at + lengths_ref[0, j]
    return starts


def stack2(a, b):
    return jnp.concatenate([a, b], axis=0)


def beside(a, b):
    return jnp.concatenate([a, b], axis=1)


def quad(a, b, c, d):
    return stack2(beside(a, b), beside(c, d))


def rows_of(i, size):
    return pl.ds(pl.multiple_of(i * size, size), size)


def greet(axis, peers):
    barrier = pltpu.get_barrier_semaphore()
    for peer in peers:
        pl.semaphore_signal(barrier, inc=1, device_id={axis: peer}, device_id_type=MESH)
    return lambda: pl.semaphore_wait(barrier, len(peers))


def remote(src, dst, send, receive, axis, peer):
    return pltpu.make_async_remote_copy(src, dst, send, receive, device_id={axis: peer}, device_id_type=MESH)


class Gather:
    def __init__(self, n, T, src, dst, sems):
        self.n, self.T, self.src, self.dst = n, T, src, dst
        self.ss, self.rs, self.fs, self.fr = sems
        self.me = lax.axis_index("seq")
        self.sib = self.me + 1 - 2 * lax.rem(self.me, 2)

    def at(self, device):
        return self.dst.at[rows_of(device, self.T)]

    def direct(self, k):
        peer = self.sib if k == 0 else lax.rem(self.me + 2 * k, self.n)
        return remote(self.src, self.at(self.me), self.ss.at[k], self.rs.at[k], "seq", peer)

    def passed(self, k):
        block = self.at(lax.rem(self.me - 2 * k + self.n, self.n))
        return remote(block, block, self.fs.at[k], self.fr.at[k], "seq", self.sib)

    def start(self):
        for k in (*range(1, self.n // 2), 0):
            self.direct(k).start()

    def forward(self):
        for k in range(1, self.n // 2):
            self.direct(k).wait_recv()
            self.passed(k).start()

    def finish(self):
        for k in range(self.n // 2):
            self.direct(k).wait_send()
            if k:
                self.passed(k).wait_send()


def gather_sems(n):
    return [DMA((n // 2,)) for _ in range(4)]


def conv_of(block, taps, docs, T):
    total = block[8:] * taps[CONV - 1 : CONV]
    for lag in range(1, CONV):
        same = (docs[0] == docs[lag]).astype(f32)
        total = total + block[8 - lag : 8 - lag + T] * (taps[CONV - 1 - lag : CONV - lag] * same)
    return total


def chunk_gates(logits, bias, rate, starts, first, T):
    lane = iota((T, HD), 1)
    shifted = logits + bias
    gate = -rate * softplus(shifted)
    place_i, place_j = iota((T, T), 0), iota((T, T), 1)
    lower = place_j <= place_i
    cumul = nn_exact(lower.astype(bf16), jnp.where(lane == NH, gate, 0.0))
    beta = 2.0 * sigmoid(logits)
    b0, b1 = beta[:, 0:1], beta[:, 1:2]
    g = cumul[:, NH : NH + 1]
    g_row = jnp.transpose(cumul)[NH : NH + 1, :]
    g_last = cumul[T - 1 : T, NH : NH + 1]
    position = first + iota((T, 1), 0)
    docs = [doc_at(starts, position - lag) for lag in range(CONV)]
    doc = docs[0]
    doc_row = doc_at(starts, first + iota((1, T), 1))
    doc_before = doc_at(starts, jnp.full((1, 1), first - 1, jnp.int32))
    doc_last = doc_at(starts, jnp.full((1, 1), first + (T - 1), jnp.int32))
    joined = lower & (doc == doc_row)
    decay = jnp.where(joined, jnp.exp(jnp.where(joined, g - g_row, 0.0)), 0.0)
    strict = jnp.where(place_i == place_j, 0.0, decay)
    from_start = jnp.exp(g) * (doc == doc_before).astype(f32)
    to_end = jnp.exp(jnp.minimum(g_last - g, 0.0)) * (doc == doc_last).astype(f32)
    whole = jnp.exp(g_last) * (doc_last == doc_before).astype(f32)
    return dict(
        shifted=shifted, beta=beta, b=stack2(b0, b1), docs=docs, decay=decay,
        decays=quad(strict, strict, decay, strict), hd=from_start, hd2=stack2(from_start, from_start),
        to_end=stack2(to_end, to_end), whole=whole,
    )


def key_scale(raw):
    return lax.rsqrt(jnp.sum(raw * raw, axis=-1, keepdims=True) + EPS)


def chunk_inputs(block, taps, docs, T):
    conv = conv_of(block, taps, docs, T)
    sig = sigmoid(conv)
    active = conv * sig
    cut = [active[:, i * HD : (i + 1) * HD] for i in range(MIXED)]
    scales = (key_scale(cut[1]), key_scale(cut[2]))
    keys = stack2(cut[1] * scales[0], cut[2] * scales[1])
    values = stack2(cut[3], cut[4])
    return conv, sig, cut[0], keys, values, stack2(*scales)


def inverses(lowers, T):
    size = NH * T
    row, col = iota((size, size), 0), iota((size, size), 1)
    differ = (row & (T - 1)) ^ (col & (T - 1))
    eye = (row == col).astype(f32)
    found = [jnp.where(row == col, 1.0, jnp.where(differ == 0, -a, 0.0)) for a in lowers]
    step = 1
    while step < T:
        level = (differ >= step) & (differ < 2 * step)
        parts = [nn(jnp.where(level, a, 0.0), x) for a, x in zip(lowers, found)]
        found = [x - nn(x, part) for x, part in zip(found, parts)]
        step *= 2
    a_cut = [halves(a) for a in lowers]
    x_cut = [halves(x) for x in found]
    errors = [
        eye - x - (nn(a[0], xc[0]) + (nn(a[0], xc[1]) + nn(a[1], xc[0])))
        for a, x, xc in zip(a_cut, found, x_cut)
    ]
    return [x + nn(xc[0], e) for x, xc, e in zip(found, x_cut, errors)]


def head_gate(mixed, raw):
    scale = norm_scale(mixed)
    return mixed * scale, scale, sigmoid(raw)


def head_taps(taps_ref, head):
    cuts = [taps_ref[:, pl.ds(pl.multiple_of(i * D + head * HD, HD), HD)] for i in range(MIXED)]
    return jnp.concatenate(cuts, axis=1)


def intra_turn(T, per, starts, bias, rate, taps, small, xbuf, invs, ubuf, wbuf, qbuf, pbuf, dbuf, gates, turn, _):
    held, lowers = [], []
    for i in range(per):
        c = turn * per + i
        first = pl.multiple_of(c * T, T)
        gate = chunk_gates(small[pl.ds(first, T), :], bias, rate, starts, first, T)
        block = xbuf[pl.ds(first, T + 8), :]
        conv, sig, query, keys, values, scales = chunk_inputs(block, taps, gate["docs"], T)
        key_pair = halves(keys)
        lowers.append(gate["b"] * (nt(key_pair, key_pair) * gate["decays"]))
        held.append((c, gate, query, keys, key_pair, values))
    found = inverses(lowers, T)
    for (c, gate, query, keys, key_pair, values), inverse in zip(held, found):
        at, two = rows_of(c, T), rows_of(c, NH * T)
        pair = halves(inverse)
        invs[0, c], invs[1, c] = pair
        both = nn(pair, halves(gate["b"] * beside(values, gate["hd2"] * keys)))
        ubuf[two, :] = both[:, :HD]
        keep(wbuf, two, both[:, HD:])
        query_pair = halves(query)
        qbuf[0, at], qbuf[1, at] = query_pair
        keep(pbuf, at, nt(query_pair, key_pair) * beside(gate["decay"], gate["decay"]))
        keep(dbuf, two, gate["to_end"] * keys)
        gates[at, :] = jnp.where(iota((T, HD), 1) == 0, gate["hd"], gate["whole"])
    return 0


def across_turn(T, gain, proj, mixed_out, states, news, head_rows, ubuf, wbuf, qbuf, pbuf, dbuf, gates, done, c, state):
    at, two = rows_of(c, T), rows_of(c, NH * T)
    state_pair = halves(state)
    states[0, c], states[1, c] = state_pair
    new = ubuf[two, :] - nn(kept(wbuf, two), state_pair)
    new_pair = halves(new)
    news[0, two], news[1, two] = new_pair
    gate = gates[at, :]
    mixed = gate[:, 0:1] * nn(kept(qbuf, at), state_pair) + nn(kept(pbuf, at), new_pair)
    mixed_out[at, :] = mixed
    raw = proj[at, MIXED * HD :].astype(f32)
    normal, _, sig = head_gate(mixed, raw)
    head_rows[at, :] = ((normal * gain[...]) * (raw * sig)).astype(bf16)
    done(c)
    return gate[0:1, 1:2] * state + tn(kept(dbuf, two), new_pair)


def forward_kernel(
    n, rep, T, per, lengths, bias_ref, rate_ref, tokens, cotangent, gain_in, w_in, w_small, taps_ref, gain,
    gated, normed, out_all, proj, small, mixed_out, states, news, invs, head_rows,
    own, w_head, w_wide, xbuf, ubuf, wbuf, qbuf, pbuf, dbuf, gates,
    w_sems, own_sem, a_ss, a_rs, *sems,
):
    me = lax.axis_index("seq")
    head = me // rep
    wait_for_all = greet("seq", [lax.rem(me + k, n) for k in range(1, n)])
    width = MIXED * HD
    loads = [
        pltpu.make_async_copy(
            w_in.at[:, pl.ds(pl.multiple_of(i * D + head * HD, HD), HD)], w_head.at[:, i * HD : (i + 1) * HD], w_sems.at[i]
        )
        for i in range(GROUPS)
    ]
    for load in loads:
        load.start()
    values = tokens[...].astype(f32)
    own[...] = (values * norm_scale(values) * gain_in[...]).astype(bf16)
    local = pltpu.make_async_copy(own, normed.at[rows_of(me, T)], own_sem)
    local.start()
    wait_for_all()
    first_gather = Gather(n, T, own, normed, sems[:4])
    first_gather.start()
    second_gather = Gather(n, T, cotangent, out_all, sems[4:8])

    starts = doc_starts(lengths)
    bias, rate = bias_ref[head], rate_ref[head]
    taps = head_taps(taps_ref, head)
    xbuf[0:8, :] = jnp.zeros((8, width), f32)
    w_wide[...] = jnp.zeros((D, HD), bf16)
    chosen = jnp.where((iota((D, SMALL * H), 1) & (H - 1)) == head, w_small[...], 0.0)
    for i, piece in enumerate(thirds(chosen)):
        w_wide[:, i * SMALL * H : (i + 1) * SMALL * H] = piece
    group = iota((HD, HD), 0) >> 3
    lane = iota((HD, HD), 1)
    picks = ((group == lane) | (group == lane + SMALL) | (group == lane + 2 * SMALL)) & (lane < SMALL)
    picks = picks.astype(bf16)
    for load in loads:
        load.wait()
    local.wait()
    for k in range(n // 2):
        if k == 1:
            first_gather.forward()
        if k:
            first_gather.passed(k).wait_recv()
        else:
            first_gather.direct(0).wait_recv()
        at = rows_of(lax.rem(me // 2 - k + n // 2, n // 2), 2 * T)
        block = normed[at, :]
        result = nn(block, w_head[...]).astype(bf16)
        proj[at, :] = result
        xbuf[pl.ds(pl.multiple_of(8 + lax.rem(me // 2 - k + n // 2, n // 2) * (2 * T), 8), 2 * T), :] = result[:, :width].astype(f32)
        raw = thirds(nn(block, w_wide[...]))
        small[at, :] = nn(raw[0], picks) + (nn(raw[1], picks) + nn(raw[2], picks))
    first_gather.finish()
    keep = pltpu.make_async_copy(cotangent, out_all.at[rows_of(me, T)], own_sem)
    keep.start()
    second_gather.start()

    intra = functools.partial(
        intra_turn, T, per, starts, bias, rate, taps, small, xbuf, invs, ubuf, wbuf, qbuf, pbuf, dbuf, gates
    )
    lax.fori_loop(0, n // per, intra, 0)
    second_gather.forward()
    column = pl.ds(pl.multiple_of(head * HD, HD), HD)

    def row_copy(c):
        return remote(head_rows.at[rows_of(c, T)], gated.at[:, column], a_ss.at[c], a_rs.at[head], "seq", c)

    def send_rows(c):
        @pl.when((c != me) & (lax.rem(me, rep) == 0))
        def _():
            row_copy(c).start()

    across = functools.partial(
        across_turn, T, gain, proj, mixed_out, states, news, head_rows, ubuf, wbuf, qbuf, pbuf, dbuf, gates, send_rows
    )
    lax.fori_loop(0, n, across, jnp.zeros((HD, HD), f32))

    @pl.when(lax.rem(me, rep) == 0)
    def _():
        mine = pltpu.make_async_copy(head_rows.at[rows_of(me, T)], gated.at[:, column], own_sem)
        keep.wait()
        mine.start()
        mine.wait()

    @pl.when(lax.rem(me, rep) != 0)
    def _():
        keep.wait()

    def settle(k, _):
        peer = lax.rem(me + k, n)

        @pl.when(lax.rem(me, rep) == 0)
        def _():
            row_copy(peer).wait_send()

        @pl.when(lax.rem(peer, rep) == 0)
        def _():
            source = peer // rep
            remote(
                head_rows.at[rows_of(me, T)], gated.at[:, pl.ds(pl.multiple_of(source * HD, HD), HD)],
                a_ss.at[peer], a_rs.at[source], "seq", peer,
            ).wait_recv()

        return 0

    lax.fori_loop(1, n, settle, 0)
    second_gather.direct(0).wait_recv()
    for k in range(1, n // 2):
        second_gather.passed(k).wait_recv()
    second_gather.finish()


def forward_scratch(n, T):
    rows = n * T
    return [
        pltpu.VMEM((rows + 8, MIXED * HD), f32), pltpu.VMEM((NH * rows, HD), f32),
        pltpu.VMEM((2, NH * rows, HD), bf16), pltpu.VMEM((2, rows, HD), bf16), pltpu.VMEM((2, rows, NH * T), bf16),
        pltpu.VMEM((2, NH * rows, HD), bf16), pltpu.VMEM((rows, HD), f32),
    ]


def run_forward(n, rep, T, lengths, bias, rate, tokens, cotangent, gain_in, w_in, w_small, taps, gain):
    rows = n * T
    return pl.pallas_call(
        functools.partial(forward_kernel, n, rep, T, 4),
        out_shape=(
            shape((T, D), bf16), shape((rows, D), bf16), shape((rows, D), bf16), shape((rows, GROUPS * HD), bf16),
            shape((rows, HD), f32), shape((rows, HD), f32), shape((2, n, HD, HD), bf16), shape((2, NH * rows, HD), bf16),
            shape((2, n, NH * T, NH * T), bf16), shape((rows, HD), bf16),
        ),
        in_specs=[SMEM] * 3 + [VMEM, ANY, VMEM, ANY, VMEM, VMEM, VMEM],
        out_specs=[VMEM, VMEM, ANY] + [VMEM] * 7,
        scratch_shapes=[
            pltpu.VMEM((T, D), bf16), pltpu.VMEM((D, GROUPS * HD), bf16), pltpu.VMEM((D, HD), bf16),
            *forward_scratch(n, T),
            DMA((GROUPS,)), DMA, DMA((n,)), DMA((H,)), *gather_sems(n), *gather_sems(n),
        ],
        compiler_params=pltpu.CompilerParams(vmem_limit_bytes=LIMIT, collective_id=1, has_side_effects=True),
        name="mixer_forward",
    )(lengths, bias, rate, tokens, cotangent, gain_in, w_in, w_small, taps, gain)


def feed_kernel(
    n, T, steps, tokens, gated, cotangent, w_out, gain_mid, w_gate, w_up, w_down,
    result, grad_residual, mid_all, gain_grad, residual, middle, total, grad_mid, own_sem, *sems,
):
    step = pl.program_id(0)
    me = lax.axis_index("seq")
    gather = Gather(n, T, middle, mid_all, sems)
    local = pltpu.make_async_copy(middle, mid_all.at[rows_of(me, T)], own_sem)

    @pl.when(step == 0)
    def _():
        peers = [gather.sib] + [lax.rem(me + 2 * k, n) for k in range(1, n // 2)]
        wait_for_all = greet("seq", peers)
        found = tokens[...].astype(f32) + nn(gated[...], w_out[...])
        residual[...] = found
        middle[...] = (found * norm_scale(found) * gain_mid[...]).astype(bf16)
        total[...] = found
        grad_mid[...] = jnp.zeros((T, D), f32)
        wait_for_all()
        gather.start()
        local.start()

    gate, up = nn(middle[...], w_gate[...]), nn(middle[...], w_up[...])
    sig = sigmoid(gate)
    silu = gate * sig
    hidden = (silu * up).astype(bf16)
    total[...] += nn(hidden, w_down[...])
    grad_hidden = nt(cotangent[...], w_down[...])
    grad_gate = (grad_hidden * up * (sig * (1.0 + gate * (1.0 - sig)))).astype(bf16)
    grad_up = (grad_hidden * silu).astype(bf16)
    grad_mid[...] += nt(grad_gate, w_gate[...]) + nt(grad_up, w_up[...])

    @pl.when(step == steps - 2)
    def _():
        gather.forward()

    @pl.when(step == steps - 1)
    def _():
        result[...] = total[...].astype(bf16)
        values = residual[...]
        back, gain_part = norm_back(values, norm_scale(values), gain_mid[...], grad_mid[...])
        gain_grad[...] = gain_part
        grad_residual[...] = cotangent[...].astype(f32) + back
        gather.direct(0).wait_recv()
        for k in range(1, n // 2):
            gather.passed(k).wait_recv()
        gather.finish()
        local.wait()


def run_feed(n, T, tokens, gated, cotangent, w_out, gain_mid, w_gate_up, w_down):
    steps = FF // TILE
    fixed = lambda *dims: pl.BlockSpec(dims, lambda i: (0, 0))
    return pl.pallas_call(
        functools.partial(feed_kernel, n, T, steps),
        grid=(steps,),
        out_shape=(shape((T, D), bf16), shape((T, D), f32), shape((n * T, D), bf16), shape((1, D), f32)),
        in_specs=[
            fixed(T, D), fixed(T, D), fixed(T, D), fixed(D, D), fixed(1, D),
            pl.BlockSpec((D, TILE), lambda i: (0, i)), pl.BlockSpec((D, TILE), lambda i: (0, i + FF // TILE)),
            pl.BlockSpec((TILE, D), lambda i: (i, 0)),
        ],
        out_specs=[fixed(T, D), fixed(T, D), ANY, fixed(1, D)],
        scratch_shapes=[
            pltpu.VMEM((T, D), f32), pltpu.VMEM((T, D), bf16), pltpu.VMEM((T, D), f32), pltpu.VMEM((T, D), f32),
            DMA, *gather_sems(n),
        ],
        compiler_params=pltpu.CompilerParams(vmem_limit_bytes=LIMIT, collective_id=2, has_side_effects=True),
        name="feed_forward",
    )(tokens, gated, cotangent, w_out, gain_mid, w_gate_up, w_gate_up, w_down)


def store_pieces(out, part, first, stream, piece):
    for i in range(part.shape[0] // piece):
        at = first // piece + i
        out[at % stream, at // stream] = part[i * piece : (i + 1) * piece].astype(bf16)


def backward_turn(
    n, T, head, starts, bias, rate, taps, gain, incoming_of, proj, small, states, fetch,
    gp, grad_small, gconv_w, xbuf, halo, gates_sum, grad_state, done, k, _,
):
    width = MIXED * HD
    lane = iota((T, HD), 1)
    place_i, place_j = iota((T, T), 0), iota((T, T), 1)
    upper = (place_j >= place_i).astype(bf16)
    under = place_j < place_i
    c = n - 1 - k
    first = pl.multiple_of(c * T, T)
    at, two = rows_of(c, T), rows_of(c, NH * T)
    gate = chunk_gates(small[at, :], bias, rate, starts, first, T)
    block = xbuf[pl.ds(first, T + 8), :]
    conv, sig, query, keys, values, scales = chunk_inputs(block, taps, gate["docs"], T)
    key_pair, query_pair = halves(keys), halves(query)
    b, hd, hd2, to_end = gate["b"], gate["hd"], gate["hd2"], gate["to_end"]
    decay2 = beside(gate["decay"], gate["decay"])
    pairs = nt(key_pair, key_pair) * gate["decays"]
    scores = nt(query_pair, key_pair) * decay2
    state = (states[0, c], states[1, c])
    state_grad = grad_state[...]
    new, inverse, mixed = fetch(c)
    raw = proj[at, width:].astype(f32)
    normal, scale, zsig = head_gate(mixed, raw)
    incoming = incoming_of(at)
    passed = incoming * (raw * zsig)
    gates_sum[0:1, :] += jnp.sum(passed * normal, axis=0, keepdims=True)
    grad_z = incoming * (normal * gain[...]) * (zsig * (1.0 + raw * (1.0 - zsig)))
    e = passed * gain[...]
    grad_mixed = scale * (e - normal * jnp.mean(e * normal, axis=-1, keepdims=True))
    gm = halves(grad_mixed)
    ended = halves(to_end * keys)
    grad_pair = halves(state_grad)
    grad_new = tn(halves(scores), gm) + nn(ended, grad_pair)
    grad_right = tn(inverse, halves(grad_new))
    moved = b * grad_right
    grad_state[...] = gate["whole"] * state_grad + tn(halves(hd * query), gm) - tn(halves(hd2 * keys), halves(moved))
    grad_ended = nt(new, grad_pair)
    grad_scores = nt(gm, new)
    grad_lower = jnp.where(gate["decays"] != 0.0, -nt(halves(grad_right), new), 0.0)
    from_grad = nt(gm, state)
    scored = grad_scores * decay2
    grad_query = hd * from_grad + nn(scored, key_pair[0])
    paired = (b * grad_lower) * gate["decays"]
    keyed = nn(key_pair, state)
    grad_keys = (
        tn(scored, query_pair[0]) + to_end * grad_ended - hd2 * nt(moved, state[0])
        + nn(paired, key_pair[0]) + tn(paired, key_pair[0])
    )
    lower_pairs = grad_lower * pairs
    grad_b = jnp.sum(grad_right * (values - hd2 * keyed), axis=-1, keepdims=True) + jnp.sum(
        lower_pairs, axis=-1, keepdims=True
    )
    four = b * lower_pairs
    both = grad_scores * scores
    joint = (four[:T, :T] + four[:T, T:]) + (four[T:, :T] + four[T:, T:]) + (both[:, :T] + both[:, T:])
    crossing = jnp.sum(jnp.where(under, nn_exact(upper, joint), 0.0), axis=-1, keepdims=True)
    start_part = -hd2 * jnp.sum(moved * keyed, axis=-1, keepdims=True)
    start_part = start_part[:T] + start_part[T:] + hd * jnp.sum(query * from_grad, axis=-1, keepdims=True)
    end_part = to_end * jnp.sum(grad_ended * keys, axis=-1, keepdims=True)
    end_part = end_part[:T] + end_part[T:]
    sums_in = jnp.where(lane == 0, start_part, jnp.where(lane == 1, end_part, 0.0))
    after = nn_exact(upper, sums_in)
    before = nn_exact(under.astype(bf16), sums_in)
    whole_part = gate["whole"] * jnp.sum(state_grad * (state[0].astype(f32) + state[1].astype(f32)), keepdims=True)
    grad_gate = crossing + after[:, 0:1] + before[:, 1:2] + whole_part
    shifted = gate["shifted"]
    grad_beta = [grad_b[i * T : (i + 1) * T] * (gate["beta"][:, i : i + 1] * (1.0 - 0.5 * gate["beta"][:, i : i + 1])) for i in range(NH)]
    grad_decay = (-grad_gate * rate * sigmoid(shifted))[:, NH : NH + 1]
    which = lane >> 3
    logit = jnp.where(which == 0, grad_beta[0], jnp.where(which == 1, grad_beta[1], grad_decay))
    grad_logits = jnp.where((lane < SMALL * H) & ((lane & (H - 1)) == head), logit, 0.0)
    gates_sum[1:2, :] += jnp.sum(jnp.where(lane == NH, grad_decay, 0.0), axis=0, keepdims=True)
    gates_sum[2:3, :] += jnp.sum(jnp.where(lane == NH, grad_gate * -softplus(shifted), 0.0), axis=0, keepdims=True)
    high = grad_logits.astype(bf16).astype(f32)
    grad_small[at, :] = (
        high + pltpu.roll(grad_logits - high, SMALL * H, 1) + pltpu.roll(high, 2 * SMALL * H, 1)
    ).astype(bf16)
    projected_out = jnp.sum(keys * grad_keys, axis=-1, keepdims=True)
    grad_raw = (grad_keys - keys * projected_out) * scales
    slope = sig * (1.0 + conv * (1.0 - sig))
    grad_active = jnp.concatenate([grad_query, grad_raw[:T], grad_raw[T:], moved[:T], moved[T:]], axis=1)
    grad_conv = grad_active * slope
    after_block = stack2(grad_conv, halo[...])
    halo[...] = grad_conv[:8]
    position = first + iota((T, 1), 0)
    total = grad_conv * taps[CONV - 1 : CONV]
    taps_grads = [None] * CONV
    taps_grads[CONV - 1] = jnp.sum(grad_conv * block[8:], axis=0, keepdims=True)
    for lag in range(1, CONV):
        same = (doc_at(starts, position + lag) == gate["docs"][0]).astype(f32)
        total = total + after_block[lag : lag + T] * (taps[CONV - 1 - lag : CONV - lag] * same)
        same = (gate["docs"][lag] == gate["docs"][0]).astype(f32)
        taps_grads[CONV - 1 - lag] = jnp.sum(
            grad_conv * (block[8 - lag : 8 - lag + T] * same), axis=0, keepdims=True
        )
    everything = beside(total, grad_z).astype(bf16)
    gp[at, :] = everything
    gconv_w[...] += jnp.concatenate(taps_grads, axis=0)
    done(k)
    return 0


class Chain:
    def __init__(self, own, up_in, down_in, sems, my, m):
        self.own, self.up_in, self.down_in = own, up_in, down_in
        self.us, self.ur, self.ds, self.dr = sems
        self.my, self.m = my, m

    def up(self, q):
        slot = q - self.my
        return self.own(self.my + self.m - 1 - q), self.up_in(slot), slot, self.my + 1, self.us, self.ur

    def down(self, q):
        slot = q - (self.m - 1 - self.my)
        return self.own(self.my - (self.m - 1 - q)), self.down_in(slot), slot, self.my - 1, self.ds, self.dr

    def copy(self, hop):
        own, arrived, slot, peer, send, receive = hop
        return remote(own, arrived, send.at[slot], receive.at[slot], "stream", peer)

    def start(self):
        for q in range(self.m - 1):

            @pl.when(self.my == 0)
            def _():
                self.copy(self.up(q)).start()

            @pl.when(self.my == self.m - 1)
            def _():
                self.copy(self.down(q)).start()

    def tick(self, q):
        for inner, way in (
            ((self.my > 0) & (self.my <= q), self.up),
            ((self.my < self.m - 1) & (self.my >= self.m - 1 - q), self.down),
        ):

            @pl.when(inner)
            def _():
                hop = way(q)
                self.copy(hop).wait_recv()
                hop[0][...] = (hop[0][...].astype(f32) + hop[1][...].astype(f32)).astype(bf16)
                self.copy(hop).start()

    def finish(self, write):
        last = self.m - 1

        @pl.when(self.my > 0)
        def _():
            slot = last - self.my
            remote(self.own(self.my), self.up_in(slot), self.us.at[slot], self.ur.at[slot], "stream", self.my - 1).wait_recv()

        @pl.when(self.my < last)
        def _():
            slot = self.my
            remote(self.own(self.my), self.down_in(slot), self.ds.at[slot], self.dr.at[slot], "stream", self.my + 1).wait_recv()

        mine = self.own(self.my)

        @pl.when((self.my > 0) & (self.my < last))
        def _():
            write(mine[...].astype(f32) + self.up_in(last - self.my)[...].astype(f32) + self.down_in(self.my)[...].astype(f32))

        @pl.when(self.my == last)
        def _():
            write(mine[...].astype(f32) + self.up_in(0)[...].astype(f32))

        @pl.when(self.my == 0)
        def _():
            write(mine[...].astype(f32) + self.down_in(0)[...].astype(f32))

    def settle(self):
        for q in range(self.m - 1):

            @pl.when(self.my <= q)
            def _():
                self.copy(self.up(q)).wait_send()

            @pl.when(self.my >= self.m - 1 - q)
            def _():
                self.copy(self.down(q)).wait_send()


class Sums:
    def __init__(self, own, arrived, every, sems, me, my, n, m):
        self.own, self.arrived, self.every = own, arrived, every
        self.zs, self.zr, self.ss, self.rs = sems
        self.me, self.my, self.n, self.m = me, my, n, m

    def across(self, k):
        peer = lax.rem(self.my + k, self.m)
        return remote(self.own, self.arrived.at[k - 1], self.zs.at[k - 1], self.zr.at[k - 1], "stream", peer)

    def along(self, k):
        block = self.every.at[self.me]
        return remote(block, block, self.ss.at[k - 1], self.rs.at[k - 1], "seq", lax.rem(self.me + k, self.n))

    def start(self):
        for k in range(1, self.m):
            self.across(k).start()

    def add(self):
        total = self.own[...]
        for k in range(1, self.m):
            self.across(k).wait()
            total = total + self.arrived[k - 1]
        self.every[self.me] = total
        for k in range(1, self.n):
            self.along(k).start()

    def settle(self):
        for k in range(1, self.n):
            self.along(k).wait()


def chain_sems(*lead):
    return [DMA(lead) for _ in range(4)]


def scatter_to(own, arrived, k, send, receive, me, size):
    peer = lax.rem(me + k, size)
    return remote(own.at[peer], arrived.at[me], send.at[k - 1], receive.at[k - 1], "seq", peer)


def back_kernel(
    n, m, rep, T, piece, shard, wide,
    lengths, bias_ref, rate_ref, tokens, grad_residual, gain_in, gain_mid_grad, w_small, taps_ref, gain,
    mid_any, out_any, w_gate_up, w_down, w_out, rows_any, proj_any, small_any, mixed_any, states_any, news_any, invs_any,
    normed_any, w_in_any,
    grad_input, q_w_in, g_out, q_gu_in, g_down, q_sum, r_sum,
    mid, cot, w_gate, w_up, w_hid, w_head, head_rows, proj, small, mixed, states, news, invs, normed, w_in, w_wide,
    low_all, hidden, grad_gate, grad_up, gp, grad_small, gconv_w, xbuf, halo, gates_sum, grad_state,
    z_gu, z_gu_up, z_gu_down, z_down, z_down_up, z_down_down, z_out, z_out_up, z_out_down, z_w, z_w_up, z_w_down,
    z_sum, z_sum_in, y_sum, y_sum_in, q_gu, q_w, part_own, part_out, part_in, chip_out, chip_in,
    l_sems, i_sems, gu_us, gu_ur, gu_ds, gu_dr, dn_us, dn_ur, dn_ds, dn_dr, ou_us, ou_ur, ou_ds, ou_dr, w_us, w_ur, w_ds, w_dr,
    sum_ss, sum_rs, qgu_ss, qgu_rs, qw_ss, qw_rs, qsum_ss, qsum_rs, p_ss, p_rs, c_ss, c_rs, *sems,
):
    me, my = lax.axis_index("seq"), lax.axis_index("stream")
    head, chip, side = me // rep, me // 2, lax.rem(me, 2)
    sib = me + 1 - 2 * side
    barrier = pltpu.get_barrier_semaphore()
    for k in range(1, n):
        pl.semaphore_signal(barrier, inc=1, device_id={"seq": lax.rem(me + k, n)}, device_id_type=MESH)
    for k in range(1, m):
        pl.semaphore_signal(barrier, inc=1, device_id={"stream": lax.rem(my + k, m)}, device_id_type=MESH)
    first_unit = me * shard
    base = (first_unit // HD - me // (n - 1)) * HD
    offset = first_unit - base
    sources = [
        mid_any, out_any, w_gate_up.at[:, pl.ds(pl.multiple_of(base, HD), wide)],
        w_gate_up.at[:, pl.ds(pl.multiple_of(FF + base, HD), wide)], w_down.at[pl.ds(pl.multiple_of(base, HD), wide)],
        w_out.at[rows_of(head, HD)], rows_any, proj_any, small_any, mixed_any, states_any, news_any, invs_any, normed_any,
    ]
    places = [mid, cot, w_gate, w_up, w_hid, w_head, head_rows, proj, small, mixed, states, news, invs, normed]
    roomy = len(normed.shape) == 2
    loads = [pltpu.make_async_copy(a, b, l_sems.at[i]) for i, (a, b) in enumerate(zip(sources, places)) if i not in (9, 11, 12, 13) or roomy]
    for i in range(GROUPS):
        column = pl.ds(pl.multiple_of(i * D + head * HD, HD), HD)
        loads.append(pltpu.make_async_copy(w_in_any.at[:, column], w_in.at[:, i * HD : (i + 1) * HD], i_sems.at[i]))
    for load in loads:
        load.start()
    low_all[rows_of(me, T), :] = grad_residual[...].astype(bf16)
    pl.semaphore_wait(barrier, n + m - 2)
    gather = Gather(n, T, low_all.at[rows_of(me, T)], low_all, sems)
    gather.start()

    for load in loads[:5]:
        load.wait()

    def feed_turn(i, _):
        at = rows_of(i, TILE)
        block = mid[at, :]
        gate, up = nn(block, w_gate[...]), nn(block, w_up[...])
        sig = sigmoid(gate)
        silu = gate * sig
        grad_hidden = nt(cot[at, :], w_hid[...])
        own = lambda x: pltpu.roll(x, wide - offset, 1)[:, :shard].astype(bf16)
        hidden[at, :] = own(silu * up)
        grad_gate[at, :] = own(grad_hidden * up * (sig * (1.0 + gate * (1.0 - sig))))
        grad_up[at, :] = own(grad_hidden * silu)
        return 0

    lax.fori_loop(0, n * T // TILE, feed_turn, 0)
    downs = Chain(lambda d: z_down.at[d], lambda i: z_down_up.at[i], lambda i: z_down_down.at[i], (dn_us, dn_ur, dn_ds, dn_dr), my, m)
    ups = [
        Chain(
            lambda d, j=j: z_gu.at[j, d], lambda i, j=j: z_gu_up.at[j, i], lambda i, j=j: z_gu_down.at[j, i],
            (gu_us.at[j], gu_ur.at[j], gu_ds.at[j], gu_dr.at[j]), my, m,
        )
        for j in range(2)
    ]
    part = tn(hidden[...], cot[...])
    for d in range(m):
        z_down[d] = part[d * (shard // m) : (d + 1) * (shard // m)].astype(bf16)
    downs.start()
    gather.forward()
    for j, grads in enumerate((grad_gate, grad_up)):
        for first in range(0, D, TILE):
            store_pieces(z_gu.at[j], tn(mid[:, first : first + TILE], grads[...]), first, m, piece)
        ups[j].start()
    w_wide[...] = jnp.zeros((D, HD), bf16)
    w_high, w_low = halves(w_small[...])
    for i, wide_part in enumerate((w_high, w_high, w_low)):
        w_wide[:, i * SMALL * H : (i + 1) * SMALL * H] = wide_part
    gather.direct(0).wait_recv()
    for k in range(1, n // 2):
        gather.passed(k).wait_recv()
    gather.finish()
    for load in loads[5:]:
        load.wait()
    rows = tn(head_rows[...], low_all[...])
    for share in range(rep):

        @pl.when(lax.rem(me, rep) == share)
        def _():
            for d in range(m):
                at = share * (HD // rep) + d * piece
                z_out[d] = rows[at : at + piece].astype(bf16)

    outs = Chain(lambda d: z_out.at[d], lambda i: z_out_up.at[i], lambda i: z_out_down.at[i], (ou_us, ou_ur, ou_ds, ou_dr), my, m)
    outs.start()
    if not roomy:
        normed = mid
        late = pltpu.make_async_copy(normed_any, normed, l_sems.at[13])
        late.start()
        late.wait()

    width = MIXED * HD
    starts = doc_starts(lengths)
    bias, rate = bias_ref[head], rate_ref[head]
    taps = head_taps(taps_ref, head)
    xbuf[0:8, :] = jnp.zeros((8, width), f32)
    halo[...] = jnp.zeros((8, width), f32)
    gconv_w[...] = jnp.zeros(gconv_w.shape, f32)
    gates_sum[...] = jnp.zeros((8, HD), f32)
    grad_state[...] = jnp.zeros((HD, HD), f32)

    def fill(c, _):
        xbuf[pl.ds(pl.multiple_of(8 + c * T, 8), T), :] = proj[rows_of(c, T), :width].astype(f32)
        return 0

    lax.fori_loop(0, n, fill, 0)

    def sibling_copy(j):
        return remote(part_out.at[j], part_in.at[j], p_ss.at[j], p_rs.at[j], "seq", sib)

    def owner_copy(j):
        return remote(chip_out.at[j], chip_in.at[chip], c_ss.at[j], c_rs.at[chip], "seq", 2 * j + side)

    def form(j):
        at = rows_of(j, 2 * T)
        found = nt(gp[at, :], w_in[...]) + nt(grad_small[at, :], w_wide[...])
        if rep > 1:
            found = found * (lax.rem(me, rep) == 0).astype(f32)
        for i in range(2):

            @pl.when(side == i)
            def _():
                part_own[j] = found[i * T : (i + 1) * T].astype(part_own.dtype)
                part_out[j] = found[(1 - i) * T : (2 - i) * T].astype(bf16)

        sibling_copy(j).start()

    def join(j):
        sibling_copy(j).wait_recv()
        found = part_own[j].astype(f32) + part_in[j].astype(f32)
        part_own[j] = found.astype(part_own.dtype)
        chip_out[j] = found.astype(bf16)

        @pl.when(chip != j)
        def _():
            owner_copy(j).start()

    hops = [(chain, q) for chain in (downs, *ups) for q in range(1, m - 1)]

    def after_turn(k):
        c = n - 1 - k

        @pl.when(lax.rem(k, 2) == 1)
        def _():
            form(c // 2)

            @pl.when(k > 1)
            def _():
                join(c // 2 + 1)

        for i, (chain, q) in enumerate(hops):

            @pl.when(k == 3 * i // 2)
            def _():
                chain.tick(q)

    def fetch(c):
        if roomy:
            return kept(news, rows_of(c, NH * T)), (invs[0, c], invs[1, c]), mixed[rows_of(c, T), :]
        late = [
            pltpu.make_async_copy(news_any.at[:, rows_of(c, NH * T)], news, l_sems.at[11]),
            pltpu.make_async_copy(invs_any.at[:, pl.ds(c, 1)], invs, l_sems.at[12]),
            pltpu.make_async_copy(mixed_any.at[rows_of(c, T)], mixed, l_sems.at[9]),
        ]
        for load in late:
            load.start()
        for load in late:
            load.wait()
        return (news[0], news[1]), (invs[0, 0], invs[1, 0]), mixed[...]

    turn = functools.partial(
        backward_turn, n, T, head, starts, bias, rate, taps, gain, lambda at: nt(low_all[at, :], w_head[...]),
        proj, small, states, fetch, gp, grad_small, gconv_w, xbuf, halo, gates_sum, grad_state, after_turn,
    )
    lax.fori_loop(0, n, turn, 0)

    units = TILE // (piece * m)
    ins = []
    for i, first in enumerate(range(0, D, TILE)):
        store_pieces(z_w, tn(normed[:, first : first + TILE], gp[...]), first, m, piece)
        at = pl.ds(i * units, units)
        ins.append(
            Chain(
                lambda d, at=at: z_w.at[d, at], lambda j, at=at: z_w_up.at[j, at], lambda j, at=at: z_w_down.at[j, at],
                (w_us.at[i], w_ur.at[i], w_ds.at[i], w_dr.at[i]), my, m,
            )
        )
        ins[-1].start()
    join(0)
    small_t = tn(grad_small[...], normed[...])
    small_t = small_t[: SMALL * H] + small_t[SMALL * H : 2 * SMALL * H]
    z_sum[0:1, :] = gain_mid_grad[...]
    for i in range(SMALL):
        z_sum[1 + i : 2 + i, :] = jnp.sum(small_t[i * H : (i + 1) * H], axis=0, keepdims=True)
    z_sum[4:8, :width] = gconv_w[...]
    for i in range(3):
        z_sum[4 + i : 5 + i, width : width + HD] = gates_sum[i : i + 1, :]
    z_sum[7:8, width : width + HD] = jnp.zeros((1, HD), f32)
    z_sum[4:8, width + HD :] = jnp.zeros((4, D - width - HD), f32)
    first_sums = Sums(z_sum, z_sum_in, q_sum, (sum_ss.at[0], sum_rs.at[0], qsum_ss.at[0], qsum_rs.at[0]), me, my, n, m)
    first_sums.start()
    for i, (chain, q) in enumerate(hops):
        if 3 * i // 2 >= n:
            chain.tick(q)

    def write_down(x):
        g_down[...] = x

    def write_out(x):
        g_out[...] = x

    downs.finish(write_down)
    q_ups = []
    for j in range(2):

        def write_up(x, j=j):
            q_gu[j] = x.astype(bf16)

        ups[j].finish(write_up)
        q_ups += [scatter_to(q_gu.at[j], q_gu_in.at[j], k, qgu_ss.at[j], qgu_rs.at[j], me, n) for k in range(1, n)]
    for copy in q_ups:
        copy.start()
    for j in range(2):
        q_gu_in[j, me] = q_gu[j, me]
    for q in range(1, m - 1):
        outs.tick(q)
    for chain in ins[:2]:
        for q in range(1, m - 1):
            chain.tick(q)
    first_sums.add()

    total = part_own[chip].astype(f32)
    for k in range(1, n // 2):
        other = lax.rem(chip + k, n // 2)
        remote(chip_out.at[other], chip_in.at[other], c_ss.at[other], c_rs.at[other], "seq", 2 * other + side).wait_recv()
        total = total + chip_in[other].astype(f32)
    values = tokens[...].astype(f32)
    part, gain_part = norm_back(values, norm_scale(values), gain_in[...], total)
    grad_input[...] = grad_residual[...] + part

    y_sum[...] = gain_part
    last_sums = Sums(y_sum, y_sum_in, r_sum, (sum_ss.at[1], sum_rs.at[1], qsum_ss.at[1], qsum_rs.at[1]), me, my, n, m)
    last_sums.start()
    q_ins = []
    for i, chain in enumerate(ins):
        if i > 1:
            for q in range(1, m - 1):
                chain.tick(q)
        if i == 2:
            outs.finish(write_out)

        def write_in(x, i=i):
            q_w[i * units : (i + 1) * units] = x.astype(bf16)

        chain.finish(write_in)
        for j in range(i * units, (i + 1) * units):

            @pl.when(me != j)
            def _():
                remote(q_w.at[j], q_w_in.at[me], qw_ss.at[j], qw_rs.at[me], "seq", j).start()

        if i == 2:
            last_sums.add()
    q_w_in[me] = q_w[me]
    for chain in (downs, *ups, outs, *ins):
        chain.settle()

    def settle(j, _):
        sibling_copy(j).wait_send()

        @pl.when(chip != j)
        def _():
            owner_copy(j).wait_send()

        return 0

    lax.fori_loop(0, n // 2, settle, 0)
    first_sums.settle()
    last_sums.settle()
    for copy in q_ups:
        copy.wait()
    for k in range(1, n):
        peer = lax.rem(me + k, n)
        remote(q_w.at[peer], q_w_in.at[me], qw_ss.at[peer], qw_rs.at[me], "seq", peer).wait_send()
        remote(q_w.at[peer], q_w_in.at[peer], qw_ss.at[peer], qw_rs.at[peer], "seq", peer).wait_recv()


def run_back(n, m, rep, T, lengths, bias, rate, tokens, grad_residual, gain_in, gain_mid_grad, w_small, taps, gain,
             mid, cot, w_gate_up, w_down, w_out, head_rows, proj, small, mixed, states, news, invs, normed, w_in):
    rows, piece, shard = n * T, D // (n * m), FF // n
    wide = -(-(shard + HD - 1) // HD) * HD
    vm, roomy = pltpu.VMEM, rows <= 1024
    band = GROUPS * HD

    def chained(*dims, lead=()):
        return [vm((*lead, m, *dims), bf16), vm((*lead, m - 1, *dims), bf16), vm((*lead, m - 1, *dims), bf16)]

    return pl.pallas_call(
        functools.partial(back_kernel, n, m, rep, T, piece, shard, wide),
        out_shape=(
            shape((T, D), f32), shape((n, piece, band), bf16), shape((piece, D), f32), shape((2, n, piece, shard), bf16),
            shape((shard // m, D), f32), shape((n, 8, D), f32), shape((n, 1, D), f32),
        ),
        in_specs=[SMEM] * 3 + [VMEM] * 7 + [ANY] * 14,
        out_specs=[VMEM] * 7,
        scratch_shapes=[
            vm((rows, D), bf16), vm((rows, D), bf16), vm((D, wide), bf16), vm((D, wide), bf16), vm((wide, D), bf16),
            vm((HD, D), bf16), vm((rows, HD), bf16), vm((rows, band), bf16), vm((rows, HD), f32), vm((rows if roomy else T, HD), f32),
            vm((2, n, HD, HD), bf16), vm((2, NH * (rows if roomy else T), HD), bf16), vm((2, n if roomy else 1, NH * T, NH * T), bf16),
            vm((rows, D) if roomy else (1, 16, HD), bf16), vm((D, band), bf16), vm((D, HD), bf16),
            vm((rows, D), bf16), vm((rows, shard), bf16), vm((rows, shard), bf16), vm((rows, shard), bf16),
            vm((rows, band), bf16), vm((rows, HD), bf16), vm((CONV, MIXED * HD), f32), vm((rows + 8, MIXED * HD), f32),
            vm((8, MIXED * HD), f32), vm((8, HD), f32), vm((HD, HD), f32),
            *chained(n, piece, shard, lead=(2,)), *chained(shard // m, D), *chained(piece, D), *chained(n, piece, band),
            vm((8, D), f32), vm((m - 1, 8, D), f32), vm((1, D), f32), vm((m - 1, 1, D), f32), vm((2, n, piece, shard), bf16), vm((n, piece, band), bf16),
            vm((n // 2, T, D), f32 if roomy else bf16), *[vm((n // 2, T, D), bf16)] * 4,
            DMA((14,)), DMA((GROUPS,)), *chain_sems(2, m - 1), *chain_sems(m - 1), *chain_sems(m - 1),
            *chain_sems(D // TILE, m - 1), DMA((2, m - 1)), DMA((2, m - 1)), DMA((2, n - 1)), DMA((2, n - 1)), DMA((n,)), DMA((n,)),
            DMA((2, n - 1)), DMA((2, n - 1)),
            *[DMA((n // 2,))] * 4, *gather_sems(n),
        ],
        compiler_params=pltpu.CompilerParams(vmem_limit_bytes=(60 if roomy else 63) * 1024 * 1024, collective_id=3, has_side_effects=True),
        name="backward",
    )(lengths, bias, rate, tokens, grad_residual, gain_in, gain_mid_grad, w_small, taps, gain,
      mid, cot, w_gate_up, w_down, w_out, head_rows, proj, small, mixed, states, news, invs, normed, w_in)


def output_kernel(
    n, rep, shard, result_in, grad_input_in, w_parts, out_part, gu_parts, down_part, sums, last,
    result, grad_input, g_in, g_out, g_gate_up, g_down, g_gain_in, g_gain_mid, g_small, g_bias, g_rate, g_taps, g_gain_head,
):
    result[...] = result_in[...]
    grad_input[...] = grad_input_in[...]
    g_out[...] = out_part[...]
    g_down[...] = down_part[...]
    for i in range(2):
        for source in range(n):
            at = i * FF + source * shard
            g_gate_up[:, at : at + shard] = gu_parts[i, source].astype(f32)
    g_gain_in[...] = jnp.sum(last[...], axis=0)
    g_gain_mid[...] = jnp.sum(sums[:, 0:1, :], axis=0)
    width = MIXED * HD
    gain_total = jnp.zeros((1, HD), f32)
    for h in range(H):
        found = sums[h * rep]
        part = w_parts[h * rep].astype(f32)
        for j in range(SMALL):
            g_small[j * H + h : j * H + h + 1, :] = found[1 + j : 2 + j, :]
        for i in range(MIXED):
            g_taps[:, i * D + h * HD : i * D + (h + 1) * HD] = found[4 : 4 + CONV, i * HD : (i + 1) * HD]
        for i in range(GROUPS):
            g_in[:, i * D + h * HD : i * D + (h + 1) * HD] = part[:, i * HD : (i + 1) * HD]
        gain_total = gain_total + found[4:5, width : width + HD]
        g_bias[h] = found[5, width + NH]
        g_rate[h] = found[6, width + NH]
    g_gain_head[...] = gain_total


def run_output(n, rep, *parts):
    result, grad_input, w_parts, out_part, gu_parts, down_part, sums, last = parts
    piece, shard = out_part.shape[0], gu_parts.shape[-1]
    return pl.pallas_call(
        functools.partial(output_kernel, n, rep, shard),
        out_shape=(
            shape(result.shape, bf16), shape(grad_input.shape, f32), shape((piece, GROUPS * D), f32), shape((piece, D), f32),
            shape((piece, 2 * FF), f32), shape(down_part.shape, f32), shape((1, D), f32), shape((1, D), f32),
            shape((SMALL * H, D), f32), shape((H,), f32), shape((H,), f32), shape((CONV, MIXED * D), f32), shape((1, HD), f32),
        ),
        in_specs=[VMEM] * 8,
        out_specs=[VMEM] * 9 + [SMEM] * 2 + [VMEM] * 2,
        compiler_params=pltpu.CompilerParams(vmem_limit_bytes=LIMIT),
        name="outputs",
    )(*parts)


def on_device(tokens, grad_out, doc_lengths, gain_in, in_weight, small_weight, gate_bias, decay_rate, conv_weight,
              gain_head, out_weight, gain_mid, gate_up_weight, down_weight):
    seq, stream = lax.axis_size("seq"), lax.axis_size("stream")
    rep = seq // H
    T = tokens.shape[1]
    gain = gain_head.reshape(1, HD)
    gain_in, gain_mid = gain_in.reshape(1, D), gain_mid.reshape(1, D)
    rows, cotangent = tokens[0], grad_out[0]
    gated, normed, out_all, proj, small, mixed, states, news, invs, head_rows = run_forward(
        seq, rep, T, doc_lengths, gate_bias, decay_rate, rows, cotangent, gain_in, in_weight, small_weight, conv_weight, gain
    )
    result, grad_residual, mid_all, grad_gain_mid = run_feed(
        seq, T, rows, gated, cotangent, out_weight, gain_mid, gate_up_weight, down_weight
    )
    parts = run_back(
        seq, stream, rep, T, doc_lengths, gate_bias, decay_rate, rows, grad_residual, gain_in, grad_gain_mid, small_weight,
        conv_weight, gain, mid_all, out_all, gate_up_weight, down_weight, out_weight, head_rows, proj, small, mixed, states,
        news, invs, normed, in_weight,
    )
    result, grad_input, g_in, g_out, g_gate_up, g_down, g_gain_in, g_gain_mid, g_small, g_bias, g_rate, g_taps, g_gain_head = (
        run_output(seq, rep, result, *parts)
    )
    return (
        result[None], grad_input[None], g_gain_in.reshape(D), g_in, g_small.T, g_bias, g_rate, g_taps,
        g_gain_head.reshape(HD), g_out, g_gain_mid.reshape(D), g_gate_up, g_down,
    )


def solution(mesh):
    rows, whole, split = P("stream", "seq", None), P(), P(("seq", "stream"), None)
    return jax.shard_map(
        on_device,
        mesh=mesh,
        in_specs=(rows, rows, P("stream", None)) + (whole,) * 11,
        out_specs=(rows, rows, whole, split, whole, whole, whole, whole, whole, split, whole, split, split),
        check_vma=False,
    )
```

```python
import functools

import jax
import jax.numpy as jnp
from jax import lax
from jax.experimental import pallas as pl
from jax.experimental.pallas import tpu as pltpu
from jax.sharding import PartitionSpec as P

D = 1024
H = 8
HD = 128
FF = 2816
NH = 2
CONV = 4
GROUPS = 2 + 2 * NH
MIXED = GROUPS - 1
SMALL = NH + 1
DOCS = 8
TILE = 256
EPS = 1e-06

f32 = jnp.float32
bf16 = jnp.bfloat16
MESH = pl.DeviceIdType.MESH
DMA = pltpu.SemaphoreType.DMA
VMEM = pl.BlockSpec(memory_space=pltpu.VMEM)
SMEM = pl.BlockSpec(memory_space=pltpu.SMEM)
ANY = pl.BlockSpec(memory_space=pl.ANY)
LIMIT = 56 * 1024 * 1024
shape = jax.ShapeDtypeStruct


def dot(a, b, dims):
    if isinstance(a, tuple) and isinstance(b, tuple):
        return dot(a[0], b[0], dims) + (dot(a[0], b[1], dims) + dot(a[1], b[0], dims))
    if isinstance(a, tuple):
        return dot(a[0], b, dims) + dot(a[1], b, dims)
    if isinstance(b, tuple):
        return dot(a, b[0], dims) + dot(a, b[1], dims)
    return lax.dot_general(
        a.astype(bf16), b.astype(bf16), ((dims[:1], dims[1:]), ((), ())), preferred_element_type=f32
    )


def nn(a, b):
    return dot(a, b, (1, 0))


def nt(a, b):
    return dot(a, b, (1, 1))


def tn(a, b):
    return dot(a, b, (0, 0))


def halves(x):
    high = x.astype(bf16)
    return high, (x - high.astype(f32)).astype(bf16)


def thirds(x):
    high, low = halves(x)
    return high, low, (x - high.astype(f32) - low.astype(f32)).astype(bf16)


def keep(ref, at, x):
    ref[0, at], ref[1, at] = halves(x)


def kept(ref, at):
    return ref[0, at], ref[1, at]


def nn_exact(ones, x):
    high, low, lowest = thirds(x)
    return nn(ones, high) + (nn(ones, low) + nn(ones, lowest))


def sigmoid(x):
    return 1.0 / (1.0 + jnp.exp(-x))


def softplus(x):
    return jnp.maximum(x, 0.0) + jnp.log(1.0 + jnp.exp(-jnp.abs(x)))


def norm_scale(values):
    return lax.rsqrt(jnp.mean(values * values, axis=-1, keepdims=True) + EPS)


def norm_back(values, scale, gain, grad):
    normal = values * scale
    e = grad * gain
    back = scale * (e - normal * jnp.mean(e * normal, axis=-1, keepdims=True))
    return back, jnp.sum(grad * normal, axis=0, keepdims=True)


def iota(dims, axis):
    return lax.broadcasted_iota(jnp.int32, dims, axis)


def doc_at(starts, positions):
    total = jnp.full(positions.shape, -1, jnp.int32)
    for start in starts:
        total = total + (start <= positions).astype(jnp.int32)
    return total


def doc_starts(lengths_ref):
    starts, at = [], jnp.int32(0)
    for j in range(DOCS):
        starts.append(at)
        at = at + lengths_ref[0, j]
    return starts


def stack2(a, b):
    return jnp.concatenate([a, b], axis=0)


def beside(a, b):
    return jnp.concatenate([a, b], axis=1)


def quad(a, b, c, d):
    return stack2(beside(a, b), beside(c, d))


def rows_of(i, size):
    return pl.ds(pl.multiple_of(i * size, size), size)


def greet(axis, peers):
    barrier = pltpu.get_barrier_semaphore()
    for peer in peers:
        pl.semaphore_signal(barrier, inc=1, device_id={axis: peer}, device_id_type=MESH)
    return lambda: pl.semaphore_wait(barrier, len(peers))


def remote(src, dst, send, receive, axis, peer):
    return pltpu.make_async_remote_copy(src, dst, send, receive, device_id={axis: peer}, device_id_type=MESH)


def flipped(chip, bits, chips):
    total, place = 0, 1
    while place < chips:
        total = total + place * lax.rem(chip // place + bits // place, 2)
        place *= 2
    return total


class Gather:
    def __init__(self, n, T, src, dst, sems):
        self.n, self.T, self.src, self.dst = n, T, src, dst
        self.ss, self.rs, self.fs, self.fr = sems
        self.me = lax.axis_index("seq")
        self.chip, self.side = self.me // 2, lax.rem(self.me, 2)
        self.sib = self.me + 1 - 2 * self.side
        order = sorted(range(1, n // 2), key=lambda k: k.bit_count())
        self.early = [k for k in order if k.bit_count() == 1]
        self.late = [k for k in order if k.bit_count() > 1]

    def at(self, device):
        return self.dst.at[rows_of(device, self.T)]

    def partner(self, k):
        return 2 * flipped(self.chip, k, self.n // 2) + self.side

    def direct(self, k):
        peer = self.sib if k == 0 else self.partner(k)
        return remote(self.src, self.at(self.me), self.ss.at[k], self.rs.at[k], "seq", peer)

    def passed(self, k):
        block = self.at(self.partner(k))
        return remote(block, block, self.fs.at[k], self.fr.at[k], "seq", self.sib)

    def relay(self, k):
        top = 1 << (k.bit_length() - 1)
        for side, last in ((0, top), (1, k & -k)):

            @pl.when(self.side == side)
            def _():
                block = self.at(self.partner(k - last))
                remote(block, block, self.ss.at[k], self.rs.at[k], "seq", self.partner(last)).start()

    def start(self):
        for k in (*self.early, 0):
            self.direct(k).start()

    def pass_on(self, k):
        self.direct(k).wait_recv()
        self.passed(k).start()

    def forward(self):
        for k in self.early:
            self.pass_on(k)
        for k in self.late:
            if k.bit_count() == 2:
                self.relay(k)

    def forward_late(self):
        for k in self.late:
            if k.bit_count() > 2:
                self.relay(k)
            self.pass_on(k)

    def arrive(self):
        self.direct(0).wait_recv()
        for k in range(1, self.n // 2):
            self.passed(k).wait_recv()

    def finish(self):
        for k in range(self.n // 2):
            self.direct(k).wait_send()
            if k:
                self.passed(k).wait_send()


def gather_sems(n):
    return [DMA((n // 2,)) for _ in range(4)]


def conv_of(block, taps, docs, T):
    total = block[8:] * taps[CONV - 1 : CONV]
    for lag in range(1, CONV):
        same = (docs[0] == docs[lag]).astype(f32)
        total = total + block[8 - lag : 8 - lag + T] * (taps[CONV - 1 - lag : CONV - lag] * same)
    return total


def chunk_gates(logits, bias, rate, starts, first, T):
    lane = iota((T, HD), 1)
    shifted = logits + bias
    gate = -rate * softplus(shifted)
    place_i, place_j = iota((T, T), 0), iota((T, T), 1)
    lower = place_j <= place_i
    cumul = nn_exact(lower.astype(bf16), jnp.where(lane == NH, gate, 0.0))
    beta = 2.0 * sigmoid(logits)
    b0, b1 = beta[:, 0:1], beta[:, 1:2]
    g = cumul[:, NH : NH + 1]
    g_row = jnp.transpose(cumul)[NH : NH + 1, :]
    g_last = cumul[T - 1 : T, NH : NH + 1]
    position = first + iota((T, 1), 0)
    docs = [doc_at(starts, position - lag) for lag in range(CONV)]
    doc = docs[0]
    doc_row = doc_at(starts, first + iota((1, T), 1))
    doc_before = doc_at(starts, jnp.full((1, 1), first - 1, jnp.int32))
    doc_last = doc_at(starts, jnp.full((1, 1), first + (T - 1), jnp.int32))
    joined = lower & (doc == doc_row)
    decay = jnp.where(joined, jnp.exp(jnp.where(joined, g - g_row, 0.0)), 0.0)
    strict = jnp.where(place_i == place_j, 0.0, decay)
    from_start = jnp.exp(g) * (doc == doc_before).astype(f32)
    to_end = jnp.exp(jnp.minimum(g_last - g, 0.0)) * (doc == doc_last).astype(f32)
    whole = jnp.exp(g_last) * (doc_last == doc_before).astype(f32)
    return dict(
        shifted=shifted, beta=beta, b=stack2(b0, b1), docs=docs, decay=decay,
        decays=quad(strict, strict, decay, strict), hd=from_start, hd2=stack2(from_start, from_start),
        to_end=stack2(to_end, to_end), whole=whole,
    )


def key_scale(raw):
    return lax.rsqrt(jnp.sum(raw * raw, axis=-1, keepdims=True) + EPS)


def chunk_inputs(block, taps, docs, T):
    conv = conv_of(block, taps, docs, T)
    sig = sigmoid(conv)
    active = conv * sig
    cut = [active[:, i * HD : (i + 1) * HD] for i in range(MIXED)]
    scales = (key_scale(cut[1]), key_scale(cut[2]))
    keys = stack2(cut[1] * scales[0], cut[2] * scales[1])
    values = stack2(cut[3], cut[4])
    return conv, sig, cut[0], keys, values, stack2(*scales)


def inverses(lowers, T):
    size = NH * T
    row, col = iota((size, size), 0), iota((size, size), 1)
    differ = (row & (T - 1)) ^ (col & (T - 1))
    eye = (row == col).astype(f32)
    found = [jnp.where(row == col, 1.0, jnp.where(differ == 0, -a, 0.0)) for a in lowers]
    step = 1
    while step < T:
        level = (differ >= step) & (differ < 2 * step)
        parts = [nn(jnp.where(level, a, 0.0), x) for a, x in zip(lowers, found)]
        found = [x - nn(x, part) for x, part in zip(found, parts)]
        step *= 2
    a_cut = [halves(a) for a in lowers]
    x_cut = [halves(x) for x in found]
    errors = [
        eye - x - (nn(a[0], xc[0]) + (nn(a[0], xc[1]) + nn(a[1], xc[0])))
        for a, x, xc in zip(a_cut, found, x_cut)
    ]
    return [x + nn(xc[0], e) for x, xc, e in zip(found, x_cut, errors)]


def head_gate(mixed, raw):
    scale = norm_scale(mixed)
    return mixed * scale, scale, sigmoid(raw)


def head_taps(taps_ref, head):
    cuts = [taps_ref[:, pl.ds(pl.multiple_of(i * D + head * HD, HD), HD)] for i in range(MIXED)]
    return jnp.concatenate(cuts, axis=1)


def intra_turn(T, starts, bias, rate, taps, small, block_of, invs, ubuf, wbuf, qbuf, pbuf, dbuf, gates, chunks):
    held, lowers = [], []
    for c in chunks:
        first = pl.multiple_of(c * T, T)
        gate = chunk_gates(small[pl.ds(first, T), :], bias, rate, starts, first, T)
        conv, sig, query, keys, values, scales = chunk_inputs(block_of(c), taps, gate["docs"], T)
        key_pair = halves(keys)
        lowers.append(gate["b"] * (nt(key_pair, key_pair) * gate["decays"]))
        held.append((c, gate, query, keys, key_pair, values))
    found = inverses(lowers, T)
    for (c, gate, query, keys, key_pair, values), inverse in zip(held, found):
        at, two = rows_of(c, T), rows_of(c, NH * T)
        pair = halves(inverse)
        invs[0, c], invs[1, c] = pair
        both = nn(pair, halves(gate["b"] * beside(values, gate["hd2"] * keys)))
        ubuf[two, :] = both[:, :HD]
        keep(wbuf, two, both[:, HD:])
        query_pair = halves(query)
        qbuf[0, at], qbuf[1, at] = query_pair
        keep(pbuf, at, nt(query_pair, key_pair) * beside(gate["decay"], gate["decay"]))
        keep(dbuf, two, gate["to_end"] * keys)
        gates[at, :] = jnp.where(iota((T, HD), 1) == 0, gate["hd"], gate["whole"])


def across_turn(T, gain, proj, mixed_out, states, news, head_rows, ubuf, wbuf, qbuf, pbuf, dbuf, gates, done, c, state):
    at, two = rows_of(c, T), rows_of(c, NH * T)
    state_pair = halves(state)
    states[0, c], states[1, c] = state_pair
    new = ubuf[two, :] - nn(kept(wbuf, two), state_pair)
    new_pair = halves(new)
    news[0, two], news[1, two] = new_pair
    gate = gates[at, :]
    mixed = gate[:, 0:1] * nn(kept(qbuf, at), state_pair) + nn(kept(pbuf, at), new_pair)
    mixed_out[at, :] = mixed
    raw = proj[at, MIXED * HD :].astype(f32)
    normal, _, sig = head_gate(mixed, raw)
    head_rows[at, :] = ((normal * gain[...]) * (raw * sig)).astype(bf16)
    done(c)
    return gate[0:1, 1:2] * state + tn(kept(dbuf, two), new_pair)


def widened(w_wide, parts):
    w_wide[...] = jnp.zeros((HD, D), bf16)
    for i, part in enumerate(parts):
        w_wide[32 * i : 32 * i + SMALL * H, :] = part


def forward_kernel(
    n, rep, T, lengths, bias_ref, rate_ref, tokens, cotangent, gain_in, w_in, w_small, taps_ref, gain,
    gated, normed, out_all, proj, small, mixed_out, states, news, invs, head_rows,
    own, tails, w_head, w_wide, tail_rows, xbuf, ubuf, wbuf, qbuf, pbuf, dbuf, gates,
    w_sems, own_sems, a_ss, a_rs, t_ss, t_rs, *sems,
):
    me = lax.axis_index("seq")
    head = me // rep
    chips = n // 2
    wait_for_all = greet("seq", [lax.rem(me + k, n) for k in range(1, n)])
    width = MIXED * HD
    loads = [
        pltpu.make_async_copy(
            w_in.at[:, pl.ds(pl.multiple_of(i * D + head * HD, HD), HD)], w_head.at[:, i * HD : (i + 1) * HD], w_sems.at[i]
        )
        for i in range(GROUPS)
    ]
    for load in loads:
        load.start()
    values = tokens[...].astype(f32)
    own[...] = (values * norm_scale(values) * gain_in[...]).astype(bf16)
    local = pltpu.make_async_copy(own, normed.at[rows_of(me, T)], own_sems.at[0])
    local.start()
    wait_for_all()
    first_gather = Gather(n, T, own, normed, sems[:4])
    second_gather = Gather(n, T, cotangent, out_all, sems[4:8])
    keep_out = pltpu.make_async_copy(cotangent, out_all.at[rows_of(me, T)], own_sems.at[2])
    keep_out.start()
    chip, side = first_gather.chip, first_gather.side
    last = own.at[T - 16 : T]

    def tail_copy(k):
        return remote(last, tails.at[chip], t_ss.at[k], t_rs.at[chip], "seq", lax.rem(me + k, n))

    mine = pltpu.make_async_copy(last, tails.at[chip], own_sems.at[1])
    early, late = first_gather.early, first_gather.late

    @pl.when(side == 1)
    def _():
        for k in range(1, n):
            tail_copy(k).start()
        mine.start()

    for k in (0, *early):
        first_gather.direct(k).start()

    starts = doc_starts(lengths)
    bias, rate = bias_ref[head], rate_ref[head]
    taps = head_taps(taps_ref, head)
    widened(w_wide, thirds(jnp.where((iota((SMALL * H, D), 0) & (H - 1)) == head, w_small[...], 0.0)))
    group, lane = iota((HD, HD), 0), iota((HD, HD), 1)
    picks = (((group & 31) >> 3) == lane) & (group < 96) & (lane < SMALL)
    picks = picks.astype(bf16)
    for load in loads:
        load.wait()
    local.wait()

    @pl.when(side == 1)
    def _():
        mine.wait()
        for k in range(1, n):
            tail_copy(k).wait_send()

    for j in range(chips):

        @pl.when(me != 2 * j + 1)
        def _():
            remote(last, tails.at[j], t_ss.at[0], t_rs.at[j], "seq", lax.rem(me + 1, n)).wait_recv()

    found = nn(tails[...].reshape(chips * 16, D), w_head[...]).astype(bf16).astype(f32)
    tail_rows[...] = found[:, :width]
    size = T + 8

    def block_of(c):
        return xbuf[pl.ds(pl.multiple_of(c * size, 8), size), :]

    def project(pair):
        at = rows_of(pair, 2 * T)
        block = normed[at, :]
        result = nn(block, w_head[...]).astype(bf16)
        proj[at, :] = result
        raw = thirds(nt(block, w_wide[...]))
        small[at, :] = nn(raw[0], picks) + (nn(raw[1], picks) + nn(raw[2], picks))
        mixing = result[:, :width].astype(f32)
        before = lax.rem(pair + chips - 1, chips)
        halo = tail_rows[pl.ds(pl.multiple_of(before * 16 + 8, 8), 8), :]
        base = pl.multiple_of(pair * (2 * size), 8)
        xbuf[pl.ds(base, 8), :] = jnp.where(pair > 0, halo, 0.0)
        xbuf[pl.ds(pl.multiple_of(base + 8, 8), T), :] = mixing[:T]
        xbuf[pl.ds(pl.multiple_of(base + size, 8), T + 8), :] = mixing[T - 8 :]

    first_gather.direct(0).wait_recv()
    for group in [(0,)] + [(*ks[i : i + 2],) for ks in (early, late) for i in range(0, len(ks), 2)]:
        if group[0] == early[0]:
            first_gather.forward()
        elif late and group[0] == late[0]:
            first_gather.forward_late()
            second_gather.start()
        for k in group:
            if k:
                first_gather.passed(k).wait_recv()
        pairs = [flipped(chip, k, chips) for k in group]
        for pair in pairs:
            project(pair)
        intra_turn(
            T, starts, bias, rate, taps, small, block_of, invs, ubuf, wbuf, qbuf, pbuf, dbuf, gates,
            [2 * pair + i for pair in pairs for i in range(2)],
        )

    first_gather.finish()
    column = pl.ds(pl.multiple_of(head * HD, HD), HD)

    def row_copy(c):
        return remote(head_rows.at[rows_of(c, T)], gated.at[:, column], a_ss.at[c], a_rs.at[head], "seq", c)

    def send_rows(c):
        @pl.when(c == n // 4)
        def _():
            second_gather.forward()

        @pl.when((c != me) & (lax.rem(me, rep) == 0))
        def _():
            row_copy(c).start()

    across = functools.partial(
        across_turn, T, gain, proj, mixed_out, states, news, head_rows, ubuf, wbuf, qbuf, pbuf, dbuf, gates, send_rows
    )
    lax.fori_loop(0, n, across, jnp.zeros((HD, HD), f32))

    @pl.when(lax.rem(me, rep) == 0)
    def _():
        kept_rows = pltpu.make_async_copy(head_rows.at[rows_of(me, T)], gated.at[:, column], own_sems.at[0])
        kept_rows.start()
        kept_rows.wait()

    keep_out.wait()
    second_gather.forward_late()

    def settle(k, _):
        peer = lax.rem(me + k, n)

        @pl.when(lax.rem(me, rep) == 0)
        def _():
            row_copy(peer).wait_send()

        @pl.when(lax.rem(peer, rep) == 0)
        def _():
            source = peer // rep
            remote(
                head_rows.at[rows_of(me, T)], gated.at[:, pl.ds(pl.multiple_of(source * HD, HD), HD)],
                a_ss.at[peer], a_rs.at[source], "seq", peer,
            ).wait_recv()

        return 0

    lax.fori_loop(1, n, settle, 0)
    second_gather.arrive()
    second_gather.finish()


def forward_scratch(n, T):
    rows = n * T
    return [
        pltpu.VMEM((rows + 8 * n, MIXED * HD), f32), pltpu.VMEM((NH * rows, HD), f32),
        pltpu.VMEM((2, NH * rows, HD), bf16), pltpu.VMEM((2, rows, HD), bf16), pltpu.VMEM((2, rows, NH * T), bf16),
        pltpu.VMEM((2, NH * rows, HD), bf16), pltpu.VMEM((rows, HD), f32),
    ]


def run_forward(n, rep, T, lengths, bias, rate, tokens, cotangent, gain_in, w_in, w_small, taps, gain):
    rows = n * T
    return pl.pallas_call(
        functools.partial(forward_kernel, n, rep, T),
        out_shape=(
            shape((T, D), bf16), shape((rows, D), bf16), shape((rows, D), bf16), shape((rows, GROUPS * HD), bf16),
            shape((rows, HD), f32), shape((rows, HD), f32), shape((2, n, HD, HD), bf16), shape((2, NH * rows, HD), bf16),
            shape((2, n, NH * T, NH * T), bf16), shape((rows, HD), bf16),
        ),
        in_specs=[SMEM] * 3 + [VMEM, VMEM, VMEM, ANY, VMEM, VMEM, VMEM],
        out_specs=[VMEM, VMEM, ANY] + [VMEM] * 7,
        scratch_shapes=[
            pltpu.VMEM((T, D), bf16), pltpu.VMEM((n // 2, 16, D), bf16), pltpu.VMEM((D, GROUPS * HD), bf16),
            pltpu.VMEM((HD, D), bf16), pltpu.VMEM((n * 8, MIXED * HD), f32),
            *forward_scratch(n, T),
            DMA((GROUPS,)), DMA((3,)), DMA((n,)), DMA((H,)), DMA((n,)), DMA((n // 2,)), *gather_sems(n), *gather_sems(n),
        ],
        compiler_params=pltpu.CompilerParams(vmem_limit_bytes=LIMIT, collective_id=1, has_side_effects=True),
        name="mixer_forward",
    )(lengths, bias, rate, tokens, cotangent, gain_in, w_in, w_small, taps, gain)


def feed_kernel(
    n, T, steps, tokens, gated, cotangent, w_out, gain_mid, w_gate, w_up, w_down,
    result, grad_residual, mid_all, gain_grad, residual, middle, total, grad_mid, own_sem, *sems,
):
    step = pl.program_id(0)
    me = lax.axis_index("seq")
    gather = Gather(n, T, middle, mid_all, sems)
    local = pltpu.make_async_copy(middle, mid_all.at[rows_of(me, T)], own_sem)

    @pl.when(step == 0)
    def _():
        peers = [gather.sib] + [gather.partner(k) for k in range(1, n // 2)]
        wait_for_all = greet("seq", peers)
        found = tokens[...].astype(f32) + nn(gated[...], w_out[...])
        residual[...] = found
        middle[...] = (found * norm_scale(found) * gain_mid[...]).astype(bf16)
        total[...] = found
        grad_mid[...] = jnp.zeros((T, D), f32)
        wait_for_all()
        gather.start()
        local.start()

    gate, up = nn(middle[...], w_gate[...]), nn(middle[...], w_up[...])
    sig = sigmoid(gate)
    silu = gate * sig
    hidden = (silu * up).astype(bf16)
    total[...] += nn(hidden, w_down[...])
    grad_hidden = nt(cotangent[...], w_down[...])
    grad_gate = (grad_hidden * up * (sig * (1.0 + gate * (1.0 - sig)))).astype(bf16)
    grad_up = (grad_hidden * silu).astype(bf16)
    grad_mid[...] += nt(grad_gate, w_gate[...]) + nt(grad_up, w_up[...])

    for at, what in ((5, gather.forward), (8, gather.forward_late)):

        @pl.when(step == at)
        def _():
            what()

    @pl.when(step == steps - 1)
    def _():
        result[...] = total[...].astype(bf16)
        values = residual[...]
        back, gain_part = norm_back(values, norm_scale(values), gain_mid[...], grad_mid[...])
        gain_grad[...] = gain_part
        grad_residual[...] = cotangent[...].astype(f32) + back
        gather.arrive()
        gather.finish()
        local.wait()


def run_feed(n, T, tokens, gated, cotangent, w_out, gain_mid, w_gate_up, w_down):
    steps = FF // TILE
    fixed = lambda *dims: pl.BlockSpec(dims, lambda i: (0, 0))
    return pl.pallas_call(
        functools.partial(feed_kernel, n, T, steps),
        grid=(steps,),
        out_shape=(shape((T, D), bf16), shape((T, D), f32), shape((n * T, D), bf16), shape((1, D), f32)),
        in_specs=[
            fixed(T, D), fixed(T, D), fixed(T, D), fixed(D, D), fixed(1, D),
            pl.BlockSpec((D, TILE), lambda i: (0, i)), pl.BlockSpec((D, TILE), lambda i: (0, i + FF // TILE)),
            pl.BlockSpec((TILE, D), lambda i: (i, 0)),
        ],
        out_specs=[fixed(T, D), fixed(T, D), ANY, fixed(1, D)],
        scratch_shapes=[
            pltpu.VMEM((T, D), f32), pltpu.VMEM((T, D), bf16), pltpu.VMEM((T, D), f32), pltpu.VMEM((T, D), f32),
            DMA, *gather_sems(n),
        ],
        compiler_params=pltpu.CompilerParams(vmem_limit_bytes=LIMIT, collective_id=2, has_side_effects=True),
        name="feed_forward",
    )(tokens, gated, cotangent, w_out, gain_mid, w_gate_up, w_gate_up, w_down)


def store_pieces(out, part, first, stream, piece):
    for i in range(part.shape[0] // piece):
        at = first // piece + i
        out[at % stream, at // stream] = part[i * piece : (i + 1) * piece].astype(bf16)


def backward_turn(
    n, T, head, starts, bias, rate, taps, gain, incoming_of, proj, small, states, fetch,
    gp, grad_small, gconv_w, xbuf, halo, gates_sum, grad_state, done, k, _,
):
    width = MIXED * HD
    lane = iota((T, HD), 1)
    place_i, place_j = iota((T, T), 0), iota((T, T), 1)
    upper = (place_j >= place_i).astype(bf16)
    under = place_j < place_i
    c = n - 1 - k
    first = pl.multiple_of(c * T, T)
    at, two = rows_of(c, T), rows_of(c, NH * T)
    gate = chunk_gates(small[at, :], bias, rate, starts, first, T)
    block = xbuf[pl.ds(first, T + 8), :]
    conv, sig, query, keys, values, scales = chunk_inputs(block, taps, gate["docs"], T)
    key_pair, query_pair = halves(keys), halves(query)
    b, hd, hd2, to_end = gate["b"], gate["hd"], gate["hd2"], gate["to_end"]
    decay2 = beside(gate["decay"], gate["decay"])
    pairs = nt(key_pair, key_pair) * gate["decays"]
    scores = nt(query_pair, key_pair) * decay2
    state = (states[0, c], states[1, c])
    state_grad = grad_state[...]
    new, inverse, mixed = fetch(c)
    raw = proj[at, width:].astype(f32)
    normal, scale, zsig = head_gate(mixed, raw)
    incoming = incoming_of(at)
    passed = incoming * (raw * zsig)
    gates_sum[0:1, :] += jnp.sum(passed * normal, axis=0, keepdims=True)
    grad_z = incoming * (normal * gain[...]) * (zsig * (1.0 + raw * (1.0 - zsig)))
    e = passed * gain[...]
    grad_mixed = scale * (e - normal * jnp.mean(e * normal, axis=-1, keepdims=True))
    gm = halves(grad_mixed)
    ended = halves(to_end * keys)
    grad_pair = halves(state_grad)
    grad_new = tn(halves(scores), gm) + nn(ended, grad_pair)
    grad_right = tn(inverse, halves(grad_new))
    moved = b * grad_right
    grad_state[...] = gate["whole"] * state_grad + tn(halves(hd * query), gm) - tn(halves(hd2 * keys), halves(moved))
    grad_ended = nt(new, grad_pair)
    grad_scores = nt(gm, new)
    grad_lower = jnp.where(gate["decays"] != 0.0, -nt(halves(grad_right), new), 0.0)
    from_grad = nt(gm, state)
    scored = grad_scores * decay2
    grad_query = hd * from_grad + nn(scored, key_pair[0])
    paired = (b * grad_lower) * gate["decays"]
    keyed = nn(key_pair, state)
    grad_keys = (
        tn(scored, query_pair[0]) + to_end * grad_ended - hd2 * nt(moved, state[0])
        + nn(paired, key_pair[0]) + tn(paired, key_pair[0])
    )
    lower_pairs = grad_lower * pairs
    grad_b = jnp.sum(grad_right * (values - hd2 * keyed), axis=-1, keepdims=True) + jnp.sum(
        lower_pairs, axis=-1, keepdims=True
    )
    four = b * lower_pairs
    both = grad_scores * scores
    joint = (four[:T, :T] + four[:T, T:]) + (four[T:, :T] + four[T:, T:]) + (both[:, :T] + both[:, T:])
    crossing = jnp.sum(jnp.where(under, nn_exact(upper, joint), 0.0), axis=-1, keepdims=True)
    start_part = -hd2 * jnp.sum(moved * keyed, axis=-1, keepdims=True)
    start_part = start_part[:T] + start_part[T:] + hd * jnp.sum(query * from_grad, axis=-1, keepdims=True)
    end_part = to_end * jnp.sum(grad_ended * keys, axis=-1, keepdims=True)
    end_part = end_part[:T] + end_part[T:]
    sums_in = jnp.where(lane == 0, start_part, jnp.where(lane == 1, end_part, 0.0))
    after = nn_exact(upper, sums_in)
    before = nn_exact(under.astype(bf16), sums_in)
    whole_part = gate["whole"] * jnp.sum(state_grad * (state[0].astype(f32) + state[1].astype(f32)), keepdims=True)
    grad_gate = crossing + after[:, 0:1] + before[:, 1:2] + whole_part
    shifted = gate["shifted"]
    grad_beta = [grad_b[i * T : (i + 1) * T] * (gate["beta"][:, i : i + 1] * (1.0 - 0.5 * gate["beta"][:, i : i + 1])) for i in range(NH)]
    grad_decay = (-grad_gate * rate * sigmoid(shifted))[:, NH : NH + 1]
    which = lane >> 3
    logit = jnp.where(which == 0, grad_beta[0], jnp.where(which == 1, grad_beta[1], grad_decay))
    grad_logits = jnp.where((lane < SMALL * H) & ((lane & (H - 1)) == head), logit, 0.0)
    gates_sum[1:2, :] += jnp.sum(jnp.where(lane == NH, grad_decay, 0.0), axis=0, keepdims=True)
    gates_sum[2:3, :] += jnp.sum(jnp.where(lane == NH, grad_gate * -softplus(shifted), 0.0), axis=0, keepdims=True)
    high = grad_logits.astype(bf16).astype(f32)
    grad_small[at, :] = (
        high + pltpu.roll(grad_logits - high, 32, 1) + pltpu.roll(high, 64, 1)
    ).astype(bf16)
    projected_out = jnp.sum(keys * grad_keys, axis=-1, keepdims=True)
    grad_raw = (grad_keys - keys * projected_out) * scales
    slope = sig * (1.0 + conv * (1.0 - sig))
    grad_active = jnp.concatenate([grad_query, grad_raw[:T], grad_raw[T:], moved[:T], moved[T:]], axis=1)
    grad_conv = grad_active * slope
    after_block = stack2(grad_conv, halo[...])
    halo[...] = grad_conv[:8]
    position = first + iota((T, 1), 0)
    total = grad_conv * taps[CONV - 1 : CONV]
    taps_grads = [None] * CONV
    taps_grads[CONV - 1] = jnp.sum(grad_conv * block[8:], axis=0, keepdims=True)
    for lag in range(1, CONV):
        same = (doc_at(starts, position + lag) == gate["docs"][0]).astype(f32)
        total = total + after_block[lag : lag + T] * (taps[CONV - 1 - lag : CONV - lag] * same)
        same = (gate["docs"][lag] == gate["docs"][0]).astype(f32)
        taps_grads[CONV - 1 - lag] = jnp.sum(
            grad_conv * (block[8 - lag : 8 - lag + T] * same), axis=0, keepdims=True
        )
    everything = beside(total, grad_z).astype(bf16)
    gp[at, :] = everything
    gconv_w[...] += jnp.concatenate(taps_grads, axis=0)
    done(k)
    return 0


class Chain:
    def __init__(self, own, up_in, down_in, sems, my, m):
        self.own, self.up_in, self.down_in = own, up_in, down_in
        self.us, self.ur, self.ds, self.dr = sems
        self.my, self.m = my, m

    def up(self, q):
        slot = q - self.my
        return self.own(self.my + self.m - 1 - q), self.up_in(slot), slot, self.my + 1, self.us, self.ur

    def down(self, q):
        slot = q - (self.m - 1 - self.my)
        return self.own(self.my - (self.m - 1 - q)), self.down_in(slot), slot, self.my - 1, self.ds, self.dr

    def copy(self, hop):
        own, arrived, slot, peer, send, receive = hop
        return remote(own, arrived, send.at[slot], receive.at[slot], "stream", peer)

    def start(self):
        for q in range(self.m - 1):

            @pl.when(self.my == 0)
            def _():
                self.copy(self.up(q)).start()

            @pl.when(self.my == self.m - 1)
            def _():
                self.copy(self.down(q)).start()

    def tick(self, q):
        for inner, way in (
            ((self.my > 0) & (self.my <= q), self.up),
            ((self.my < self.m - 1) & (self.my >= self.m - 1 - q), self.down),
        ):

            @pl.when(inner)
            def _():
                hop = way(q)
                self.copy(hop).wait_recv()
                hop[0][...] = (hop[0][...].astype(f32) + hop[1][...].astype(f32)).astype(bf16)
                self.copy(hop).start()

    def finish(self, write):
        last = self.m - 1

        @pl.when(self.my > 0)
        def _():
            slot = last - self.my
            remote(self.own(self.my), self.up_in(slot), self.us.at[slot], self.ur.at[slot], "stream", self.my - 1).wait_recv()

        @pl.when(self.my < last)
        def _():
            slot = self.my
            remote(self.own(self.my), self.down_in(slot), self.ds.at[slot], self.dr.at[slot], "stream", self.my + 1).wait_recv()

        mine = self.own(self.my)

        @pl.when((self.my > 0) & (self.my < last))
        def _():
            write(mine[...].astype(f32) + self.up_in(last - self.my)[...].astype(f32) + self.down_in(self.my)[...].astype(f32))

        @pl.when(self.my == last)
        def _():
            write(mine[...].astype(f32) + self.up_in(0)[...].astype(f32))

        @pl.when(self.my == 0)
        def _():
            write(mine[...].astype(f32) + self.down_in(0)[...].astype(f32))

    def settle(self):
        for q in range(self.m - 1):

            @pl.when(self.my <= q)
            def _():
                self.copy(self.up(q)).wait_send()

            @pl.when(self.my >= self.m - 1 - q)
            def _():
                self.copy(self.down(q)).wait_send()


class Sums:
    def __init__(self, own, arrived, every, sems, me, my, n, m):
        self.own, self.arrived, self.every = own, arrived, every
        self.zs, self.zr, self.ss, self.rs = sems
        self.me, self.my, self.n, self.m = me, my, n, m

    def across(self, k):
        peer = lax.rem(self.my + k, self.m)
        return remote(self.own, self.arrived.at[k - 1], self.zs.at[k - 1], self.zr.at[k - 1], "stream", peer)

    def along(self, k):
        block = self.every.at[self.me]
        return remote(block, block, self.ss.at[k - 1], self.rs.at[k - 1], "seq", lax.rem(self.me + k, self.n))

    def start(self):
        for k in range(1, self.m):
            self.across(k).start()

    def add(self):
        total = self.own[...]
        for k in range(1, self.m):
            self.across(k).wait()
            total = total + self.arrived[k - 1]
        self.every[self.me] = total
        for k in range(1, self.n):
            self.along(k).start()

    def settle(self):
        for k in range(1, self.n):
            self.along(k).wait()


def chain_sems(*lead):
    return [DMA(lead) for _ in range(4)]


def scatter_to(own, arrived, k, send, receive, me, size):
    peer = lax.rem(me + k, size)
    return remote(own.at[peer], arrived.at[me], send.at[k - 1], receive.at[k - 1], "seq", peer)


def back_kernel(
    n, m, rep, T, piece, shard, wide,
    lengths, bias_ref, rate_ref, tokens, grad_residual, gain_in, gain_mid_grad, w_small, taps_ref, gain,
    mid_any, out_any, w_gate_up, w_down, w_out, rows_any, proj_any, small_any, mixed_any, states_any, news_any, invs_any,
    normed_any, w_in_any,
    grad_input, q_w_in, g_out, q_gu_in, g_down, q_sum, r_sum,
    mid, cot, w_gate, w_up, w_hid, w_head, head_rows, proj, small, mixed, states, news, invs, normed, w_in, w_wide,
    low_all, hidden, grad_gate, grad_up, gp, grad_small, gconv_w, xbuf, halo, gates_sum, grad_state,
    z_gu, z_gu_up, z_gu_down, z_down, z_down_up, z_down_down, z_out, z_out_up, z_out_down, z_w, z_w_up, z_w_down,
    z_sum, z_sum_in, y_sum, y_sum_in, q_gu, q_w, part_own, part_out, part_in, chip_out, chip_in,
    l_sems, i_sems, gu_us, gu_ur, gu_ds, gu_dr, dn_us, dn_ur, dn_ds, dn_dr, ou_us, ou_ur, ou_ds, ou_dr, w_us, w_ur, w_ds, w_dr,
    sum_ss, sum_rs, qgu_ss, qgu_rs, qw_ss, qw_rs, qsum_ss, qsum_rs, p_ss, p_rs, c_ss, c_rs, *sems,
):
    me, my = lax.axis_index("seq"), lax.axis_index("stream")
    head, chip, side = me // rep, me // 2, lax.rem(me, 2)
    sib = me + 1 - 2 * side
    barrier = pltpu.get_barrier_semaphore()
    for k in range(1, n):
        pl.semaphore_signal(barrier, inc=1, device_id={"seq": lax.rem(me + k, n)}, device_id_type=MESH)
    for k in range(1, m):
        pl.semaphore_signal(barrier, inc=1, device_id={"stream": lax.rem(my + k, m)}, device_id_type=MESH)
    first_unit = me * shard
    base = (first_unit // HD - me // (n - 1)) * HD
    offset = first_unit - base
    sources = [
        mid_any, out_any, w_gate_up.at[:, pl.ds(pl.multiple_of(base, HD), wide)],
        w_gate_up.at[:, pl.ds(pl.multiple_of(FF + base, HD), wide)], w_down.at[pl.ds(pl.multiple_of(base, HD), wide)],
        w_out.at[rows_of(head, HD)], rows_any, proj_any, small_any, mixed_any, states_any, news_any, invs_any, normed_any,
    ]
    places = [mid, cot, w_gate, w_up, w_hid, w_head, head_rows, proj, small, mixed, states, news, invs, normed]
    roomy = len(normed.shape) == 2
    loads = [pltpu.make_async_copy(a, b, l_sems.at[i]) for i, (a, b) in enumerate(zip(sources, places)) if i not in (9, 11, 12, 13) or roomy]
    for i in range(GROUPS):
        column = pl.ds(pl.multiple_of(i * D + head * HD, HD), HD)
        loads.append(pltpu.make_async_copy(w_in_any.at[:, column], w_in.at[:, i * HD : (i + 1) * HD], i_sems.at[i]))
    for load in loads[:5]:
        load.start()
    low_all[rows_of(me, T), :] = grad_residual[...].astype(bf16)
    pl.semaphore_wait(barrier, n + m - 2)
    gather = Gather(n, T, low_all.at[rows_of(me, T)], low_all, sems)
    gather.start()

    for load in loads[:5]:
        load.wait()
    for load in loads[5:]:
        load.start()

    def feed_turn(i, _):
        at = rows_of(i, TILE)
        block = mid[at, :]
        gate, up = nn(block, w_gate[...]), nn(block, w_up[...])
        sig = sigmoid(gate)
        silu = gate * sig
        grad_hidden = nt(cot[at, :], w_hid[...])
        own = lambda x: pltpu.roll(x, wide - offset, 1)[:, :shard].astype(bf16)
        hidden[at, :] = own(silu * up)
        grad_gate[at, :] = own(grad_hidden * up * (sig * (1.0 + gate * (1.0 - sig))))
        grad_up[at, :] = own(grad_hidden * silu)
        return 0

    lax.fori_loop(0, n * T // TILE, feed_turn, 0)
    downs = Chain(lambda d: z_down.at[d], lambda i: z_down_up.at[i], lambda i: z_down_down.at[i], (dn_us, dn_ur, dn_ds, dn_dr), my, m)
    ups = [
        Chain(
            lambda d, j=j: z_gu.at[j, d], lambda i, j=j: z_gu_up.at[j, i], lambda i, j=j: z_gu_down.at[j, i],
            (gu_us.at[j], gu_ur.at[j], gu_ds.at[j], gu_dr.at[j]), my, m,
        )
        for j in range(2)
    ]
    part = tn(hidden[...], cot[...])
    for d in range(m):
        z_down[d] = part[d * (shard // m) : (d + 1) * (shard // m)].astype(bf16)
    downs.start()
    gather.forward()
    for j, grads in enumerate((grad_gate, grad_up)):
        if j:
            gather.forward_late()
        for first in range(0, D, TILE):
            store_pieces(z_gu.at[j], tn(mid[:, first : first + TILE], grads[...]), first, m, piece)
        ups[j].start()
    w_high, w_low = halves(w_small[...])
    widened(w_wide, (w_high, w_high, w_low))
    gather.arrive()
    gather.finish()
    for load in loads[5:]:
        load.wait()
    rows = tn(head_rows[...], low_all[...])
    for share in range(rep):

        @pl.when(lax.rem(me, rep) == share)
        def _():
            for d in range(m):
                at = share * (HD // rep) + d * piece
                z_out[d] = rows[at : at + piece].astype(bf16)

    outs = Chain(lambda d: z_out.at[d], lambda i: z_out_up.at[i], lambda i: z_out_down.at[i], (ou_us, ou_ur, ou_ds, ou_dr), my, m)
    outs.start()
    if not roomy:
        normed = mid
        late = pltpu.make_async_copy(normed_any, normed, l_sems.at[13])
        late.start()
        late.wait()

    width = MIXED * HD
    starts = doc_starts(lengths)
    bias, rate = bias_ref[head], rate_ref[head]
    taps = head_taps(taps_ref, head)
    xbuf[0:8, :] = jnp.zeros((8, width), f32)
    halo[...] = jnp.zeros((8, width), f32)
    gconv_w[...] = jnp.zeros(gconv_w.shape, f32)
    gates_sum[...] = jnp.zeros((8, HD), f32)
    grad_state[...] = jnp.zeros((HD, HD), f32)

    def fill(c, _):
        xbuf[pl.ds(pl.multiple_of(8 + c * T, 8), T), :] = proj[rows_of(c, T), :width].astype(f32)
        return 0

    lax.fori_loop(0, n, fill, 0)

    def sibling_copy(j):
        return remote(part_out.at[j], part_in.at[j], p_ss.at[j], p_rs.at[j], "seq", sib)

    def owner_copy(j):
        return remote(chip_out.at[j], chip_in.at[chip], c_ss.at[j], c_rs.at[chip], "seq", 2 * j + side)

    def form(j):
        at = rows_of(j, 2 * T)
        found = nt(gp[at, :], w_in[...]) + nn(grad_small[at, :], w_wide[...])
        if rep > 1:
            found = found * (lax.rem(me, rep) == 0).astype(f32)
        for i in range(2):

            @pl.when(side == i)
            def _():
                part_own[j] = found[i * T : (i + 1) * T].astype(part_own.dtype)
                part_out[j] = found[(1 - i) * T : (2 - i) * T].astype(bf16)

        sibling_copy(j).start()

    def join(j):
        sibling_copy(j).wait_recv()
        found = part_own[j].astype(f32) + part_in[j].astype(f32)
        part_own[j] = found.astype(part_own.dtype)
        chip_out[j] = found.astype(bf16)

        @pl.when(chip != j)
        def _():
            owner_copy(j).start()

    hops = [(chain, q) for chain in (downs, *ups) for q in range(1, m - 1)]

    def after_turn(k):
        c = n - 1 - k

        @pl.when(lax.rem(k, 2) == 1)
        def _():
            form(c // 2)

        @pl.when((lax.rem(k, 2) == 0) & (k > 0))
        def _():
            join((c + 1) // 2)

        for i, (chain, q) in enumerate(hops):

            @pl.when(k == 3 * i // 2)
            def _():
                chain.tick(q)

    def fetch(c):
        if roomy:
            return kept(news, rows_of(c, NH * T)), (invs[0, c], invs[1, c]), mixed[rows_of(c, T), :]
        late = [
            pltpu.make_async_copy(news_any.at[:, rows_of(c, NH * T)], news, l_sems.at[11]),
            pltpu.make_async_copy(invs_any.at[:, pl.ds(c, 1)], invs, l_sems.at[12]),
            pltpu.make_async_copy(mixed_any.at[rows_of(c, T)], mixed, l_sems.at[9]),
        ]
        for load in late:
            load.start()
        for load in late:
            load.wait()
        return (news[0], news[1]), (invs[0, 0], invs[1, 0]), mixed[...]

    turn = functools.partial(
        backward_turn, n, T, head, starts, bias, rate, taps, gain, lambda at: nt(low_all[at, :], w_head[...]),
        proj, small, states, fetch, gp, grad_small, gconv_w, xbuf, halo, gates_sum, grad_state, after_turn,
    )
    lax.fori_loop(0, n, turn, 0)

    small_t = tn(grad_small[...], normed[...])
    small_t = small_t[: SMALL * H] + small_t[32 : 32 + SMALL * H]
    z_sum[0:1, :] = gain_mid_grad[...]
    for i in range(SMALL):
        z_sum[1 + i : 2 + i, :] = jnp.sum(small_t[i * H : (i + 1) * H], axis=0, keepdims=True)
    z_sum[4:8, :width] = gconv_w[...]
    for i in range(3):
        z_sum[4 + i : 5 + i, width : width + HD] = gates_sum[i : i + 1, :]
    z_sum[7:8, width : width + HD] = jnp.zeros((1, HD), f32)
    z_sum[4:8, width + HD :] = jnp.zeros((4, D - width - HD), f32)
    first_sums = Sums(z_sum, z_sum_in, q_sum, (sum_ss.at[0], sum_rs.at[0], qsum_ss.at[0], qsum_rs.at[0]), me, my, n, m)
    first_sums.start()

    units = TILE // (piece * m)
    ins = []
    for i, first in enumerate(range(0, D, TILE)):
        store_pieces(z_w, tn(normed[:, first : first + TILE], gp[...]), first, m, piece)
        at = pl.ds(i * units, units)
        ins.append(
            Chain(
                lambda d, at=at: z_w.at[d, at], lambda j, at=at: z_w_up.at[j, at], lambda j, at=at: z_w_down.at[j, at],
                (w_us.at[i], w_ur.at[i], w_ds.at[i], w_dr.at[i]), my, m,
            )
        )
        ins[-1].start()
        if i == 0:
            join(0)
    for i, (chain, q) in enumerate(hops):
        if 3 * i // 2 >= n:
            chain.tick(q)

    def write_down(x):
        g_down[...] = x

    def write_out(x):
        g_out[...] = x

    downs.finish(write_down)
    for j in range(2):

        def write_up(x, j=j):
            q_gu[:, j] = x.astype(bf16)

        ups[j].finish(write_up)
    q_ups = [scatter_to(q_gu, q_gu_in, k, qgu_ss, qgu_rs, me, n) for k in range(1, n)]
    for copy in q_ups:
        copy.start()
    q_gu_in[me] = q_gu[me]
    for q in range(1, m - 1):
        outs.tick(q)
    y_sum_in_use = (sum_ss.at[1], sum_rs.at[1], qsum_ss.at[1], qsum_rs.at[1])
    last_sums = Sums(y_sum, y_sum_in, r_sum, y_sum_in_use, me, my, n, m)

    def input_gradient():
        total = part_own[chip].astype(f32)
        for k in range(1, n // 2):
            other = lax.rem(chip + k, n // 2)
            remote(chip_out.at[other], chip_in.at[other], c_ss.at[other], c_rs.at[other], "seq", 2 * other + side).wait_recv()
            total = total + chip_in[other].astype(f32)
        values = tokens[...].astype(f32)
        part, gain_part = norm_back(values, norm_scale(values), gain_in[...], total)
        grad_input[...] = grad_residual[...] + part
        y_sum[...] = gain_part
        last_sums.start()

    def deliver(i):
        def write_in(x):
            q_w[i * units : (i + 1) * units] = x.astype(bf16)

        ins[i].finish(write_in)
        for j in range(i * units, (i + 1) * units):

            @pl.when(me != j)
            def _():
                remote(q_w.at[j], q_w_in.at[me], qw_ss.at[j], qw_rs.at[me], "seq", j).start()

    first_sums.add()
    for i, chain in enumerate(ins):
        for q in range(1, m - 1):
            chain.tick(q)
        if i:
            deliver(i - 1)
        if i == 1:
            outs.finish(write_out)
        if i == 2:
            input_gradient()
    deliver(len(ins) - 1)
    last_sums.add()
    q_w_in[me] = q_w[me]
    for chain in (downs, *ups, outs, *ins):
        chain.settle()

    def settle(j, _):
        sibling_copy(j).wait_send()

        @pl.when(chip != j)
        def _():
            owner_copy(j).wait_send()

        return 0

    lax.fori_loop(0, n // 2, settle, 0)
    first_sums.settle()
    last_sums.settle()
    for copy in q_ups:
        copy.wait()
    for k in range(1, n):
        peer = lax.rem(me + k, n)
        remote(q_w.at[peer], q_w_in.at[me], qw_ss.at[peer], qw_rs.at[me], "seq", peer).wait_send()
        remote(q_w.at[peer], q_w_in.at[peer], qw_ss.at[peer], qw_rs.at[peer], "seq", peer).wait_recv()


def run_back(n, m, rep, T, lengths, bias, rate, tokens, grad_residual, gain_in, gain_mid_grad, w_small, taps, gain,
             mid, cot, w_gate_up, w_down, w_out, head_rows, proj, small, mixed, states, news, invs, normed, w_in):
    rows, piece, shard = n * T, D // (n * m), FF // n
    wide = -(-(shard + HD - 1) // HD) * HD
    vm, roomy = pltpu.VMEM, rows <= 1024
    band = GROUPS * HD

    def chained(*dims, lead=()):
        return [vm((*lead, m, *dims), bf16), vm((*lead, m - 1, *dims), bf16), vm((*lead, m - 1, *dims), bf16)]

    return pl.pallas_call(
        functools.partial(back_kernel, n, m, rep, T, piece, shard, wide),
        out_shape=(
            shape((T, D), f32), shape((n, piece, band), bf16), shape((piece, D), f32), shape((n, 2, piece, shard), bf16),
            shape((shard // m, D), f32), shape((n, 8, D), f32), shape((n, 1, D), f32),
        ),
        in_specs=[SMEM] * 3 + [VMEM] * 7 + [ANY] * 14,
        out_specs=[VMEM] * 7,
        scratch_shapes=[
            vm((rows, D), bf16), vm((rows, D), bf16), vm((D, wide), bf16), vm((D, wide), bf16), vm((wide, D), bf16),
            vm((HD, D), bf16), vm((rows, HD), bf16), vm((rows, band), bf16), vm((rows, HD), f32), vm((rows if roomy else T, HD), f32),
            vm((2, n, HD, HD), bf16), vm((2, NH * (rows if roomy else T), HD), bf16), vm((2, n if roomy else 1, NH * T, NH * T), bf16),
            vm((rows, D) if roomy else (1, 16, HD), bf16), vm((D, band), bf16), vm((HD, D), bf16),
            vm((rows, D), bf16), vm((rows, shard), bf16), vm((rows, shard), bf16), vm((rows, shard), bf16),
            vm((rows, band), bf16), vm((rows, HD), bf16), vm((CONV, MIXED * HD), f32), vm((rows + 8, MIXED * HD), f32),
            vm((8, MIXED * HD), f32), vm((8, HD), f32), vm((HD, HD), f32),
            *chained(n, piece, shard, lead=(2,)), *chained(shard // m, D), *chained(piece, D), *chained(n, piece, band),
            vm((8, D), f32), vm((m - 1, 8, D), f32), vm((1, D), f32), vm((m - 1, 1, D), f32), vm((n, 2, piece, shard), bf16), vm((n, piece, band), bf16),
            vm((n // 2, T, D), f32 if roomy else bf16), *[vm((n // 2, T, D), bf16)] * 4,
            DMA((14,)), DMA((GROUPS,)), *chain_sems(2, m - 1), *chain_sems(m - 1), *chain_sems(m - 1),
            *chain_sems(D // TILE, m - 1), DMA((2, m - 1)), DMA((2, m - 1)), DMA((n - 1,)), DMA((n - 1,)), DMA((n,)), DMA((n,)),
            DMA((2, n - 1)), DMA((2, n - 1)),
            *[DMA((n // 2,))] * 4, *gather_sems(n),
        ],
        compiler_params=pltpu.CompilerParams(vmem_limit_bytes=(60 if roomy else 63) * 1024 * 1024, collective_id=3, has_side_effects=True),
        name="backward",
    )(lengths, bias, rate, tokens, grad_residual, gain_in, gain_mid_grad, w_small, taps, gain,
      mid, cot, w_gate_up, w_down, w_out, head_rows, proj, small, mixed, states, news, invs, normed, w_in)


def output_kernel(
    n, rep, shard, result_in, grad_input_in, w_parts, out_part, gu_parts, down_part, sums, last,
    result, grad_input, g_in, g_out, g_gate_up, g_down, g_gain_in, g_gain_mid, g_small, g_bias, g_rate, g_taps, g_gain_head,
):
    result[...] = result_in[...]
    grad_input[...] = grad_input_in[...]
    g_out[...] = out_part[...]
    g_down[...] = down_part[...]
    for i in range(2):
        for source in range(n):
            at = i * FF + source * shard
            g_gate_up[:, at : at + shard] = gu_parts[source, i].astype(f32)
    g_gain_in[...] = jnp.sum(last[...], axis=0)
    g_gain_mid[...] = jnp.sum(sums[:, 0:1, :], axis=0)
    width = MIXED * HD
    gain_total = jnp.zeros((1, HD), f32)
    for h in range(H):
        found = sums[h * rep]
        part = w_parts[h * rep].astype(f32)
        for j in range(SMALL):
            g_small[j * H + h : j * H + h + 1, :] = found[1 + j : 2 + j, :]
        for i in range(MIXED):
            g_taps[:, i * D + h * HD : i * D + (h + 1) * HD] = found[4 : 4 + CONV, i * HD : (i + 1) * HD]
        for i in range(GROUPS):
            g_in[:, i * D + h * HD : i * D + (h + 1) * HD] = part[:, i * HD : (i + 1) * HD]
        gain_total = gain_total + found[4:5, width : width + HD]
        g_bias[h] = found[5, width + NH]
        g_rate[h] = found[6, width + NH]
    g_gain_head[...] = gain_total


def run_output(n, rep, *parts):
    result, grad_input, w_parts, out_part, gu_parts, down_part, sums, last = parts
    piece, shard = out_part.shape[0], gu_parts.shape[-1]
    return pl.pallas_call(
        functools.partial(output_kernel, n, rep, shard),
        out_shape=(
            shape(result.shape, bf16), shape(grad_input.shape, f32), shape((piece, GROUPS * D), f32), shape((piece, D), f32),
            shape((piece, 2 * FF), f32), shape(down_part.shape, f32), shape((1, D), f32), shape((1, D), f32),
            shape((SMALL * H, D), f32), shape((H,), f32), shape((H,), f32), shape((CONV, MIXED * D), f32), shape((1, HD), f32),
        ),
        in_specs=[VMEM] * 8,
        out_specs=[VMEM] * 9 + [SMEM] * 2 + [VMEM] * 2,
        compiler_params=pltpu.CompilerParams(vmem_limit_bytes=LIMIT),
        name="outputs",
    )(*parts)


def on_device(tokens, grad_out, doc_lengths, gain_in, in_weight, small_weight, gate_bias, decay_rate, conv_weight,
              gain_head, out_weight, gain_mid, gate_up_weight, down_weight):
    seq, stream = lax.axis_size("seq"), lax.axis_size("stream")
    rep = seq // H
    T = tokens.shape[1]
    gain = gain_head.reshape(1, HD)
    gain_in, gain_mid = gain_in.reshape(1, D), gain_mid.reshape(1, D)
    rows, cotangent, small_weight = tokens[0], grad_out[0], small_weight.T
    gated, normed, out_all, proj, small, mixed, states, news, invs, head_rows = run_forward(
        seq, rep, T, doc_lengths, gate_bias, decay_rate, rows, cotangent, gain_in, in_weight, small_weight, conv_weight, gain
    )
    result, grad_residual, mid_all, grad_gain_mid = run_feed(
        seq, T, rows, gated, cotangent, out_weight, gain_mid, gate_up_weight, down_weight
    )
    parts = run_back(
        seq, stream, rep, T, doc_lengths, gate_bias, decay_rate, rows, grad_residual, gain_in, grad_gain_mid, small_weight,
        conv_weight, gain, mid_all, out_all, gate_up_weight, down_weight, out_weight, head_rows, proj, small, mixed, states,
        news, invs, normed, in_weight,
    )
    result, grad_input, g_in, g_out, g_gate_up, g_down, g_gain_in, g_gain_mid, g_small, g_bias, g_rate, g_taps, g_gain_head = (
        run_output(seq, rep, result, *parts)
    )
    return (
        result[None], grad_input[None], g_gain_in.reshape(D), g_in, g_small.T, g_bias, g_rate, g_taps,
        g_gain_head.reshape(HD), g_out, g_gain_mid.reshape(D), g_gate_up, g_down,
    )


def solution(mesh):
    rows, whole, split = P("stream", "seq", None), P(), P(("seq", "stream"), None)
    return jax.shard_map(
        on_device,
        mesh=mesh,
        in_specs=(rows, rows, P("stream", None)) + (whole,) * 11,
        out_specs=(rows, rows, whole, split, whole, whole, whole, whole, whole, split, whole, split, split),
        check_vma=False,
    )
```

```python
import functools

import jax
import jax.numpy as jnp
from jax import lax
from jax.experimental import pallas as pl
from jax.experimental.pallas import tpu as pltpu
from jax.sharding import PartitionSpec as P

D = 1024
H = 8
HD = 128
FF = 2816
NH = 2
CONV = 4
GROUPS = 2 + 2 * NH
MIXED = GROUPS - 1
SMALL = NH + 1
DOCS = 8
TILE = 256
EPS = 1e-06

f32 = jnp.float32
bf16 = jnp.bfloat16
MESH = pl.DeviceIdType.MESH
DMA = pltpu.SemaphoreType.DMA
VMEM = pl.BlockSpec(memory_space=pltpu.VMEM)
SMEM = pl.BlockSpec(memory_space=pltpu.SMEM)
ANY = pl.BlockSpec(memory_space=pl.ANY)
LIMIT = 56 * 1024 * 1024
shape = jax.ShapeDtypeStruct


def dot(a, b, dims):
    if isinstance(a, tuple) and isinstance(b, tuple):
        return dot(a[0], b[0], dims) + (dot(a[0], b[1], dims) + dot(a[1], b[0], dims))
    if isinstance(a, tuple):
        return dot(a[0], b, dims) + dot(a[1], b, dims)
    if isinstance(b, tuple):
        return dot(a, b[0], dims) + dot(a, b[1], dims)
    return lax.dot_general(
        a.astype(bf16), b.astype(bf16), ((dims[:1], dims[1:]), ((), ())), preferred_element_type=f32
    )


def nn(a, b):
    return dot(a, b, (1, 0))


def nt(a, b):
    return dot(a, b, (1, 1))


def tn(a, b):
    return dot(a, b, (0, 0))


def halves(x):
    high = x.astype(bf16)
    return high, (x - high.astype(f32)).astype(bf16)


def thirds(x):
    high, low = halves(x)
    return high, low, (x - high.astype(f32) - low.astype(f32)).astype(bf16)


def keep(ref, at, x):
    ref[0, at], ref[1, at] = halves(x)


def kept(ref, at):
    return ref[0, at], ref[1, at]


def nn_exact(ones, x):
    high, low, lowest = thirds(x)
    return nn(ones, high) + (nn(ones, low) + nn(ones, lowest))


def sigmoid(x):
    return 1.0 / (1.0 + jnp.exp(-x))


def softplus(x):
    return jnp.maximum(x, 0.0) + jnp.log(1.0 + jnp.exp(-jnp.abs(x)))


def norm_scale(values):
    return lax.rsqrt(jnp.mean(values * values, axis=-1, keepdims=True) + EPS)


def norm_back(values, scale, gain, grad):
    normal = values * scale
    e = grad * gain
    back = scale * (e - normal * jnp.mean(e * normal, axis=-1, keepdims=True))
    return back, jnp.sum(grad * normal, axis=0, keepdims=True)


def iota(dims, axis):
    return lax.broadcasted_iota(jnp.int32, dims, axis)


def doc_at(starts, positions):
    total = jnp.full(positions.shape, -1, jnp.int32)
    for start in starts:
        total = total + (start <= positions).astype(jnp.int32)
    return total


def doc_starts(lengths_ref):
    starts, at = [], jnp.int32(0)
    for j in range(DOCS):
        starts.append(at)
        at = at + lengths_ref[0, j]
    return starts


def stack2(a, b):
    return jnp.concatenate([a, b], axis=0)


def beside(a, b):
    return jnp.concatenate([a, b], axis=1)


def quad(a, b, c, d):
    return stack2(beside(a, b), beside(c, d))


def rows_of(i, size):
    return pl.ds(pl.multiple_of(i * size, size), size)


def greet(axis, peers):
    barrier = pltpu.get_barrier_semaphore()
    for peer in peers:
        pl.semaphore_signal(barrier, inc=1, device_id={axis: peer}, device_id_type=MESH)
    return lambda: pl.semaphore_wait(barrier, len(peers))


def remote(src, dst, send, receive, axis, peer):
    return pltpu.make_async_remote_copy(src, dst, send, receive, device_id={axis: peer}, device_id_type=MESH)


def flipped(chip, bits, chips):
    total, place = 0, 1
    while place < chips:
        total = total + place * lax.rem(chip // place + bits // place, 2)
        place *= 2
    return total


class Gather:
    def __init__(self, n, T, src, dst, sems):
        self.n, self.T, self.src, self.dst = n, T, src, dst
        self.ss, self.rs, self.fs, self.fr = sems
        self.me = lax.axis_index("seq")
        self.chip, self.side = self.me // 2, lax.rem(self.me, 2)
        self.sib = self.me + 1 - 2 * self.side
        order = sorted(range(1, n // 2), key=lambda k: k.bit_count())
        self.early = [k for k in order if k.bit_count() == 1]
        self.late = [k for k in order if k.bit_count() > 1]

    def at(self, device):
        return self.dst.at[rows_of(device, self.T)]

    def partner(self, k):
        return 2 * flipped(self.chip, k, self.n // 2) + self.side

    def direct(self, k):
        peer = self.sib if k == 0 else self.partner(k)
        return remote(self.src, self.at(self.me), self.ss.at[k], self.rs.at[k], "seq", peer)

    def passed(self, k):
        block = self.at(self.partner(k))
        return remote(block, block, self.fs.at[k], self.fr.at[k], "seq", self.sib)

    def relay(self, k):
        top = 1 << (k.bit_length() - 1)
        for side, last in ((0, top), (1, k & -k)):

            @pl.when(self.side == side)
            def _():
                block = self.at(self.partner(k - last))
                remote(block, block, self.ss.at[k], self.rs.at[k], "seq", self.partner(last)).start()

    def start(self):
        for k in (*self.early, 0):
            self.direct(k).start()

    def pass_on(self, k):
        self.direct(k).wait_recv()
        self.passed(k).start()

    def forward(self):
        for k in self.early:
            self.pass_on(k)
        for k in self.late:
            if k.bit_count() == 2:
                self.relay(k)

    def forward_late(self):
        for k in self.late:
            if k.bit_count() > 2:
                self.relay(k)
            self.pass_on(k)

    def arrive(self):
        self.direct(0).wait_recv()
        for k in range(1, self.n // 2):
            self.passed(k).wait_recv()

    def finish(self):
        for k in range(self.n // 2):
            self.direct(k).wait_send()
            if k:
                self.passed(k).wait_send()


def gather_sems(n):
    return [DMA((n // 2,)) for _ in range(4)]


def conv_of(block, taps, docs, T):
    total = block[8:] * taps[CONV - 1 : CONV]
    for lag in range(1, CONV):
        same = (docs[0] == docs[lag]).astype(f32)
        total = total + block[8 - lag : 8 - lag + T] * (taps[CONV - 1 - lag : CONV - lag] * same)
    return total


def chunk_gates(logits, bias, rate, starts, first, T):
    lane = iota((T, HD), 1)
    shifted = logits + bias
    gate = -rate * softplus(shifted)
    place_i, place_j = iota((T, T), 0), iota((T, T), 1)
    lower = place_j <= place_i
    cumul = nn_exact(lower.astype(bf16), jnp.where(lane == NH, gate, 0.0))
    beta = 2.0 * sigmoid(logits)
    b0, b1 = beta[:, 0:1], beta[:, 1:2]
    g = cumul[:, NH : NH + 1]
    g_row = jnp.transpose(cumul)[NH : NH + 1, :]
    g_last = cumul[T - 1 : T, NH : NH + 1]
    position = first + iota((T, 1), 0)
    docs = [doc_at(starts, position - lag) for lag in range(CONV)]
    doc = docs[0]
    doc_row = doc_at(starts, first + iota((1, T), 1))
    doc_before = doc_at(starts, jnp.full((1, 1), first - 1, jnp.int32))
    doc_last = doc_at(starts, jnp.full((1, 1), first + (T - 1), jnp.int32))
    joined = lower & (doc == doc_row)
    decay = jnp.where(joined, jnp.exp(jnp.where(joined, g - g_row, 0.0)), 0.0)
    strict = jnp.where(place_i == place_j, 0.0, decay)
    from_start = jnp.exp(g) * (doc == doc_before).astype(f32)
    to_end = jnp.exp(jnp.minimum(g_last - g, 0.0)) * (doc == doc_last).astype(f32)
    whole = jnp.exp(g_last) * (doc_last == doc_before).astype(f32)
    return dict(
        shifted=shifted, beta=beta, b=stack2(b0, b1), docs=docs, decay=decay,
        decays=quad(strict, strict, decay, strict), hd=from_start, hd2=stack2(from_start, from_start),
        to_end=stack2(to_end, to_end), whole=whole,
    )


def key_scale(raw):
    return lax.rsqrt(jnp.sum(raw * raw, axis=-1, keepdims=True) + EPS)


def chunk_inputs(block, taps, docs, T):
    conv = conv_of(block, taps, docs, T)
    sig = sigmoid(conv)
    active = conv * sig
    cut = [active[:, i * HD : (i + 1) * HD] for i in range(MIXED)]
    scales = (key_scale(cut[1]), key_scale(cut[2]))
    keys = stack2(cut[1] * scales[0], cut[2] * scales[1])
    values = stack2(cut[3], cut[4])
    return conv, sig, cut[0], keys, values, stack2(*scales)


def inverses(lowers, T):
    size = NH * T
    row, col = iota((size, size), 0), iota((size, size), 1)
    differ = (row & (T - 1)) ^ (col & (T - 1))
    eye = (row == col).astype(f32)
    found = [jnp.where(row == col, 1.0, jnp.where(differ == 0, -a, 0.0)) for a in lowers]
    step = 1
    while step < T:
        level = (differ >= step) & (differ < 2 * step)
        parts = [nn(jnp.where(level, a, 0.0), x) for a, x in zip(lowers, found)]
        found = [x - nn(x, part) for x, part in zip(found, parts)]
        step *= 2
    a_cut = [halves(a) for a in lowers]
    x_cut = [halves(x) for x in found]
    errors = [
        eye - x - (nn(a[0], xc[0]) + (nn(a[0], xc[1]) + nn(a[1], xc[0])))
        for a, x, xc in zip(a_cut, found, x_cut)
    ]
    return [x + nn(xc[0], e) for x, xc, e in zip(found, x_cut, errors)]


def head_gate(mixed, raw):
    scale = norm_scale(mixed)
    return mixed * scale, scale, sigmoid(raw)


def head_taps(taps_ref, head):
    cuts = [taps_ref[:, pl.ds(pl.multiple_of(i * D + head * HD, HD), HD)] for i in range(MIXED)]
    return jnp.concatenate(cuts, axis=1)


def intra_turn(T, starts, bias, rate, taps, small, block_of, invs, ubuf, wbuf, qbuf, pbuf, dbuf, gates, chunks, midway):
    held, lowers = [], []
    for c in chunks:
        first = pl.multiple_of(c * T, T)
        gate = chunk_gates(small[pl.ds(first, T), :], bias, rate, starts, first, T)
        conv, sig, query, keys, values, scales = chunk_inputs(block_of(c), taps, gate["docs"], T)
        key_pair = halves(keys)
        lowers.append(gate["b"] * (nt(key_pair, key_pair) * gate["decays"]))
        held.append((c, gate, query, keys, key_pair, values))
    found = inverses(lowers, T)
    midway()
    for (c, gate, query, keys, key_pair, values), inverse in zip(held, found):
        at, two = rows_of(c, T), rows_of(c, NH * T)
        pair = halves(inverse)
        invs[0, c], invs[1, c] = pair
        both = nn(pair, halves(gate["b"] * beside(values, gate["hd2"] * keys)))
        ubuf[two, :] = both[:, :HD]
        keep(wbuf, two, both[:, HD:])
        query_pair = halves(query)
        qbuf[0, at], qbuf[1, at] = query_pair
        keep(pbuf, at, nt(query_pair, key_pair) * beside(gate["decay"], gate["decay"]))
        keep(dbuf, two, gate["to_end"] * keys)
        gates[at, :] = jnp.where(iota((T, HD), 1) == 0, gate["hd"], gate["whole"])


def across_turn(T, gain, proj, mixed_out, states, news, head_rows, ubuf, wbuf, qbuf, pbuf, dbuf, gates, done, c, state):
    at, two = rows_of(c, T), rows_of(c, NH * T)
    state_pair = halves(state)
    states[0, c], states[1, c] = state_pair
    new = ubuf[two, :] - nn(kept(wbuf, two), state_pair)
    new_pair = halves(new)
    news[0, two], news[1, two] = new_pair
    gate = gates[at, :]
    mixed = gate[:, 0:1] * nn(kept(qbuf, at), state_pair) + nn(kept(pbuf, at), new_pair)
    mixed_out[at, :] = mixed
    raw = proj[at, MIXED * HD :].astype(f32)
    normal, _, sig = head_gate(mixed, raw)
    head_rows[at, :] = ((normal * gain[...]) * (raw * sig)).astype(bf16)
    done(c)
    return gate[0:1, 1:2] * state + tn(kept(dbuf, two), new_pair)


def widened(w_wide, parts):
    w_wide[...] = jnp.zeros((HD, D), bf16)
    for i, part in enumerate(parts):
        w_wide[32 * i : 32 * i + SMALL * H, :] = part


def forward_kernel(
    n, rep, T, lengths, bias_ref, rate_ref, tokens, cotangent, gain_in, w_in, w_small, taps_ref, gain,
    gated, normed_out, out_all, proj_out, small_out, mixed_out, states, news, invs_out, head_rows,
    normed, proj, small, invs, own, tails, w_head, w_wide, tail_rows, xbuf, ubuf, wbuf, qbuf, pbuf, dbuf, gates,
    w_sems, own_sems, o_sems, a_ss, a_rs, t_ss, t_rs, *sems,
):
    me = lax.axis_index("seq")
    head = me // rep
    chips = n // 2
    wait_for_all = greet("seq", [lax.rem(me + k, n) for k in range(1, n)])
    width = MIXED * HD
    loads = [
        pltpu.make_async_copy(
            w_in.at[:, pl.ds(pl.multiple_of(i * D + head * HD, HD), HD)], w_head.at[:, i * HD : (i + 1) * HD], w_sems.at[i]
        )
        for i in range(GROUPS)
    ]
    for load in loads:
        load.start()
    values = tokens[...].astype(f32)
    own[...] = (values * norm_scale(values) * gain_in[...]).astype(bf16)
    local = pltpu.make_async_copy(own, normed.at[rows_of(me, T)], own_sems.at[0])
    local.start()
    wait_for_all()
    first_gather = Gather(n, T, own, normed, sems[:4])
    second_gather = Gather(n, T, cotangent, out_all, sems[4:8])
    keep_out = pltpu.make_async_copy(cotangent, out_all.at[rows_of(me, T)], own_sems.at[2])
    keep_out.start()
    chip, side = first_gather.chip, first_gather.side
    last = own.at[T - 16 : T]

    def tail_copy(k):
        return remote(last, tails.at[chip], t_ss.at[k], t_rs.at[chip], "seq", lax.rem(me + k, n))

    mine = pltpu.make_async_copy(last, tails.at[chip], own_sems.at[1])
    early, late = first_gather.early, first_gather.late

    @pl.when(side == 1)
    def _():
        for k in range(1, n):
            tail_copy(k).start()
        mine.start()

    for k in (0, *early):
        first_gather.direct(k).start()

    starts = doc_starts(lengths)
    bias, rate = bias_ref[head], rate_ref[head]
    taps = head_taps(taps_ref, head)
    widened(w_wide, thirds(jnp.where((iota((SMALL * H, D), 0) & (H - 1)) == head, w_small[...], 0.0)))
    group, lane = iota((HD, HD), 0), iota((HD, HD), 1)
    picks = (((group & 31) >> 3) == lane) & (group < 96) & (lane < SMALL)
    picks = picks.astype(bf16)
    for load in loads:
        load.wait()
    local.wait()

    @pl.when(side == 1)
    def _():
        mine.wait()
        for k in range(1, n):
            tail_copy(k).wait_send()

    for j in range(chips):

        @pl.when(me != 2 * j + 1)
        def _():
            remote(last, tails.at[j], t_ss.at[0], t_rs.at[j], "seq", lax.rem(me + 1, n)).wait_recv()

    found = nn(tails[...].reshape(chips * 16, D), w_head[...]).astype(bf16).astype(f32)
    tail_rows[...] = found[:, :width]
    size = T + 8

    def block_of(c):
        return xbuf[pl.ds(pl.multiple_of(c * size, 8), size), :]

    def project(pair):
        at = rows_of(pair, 2 * T)
        block = normed[at, :]
        result = nn(block, w_head[...]).astype(bf16)
        proj[at, :] = result
        raw = thirds(nt(block, w_wide[...]))
        small[at, :] = nn(raw[0], picks) + (nn(raw[1], picks) + nn(raw[2], picks))
        mixing = result[:, :width].astype(f32)
        before = lax.rem(pair + chips - 1, chips)
        halo = tail_rows[pl.ds(pl.multiple_of(before * 16 + 8, 8), 8), :]
        base = pl.multiple_of(pair * (2 * size), 8)
        xbuf[pl.ds(base, 8), :] = jnp.where(pair > 0, halo, 0.0)
        xbuf[pl.ds(pl.multiple_of(base + 8, 8), T), :] = mixing[:T]
        xbuf[pl.ds(pl.multiple_of(base + size, 8), T + 8), :] = mixing[T - 8 :]

    first_gather.direct(0).wait_recv()
    groups = [(0,)] + [(*ks[i : i + 2],) for ks in (early, late) for i in range(0, len(ks), 2)]
    to_late = (len(early) + 1) // 2

    def midway(g):
        if g == 0:
            first_gather.forward()
        if g == to_late:
            first_gather.forward_late()
            second_gather.start()
        if g == len(groups) - 1:
            second_gather.forward()

    for g, group in enumerate(groups):
        for k in group:
            if k:
                first_gather.passed(k).wait_recv()
        pairs = [flipped(chip, k, chips) for k in group]
        for pair in pairs:
            project(pair)
        intra_turn(
            T, starts, bias, rate, taps, small, block_of, invs, ubuf, wbuf, qbuf, pbuf, dbuf, gates,
            [2 * pair + i for pair in pairs for i in range(2)], functools.partial(midway, g),
        )

    first_gather.finish()
    stores = [
        pltpu.make_async_copy(a, b, o_sems.at[i])
        for i, (a, b) in enumerate(((normed, normed_out), (proj, proj_out), (small, small_out), (invs, invs_out)))
    ]
    for store in stores:
        store.start()
    column = pl.ds(pl.multiple_of(head * HD, HD), HD)

    def row_copy(c):
        return remote(head_rows.at[rows_of(c, T)], gated.at[:, column], a_ss.at[c], a_rs.at[head], "seq", c)

    def send_rows(c):
        @pl.when((c != me) & (lax.rem(me, rep) == 0))
        def _():
            row_copy(c).start()

    across = functools.partial(
        across_turn, T, gain, proj, mixed_out, states, news, head_rows, ubuf, wbuf, qbuf, pbuf, dbuf, gates, send_rows
    )
    lax.fori_loop(0, n, across, jnp.zeros((HD, HD), f32))

    @pl.when(lax.rem(me, rep) == 0)
    def _():
        kept_rows = pltpu.make_async_copy(head_rows.at[rows_of(me, T)], gated.at[:, column], own_sems.at[0])
        kept_rows.start()
        kept_rows.wait()

    keep_out.wait()
    second_gather.forward_late()

    def settle(k, _):
        peer = lax.rem(me + k, n)

        @pl.when(lax.rem(me, rep) == 0)
        def _():
            row_copy(peer).wait_send()

        @pl.when(lax.rem(peer, rep) == 0)
        def _():
            source = peer // rep
            remote(
                head_rows.at[rows_of(me, T)], gated.at[:, pl.ds(pl.multiple_of(source * HD, HD), HD)],
                a_ss.at[peer], a_rs.at[source], "seq", peer,
            ).wait_recv()

        return 0

    lax.fori_loop(1, n, settle, 0)
    second_gather.arrive()
    second_gather.finish()
    for store in stores:
        store.wait()


def forward_scratch(n, T):
    rows = n * T
    return [
        pltpu.VMEM((rows + 8 * n, MIXED * HD), f32), pltpu.VMEM((NH * rows, HD), f32),
        pltpu.VMEM((2, NH * rows, HD), bf16), pltpu.VMEM((2, rows, HD), bf16), pltpu.VMEM((2, rows, NH * T), bf16),
        pltpu.VMEM((2, NH * rows, HD), bf16), pltpu.VMEM((rows, HD), f32),
    ]


def run_forward(n, rep, T, lengths, bias, rate, tokens, cotangent, gain_in, w_in, w_small, taps, gain):
    rows = n * T
    return pl.pallas_call(
        functools.partial(forward_kernel, n, rep, T),
        out_shape=(
            shape((T, D), bf16), shape((rows, D), bf16), shape((rows, D), bf16), shape((rows, GROUPS * HD), bf16),
            shape((rows, HD), f32), shape((rows, HD), f32), shape((2, n, HD, HD), bf16), shape((2, NH * rows, HD), bf16),
            shape((2, n, NH * T, NH * T), bf16), shape((rows, HD), bf16),
        ),
        in_specs=[SMEM] * 3 + [VMEM, VMEM, VMEM, ANY, VMEM, VMEM, VMEM],
        out_specs=[VMEM, ANY, ANY, ANY, ANY, VMEM, VMEM, VMEM, ANY, VMEM],
        scratch_shapes=[
            pltpu.VMEM((rows, D), bf16), pltpu.VMEM((rows, GROUPS * HD), bf16), pltpu.VMEM((rows, HD), f32),
            pltpu.VMEM((2, n, NH * T, NH * T), bf16),
            pltpu.VMEM((T, D), bf16), pltpu.VMEM((n // 2, 16, D), bf16), pltpu.VMEM((D, GROUPS * HD), bf16),
            pltpu.VMEM((HD, D), bf16), pltpu.VMEM((n * 8, MIXED * HD), f32),
            *forward_scratch(n, T),
            DMA((GROUPS,)), DMA((3,)), DMA((4,)), DMA((n,)), DMA((H,)), DMA((n,)), DMA((n // 2,)), *gather_sems(n), *gather_sems(n),
        ],
        compiler_params=pltpu.CompilerParams(vmem_limit_bytes=LIMIT, collective_id=1, has_side_effects=True),
        name="mixer_forward",
    )(lengths, bias, rate, tokens, cotangent, gain_in, w_in, w_small, taps, gain)


def feed_kernel(
    n, T, steps, tokens, gated, cotangent, w_out, gain_mid, w_gate, w_up, w_down,
    result, grad_residual, mid_all, gain_grad, residual, middle, total, grad_mid, own_sem, *sems,
):
    step = pl.program_id(0)
    me = lax.axis_index("seq")
    gather = Gather(n, T, middle, mid_all, sems)
    local = pltpu.make_async_copy(middle, mid_all.at[rows_of(me, T)], own_sem)

    @pl.when(step == 0)
    def _():
        peers = [gather.sib] + [gather.partner(k) for k in range(1, n // 2)]
        wait_for_all = greet("seq", peers)
        found = tokens[...].astype(f32) + nn(gated[...], w_out[...])
        residual[...] = found
        middle[...] = (found * norm_scale(found) * gain_mid[...]).astype(bf16)
        total[...] = found
        grad_mid[...] = jnp.zeros((T, D), f32)
        wait_for_all()
        gather.start()
        local.start()

    gate, up = nn(middle[...], w_gate[...]), nn(middle[...], w_up[...])
    sig = sigmoid(gate)
    silu = gate * sig
    hidden = (silu * up).astype(bf16)
    total[...] += nn(hidden, w_down[...])
    grad_hidden = nt(cotangent[...], w_down[...])
    grad_gate = (grad_hidden * up * (sig * (1.0 + gate * (1.0 - sig)))).astype(bf16)
    grad_up = (grad_hidden * silu).astype(bf16)
    grad_mid[...] += nt(grad_gate, w_gate[...]) + nt(grad_up, w_up[...])

    for at, what in ((5, gather.forward), (8, gather.forward_late)):

        @pl.when(step == at)
        def _():
            what()

    @pl.when(step == steps - 1)
    def _():
        result[...] = total[...].astype(bf16)
        values = residual[...]
        back, gain_part = norm_back(values, norm_scale(values), gain_mid[...], grad_mid[...])
        gain_grad[...] = gain_part
        grad_residual[...] = cotangent[...].astype(f32) + back
        gather.arrive()
        gather.finish()
        local.wait()


def run_feed(n, T, tokens, gated, cotangent, w_out, gain_mid, w_gate_up, w_down):
    steps = FF // TILE
    fixed = lambda *dims: pl.BlockSpec(dims, lambda i: (0, 0))
    return pl.pallas_call(
        functools.partial(feed_kernel, n, T, steps),
        grid=(steps,),
        out_shape=(shape((T, D), bf16), shape((T, D), f32), shape((n * T, D), bf16), shape((1, D), f32)),
        in_specs=[
            fixed(T, D), fixed(T, D), fixed(T, D), fixed(D, D), fixed(1, D),
            pl.BlockSpec((D, TILE), lambda i: (0, i)), pl.BlockSpec((D, TILE), lambda i: (0, i + FF // TILE)),
            pl.BlockSpec((TILE, D), lambda i: (i, 0)),
        ],
        out_specs=[fixed(T, D), fixed(T, D), ANY, fixed(1, D)],
        scratch_shapes=[
            pltpu.VMEM((T, D), f32), pltpu.VMEM((T, D), bf16), pltpu.VMEM((T, D), f32), pltpu.VMEM((T, D), f32),
            DMA, *gather_sems(n),
        ],
        compiler_params=pltpu.CompilerParams(vmem_limit_bytes=LIMIT, collective_id=2, has_side_effects=True),
        name="feed_forward",
    )(tokens, gated, cotangent, w_out, gain_mid, w_gate_up, w_gate_up, w_down)


def store_pieces(out, part, first, stream, piece):
    for i in range(part.shape[0] // piece):
        at = first // piece + i
        out[at % stream, at // stream] = part[i * piece : (i + 1) * piece].astype(bf16)


def backward_turn(
    n, T, head, starts, bias, rate, taps, gain, incoming_of, proj, small, states, fetch,
    gp, grad_small, gconv_w, xbuf, halo, gates_sum, grad_state, done, k, _,
):
    width = MIXED * HD
    lane = iota((T, HD), 1)
    place_i, place_j = iota((T, T), 0), iota((T, T), 1)
    upper = (place_j >= place_i).astype(bf16)
    under = place_j < place_i
    c = n - 1 - k
    first = pl.multiple_of(c * T, T)
    at, two = rows_of(c, T), rows_of(c, NH * T)
    gate = chunk_gates(small[at, :], bias, rate, starts, first, T)
    block = xbuf[pl.ds(first, T + 8), :]
    conv, sig, query, keys, values, scales = chunk_inputs(block, taps, gate["docs"], T)
    key_pair, query_pair = halves(keys), halves(query)
    b, hd, hd2, to_end = gate["b"], gate["hd"], gate["hd2"], gate["to_end"]
    decay2 = beside(gate["decay"], gate["decay"])
    pairs = nt(key_pair, key_pair) * gate["decays"]
    scores = nt(query_pair, key_pair) * decay2
    state = (states[0, c], states[1, c])
    state_grad = grad_state[...]
    new, inverse, mixed = fetch(c)
    raw = proj[at, width:].astype(f32)
    normal, scale, zsig = head_gate(mixed, raw)
    incoming = incoming_of(at)
    passed = incoming * (raw * zsig)
    gates_sum[0:1, :] += jnp.sum(passed * normal, axis=0, keepdims=True)
    grad_z = incoming * (normal * gain[...]) * (zsig * (1.0 + raw * (1.0 - zsig)))
    e = passed * gain[...]
    grad_mixed = scale * (e - normal * jnp.mean(e * normal, axis=-1, keepdims=True))
    gm = halves(grad_mixed)
    ended = halves(to_end * keys)
    grad_pair = halves(state_grad)
    grad_new = tn(halves(scores), gm) + nn(ended, grad_pair)
    grad_right = tn(inverse, halves(grad_new))
    moved = b * grad_right
    grad_state[...] = gate["whole"] * state_grad + tn(halves(hd * query), gm) - tn(halves(hd2 * keys), halves(moved))
    grad_ended = nt(new, grad_pair)
    grad_scores = nt(gm, new)
    grad_lower = jnp.where(gate["decays"] != 0.0, -nt(halves(grad_right), new), 0.0)
    from_grad = nt(gm, state)
    scored = grad_scores * decay2
    grad_query = hd * from_grad + nn(scored, key_pair[0])
    paired = (b * grad_lower) * gate["decays"]
    keyed = nn(key_pair, state)
    grad_keys = (
        tn(scored, query_pair[0]) + to_end * grad_ended - hd2 * nt(moved, state[0])
        + nn(paired, key_pair[0]) + tn(paired, key_pair[0])
    )
    lower_pairs = grad_lower * pairs
    grad_b = jnp.sum(grad_right * (values - hd2 * keyed), axis=-1, keepdims=True) + jnp.sum(
        lower_pairs, axis=-1, keepdims=True
    )
    four = b * lower_pairs
    both = grad_scores * scores
    joint = (four[:T, :T] + four[:T, T:]) + (four[T:, :T] + four[T:, T:]) + (both[:, :T] + both[:, T:])
    crossing = jnp.sum(jnp.where(under, nn_exact(upper, joint), 0.0), axis=-1, keepdims=True)
    start_part = -hd2 * jnp.sum(moved * keyed, axis=-1, keepdims=True)
    start_part = start_part[:T] + start_part[T:] + hd * jnp.sum(query * from_grad, axis=-1, keepdims=True)
    end_part = to_end * jnp.sum(grad_ended * keys, axis=-1, keepdims=True)
    end_part = end_part[:T] + end_part[T:]
    sums_in = jnp.where(lane == 0, start_part, jnp.where(lane == 1, end_part, 0.0))
    after = nn_exact(upper, sums_in)
    before = nn_exact(under.astype(bf16), sums_in)
    whole_part = gate["whole"] * jnp.sum(state_grad * (state[0].astype(f32) + state[1].astype(f32)), keepdims=True)
    grad_gate = crossing + after[:, 0:1] + before[:, 1:2] + whole_part
    shifted = gate["shifted"]
    grad_beta = [grad_b[i * T : (i + 1) * T] * (gate["beta"][:, i : i + 1] * (1.0 - 0.5 * gate["beta"][:, i : i + 1])) for i in range(NH)]
    grad_decay = (-grad_gate * rate * sigmoid(shifted))[:, NH : NH + 1]
    which = lane >> 3
    logit = jnp.where(which == 0, grad_beta[0], jnp.where(which == 1, grad_beta[1], grad_decay))
    grad_logits = jnp.where((lane < SMALL * H) & ((lane & (H - 1)) == head), logit, 0.0)
    gates_sum[1:2, :] += jnp.sum(jnp.where(lane == NH, grad_decay, 0.0), axis=0, keepdims=True)
    gates_sum[2:3, :] += jnp.sum(jnp.where(lane == NH, grad_gate * -softplus(shifted), 0.0), axis=0, keepdims=True)
    high = grad_logits.astype(bf16).astype(f32)
    grad_small[at, :] = (
        high + pltpu.roll(grad_logits - high, 32, 1) + pltpu.roll(high, 64, 1)
    ).astype(bf16)
    projected_out = jnp.sum(keys * grad_keys, axis=-1, keepdims=True)
    grad_raw = (grad_keys - keys * projected_out) * scales
    slope = sig * (1.0 + conv * (1.0 - sig))
    grad_active = jnp.concatenate([grad_query, grad_raw[:T], grad_raw[T:], moved[:T], moved[T:]], axis=1)
    grad_conv = grad_active * slope
    after_block = stack2(grad_conv, halo[...])
    halo[...] = grad_conv[:8]
    position = first + iota((T, 1), 0)
    total = grad_conv * taps[CONV - 1 : CONV]
    taps_grads = [None] * CONV
    taps_grads[CONV - 1] = jnp.sum(grad_conv * block[8:], axis=0, keepdims=True)
    for lag in range(1, CONV):
        same = (doc_at(starts, position + lag) == gate["docs"][0]).astype(f32)
        total = total + after_block[lag : lag + T] * (taps[CONV - 1 - lag : CONV - lag] * same)
        same = (gate["docs"][lag] == gate["docs"][0]).astype(f32)
        taps_grads[CONV - 1 - lag] = jnp.sum(
            grad_conv * (block[8 - lag : 8 - lag + T] * same), axis=0, keepdims=True
        )
    everything = beside(total, grad_z).astype(bf16)
    gp[at, :] = everything
    gconv_w[...] += jnp.concatenate(taps_grads, axis=0)
    done(k)
    return 0


class Chain:
    def __init__(self, own, up_in, down_in, sems, my, m):
        self.own, self.up_in, self.down_in = own, up_in, down_in
        self.us, self.ur, self.ds, self.dr = sems
        self.my, self.m = my, m

    def up(self, q):
        slot = q - self.my
        return self.own(self.my + self.m - 1 - q), self.up_in(slot), slot, self.my + 1, self.us, self.ur

    def down(self, q):
        slot = q - (self.m - 1 - self.my)
        return self.own(self.my - (self.m - 1 - q)), self.down_in(slot), slot, self.my - 1, self.ds, self.dr

    def copy(self, hop):
        own, arrived, slot, peer, send, receive = hop
        return remote(own, arrived, send.at[slot], receive.at[slot], "stream", peer)

    def start(self):
        for q in range(self.m - 1):

            @pl.when(self.my == 0)
            def _():
                self.copy(self.up(q)).start()

            @pl.when(self.my == self.m - 1)
            def _():
                self.copy(self.down(q)).start()

    def tick(self, q):
        for inner, way in (
            ((self.my > 0) & (self.my <= q), self.up),
            ((self.my < self.m - 1) & (self.my >= self.m - 1 - q), self.down),
        ):

            @pl.when(inner)
            def _():
                hop = way(q)
                self.copy(hop).wait_recv()
                hop[0][...] = (hop[0][...].astype(f32) + hop[1][...].astype(f32)).astype(bf16)
                self.copy(hop).start()

    def finish(self, write):
        last = self.m - 1

        @pl.when(self.my > 0)
        def _():
            slot = last - self.my
            remote(self.own(self.my), self.up_in(slot), self.us.at[slot], self.ur.at[slot], "stream", self.my - 1).wait_recv()

        @pl.when(self.my < last)
        def _():
            slot = self.my
            remote(self.own(self.my), self.down_in(slot), self.ds.at[slot], self.dr.at[slot], "stream", self.my + 1).wait_recv()

        mine = self.own(self.my)

        @pl.when((self.my > 0) & (self.my < last))
        def _():
            write(mine[...].astype(f32) + self.up_in(last - self.my)[...].astype(f32) + self.down_in(self.my)[...].astype(f32))

        @pl.when(self.my == last)
        def _():
            write(mine[...].astype(f32) + self.up_in(0)[...].astype(f32))

        @pl.when(self.my == 0)
        def _():
            write(mine[...].astype(f32) + self.down_in(0)[...].astype(f32))

    def settle(self):
        for q in range(self.m - 1):

            @pl.when(self.my <= q)
            def _():
                self.copy(self.up(q)).wait_send()

            @pl.when(self.my >= self.m - 1 - q)
            def _():
                self.copy(self.down(q)).wait_send()


class Sums:
    def __init__(self, own, arrived, every, sems, me, my, n, m):
        self.own, self.arrived, self.every = own, arrived, every
        self.zs, self.zr, self.ss, self.rs = sems
        self.me, self.my, self.n, self.m = me, my, n, m

    def across(self, k):
        peer = lax.rem(self.my + k, self.m)
        return remote(self.own, self.arrived.at[k - 1], self.zs.at[k - 1], self.zr.at[k - 1], "stream", peer)

    def along(self, k):
        block = self.every.at[self.me]
        return remote(block, block, self.ss.at[k - 1], self.rs.at[k - 1], "seq", lax.rem(self.me + k, self.n))

    def start(self):
        for k in range(1, self.m):
            self.across(k).start()

    def add(self):
        total = self.own[...]
        for k in range(1, self.m):
            self.across(k).wait()
            total = total + self.arrived[k - 1]
        self.every[self.me] = total
        for k in range(1, self.n):
            self.along(k).start()

    def settle(self):
        for k in range(1, self.n):
            self.along(k).wait()


def chain_sems(*lead):
    return [DMA(lead) for _ in range(4)]


def scatter_to(own, arrived, k, send, receive, me, size):
    peer = lax.rem(me + k, size)
    return remote(own.at[peer], arrived.at[me], send.at[k - 1], receive.at[k - 1], "seq", peer)


def back_kernel(
    n, m, rep, T, piece, shard, wide,
    lengths, bias_ref, rate_ref, tokens, grad_residual, gain_in, gain_mid_grad, w_small, taps_ref, gain,
    mid_any, out_any, w_gate_up, w_down, w_out, rows_any, proj_any, small_any, mixed_any, states_any, news_any, invs_any,
    normed_any, w_in_any,
    grad_input, q_w_in, g_out, q_gu_in, g_down, q_sum,
    mid, cot, w_gate, w_up, w_hid, w_head, head_rows, proj, small, mixed, states, news, invs, normed, w_in, w_wide,
    low_all, hidden, grad_gate, grad_up, gp, grad_small, gconv_w, xbuf, halo, gates_sum, grad_state,
    z_gu, z_gu_up, z_gu_down, z_down, z_down_up, z_down_down, z_out, z_out_up, z_out_down, z_w, z_w_up, z_w_down,
    z_sum, z_sum_in, gain_sum, q_gu, q_w, part_own, part_out, part_in, chip_out, chip_in,
    l_sems, i_sems, gu_us, gu_ur, gu_ds, gu_dr, dn_us, dn_ur, dn_ds, dn_dr, ou_us, ou_ur, ou_ds, ou_dr, w_us, w_ur, w_ds, w_dr,
    sum_ss, sum_rs, qgu_ss, qgu_rs, qw_ss, qw_rs, qsum_ss, qsum_rs, p_ss, p_rs, c_ss, c_rs, *sems,
):
    me, my = lax.axis_index("seq"), lax.axis_index("stream")
    head, chip, side = me // rep, me // 2, lax.rem(me, 2)
    sib = me + 1 - 2 * side
    barrier = pltpu.get_barrier_semaphore()
    for k in range(1, n):
        pl.semaphore_signal(barrier, inc=1, device_id={"seq": lax.rem(me + k, n)}, device_id_type=MESH)
    for k in range(1, m):
        pl.semaphore_signal(barrier, inc=1, device_id={"stream": lax.rem(my + k, m)}, device_id_type=MESH)
    first_unit = me * shard
    base = (first_unit // HD - me // (n - 1)) * HD
    offset = first_unit - base
    sources = [
        mid_any, out_any, w_gate_up.at[:, pl.ds(pl.multiple_of(base, HD), wide)],
        w_gate_up.at[:, pl.ds(pl.multiple_of(FF + base, HD), wide)], w_down.at[pl.ds(pl.multiple_of(base, HD), wide)],
        w_out.at[rows_of(head, HD)], rows_any, proj_any, small_any, mixed_any, states_any, news_any, invs_any, normed_any,
    ]
    places = [mid, cot, w_gate, w_up, w_hid, w_head, head_rows, proj, small, mixed, states, news, invs, normed]
    roomy = len(normed.shape) == 2
    loads = [pltpu.make_async_copy(a, b, l_sems.at[i]) for i, (a, b) in enumerate(zip(sources, places)) if i not in (9, 11, 12, 13) or roomy]
    for i in range(GROUPS):
        column = pl.ds(pl.multiple_of(i * D + head * HD, HD), HD)
        loads.append(pltpu.make_async_copy(w_in_any.at[:, column], w_in.at[:, i * HD : (i + 1) * HD], i_sems.at[i]))
    for load in loads[:5]:
        load.start()
    low_all[rows_of(me, T), :] = grad_residual[...].astype(bf16)
    pl.semaphore_wait(barrier, n + m - 2)
    gather = Gather(n, T, low_all.at[rows_of(me, T)], low_all, sems)
    gather.start()

    for load in loads[:5]:
        load.wait()
    for load in loads[5:]:
        load.start()

    def feed_turn(i, _):
        at = rows_of(i, TILE)
        block = mid[at, :]
        gate, up = nn(block, w_gate[...]), nn(block, w_up[...])
        sig = sigmoid(gate)
        silu = gate * sig
        grad_hidden = nt(cot[at, :], w_hid[...])
        own = lambda x: pltpu.roll(x, wide - offset, 1)[:, :shard].astype(bf16)
        hidden[at, :] = own(silu * up)
        grad_gate[at, :] = own(grad_hidden * up * (sig * (1.0 + gate * (1.0 - sig))))
        grad_up[at, :] = own(grad_hidden * silu)
        return 0

    lax.fori_loop(0, n * T // TILE, feed_turn, 0)
    downs = Chain(lambda d: z_down.at[d], lambda i: z_down_up.at[i], lambda i: z_down_down.at[i], (dn_us, dn_ur, dn_ds, dn_dr), my, m)
    ups = [
        Chain(
            lambda d, j=j: z_gu.at[j, d], lambda i, j=j: z_gu_up.at[j, i], lambda i, j=j: z_gu_down.at[j, i],
            (gu_us.at[j], gu_ur.at[j], gu_ds.at[j], gu_dr.at[j]), my, m,
        )
        for j in range(2)
    ]
    part = tn(hidden[...], cot[...])
    for d in range(m):
        z_down[d] = part[d * (shard // m) : (d + 1) * (shard // m)].astype(bf16)
    downs.start()
    gather.forward()
    for j, grads in enumerate((grad_gate, grad_up)):
        if j:
            gather.forward_late()
        for first in range(0, D, TILE):
            store_pieces(z_gu.at[j], tn(mid[:, first : first + TILE], grads[...]), first, m, piece)
        ups[j].start()
    w_high, w_low = halves(w_small[...])
    widened(w_wide, (w_high, w_high, w_low))
    gather.arrive()
    gather.finish()
    for load in loads[5:]:
        load.wait()
    rows = tn(head_rows[...], low_all[...])
    for share in range(rep):

        @pl.when(lax.rem(me, rep) == share)
        def _():
            for d in range(m):
                at = share * (HD // rep) + d * piece
                z_out[d] = rows[at : at + piece].astype(bf16)

    outs = Chain(lambda d: z_out.at[d], lambda i: z_out_up.at[i], lambda i: z_out_down.at[i], (ou_us, ou_ur, ou_ds, ou_dr), my, m)
    outs.start()
    if not roomy:
        normed = mid
        late = pltpu.make_async_copy(normed_any, normed, l_sems.at[13])
        late.start()
        late.wait()

    width = MIXED * HD
    starts = doc_starts(lengths)
    bias, rate = bias_ref[head], rate_ref[head]
    taps = head_taps(taps_ref, head)
    xbuf[0:8, :] = jnp.zeros((8, width), f32)
    halo[...] = jnp.zeros((8, width), f32)
    gconv_w[...] = jnp.zeros(gconv_w.shape, f32)
    gates_sum[...] = jnp.zeros((8, HD), f32)
    grad_state[...] = jnp.zeros((HD, HD), f32)

    def fill(c, _):
        xbuf[pl.ds(pl.multiple_of(8 + c * T, 8), T), :] = proj[rows_of(c, T), :width].astype(f32)
        return 0

    lax.fori_loop(0, n, fill, 0)

    def normed_rows(at):
        if roomy:
            return normed[at, :].astype(f32)
        return mid[at, :].astype(f32)

    gain_sum[...] = jnp.zeros((1, D), f32)

    def sibling_copy(j):
        return remote(part_out.at[j], part_in.at[j], p_ss.at[j], p_rs.at[j], "seq", sib)

    def owner_copy(j):
        return remote(chip_out.at[j], chip_in.at[chip], c_ss.at[j], c_rs.at[chip], "seq", 2 * j + side)

    def form(j):
        at = rows_of(j, 2 * T)
        found = nt(gp[at, :], w_in[...]) + nn(grad_small[at, :], w_wide[...])
        if rep > 1:
            found = found * (lax.rem(me, rep) == 0).astype(f32)
        gain_sum[...] += jnp.sum(found * normed_rows(at), axis=0, keepdims=True)
        for i in range(2):

            @pl.when(side == i)
            def _():
                part_own[j] = found[i * T : (i + 1) * T].astype(part_own.dtype)
                part_out[j] = found[(1 - i) * T : (2 - i) * T].astype(bf16)

        sibling_copy(j).start()

    def join(j):
        sibling_copy(j).wait_recv()
        found = part_own[j].astype(f32) + part_in[j].astype(f32)
        part_own[j] = found.astype(part_own.dtype)
        chip_out[j] = found.astype(bf16)

        @pl.when(chip != j)
        def _():
            owner_copy(j).start()

    hops = [(chain, q) for chain in (downs, *ups) for q in range(1, m - 1)]

    def after_turn(k):
        c = n - 1 - k

        @pl.when(lax.rem(k, 2) == 1)
        def _():
            form(c // 2)

        @pl.when((lax.rem(k, 2) == 0) & (k > 0))
        def _():
            join((c + 1) // 2)

        for i, (chain, q) in enumerate(hops):

            @pl.when(k == 3 * i // 2)
            def _():
                chain.tick(q)

    def fetch(c):
        if roomy:
            return kept(news, rows_of(c, NH * T)), (invs[0, c], invs[1, c]), mixed[rows_of(c, T), :]
        late = [
            pltpu.make_async_copy(news_any.at[:, rows_of(c, NH * T)], news, l_sems.at[11]),
            pltpu.make_async_copy(invs_any.at[:, pl.ds(c, 1)], invs, l_sems.at[12]),
            pltpu.make_async_copy(mixed_any.at[rows_of(c, T)], mixed, l_sems.at[9]),
        ]
        for load in late:
            load.start()
        for load in late:
            load.wait()
        return (news[0], news[1]), (invs[0, 0], invs[1, 0]), mixed[...]

    turn = functools.partial(
        backward_turn, n, T, head, starts, bias, rate, taps, gain, lambda at: nt(low_all[at, :], w_head[...]),
        proj, small, states, fetch, gp, grad_small, gconv_w, xbuf, halo, gates_sum, grad_state, after_turn,
    )
    lax.fori_loop(0, n, turn, 0)

    small_t = tn(grad_small[...], normed[...])
    small_t = small_t[: SMALL * H] + small_t[32 : 32 + SMALL * H]
    z_sum[0:1, :] = gain_mid_grad[...]
    for i in range(SMALL):
        z_sum[1 + i : 2 + i, :] = jnp.sum(small_t[i * H : (i + 1) * H], axis=0, keepdims=True)
    z_sum[4:8, :width] = gconv_w[...]
    for i in range(3):
        z_sum[4 + i : 5 + i, width : width + HD] = gates_sum[i : i + 1, :]
    z_sum[7:8, width : width + HD] = jnp.zeros((1, HD), f32)
    gain_part = gain_sum[...] / gain_in[...]
    cut = D - width - HD
    for i in range(4):
        z_sum[4 + i : 5 + i, width + HD :] = gain_part[:, i * cut : (i + 1) * cut]
    first_sums = Sums(z_sum, z_sum_in, q_sum, (sum_ss, sum_rs, qsum_ss, qsum_rs), me, my, n, m)
    first_sums.start()

    lines = D // TILE
    units, strip = n // lines, piece * m
    ins = []
    for i in range(lines):
        firsts = [(i + u * lines) * strip for u in range(units)]
        found = tn(jnp.concatenate([normed[:, first : first + strip] for first in firsts], axis=1), gp[...])
        for u in range(units):
            for d in range(m):
                at = u * strip + d * piece
                z_w[i, d, u] = found[at : at + piece].astype(bf16)
        ins.append(
            Chain(
                lambda d, i=i: z_w.at[i, d], lambda j, i=i: z_w_up.at[i, j], lambda j, i=i: z_w_down.at[i, j],
                (w_us.at[i], w_ur.at[i], w_ds.at[i], w_dr.at[i]), my, m,
            )
        )
        ins[-1].start()
        if i == 0:
            join(0)
    for i, (chain, q) in enumerate(hops):
        if 3 * i // 2 >= n:
            chain.tick(q)

    def write_down(x):
        g_down[...] = x

    def write_out(x):
        g_out[...] = x

    downs.finish(write_down)
    for j in range(2):

        def write_up(x, j=j):
            q_gu[:, j] = x.astype(bf16)

        ups[j].finish(write_up)
    q_ups = [scatter_to(q_gu, q_gu_in, k, qgu_ss, qgu_rs, me, n) for k in range(1, n)]
    for copy in q_ups:
        copy.start()
    q_gu_in[me] = q_gu[me]
    for q in range(1, m - 1):
        outs.tick(q)

    def input_gradient():
        total = part_own[chip].astype(f32)
        for k in range(1, n // 2):
            other = lax.rem(chip + k, n // 2)
            remote(chip_out.at[other], chip_in.at[other], c_ss.at[other], c_rs.at[other], "seq", 2 * other + side).wait_recv()
            total = total + chip_in[other].astype(f32)
        values = tokens[...].astype(f32)
        part, _ = norm_back(values, norm_scale(values), gain_in[...], total)
        grad_input[...] = grad_residual[...] + part

    def deliver(i):
        def write_in(x):
            for u in range(units):
                q_w[i + u * lines] = x[u].astype(bf16)

        ins[i].finish(write_in)
        for j in range(i, n, lines):

            @pl.when(me != j)
            def _():
                remote(q_w.at[j], q_w_in.at[me], qw_ss.at[j], qw_rs.at[me], "seq", j).start()

    first_sums.add()
    for i, chain in enumerate(ins):
        for q in range(1, m - 1):
            chain.tick(q)
        if i:
            deliver(i - 1)
        if i == 1:
            outs.finish(write_out)
        if i == 2:
            input_gradient()
    deliver(len(ins) - 1)
    q_w_in[me] = q_w[me]
    for chain in (downs, *ups, outs, *ins):
        chain.settle()

    def settle(j, _):
        sibling_copy(j).wait_send()

        @pl.when(chip != j)
        def _():
            owner_copy(j).wait_send()

        return 0

    lax.fori_loop(0, n // 2, settle, 0)
    first_sums.settle()
    for copy in q_ups:
        copy.wait()
    for k in range(1, n):
        peer = lax.rem(me + k, n)
        remote(q_w.at[peer], q_w_in.at[me], qw_ss.at[peer], qw_rs.at[me], "seq", peer).wait_send()
        remote(q_w.at[peer], q_w_in.at[peer], qw_ss.at[peer], qw_rs.at[peer], "seq", peer).wait_recv()


def run_back(n, m, rep, T, lengths, bias, rate, tokens, grad_residual, gain_in, gain_mid_grad, w_small, taps, gain,
             mid, cot, w_gate_up, w_down, w_out, head_rows, proj, small, mixed, states, news, invs, normed, w_in):
    rows, piece, shard = n * T, D // (n * m), FF // n
    wide = -(-(shard + HD - 1) // HD) * HD
    vm, roomy = pltpu.VMEM, rows <= 1024
    band = GROUPS * HD

    def chained(*dims, lead=()):
        return [vm((*lead, m, *dims), bf16), vm((*lead, m - 1, *dims), bf16), vm((*lead, m - 1, *dims), bf16)]

    return pl.pallas_call(
        functools.partial(back_kernel, n, m, rep, T, piece, shard, wide),
        out_shape=(
            shape((T, D), f32), shape((n, piece, band), bf16), shape((piece, D), f32), shape((n, 2, piece, shard), bf16),
            shape((shard // m, D), f32), shape((n, 8, D), f32),
        ),
        in_specs=[SMEM] * 3 + [VMEM] * 7 + [ANY] * 14,
        out_specs=[VMEM] * 6,
        scratch_shapes=[
            vm((rows, D), bf16), vm((rows, D), bf16), vm((D, wide), bf16), vm((D, wide), bf16), vm((wide, D), bf16),
            vm((HD, D), bf16), vm((rows, HD), bf16), vm((rows, band), bf16), vm((rows, HD), f32), vm((rows if roomy else T, HD), f32),
            vm((2, n, HD, HD), bf16), vm((2, NH * (rows if roomy else T), HD), bf16), vm((2, n if roomy else 1, NH * T, NH * T), bf16),
            vm((rows, D) if roomy else (1, 16, HD), bf16), vm((D, band), bf16), vm((HD, D), bf16),
            vm((rows, D), bf16), vm((rows, shard), bf16), vm((rows, shard), bf16), vm((rows, shard), bf16),
            vm((rows, band), bf16), vm((rows, HD), bf16), vm((CONV, MIXED * HD), f32), vm((rows + 8, MIXED * HD), f32),
            vm((8, MIXED * HD), f32), vm((8, HD), f32), vm((HD, HD), f32),
            *chained(n, piece, shard, lead=(2,)), *chained(shard // m, D), *chained(piece, D), *chained(n * TILE // D, piece, band, lead=(D // TILE,)),
            vm((8, D), f32), vm((m - 1, 8, D), f32), vm((1, D), f32), vm((n, 2, piece, shard), bf16), vm((n, piece, band), bf16),
            vm((n // 2, T, D), f32 if roomy else bf16), *[vm((n // 2, T, D), bf16)] * 4,
            DMA((14,)), DMA((GROUPS,)), *chain_sems(2, m - 1), *chain_sems(m - 1), *chain_sems(m - 1),
            *chain_sems(D // TILE, m - 1), DMA((m - 1,)), DMA((m - 1,)), DMA((n - 1,)), DMA((n - 1,)), DMA((n,)), DMA((n,)),
            DMA((n - 1,)), DMA((n - 1,)),
            *[DMA((n // 2,))] * 4, *gather_sems(n),
        ],
        compiler_params=pltpu.CompilerParams(vmem_limit_bytes=(60 if roomy else 63) * 1024 * 1024, collective_id=3, has_side_effects=True),
        name="backward",
    )(lengths, bias, rate, tokens, grad_residual, gain_in, gain_mid_grad, w_small, taps, gain,
      mid, cot, w_gate_up, w_down, w_out, head_rows, proj, small, mixed, states, news, invs, normed, w_in)


def output_kernel(
    n, rep, shard, result_in, grad_input_in, w_parts, out_part, gu_parts, down_part, sums,
    result, grad_input, g_in, g_out, g_gate_up, g_down, g_gain_in, g_gain_mid, g_small, g_bias, g_rate, g_taps, g_gain_head,
):
    result[...] = result_in[...]
    grad_input[...] = grad_input_in[...]
    g_out[...] = out_part[...]
    g_down[...] = down_part[...]
    for i in range(2):
        for source in range(n):
            at = i * FF + source * shard
            g_gate_up[:, at : at + shard] = gu_parts[source, i].astype(f32)
    g_gain_mid[...] = jnp.sum(sums[:, 0:1, :], axis=0)
    width = MIXED * HD
    cut = D - width - HD
    for i in range(4):
        g_gain_in[:, i * cut : (i + 1) * cut] = jnp.sum(sums[:, 4 + i : 5 + i, width + HD :], axis=0)
    gain_total = jnp.zeros((1, HD), f32)
    for h in range(H):
        found = sums[h * rep]
        part = w_parts[h * rep].astype(f32)
        for j in range(SMALL):
            g_small[j * H + h : j * H + h + 1, :] = found[1 + j : 2 + j, :]
        for i in range(MIXED):
            g_taps[:, i * D + h * HD : i * D + (h + 1) * HD] = found[4 : 4 + CONV, i * HD : (i + 1) * HD]
        for i in range(GROUPS):
            g_in[:, i * D + h * HD : i * D + (h + 1) * HD] = part[:, i * HD : (i + 1) * HD]
        gain_total = gain_total + found[4:5, width : width + HD]
        g_bias[h] = found[5, width + NH]
        g_rate[h] = found[6, width + NH]
    g_gain_head[...] = gain_total


def run_output(n, rep, *parts):
    result, grad_input, w_parts, out_part, gu_parts, down_part, sums = parts
    piece, shard = out_part.shape[0], gu_parts.shape[-1]
    return pl.pallas_call(
        functools.partial(output_kernel, n, rep, shard),
        out_shape=(
            shape(result.shape, bf16), shape(grad_input.shape, f32), shape((piece, GROUPS * D), f32), shape((piece, D), f32),
            shape((piece, 2 * FF), f32), shape(down_part.shape, f32), shape((1, D), f32), shape((1, D), f32),
            shape((SMALL * H, D), f32), shape((H,), f32), shape((H,), f32), shape((CONV, MIXED * D), f32), shape((1, HD), f32),
        ),
        in_specs=[VMEM] * 7,
        out_specs=[VMEM] * 9 + [SMEM] * 2 + [VMEM] * 2,
        compiler_params=pltpu.CompilerParams(vmem_limit_bytes=LIMIT),
        name="outputs",
    )(*parts)


def on_device(tokens, grad_out, doc_lengths, gain_in, in_weight, small_weight, gate_bias, decay_rate, conv_weight,
              gain_head, out_weight, gain_mid, gate_up_weight, down_weight):
    seq, stream = lax.axis_size("seq"), lax.axis_size("stream")
    rep = seq // H
    T = tokens.shape[1]
    gain = gain_head.reshape(1, HD)
    gain_in, gain_mid = gain_in.reshape(1, D), gain_mid.reshape(1, D)
    rows, cotangent, small_weight = tokens[0], grad_out[0], small_weight.T
    gated, normed, out_all, proj, small, mixed, states, news, invs, head_rows = run_forward(
        seq, rep, T, doc_lengths, gate_bias, decay_rate, rows, cotangent, gain_in, in_weight, small_weight, conv_weight, gain
    )
    result, grad_residual, mid_all, grad_gain_mid = run_feed(
        seq, T, rows, gated, cotangent, out_weight, gain_mid, gate_up_weight, down_weight
    )
    parts = run_back(
        seq, stream, rep, T, doc_lengths, gate_bias, decay_rate, rows, grad_residual, gain_in, grad_gain_mid, small_weight,
        conv_weight, gain, mid_all, out_all, gate_up_weight, down_weight, out_weight, head_rows, proj, small, mixed, states,
        news, invs, normed, in_weight,
    )
    result, grad_input, g_in, g_out, g_gate_up, g_down, g_gain_in, g_gain_mid, g_small, g_bias, g_rate, g_taps, g_gain_head = (
        run_output(seq, rep, result, *parts)
    )
    return (
        result[None], grad_input[None], g_gain_in.reshape(D), g_in, g_small.T, g_bias, g_rate, g_taps,
        g_gain_head.reshape(HD), g_out, g_gain_mid.reshape(D), g_gate_up, g_down,
    )


def solution(mesh):
    rows, whole, split = P("stream", "seq", None), P(), P(("seq", "stream"), None)
    return jax.shard_map(
        on_device,
        mesh=mesh,
        in_specs=(rows, rows, P("stream", None)) + (whole,) * 11,
        out_specs=(rows, rows, whole, split, whole, whole, whole, whole, whole, split, whole, split, split),
        check_vma=False,
    )
```

```python
import functools

import jax
import jax.numpy as jnp
from jax import lax
from jax.experimental import pallas as pl
from jax.experimental.pallas import tpu as pltpu
from jax.sharding import PartitionSpec as P

D = 1024
H = 8
HD = 128
FF = 2816
NH = 2
CONV = 4
GROUPS = 2 + 2 * NH
MIXED = GROUPS - 1
SMALL = NH + 1
DOCS = 8
TILE = 256
EPS = 1e-06

f32 = jnp.float32
bf16 = jnp.bfloat16
MESH = pl.DeviceIdType.MESH
DMA = pltpu.SemaphoreType.DMA
VMEM = pl.BlockSpec(memory_space=pltpu.VMEM)
SMEM = pl.BlockSpec(memory_space=pltpu.SMEM)
ANY = pl.BlockSpec(memory_space=pl.ANY)
LIMIT = 56 * 1024 * 1024
shape = jax.ShapeDtypeStruct


def dot(a, b, dims):
    if isinstance(a, tuple) and isinstance(b, tuple):
        return dot(a[0], b[0], dims) + (dot(a[0], b[1], dims) + dot(a[1], b[0], dims))
    if isinstance(a, tuple):
        return dot(a[0], b, dims) + dot(a[1], b, dims)
    if isinstance(b, tuple):
        return dot(a, b[0], dims) + dot(a, b[1], dims)
    return lax.dot_general(
        a.astype(bf16), b.astype(bf16), ((dims[:1], dims[1:]), ((), ())), preferred_element_type=f32
    )


def nn(a, b):
    return dot(a, b, (1, 0))


def nt(a, b):
    return dot(a, b, (1, 1))


def tn(a, b):
    return dot(a, b, (0, 0))


def halves(x):
    high = x.astype(bf16)
    return high, (x - high.astype(f32)).astype(bf16)


def thirds(x):
    high, low = halves(x)
    return high, low, (x - high.astype(f32) - low.astype(f32)).astype(bf16)


def keep(ref, at, x):
    ref[0, at], ref[1, at] = halves(x)


def kept(ref, at):
    return ref[0, at], ref[1, at]


def nn_exact(ones, x):
    high, low, lowest = thirds(x)
    return nn(ones, high) + (nn(ones, low) + nn(ones, lowest))


def sigmoid(x):
    return 1.0 / (1.0 + jnp.exp(-x))


def softplus(x):
    return jnp.maximum(x, 0.0) + jnp.log(1.0 + jnp.exp(-jnp.abs(x)))


def norm_scale(values):
    return lax.rsqrt(jnp.mean(values * values, axis=-1, keepdims=True) + EPS)


def norm_back(values, scale, gain, grad):
    normal = values * scale
    e = grad * gain
    back = scale * (e - normal * jnp.mean(e * normal, axis=-1, keepdims=True))
    return back, jnp.sum(grad * normal, axis=0, keepdims=True)


def iota(dims, axis):
    return lax.broadcasted_iota(jnp.int32, dims, axis)


def doc_at(starts, positions):
    total = jnp.full(positions.shape, -1, jnp.int32)
    for start in starts:
        total = total + (start <= positions).astype(jnp.int32)
    return total


def doc_starts(lengths_ref):
    starts, at = [], jnp.int32(0)
    for j in range(DOCS):
        starts.append(at)
        at = at + lengths_ref[0, j]
    return starts


def stack2(a, b):
    return jnp.concatenate([a, b], axis=0)


def beside(a, b):
    return jnp.concatenate([a, b], axis=1)


def quad(a, b, c, d):
    return stack2(beside(a, b), beside(c, d))


def rows_of(i, size):
    return pl.ds(pl.multiple_of(i * size, size), size)


def greet(axis, peers):
    barrier = pltpu.get_barrier_semaphore()
    for peer in peers:
        pl.semaphore_signal(barrier, inc=1, device_id={axis: peer}, device_id_type=MESH)
    return lambda: pl.semaphore_wait(barrier, len(peers))


def remote(src, dst, send, receive, axis, peer):
    return pltpu.make_async_remote_copy(src, dst, send, receive, device_id={axis: peer}, device_id_type=MESH)


def flipped(chip, bits, chips):
    total, place = 0, 1
    while place < chips:
        total = total + place * lax.rem(chip // place + bits // place, 2)
        place *= 2
    return total


class Gather:
    def __init__(self, n, T, src, dst, sems):
        self.n, self.T, self.src, self.dst = n, T, src, dst
        self.ss, self.rs, self.fs, self.fr = sems
        self.me = lax.axis_index("seq")
        self.chip, self.side = self.me // 2, lax.rem(self.me, 2)
        self.sib = self.me + 1 - 2 * self.side
        order = sorted(range(1, n // 2), key=lambda k: k.bit_count())
        self.early = [k for k in order if k.bit_count() == 1]
        self.late = [k for k in order if k.bit_count() > 1]

    def at(self, device):
        return self.dst.at[rows_of(device, self.T)]

    def partner(self, k):
        return 2 * flipped(self.chip, k, self.n // 2) + self.side

    def direct(self, k):
        peer = self.sib if k == 0 else self.partner(k)
        return remote(self.src, self.at(self.me), self.ss.at[k], self.rs.at[k], "seq", peer)

    def passed(self, k):
        block = self.at(self.partner(k))
        return remote(block, block, self.fs.at[k], self.fr.at[k], "seq", self.sib)

    def relay(self, k):
        top = 1 << (k.bit_length() - 1)
        for side, last in ((0, top), (1, k & -k)):

            @pl.when(self.side == side)
            def _():
                block = self.at(self.partner(k - last))
                remote(block, block, self.ss.at[k], self.rs.at[k], "seq", self.partner(last)).start()

    def start(self):
        for k in (*self.early, 0):
            self.direct(k).start()

    def pass_on(self, k):
        self.direct(k).wait_recv()
        self.passed(k).start()

    def forward(self):
        for k in self.early:
            self.pass_on(k)
        for k in self.late:
            if k.bit_count() == 2:
                self.relay(k)

    def forward_late(self):
        for k in self.late:
            if k.bit_count() > 2:
                self.relay(k)
            self.pass_on(k)

    def arrive(self):
        self.direct(0).wait_recv()
        for k in range(1, self.n // 2):
            self.passed(k).wait_recv()

    def finish(self):
        for k in range(self.n // 2):
            self.direct(k).wait_send()
            if k:
                self.passed(k).wait_send()


def gather_sems(n):
    return [DMA((n // 2,)) for _ in range(4)]


def conv_of(block, taps, docs, T):
    total = block[8:] * taps[CONV - 1 : CONV]
    for lag in range(1, CONV):
        same = (docs[0] == docs[lag]).astype(f32)
        total = total + block[8 - lag : 8 - lag + T] * (taps[CONV - 1 - lag : CONV - lag] * same)
    return total


def chunk_gates(logits, bias, rate, starts, first, T):
    lane = iota((T, HD), 1)
    shifted = logits + bias
    gate = -rate * softplus(shifted)
    place_i, place_j = iota((T, T), 0), iota((T, T), 1)
    lower = place_j <= place_i
    cumul = nn_exact(lower.astype(bf16), jnp.where(lane == NH, gate, 0.0))
    beta = 2.0 * sigmoid(logits)
    b0, b1 = beta[:, 0:1], beta[:, 1:2]
    g = cumul[:, NH : NH + 1]
    g_row = jnp.transpose(cumul)[NH : NH + 1, :]
    g_last = cumul[T - 1 : T, NH : NH + 1]
    position = first + iota((T, 1), 0)
    docs = [doc_at(starts, position - lag) for lag in range(CONV)]
    doc = docs[0]
    doc_row = doc_at(starts, first + iota((1, T), 1))
    doc_before = doc_at(starts, jnp.full((1, 1), first - 1, jnp.int32))
    doc_last = doc_at(starts, jnp.full((1, 1), first + (T - 1), jnp.int32))
    joined = lower & (doc == doc_row)
    decay = jnp.where(joined, jnp.exp(jnp.where(joined, g - g_row, 0.0)), 0.0)
    strict = jnp.where(place_i == place_j, 0.0, decay)
    from_start = jnp.exp(g) * (doc == doc_before).astype(f32)
    to_end = jnp.exp(jnp.minimum(g_last - g, 0.0)) * (doc == doc_last).astype(f32)
    whole = jnp.exp(g_last) * (doc_last == doc_before).astype(f32)
    return dict(
        shifted=shifted, beta=beta, b=stack2(b0, b1), docs=docs, decay=decay,
        decays=quad(strict, strict, decay, strict), hd=from_start, hd2=stack2(from_start, from_start),
        to_end=stack2(to_end, to_end), whole=whole,
    )


def key_scale(raw):
    return lax.rsqrt(jnp.sum(raw * raw, axis=-1, keepdims=True) + EPS)


def chunk_inputs(block, taps, docs, T):
    conv = conv_of(block, taps, docs, T)
    sig = sigmoid(conv)
    active = conv * sig
    cut = [active[:, i * HD : (i + 1) * HD] for i in range(MIXED)]
    scales = (key_scale(cut[1]), key_scale(cut[2]))
    keys = stack2(cut[1] * scales[0], cut[2] * scales[1])
    values = stack2(cut[3], cut[4])
    return conv, sig, cut[0], keys, values, stack2(*scales)


def inverses(lowers, T):
    size = NH * T
    row, col = iota((size, size), 0), iota((size, size), 1)
    differ = (row & (T - 1)) ^ (col & (T - 1))
    eye = (row == col).astype(f32)
    found = [jnp.where(row == col, 1.0, jnp.where(differ == 0, -a, 0.0)) for a in lowers]
    step = 1
    while step < T:
        level = (differ >= step) & (differ < 2 * step)
        parts = [nn(jnp.where(level, a, 0.0), x) for a, x in zip(lowers, found)]
        found = [x - nn(x, part) for x, part in zip(found, parts)]
        step *= 2
    a_cut = [halves(a) for a in lowers]
    x_cut = [halves(x) for x in found]
    errors = [
        eye - x - (nn(a[0], xc[0]) + (nn(a[0], xc[1]) + nn(a[1], xc[0])))
        for a, x, xc in zip(a_cut, found, x_cut)
    ]
    return [x + nn(xc[0], e) for x, xc, e in zip(found, x_cut, errors)]


def head_gate(mixed, raw):
    scale = norm_scale(mixed)
    return mixed * scale, scale, sigmoid(raw)


def head_taps(taps_ref, head):
    cuts = [taps_ref[:, pl.ds(pl.multiple_of(i * D + head * HD, HD), HD)] for i in range(MIXED)]
    return jnp.concatenate(cuts, axis=1)


def intra_turn(T, starts, bias, rate, taps, small, block_of, invs, ubuf, wbuf, qbuf, pbuf, dbuf, gates, chunks, midway):
    held, lowers = [], []
    for c in chunks:
        first = pl.multiple_of(c * T, T)
        gate = chunk_gates(small[pl.ds(first, T), :], bias, rate, starts, first, T)
        conv, sig, query, keys, values, scales = chunk_inputs(block_of(c), taps, gate["docs"], T)
        key_pair = halves(keys)
        lowers.append(gate["b"] * (nt(key_pair, key_pair) * gate["decays"]))
        held.append((c, gate, query, keys, key_pair, values))
    found = inverses(lowers, T)
    midway()
    for (c, gate, query, keys, key_pair, values), inverse in zip(held, found):
        at, two = rows_of(c, T), rows_of(c, NH * T)
        pair = halves(inverse)
        invs[0, c], invs[1, c] = pair
        both = nn(pair, halves(gate["b"] * beside(values, gate["hd2"] * keys)))
        ubuf[two, :] = both[:, :HD]
        keep(wbuf, two, both[:, HD:])
        query_pair = halves(query)
        qbuf[0, at], qbuf[1, at] = query_pair
        keep(pbuf, at, nt(query_pair, key_pair) * beside(gate["decay"], gate["decay"]))
        keep(dbuf, two, gate["to_end"] * keys)
        gates[at, :] = jnp.where(iota((T, HD), 1) == 0, gate["hd"], gate["whole"])


def across_turn(T, gain, proj, mixed_out, states, news, head_rows, ubuf, wbuf, qbuf, pbuf, dbuf, gates, done, c, state):
    at, two = rows_of(c, T), rows_of(c, NH * T)
    state_pair = halves(state)
    states[0, c], states[1, c] = state_pair
    new = ubuf[two, :] - nn(kept(wbuf, two), state_pair)
    new_pair = halves(new)
    news[0, two], news[1, two] = new_pair
    gate = gates[at, :]
    mixed = gate[:, 0:1] * nn(kept(qbuf, at), state_pair) + nn(kept(pbuf, at), new_pair)
    mixed_out[at, :] = mixed
    raw = proj[at, MIXED * HD :].astype(f32)
    normal, _, sig = head_gate(mixed, raw)
    head_rows[at, :] = ((normal * gain[...]) * (raw * sig)).astype(bf16)
    done(c)
    return gate[0:1, 1:2] * state + tn(kept(dbuf, two), new_pair)


def widened(w_wide, parts):
    w_wide[...] = jnp.zeros((HD, D), bf16)
    for i, part in enumerate(parts):
        w_wide[32 * i : 32 * i + SMALL * H, :] = part


def forward_kernel(
    n, rep, T, lengths, bias_ref, rate_ref, tokens, cotangent, gain_in, w_in, w_small, taps_ref, gain,
    gated, normed_out, out_all, proj_out, small_out, mixed_out, states, news, invs_out, head_rows,
    normed, proj, small, invs, own, tails, w_head, w_wide, tail_rows, xbuf, ubuf, wbuf, qbuf, pbuf, dbuf, gates,
    w_sems, own_sems, o_sems, a_ss, a_rs, t_ss, t_rs, *sems,
):
    me = lax.axis_index("seq")
    head = me // rep
    chips = n // 2
    wait_for_all = greet("seq", [lax.rem(me + k, n) for k in range(1, n)])
    width = MIXED * HD
    loads = [
        pltpu.make_async_copy(
            w_in.at[:, pl.ds(pl.multiple_of(i * D + head * HD, HD), HD)], w_head.at[:, i * HD : (i + 1) * HD], w_sems.at[i]
        )
        for i in range(GROUPS)
    ]
    for load in loads:
        load.start()
    values = tokens[...].astype(f32)
    own[...] = (values * norm_scale(values) * gain_in[...]).astype(bf16)
    local = pltpu.make_async_copy(own, normed.at[rows_of(me, T)], own_sems.at[0])
    local.start()
    wait_for_all()
    first_gather = Gather(n, T, own, normed, sems[:4])
    second_gather = Gather(n, T, cotangent, out_all, sems[4:8])
    keep_out = pltpu.make_async_copy(cotangent, out_all.at[rows_of(me, T)], own_sems.at[2])
    keep_out.start()
    chip, side = first_gather.chip, first_gather.side
    last = own.at[T - 16 : T]

    def tail_copy(k):
        return remote(last, tails.at[chip], t_ss.at[k], t_rs.at[chip], "seq", lax.rem(me + k, n))

    mine = pltpu.make_async_copy(last, tails.at[chip], own_sems.at[1])
    early, late = first_gather.early, first_gather.late

    @pl.when(side == 1)
    def _():
        for k in range(1, n):
            tail_copy(k).start()
        mine.start()

    for k in (0, *early):
        first_gather.direct(k).start()

    starts = doc_starts(lengths)
    bias, rate = bias_ref[head], rate_ref[head]
    taps = head_taps(taps_ref, head)
    widened(w_wide, thirds(jnp.where((iota((SMALL * H, D), 0) & (H - 1)) == head, w_small[...], 0.0)))
    group, lane = iota((HD, HD), 0), iota((HD, HD), 1)
    picks = (((group & 31) >> 3) == lane) & (group < 96) & (lane < SMALL)
    picks = picks.astype(bf16)
    for load in loads:
        load.wait()
    local.wait()

    @pl.when(side == 1)
    def _():
        mine.wait()
        for k in range(1, n):
            tail_copy(k).wait_send()

    for j in range(chips):

        @pl.when(me != 2 * j + 1)
        def _():
            remote(last, tails.at[j], t_ss.at[0], t_rs.at[j], "seq", lax.rem(me + 1, n)).wait_recv()

    found = nn(tails[...].reshape(chips * 16, D), w_head[...]).astype(bf16).astype(f32)
    tail_rows[...] = found[:, :width]
    size = T + 8

    def block_of(c):
        return xbuf[pl.ds(pl.multiple_of(c * size, 8), size), :]

    def project(pair):
        at = rows_of(pair, 2 * T)
        block = normed[at, :]
        result = nn(block, w_head[...]).astype(bf16)
        proj[at, :] = result
        raw = thirds(nt(block, w_wide[...]))
        small[at, :] = nn(raw[0], picks) + (nn(raw[1], picks) + nn(raw[2], picks))
        mixing = result[:, :width].astype(f32)
        before = lax.rem(pair + chips - 1, chips)
        halo = tail_rows[pl.ds(pl.multiple_of(before * 16 + 8, 8), 8), :]
        base = pl.multiple_of(pair * (2 * size), 8)
        xbuf[pl.ds(base, 8), :] = jnp.where(pair > 0, halo, 0.0)
        xbuf[pl.ds(pl.multiple_of(base + 8, 8), T), :] = mixing[:T]
        xbuf[pl.ds(pl.multiple_of(base + size, 8), T + 8), :] = mixing[T - 8 :]

    first_gather.direct(0).wait_recv()
    groups = [(0,)] + [(*ks[i : i + 2],) for ks in (early, late) for i in range(0, len(ks), 2)]
    to_late = (len(early) + 1) // 2

    def midway(g):
        if g == 0:
            first_gather.forward()
        if g == to_late:
            first_gather.forward_late()
            second_gather.start()
        if g == len(groups) - 1:
            second_gather.forward()

    for g, group in enumerate(groups):
        for k in group:
            if k:
                first_gather.passed(k).wait_recv()
        pairs = [flipped(chip, k, chips) for k in group]
        for pair in pairs:
            project(pair)
        intra_turn(
            T, starts, bias, rate, taps, small, block_of, invs, ubuf, wbuf, qbuf, pbuf, dbuf, gates,
            [2 * pair + i for pair in pairs for i in range(2)], functools.partial(midway, g),
        )

    first_gather.finish()
    stores = [
        pltpu.make_async_copy(a, b, o_sems.at[i])
        for i, (a, b) in enumerate(((normed, normed_out), (proj, proj_out), (small, small_out), (invs, invs_out)))
    ]
    for store in stores:
        store.start()
    column = pl.ds(pl.multiple_of(head * HD, HD), HD)

    def row_copy(c):
        return remote(head_rows.at[rows_of(c, T)], gated.at[:, column], a_ss.at[c], a_rs.at[head], "seq", c)

    def send_rows(c):
        @pl.when((c != me) & (lax.rem(me, rep) == 0))
        def _():
            row_copy(c).start()

    across = functools.partial(
        across_turn, T, gain, proj, mixed_out, states, news, head_rows, ubuf, wbuf, qbuf, pbuf, dbuf, gates, send_rows
    )
    lax.fori_loop(0, n, across, jnp.zeros((HD, HD), f32))

    @pl.when(lax.rem(me, rep) == 0)
    def _():
        kept_rows = pltpu.make_async_copy(head_rows.at[rows_of(me, T)], gated.at[:, column], own_sems.at[0])
        kept_rows.start()
        kept_rows.wait()

    keep_out.wait()
    second_gather.forward_late()

    def settle(k, _):
        peer = lax.rem(me + k, n)

        @pl.when(lax.rem(me, rep) == 0)
        def _():
            row_copy(peer).wait_send()

        @pl.when(lax.rem(peer, rep) == 0)
        def _():
            source = peer // rep
            remote(
                head_rows.at[rows_of(me, T)], gated.at[:, pl.ds(pl.multiple_of(source * HD, HD), HD)],
                a_ss.at[peer], a_rs.at[source], "seq", peer,
            ).wait_recv()

        return 0

    lax.fori_loop(1, n, settle, 0)
    second_gather.arrive()
    second_gather.finish()
    for store in stores:
        store.wait()


def forward_scratch(n, T):
    rows = n * T
    return [
        pltpu.VMEM((rows + 8 * n, MIXED * HD), f32), pltpu.VMEM((NH * rows, HD), f32),
        pltpu.VMEM((2, NH * rows, HD), bf16), pltpu.VMEM((2, rows, HD), bf16), pltpu.VMEM((2, rows, NH * T), bf16),
        pltpu.VMEM((2, NH * rows, HD), bf16), pltpu.VMEM((rows, HD), f32),
    ]


def run_forward(n, rep, T, lengths, bias, rate, tokens, cotangent, gain_in, w_in, w_small, taps, gain):
    rows = n * T
    return pl.pallas_call(
        functools.partial(forward_kernel, n, rep, T),
        out_shape=(
            shape((T, D), bf16), shape((rows, D), bf16), shape((rows, D), bf16), shape((rows, GROUPS * HD), bf16),
            shape((rows, HD), f32), shape((rows, HD), f32), shape((2, n, HD, HD), bf16), shape((2, NH * rows, HD), bf16),
            shape((2, n, NH * T, NH * T), bf16), shape((rows, HD), bf16),
        ),
        in_specs=[SMEM] * 3 + [VMEM, VMEM, VMEM, ANY, VMEM, VMEM, VMEM],
        out_specs=[VMEM, ANY, ANY, ANY, ANY, VMEM, VMEM, VMEM, ANY, VMEM],
        scratch_shapes=[
            pltpu.VMEM((rows, D), bf16), pltpu.VMEM((rows, GROUPS * HD), bf16), pltpu.VMEM((rows, HD), f32),
            pltpu.VMEM((2, n, NH * T, NH * T), bf16),
            pltpu.VMEM((T, D), bf16), pltpu.VMEM((n // 2, 16, D), bf16), pltpu.VMEM((D, GROUPS * HD), bf16),
            pltpu.VMEM((HD, D), bf16), pltpu.VMEM((n * 8, MIXED * HD), f32),
            *forward_scratch(n, T),
            DMA((GROUPS,)), DMA((3,)), DMA((4,)), DMA((n,)), DMA((H,)), DMA((n,)), DMA((n // 2,)), *gather_sems(n), *gather_sems(n),
        ],
        compiler_params=pltpu.CompilerParams(vmem_limit_bytes=LIMIT, collective_id=1, has_side_effects=True),
        name="mixer_forward",
    )(lengths, bias, rate, tokens, cotangent, gain_in, w_in, w_small, taps, gain)


def feed_kernel(
    n, T, steps, tokens, gated, cotangent, w_out, gain_mid, w_gate, w_up, w_down,
    result, grad_residual, mid_all, gain_grad, residual, middle, total, grad_mid, own_sem, *sems,
):
    step = pl.program_id(0)
    me = lax.axis_index("seq")
    gather = Gather(n, T, middle, mid_all, sems)
    local = pltpu.make_async_copy(middle, mid_all.at[rows_of(me, T)], own_sem)

    @pl.when(step == 0)
    def _():
        peers = [gather.sib] + [gather.partner(k) for k in range(1, n // 2)]
        wait_for_all = greet("seq", peers)
        found = tokens[...].astype(f32) + nn(gated[...], w_out[...])
        residual[...] = found
        middle[...] = (found * norm_scale(found) * gain_mid[...]).astype(bf16)
        total[...] = found
        grad_mid[...] = jnp.zeros((T, D), f32)
        wait_for_all()
        gather.start()
        local.start()

    gate, up = nn(middle[...], w_gate[...]), nn(middle[...], w_up[...])
    sig = sigmoid(gate)
    silu = gate * sig
    hidden = (silu * up).astype(bf16)
    total[...] += nn(hidden, w_down[...])
    grad_hidden = nt(cotangent[...], w_down[...])
    grad_gate = (grad_hidden * up * (sig * (1.0 + gate * (1.0 - sig)))).astype(bf16)
    grad_up = (grad_hidden * silu).astype(bf16)
    grad_mid[...] += nt(grad_gate, w_gate[...]) + nt(grad_up, w_up[...])

    for at, what in ((5, gather.forward), (8, gather.forward_late)):

        @pl.when(step == at)
        def _():
            what()

    @pl.when(step == steps - 1)
    def _():
        result[...] = total[...].astype(bf16)
        values = residual[...]
        back, gain_part = norm_back(values, norm_scale(values), gain_mid[...], grad_mid[...])
        gain_grad[...] = gain_part
        grad_residual[...] = cotangent[...].astype(f32) + back
        gather.arrive()
        gather.finish()
        local.wait()


def run_feed(n, T, tokens, gated, cotangent, w_out, gain_mid, w_gate_up, w_down):
    steps = FF // TILE
    fixed = lambda *dims: pl.BlockSpec(dims, lambda i: (0, 0))
    return pl.pallas_call(
        functools.partial(feed_kernel, n, T, steps),
        grid=(steps,),
        out_shape=(shape((T, D), bf16), shape((T, D), f32), shape((n * T, D), bf16), shape((1, D), f32)),
        in_specs=[
            fixed(T, D), fixed(T, D), fixed(T, D), fixed(D, D), fixed(1, D),
            pl.BlockSpec((D, TILE), lambda i: (0, i)), pl.BlockSpec((D, TILE), lambda i: (0, i + FF // TILE)),
            pl.BlockSpec((TILE, D), lambda i: (i, 0)),
        ],
        out_specs=[fixed(T, D), fixed(T, D), ANY, fixed(1, D)],
        scratch_shapes=[
            pltpu.VMEM((T, D), f32), pltpu.VMEM((T, D), bf16), pltpu.VMEM((T, D), f32), pltpu.VMEM((T, D), f32),
            DMA, *gather_sems(n),
        ],
        compiler_params=pltpu.CompilerParams(vmem_limit_bytes=LIMIT, collective_id=2, has_side_effects=True),
        name="feed_forward",
    )(tokens, gated, cotangent, w_out, gain_mid, w_gate_up, w_gate_up, w_down)


def backward_turn(
    n, T, head, starts, bias, rate, taps, gain, incoming_of, proj, small, states, fetch,
    gp, grad_small, gconv_w, xbuf, halo, gates_sum, grad_state, done, k, _,
):
    width = MIXED * HD
    lane = iota((T, HD), 1)
    place_i, place_j = iota((T, T), 0), iota((T, T), 1)
    upper = (place_j >= place_i).astype(bf16)
    under = place_j < place_i
    c = n - 1 - k
    first = pl.multiple_of(c * T, T)
    at, two = rows_of(c, T), rows_of(c, NH * T)
    gate = chunk_gates(small[at, :], bias, rate, starts, first, T)
    block = xbuf[pl.ds(first, T + 8), :]
    conv, sig, query, keys, values, scales = chunk_inputs(block, taps, gate["docs"], T)
    key_pair, query_pair = halves(keys), halves(query)
    b, hd, hd2, to_end = gate["b"], gate["hd"], gate["hd2"], gate["to_end"]
    decay2 = beside(gate["decay"], gate["decay"])
    pairs = nt(key_pair, key_pair) * gate["decays"]
    scores = nt(query_pair, key_pair) * decay2
    state = (states[0, c], states[1, c])
    state_grad = grad_state[...]
    new, inverse, mixed = fetch(c)
    raw = proj[at, width:].astype(f32)
    normal, scale, zsig = head_gate(mixed, raw)
    incoming = incoming_of(at)
    passed = incoming * (raw * zsig)
    gates_sum[0:1, :] += jnp.sum(passed * normal, axis=0, keepdims=True)
    grad_z = incoming * (normal * gain[...]) * (zsig * (1.0 + raw * (1.0 - zsig)))
    e = passed * gain[...]
    grad_mixed = scale * (e - normal * jnp.mean(e * normal, axis=-1, keepdims=True))
    gm = halves(grad_mixed)
    ended = halves(to_end * keys)
    grad_pair = halves(state_grad)
    grad_new = tn(halves(scores), gm) + nn(ended, grad_pair)
    grad_right = tn(inverse, halves(grad_new))
    moved = b * grad_right
    grad_state[...] = gate["whole"] * state_grad + tn(halves(hd * query), gm) - tn(halves(hd2 * keys), halves(moved))
    grad_ended = nt(new, grad_pair)
    grad_scores = nt(gm, new)
    grad_lower = jnp.where(gate["decays"] != 0.0, -nt(halves(grad_right), new), 0.0)
    from_grad = nt(gm, state)
    scored = grad_scores * decay2
    grad_query = hd * from_grad + nn(scored, key_pair[0])
    paired = (b * grad_lower) * gate["decays"]
    keyed = nn(key_pair, state)
    grad_keys = (
        tn(scored, query_pair[0]) + to_end * grad_ended - hd2 * nt(moved, state[0])
        + nn(paired, key_pair[0]) + tn(paired, key_pair[0])
    )
    lower_pairs = grad_lower * pairs
    grad_b = jnp.sum(grad_right * (values - hd2 * keyed), axis=-1, keepdims=True) + jnp.sum(
        lower_pairs, axis=-1, keepdims=True
    )
    four = b * lower_pairs
    both = grad_scores * scores
    joint = (four[:T, :T] + four[:T, T:]) + (four[T:, :T] + four[T:, T:]) + (both[:, :T] + both[:, T:])
    crossing = jnp.sum(jnp.where(under, nn_exact(upper, joint), 0.0), axis=-1, keepdims=True)
    start_part = -hd2 * jnp.sum(moved * keyed, axis=-1, keepdims=True)
    start_part = start_part[:T] + start_part[T:] + hd * jnp.sum(query * from_grad, axis=-1, keepdims=True)
    end_part = to_end * jnp.sum(grad_ended * keys, axis=-1, keepdims=True)
    end_part = end_part[:T] + end_part[T:]
    sums_in = jnp.where(lane == 0, start_part, jnp.where(lane == 1, end_part, 0.0))
    after = nn_exact(upper, sums_in)
    before = nn_exact(under.astype(bf16), sums_in)
    whole_part = gate["whole"] * jnp.sum(state_grad * (state[0].astype(f32) + state[1].astype(f32)), keepdims=True)
    grad_gate = crossing + after[:, 0:1] + before[:, 1:2] + whole_part
    shifted = gate["shifted"]
    grad_beta = [grad_b[i * T : (i + 1) * T] * (gate["beta"][:, i : i + 1] * (1.0 - 0.5 * gate["beta"][:, i : i + 1])) for i in range(NH)]
    grad_decay = (-grad_gate * rate * sigmoid(shifted))[:, NH : NH + 1]
    which = lane >> 3
    logit = jnp.where(which == 0, grad_beta[0], jnp.where(which == 1, grad_beta[1], grad_decay))
    grad_logits = jnp.where((lane < SMALL * H) & ((lane & (H - 1)) == head), logit, 0.0)
    gates_sum[1:2, :] += jnp.sum(jnp.where(lane == NH, grad_decay, 0.0), axis=0, keepdims=True)
    gates_sum[2:3, :] += jnp.sum(jnp.where(lane == NH, grad_gate * -softplus(shifted), 0.0), axis=0, keepdims=True)
    high = grad_logits.astype(bf16).astype(f32)
    grad_small[at, :] = (
        high + pltpu.roll(grad_logits - high, 32, 1) + pltpu.roll(high, 64, 1)
    ).astype(bf16)
    projected_out = jnp.sum(keys * grad_keys, axis=-1, keepdims=True)
    grad_raw = (grad_keys - keys * projected_out) * scales
    slope = sig * (1.0 + conv * (1.0 - sig))
    grad_active = jnp.concatenate([grad_query, grad_raw[:T], grad_raw[T:], moved[:T], moved[T:]], axis=1)
    grad_conv = grad_active * slope
    after_block = stack2(grad_conv, halo[...])
    halo[...] = grad_conv[:8]
    position = first + iota((T, 1), 0)
    total = grad_conv * taps[CONV - 1 : CONV]
    taps_grads = [None] * CONV
    taps_grads[CONV - 1] = jnp.sum(grad_conv * block[8:], axis=0, keepdims=True)
    for lag in range(1, CONV):
        same = (doc_at(starts, position + lag) == gate["docs"][0]).astype(f32)
        total = total + after_block[lag : lag + T] * (taps[CONV - 1 - lag : CONV - lag] * same)
        same = (gate["docs"][lag] == gate["docs"][0]).astype(f32)
        taps_grads[CONV - 1 - lag] = jnp.sum(
            grad_conv * (block[8 - lag : 8 - lag + T] * same), axis=0, keepdims=True
        )
    everything = beside(total, grad_z).astype(bf16)
    gp[at, :] = everything
    gconv_w[...] += jnp.concatenate(taps_grads, axis=0)
    done(k)
    return 0


class Chain:
    def __init__(self, own, up_in, down_in, sems, my, m):
        self.own, self.up_in, self.down_in = own, up_in, down_in
        self.us, self.ur, self.ds, self.dr = sems
        self.my, self.m = my, m

    def up(self, q):
        slot = q - self.my
        return self.own(self.my + self.m - 1 - q), self.up_in(slot), slot, self.my + 1, self.us, self.ur

    def down(self, q):
        slot = q - (self.m - 1 - self.my)
        return self.own(self.my - (self.m - 1 - q)), self.down_in(slot), slot, self.my - 1, self.ds, self.dr

    def copy(self, hop):
        own, arrived, slot, peer, send, receive = hop
        return remote(own, arrived, send.at[slot], receive.at[slot], "stream", peer)

    def start(self):
        for q in range(self.m - 1):

            @pl.when(self.my == 0)
            def _():
                self.copy(self.up(q)).start()

            @pl.when(self.my == self.m - 1)
            def _():
                self.copy(self.down(q)).start()

    def tick(self, q):
        for inner, way in (
            ((self.my > 0) & (self.my <= q), self.up),
            ((self.my < self.m - 1) & (self.my >= self.m - 1 - q), self.down),
        ):

            @pl.when(inner)
            def _():
                hop = way(q)
                self.copy(hop).wait_recv()
                own, arrived = hop[:2]

                def add(i, _):
                    own[i] = (own[i].astype(f32) + arrived[i].astype(f32)).astype(bf16)
                    return 0

                if len(own.shape) == 3 and own.shape[0] > 2:
                    lax.fori_loop(0, own.shape[0], add, 0)
                else:
                    own[...] = (own[...].astype(f32) + arrived[...].astype(f32)).astype(bf16)
                self.copy(hop).start()

    def finish(self, write):
        last = self.m - 1

        @pl.when(self.my > 0)
        def _():
            slot = last - self.my
            remote(self.own(self.my), self.up_in(slot), self.us.at[slot], self.ur.at[slot], "stream", self.my - 1).wait_recv()

        @pl.when(self.my < last)
        def _():
            slot = self.my
            remote(self.own(self.my), self.down_in(slot), self.ds.at[slot], self.dr.at[slot], "stream", self.my + 1).wait_recv()

        from_below, from_above = self.up_in(lax.rem(last - self.my, last)), self.down_in(lax.rem(self.my, last))
        found = self.own(self.my)[...].astype(f32) + jnp.where(self.my > 0, from_below[...].astype(f32), 0.0)
        write(found + jnp.where(self.my < last, from_above[...].astype(f32), 0.0))

    def settle(self):
        for q in range(self.m - 1):

            @pl.when(self.my <= q)
            def _():
                self.copy(self.up(q)).wait_send()

            @pl.when(self.my >= self.m - 1 - q)
            def _():
                self.copy(self.down(q)).wait_send()


class Sums:
    def __init__(self, own, arrived, every, sems, me, my, n, m):
        self.own, self.arrived, self.every = own, arrived, every
        self.zs, self.zr, self.ss, self.rs = sems
        self.me, self.my, self.n, self.m = me, my, n, m

    def across(self, k):
        peer = lax.rem(self.my + k, self.m)
        return remote(self.own, self.arrived.at[k - 1], self.zs.at[k - 1], self.zr.at[k - 1], "stream", peer)

    def along(self, k):
        block = self.every.at[self.me]
        return remote(block, block, self.ss.at[k - 1], self.rs.at[k - 1], "seq", lax.rem(self.me + k, self.n))

    def start(self):
        for k in range(1, self.m):
            self.across(k).start()

    def add(self):
        total = self.own[...]
        for k in range(1, self.m):
            self.across(k).wait()
            total = total + self.arrived[k - 1]
        self.every[self.me] = total
        for k in range(1, self.n):
            self.along(k).start()

    def settle(self):
        for k in range(1, self.n):
            self.along(k).wait()


def chain_sems(*lead):
    return [DMA(lead) for _ in range(4)]


def scatter_to(own, arrived, k, send, receive, me, size):
    peer = lax.rem(me + k, size)
    return remote(own.at[peer], arrived.at[me], send.at[k - 1], receive.at[k - 1], "seq", peer)


def back_kernel(
    n, m, rep, T, piece, shard, wide,
    lengths, bias_ref, rate_ref, tokens, grad_residual, gain_in, gain_mid_grad, w_small, taps_ref, gain,
    mid_any, out_any, w_gate_up, w_down, w_out, rows_any, proj_any, small_any, mixed_any, states_any, news_any, invs_any,
    normed_any, w_in_any,
    grad_input, q_w_in, g_out, q_gu_in, g_down, q_sum,
    mid, cot, w_gate, w_up, w_hid, w_head, head_rows, proj, small, mixed, states, news, invs, normed, w_in, w_wide,
    low_all, hidden, grad_gate, grad_up, gp, grad_small, gconv_w, xbuf, halo, gates_sum, grad_state,
    z_gu, z_gu_up, z_gu_down, z_down, z_down_up, z_down_down, z_out, z_out_up, z_out_down, z_w, z_w_up, z_w_down,
    z_sum, z_sum_in, gain_sum, q_gu, q_w, part_own, part_out, part_in, chip_out, chip_in,
    l_sems, i_sems, gu_us, gu_ur, gu_ds, gu_dr, dn_us, dn_ur, dn_ds, dn_dr, ou_us, ou_ur, ou_ds, ou_dr, w_us, w_ur, w_ds, w_dr,
    sum_ss, sum_rs, qgu_ss, qgu_rs, qw_ss, qw_rs, qsum_ss, qsum_rs, p_ss, p_rs, c_ss, c_rs, *sems,
):
    me, my = lax.axis_index("seq"), lax.axis_index("stream")
    head, chip, side = me // rep, me // 2, lax.rem(me, 2)
    sib = me + 1 - 2 * side
    barrier = pltpu.get_barrier_semaphore()
    for k in range(1, n):
        pl.semaphore_signal(barrier, inc=1, device_id={"seq": lax.rem(me + k, n)}, device_id_type=MESH)
    for k in range(1, m):
        pl.semaphore_signal(barrier, inc=1, device_id={"stream": lax.rem(my + k, m)}, device_id_type=MESH)
    first_unit = me * shard
    base = (first_unit // HD - me // (n - 1)) * HD
    offset = first_unit - base
    sources = [
        mid_any, out_any, w_gate_up.at[:, pl.ds(pl.multiple_of(base, HD), wide)],
        w_gate_up.at[:, pl.ds(pl.multiple_of(FF + base, HD), wide)], w_down.at[pl.ds(pl.multiple_of(base, HD), wide)],
        w_out.at[rows_of(head, HD)], rows_any, proj_any, small_any, mixed_any, states_any, news_any, invs_any, normed_any,
    ]
    places = [mid, cot, w_gate, w_up, w_hid, w_head, head_rows, proj, small, mixed, states, news, invs, normed]
    roomy = len(normed.shape) == 2
    loads = [pltpu.make_async_copy(a, b, l_sems.at[i]) for i, (a, b) in enumerate(zip(sources, places)) if i not in (9, 11, 12, 13) or roomy]
    for i in range(GROUPS):
        column = pl.ds(pl.multiple_of(i * D + head * HD, HD), HD)
        loads.append(pltpu.make_async_copy(w_in_any.at[:, column], w_in.at[:, i * HD : (i + 1) * HD], i_sems.at[i]))
    for load in loads[:5]:
        load.start()
    low_all[rows_of(me, T), :] = grad_residual[...].astype(bf16)
    pl.semaphore_wait(barrier, n + m - 2)
    gather = Gather(n, T, low_all.at[rows_of(me, T)], low_all, sems)
    gather.start()

    for load in loads[:5]:
        load.wait()
    for load in loads[5:]:
        load.start()

    def feed_turn(i, _):
        at = rows_of(i, TILE)
        block = mid[at, :]
        gate, up = nn(block, w_gate[...]), nn(block, w_up[...])
        sig = sigmoid(gate)
        silu = gate * sig
        grad_hidden = nt(cot[at, :], w_hid[...])
        own = lambda x: pltpu.roll(x, wide - offset, 1)[:, :shard].astype(bf16)
        hidden[at, :] = own(silu * up)
        grad_gate[at, :] = own(grad_hidden * up * (sig * (1.0 + gate * (1.0 - sig))))
        grad_up[at, :] = own(grad_hidden * silu)
        return 0

    lax.fori_loop(0, n * T // TILE, feed_turn, 0)
    downs = Chain(lambda d: z_down.at[d], lambda i: z_down_up.at[i], lambda i: z_down_down.at[i], (dn_us, dn_ur, dn_ds, dn_dr), my, m)
    ups = [
        Chain(
            lambda d, j=j: z_gu.at[j, d], lambda i, j=j: z_gu_up.at[j, i], lambda i, j=j: z_gu_down.at[j, i],
            (gu_us.at[j], gu_ur.at[j], gu_ds.at[j], gu_dr.at[j]), my, m,
        )
        for j in range(2)
    ]
    part = tn(hidden[...], cot[...])
    for d in range(m):
        z_down[d] = part[d * (shard // m) : (d + 1) * (shard // m)].astype(bf16)
    downs.start()
    gather.forward()
    for j, grads in enumerate((grad_gate, grad_up)):
        if j:
            gather.forward_late()

        def strip_turn(t, _, j=j, grads=grads):
            found = tn(mid[:, rows_of(t, TILE)], grads[...])
            for i in range(TILE // piece):
                z_gu[j, i % m, t * (TILE // piece // m) + i // m] = found[i * piece : (i + 1) * piece].astype(bf16)
            return 0

        lax.fori_loop(0, D // TILE, strip_turn, 0)
        ups[j].start()
    w_high, w_low = halves(w_small[...])
    widened(w_wide, (w_high, w_high, w_low))
    gather.arrive()
    gather.finish()
    for load in loads[5:]:
        load.wait()
    rows = tn(head_rows[...], low_all[...])
    for share in range(rep):

        @pl.when(lax.rem(me, rep) == share)
        def _():
            for d in range(m):
                at = share * (HD // rep) + d * piece
                z_out[d] = rows[at : at + piece].astype(bf16)

    outs = Chain(lambda d: z_out.at[d], lambda i: z_out_up.at[i], lambda i: z_out_down.at[i], (ou_us, ou_ur, ou_ds, ou_dr), my, m)
    outs.start()
    if not roomy:
        normed = mid
        late = pltpu.make_async_copy(normed_any, normed, l_sems.at[13])
        late.start()
        late.wait()

    width = MIXED * HD
    starts = doc_starts(lengths)
    bias, rate = bias_ref[head], rate_ref[head]
    taps = head_taps(taps_ref, head)
    xbuf[0:8, :] = jnp.zeros((8, width), f32)
    halo[...] = jnp.zeros((8, width), f32)
    gconv_w[...] = jnp.zeros(gconv_w.shape, f32)
    gates_sum[...] = jnp.zeros((8, HD), f32)
    grad_state[...] = jnp.zeros((HD, HD), f32)

    def fill(c, _):
        xbuf[pl.ds(pl.multiple_of(8 + c * T, 8), T), :] = proj[rows_of(c, T), :width].astype(f32)
        return 0

    lax.fori_loop(0, n, fill, 0)

    def normed_rows(at):
        if roomy:
            return normed[at, :].astype(f32)
        return mid[at, :].astype(f32)

    gain_sum[...] = jnp.zeros((1, D), f32)

    def sibling_copy(j):
        return remote(part_out.at[j], part_in.at[j], p_ss.at[j], p_rs.at[j], "seq", sib)

    def owner_copy(j):
        return remote(chip_out.at[j], chip_in.at[chip], c_ss.at[j], c_rs.at[chip], "seq", 2 * j + side)

    def form(j):
        at = rows_of(j, 2 * T)
        found = nt(gp[at, :], w_in[...]) + nn(grad_small[at, :], w_wide[...])
        if rep > 1:
            found = found * (lax.rem(me, rep) == 0).astype(f32)
        gain_sum[...] += jnp.sum(found * normed_rows(at), axis=0, keepdims=True)
        for i in range(2):

            @pl.when(side == i)
            def _():
                part_own[j] = found[i * T : (i + 1) * T].astype(part_own.dtype)
                part_out[j] = found[(1 - i) * T : (2 - i) * T].astype(bf16)

        sibling_copy(j).start()

    def join(j):
        sibling_copy(j).wait_recv()
        found = part_own[j].astype(f32) + part_in[j].astype(f32)
        part_own[j] = found.astype(part_own.dtype)
        chip_out[j] = found.astype(bf16)

        @pl.when(chip != j)
        def _():
            owner_copy(j).start()

    hops = [(chain, q) for chain in (downs, *ups) for q in range(1, m - 1)]

    def after_turn(k):
        c = n - 1 - k

        @pl.when(lax.rem(k, 2) == 1)
        def _():
            form(c // 2)

        @pl.when((lax.rem(k, 2) == 0) & (k > 0))
        def _():
            join((c + 1) // 2)

        for i, (chain, q) in enumerate(hops):

            @pl.when(k == 3 * i // 2)
            def _():
                chain.tick(q)

    def fetch(c):
        if roomy:
            return kept(news, rows_of(c, NH * T)), (invs[0, c], invs[1, c]), mixed[rows_of(c, T), :]
        late = [
            pltpu.make_async_copy(news_any.at[:, rows_of(c, NH * T)], news, l_sems.at[11]),
            pltpu.make_async_copy(invs_any.at[:, pl.ds(c, 1)], invs, l_sems.at[12]),
            pltpu.make_async_copy(mixed_any.at[rows_of(c, T)], mixed, l_sems.at[9]),
        ]
        for load in late:
            load.start()
        for load in late:
            load.wait()
        return (news[0], news[1]), (invs[0, 0], invs[1, 0]), mixed[...]

    turn = functools.partial(
        backward_turn, n, T, head, starts, bias, rate, taps, gain, lambda at: nt(low_all[at, :], w_head[...]),
        proj, small, states, fetch, gp, grad_small, gconv_w, xbuf, halo, gates_sum, grad_state, after_turn,
    )
    lax.fori_loop(0, n, turn, 0)

    small_t = tn(grad_small[...], normed[...])
    small_t = small_t[: SMALL * H] + small_t[32 : 32 + SMALL * H]
    z_sum[0:1, :] = gain_mid_grad[...]
    for i in range(SMALL):
        z_sum[1 + i : 2 + i, :] = jnp.sum(small_t[i * H : (i + 1) * H], axis=0, keepdims=True)
    z_sum[4:8, :width] = gconv_w[...]
    for i in range(3):
        z_sum[4 + i : 5 + i, width : width + HD] = gates_sum[i : i + 1, :]
    z_sum[7:8, width : width + HD] = jnp.zeros((1, HD), f32)
    gain_part = gain_sum[...] / gain_in[...]
    cut = D - width - HD
    for i in range(4):
        z_sum[4 + i : 5 + i, width + HD :] = gain_part[:, i * cut : (i + 1) * cut]
    first_sums = Sums(z_sum, z_sum_in, q_sum, (sum_ss, sum_rs, qsum_ss, qsum_rs), me, my, n, m)
    first_sums.start()

    lines = D // TILE
    units, strip = n // lines, piece * m

    def line(i):
        return Chain(
            lambda d: z_w.at[i, d], lambda j: z_w_up.at[i, j], lambda j: z_w_down.at[i, j],
            (w_us.at[i], w_ur.at[i], w_ds.at[i], w_dr.at[i]), my, m,
        )

    def line_turn(i, _):
        cuts = []
        for u in range(units):
            first = (i + u * lines) * strip
            if strip % HD == 0:
                first = pl.multiple_of(first, HD)
            cuts.append(normed[:, pl.ds(first, strip)])
        found = tn(jnp.concatenate(cuts, axis=1), gp[...])
        for u in range(units):
            for d in range(m):
                at = u * strip + d * piece
                z_w[i, d, u] = found[at : at + piece].astype(bf16)
        line(i).start()
        return 0

    if strip % HD == 0:
        line_turn(0, 0)
        join(0)
        lax.fori_loop(1, lines, line_turn, 0)
    else:
        for i in range(lines):
            line_turn(i, 0)
        join(0)
    ins = [line(i) for i in range(lines)]
    for i, (chain, q) in enumerate(hops):
        if 3 * i // 2 >= n:
            chain.tick(q)

    def write_down(x):
        g_down[...] = x

    def write_out(x):
        g_out[...] = x

    downs.finish(write_down)
    for j in range(2):

        def write_up(x, j=j):
            q_gu[:, j] = x.astype(bf16)

        ups[j].finish(write_up)
    q_ups = [scatter_to(q_gu, q_gu_in, k, qgu_ss, qgu_rs, me, n) for k in range(1, n)]
    for copy in q_ups:
        copy.start()
    q_gu_in[me] = q_gu[me]
    for q in range(1, m - 1):
        outs.tick(q)

    def input_gradient():
        total = part_own[chip].astype(f32)
        for k in range(1, n // 2):
            other = lax.rem(chip + k, n // 2)
            remote(chip_out.at[other], chip_in.at[other], c_ss.at[other], c_rs.at[other], "seq", 2 * other + side).wait_recv()
            total = total + chip_in[other].astype(f32)
        values = tokens[...].astype(f32)
        part, _ = norm_back(values, norm_scale(values), gain_in[...], total)
        grad_input[...] = grad_residual[...] + part

    def deliver(i):
        def write_in(x):
            for u in range(units):
                q_w[i + u * lines] = x[u].astype(bf16)

        ins[i].finish(write_in)
        for j in range(i, n, lines):

            @pl.when(me != j)
            def _():
                remote(q_w.at[j], q_w_in.at[me], qw_ss.at[j], qw_rs.at[me], "seq", j).start()

    first_sums.add()
    for i, chain in enumerate(ins):
        for q in range(1, m - 1):
            chain.tick(q)
        if i:
            deliver(i - 1)
        if i == 1:
            outs.finish(write_out)
        if i == 2:
            input_gradient()
    deliver(len(ins) - 1)
    q_w_in[me] = q_w[me]
    for chain in (downs, *ups, outs, *ins):
        chain.settle()

    def settle(j, _):
        sibling_copy(j).wait_send()

        @pl.when(chip != j)
        def _():
            owner_copy(j).wait_send()

        return 0

    lax.fori_loop(0, n // 2, settle, 0)
    first_sums.settle()
    for copy in q_ups:
        copy.wait()
    for k in range(1, n):
        peer = lax.rem(me + k, n)
        remote(q_w.at[peer], q_w_in.at[me], qw_ss.at[peer], qw_rs.at[me], "seq", peer).wait_send()
        remote(q_w.at[peer], q_w_in.at[peer], qw_ss.at[peer], qw_rs.at[peer], "seq", peer).wait_recv()


def run_back(n, m, rep, T, lengths, bias, rate, tokens, grad_residual, gain_in, gain_mid_grad, w_small, taps, gain,
             mid, cot, w_gate_up, w_down, w_out, head_rows, proj, small, mixed, states, news, invs, normed, w_in):
    rows, piece, shard = n * T, D // (n * m), FF // n
    wide = -(-(shard + HD - 1) // HD) * HD
    vm, roomy = pltpu.VMEM, rows <= 1024
    band = GROUPS * HD

    def chained(*dims, lead=()):
        return [vm((*lead, m, *dims), bf16), vm((*lead, m - 1, *dims), bf16), vm((*lead, m - 1, *dims), bf16)]

    return pl.pallas_call(
        functools.partial(back_kernel, n, m, rep, T, piece, shard, wide),
        out_shape=(
            shape((T, D), f32), shape((n, piece, band), bf16), shape((piece, D), f32), shape((n, 2, piece, shard), bf16),
            shape((shard // m, D), f32), shape((n, 8, D), f32),
        ),
        in_specs=[SMEM] * 3 + [VMEM] * 7 + [ANY] * 14,
        out_specs=[VMEM] * 6,
        scratch_shapes=[
            vm((rows, D), bf16), vm((rows, D), bf16), vm((D, wide), bf16), vm((D, wide), bf16), vm((wide, D), bf16),
            vm((HD, D), bf16), vm((rows, HD), bf16), vm((rows, band), bf16), vm((rows, HD), f32), vm((rows if roomy else T, HD), f32),
            vm((2, n, HD, HD), bf16), vm((2, NH * (rows if roomy else T), HD), bf16), vm((2, n if roomy else 1, NH * T, NH * T), bf16),
            vm((rows, D) if roomy else (1, 16, HD), bf16), vm((D, band), bf16), vm((HD, D), bf16),
            vm((rows, D), bf16), vm((rows, shard), bf16), vm((rows, shard), bf16), vm((rows, shard), bf16),
            vm((rows, band), bf16), vm((rows, HD), bf16), vm((CONV, MIXED * HD), f32), vm((rows + 8, MIXED * HD), f32),
            vm((8, MIXED * HD), f32), vm((8, HD), f32), vm((HD, HD), f32),
            *chained(n, piece, shard, lead=(2,)), *chained(shard // m, D), *chained(piece, D), *chained(n * TILE // D, piece, band, lead=(D // TILE,)),
            vm((8, D), f32), vm((m - 1, 8, D), f32), vm((1, D), f32), vm((n, 2, piece, shard), bf16), vm((n, piece, band), bf16),
            vm((n // 2, T, D), f32 if roomy else bf16), *[vm((n // 2, T, D), bf16)] * 4,
            DMA((14,)), DMA((GROUPS,)), *chain_sems(2, m - 1), *chain_sems(m - 1), *chain_sems(m - 1),
            *chain_sems(D // TILE, m - 1), DMA((m - 1,)), DMA((m - 1,)), DMA((n - 1,)), DMA((n - 1,)), DMA((n,)), DMA((n,)),
            DMA((n - 1,)), DMA((n - 1,)),
            *[DMA((n // 2,))] * 4, *gather_sems(n),
        ],
        compiler_params=pltpu.CompilerParams(vmem_limit_bytes=(60 if roomy else 63) * 1024 * 1024, collective_id=3, has_side_effects=True),
        name="backward",
    )(lengths, bias, rate, tokens, grad_residual, gain_in, gain_mid_grad, w_small, taps, gain,
      mid, cot, w_gate_up, w_down, w_out, head_rows, proj, small, mixed, states, news, invs, normed, w_in)


def output_kernel(
    n, rep, shard, result_in, grad_input_in, w_parts, out_part, gu_parts, down_part, sums,
    result, grad_input, g_in, g_out, g_gate_up, g_down, g_gain_in, g_gain_mid, g_small, g_bias, g_rate, g_taps, g_gain_head,
):
    result[...] = result_in[...]
    grad_input[...] = grad_input_in[...]
    g_out[...] = out_part[...]
    g_down[...] = down_part[...]
    for i in range(2):
        for source in range(n):
            at = i * FF + source * shard
            g_gate_up[:, at : at + shard] = gu_parts[source, i].astype(f32)
    g_gain_mid[...] = jnp.sum(sums[:, 0:1, :], axis=0)
    width = MIXED * HD
    cut = D - width - HD
    for i in range(4):
        g_gain_in[:, i * cut : (i + 1) * cut] = jnp.sum(sums[:, 4 + i : 5 + i, width + HD :], axis=0)
    gain_total = jnp.zeros((1, HD), f32)
    for h in range(H):
        found = sums[h * rep]
        part = w_parts[h * rep].astype(f32)
        for j in range(SMALL):
            g_small[j * H + h : j * H + h + 1, :] = found[1 + j : 2 + j, :]
        for i in range(MIXED):
            g_taps[:, i * D + h * HD : i * D + (h + 1) * HD] = found[4 : 4 + CONV, i * HD : (i + 1) * HD]
        for i in range(GROUPS):
            g_in[:, i * D + h * HD : i * D + (h + 1) * HD] = part[:, i * HD : (i + 1) * HD]
        gain_total = gain_total + found[4:5, width : width + HD]
        g_bias[h] = found[5, width + NH]
        g_rate[h] = found[6, width + NH]
    g_gain_head[...] = gain_total


def run_output(n, rep, *parts):
    result, grad_input, w_parts, out_part, gu_parts, down_part, sums = parts
    piece, shard = out_part.shape[0], gu_parts.shape[-1]
    return pl.pallas_call(
        functools.partial(output_kernel, n, rep, shard),
        out_shape=(
            shape(result.shape, bf16), shape(grad_input.shape, f32), shape((piece, GROUPS * D), f32), shape((piece, D), f32),
            shape((piece, 2 * FF), f32), shape(down_part.shape, f32), shape((1, D), f32), shape((1, D), f32),
            shape((SMALL * H, D), f32), shape((H,), f32), shape((H,), f32), shape((CONV, MIXED * D), f32), shape((1, HD), f32),
        ),
        in_specs=[VMEM] * 7,
        out_specs=[VMEM] * 9 + [SMEM] * 2 + [VMEM] * 2,
        compiler_params=pltpu.CompilerParams(vmem_limit_bytes=LIMIT),
        name="outputs",
    )(*parts)


def on_device(tokens, grad_out, doc_lengths, gain_in, in_weight, small_weight, gate_bias, decay_rate, conv_weight,
              gain_head, out_weight, gain_mid, gate_up_weight, down_weight):
    seq, stream = lax.axis_size("seq"), lax.axis_size("stream")
    rep = seq // H
    T = tokens.shape[1]
    gain = gain_head.reshape(1, HD)
    gain_in, gain_mid = gain_in.reshape(1, D), gain_mid.reshape(1, D)
    rows, cotangent, small_weight = tokens[0], grad_out[0], small_weight.T
    gated, normed, out_all, proj, small, mixed, states, news, invs, head_rows = run_forward(
        seq, rep, T, doc_lengths, gate_bias, decay_rate, rows, cotangent, gain_in, in_weight, small_weight, conv_weight, gain
    )
    result, grad_residual, mid_all, grad_gain_mid = run_feed(
        seq, T, rows, gated, cotangent, out_weight, gain_mid, gate_up_weight, down_weight
    )
    parts = run_back(
        seq, stream, rep, T, doc_lengths, gate_bias, decay_rate, rows, grad_residual, gain_in, grad_gain_mid, small_weight,
        conv_weight, gain, mid_all, out_all, gate_up_weight, down_weight, out_weight, head_rows, proj, small, mixed, states,
        news, invs, normed, in_weight,
    )
    result, grad_input, g_in, g_out, g_gate_up, g_down, g_gain_in, g_gain_mid, g_small, g_bias, g_rate, g_taps, g_gain_head = (
        run_output(seq, rep, result, *parts)
    )
    return (
        result[None], grad_input[None], g_gain_in.reshape(D), g_in, g_small.T, g_bias, g_rate, g_taps,
        g_gain_head.reshape(HD), g_out, g_gain_mid.reshape(D), g_gate_up, g_down,
    )


def solution(mesh):
    rows, whole, split = P("stream", "seq", None), P(), P(("seq", "stream"), None)
    return jax.shard_map(
        on_device,
        mesh=mesh,
        in_specs=(rows, rows, P("stream", None)) + (whole,) * 11,
        out_specs=(rows, rows, whole, split, whole, whole, whole, whole, whole, split, whole, split, split),
        check_vma=False,
    )
```

```python
import functools

import jax
import jax.numpy as jnp
from jax import lax
from jax.experimental import pallas as pl
from jax.experimental.pallas import tpu as pltpu
from jax.sharding import PartitionSpec as P

D = 1024
H = 8
HD = 128
FF = 2816
NH = 2
CONV = 4
GROUPS = 2 + 2 * NH
MIXED = GROUPS - 1
SMALL = NH + 1
DOCS = 8
TILE = 256
EPS = 1e-06

f32 = jnp.float32
bf16 = jnp.bfloat16
MESH = pl.DeviceIdType.MESH
DMA = pltpu.SemaphoreType.DMA
VMEM = pl.BlockSpec(memory_space=pltpu.VMEM)
SMEM = pl.BlockSpec(memory_space=pltpu.SMEM)
ANY = pl.BlockSpec(memory_space=pl.ANY)
LIMIT = 56 * 1024 * 1024
shape = jax.ShapeDtypeStruct


def dot(a, b, dims):
    if isinstance(a, tuple) and isinstance(b, tuple):
        return dot(a[0], b[0], dims) + (dot(a[0], b[1], dims) + dot(a[1], b[0], dims))
    if isinstance(a, tuple):
        return dot(a[0], b, dims) + dot(a[1], b, dims)
    if isinstance(b, tuple):
        return dot(a, b[0], dims) + dot(a, b[1], dims)
    return lax.dot_general(
        a.astype(bf16), b.astype(bf16), ((dims[:1], dims[1:]), ((), ())), preferred_element_type=f32
    )


def nn(a, b):
    return dot(a, b, (1, 0))


def nt(a, b):
    return dot(a, b, (1, 1))


def tn(a, b):
    return dot(a, b, (0, 0))


def halves(x):
    high = x.astype(bf16)
    return high, (x - high.astype(f32)).astype(bf16)


def thirds(x):
    high, low = halves(x)
    return high, low, (x - high.astype(f32) - low.astype(f32)).astype(bf16)


def keep(ref, at, x):
    ref[0, at], ref[1, at] = halves(x)


def kept(ref, at):
    return ref[0, at], ref[1, at]


def nn_exact(ones, x):
    high, low, lowest = thirds(x)
    return nn(ones, high) + (nn(ones, low) + nn(ones, lowest))


def sigmoid(x):
    return 1.0 / (1.0 + jnp.exp(-x))


def softplus(x):
    return jnp.maximum(x, 0.0) + jnp.log(1.0 + jnp.exp(-jnp.abs(x)))


def norm_scale(values):
    return lax.rsqrt(jnp.mean(values * values, axis=-1, keepdims=True) + EPS)


def norm_back(values, scale, gain, grad):
    normal = values * scale
    e = grad * gain
    back = scale * (e - normal * jnp.mean(e * normal, axis=-1, keepdims=True))
    return back, jnp.sum(grad * normal, axis=0, keepdims=True)


def iota(dims, axis):
    return lax.broadcasted_iota(jnp.int32, dims, axis)


def doc_at(starts, positions):
    total = jnp.full(positions.shape, -1, jnp.int32)
    for start in starts:
        total = total + (start <= positions).astype(jnp.int32)
    return total


def doc_starts(lengths_ref):
    starts, at = [], jnp.int32(0)
    for j in range(DOCS):
        starts.append(at)
        at = at + lengths_ref[0, j]
    return starts


def stack2(a, b):
    return jnp.concatenate([a, b], axis=0)


def beside(a, b):
    return jnp.concatenate([a, b], axis=1)


def quad(a, b, c, d):
    return stack2(beside(a, b), beside(c, d))


def rows_of(i, size):
    return pl.ds(pl.multiple_of(i * size, size), size)


def greet(axis, peers):
    barrier = pltpu.get_barrier_semaphore()
    for peer in peers:
        pl.semaphore_signal(barrier, inc=1, device_id={axis: peer}, device_id_type=MESH)
    return lambda: pl.semaphore_wait(barrier, len(peers))


def remote(src, dst, send, receive, axis, peer):
    return pltpu.make_async_remote_copy(src, dst, send, receive, device_id={axis: peer}, device_id_type=MESH)


def flipped(chip, bits, chips):
    total, place = 0, 1
    while place < chips:
        total = total + place * lax.rem(chip // place + bits // place, 2)
        place *= 2
    return total


class Gather:
    def __init__(self, n, T, src, dst, sems):
        self.n, self.T, self.src, self.dst = n, T, src, dst
        self.ss, self.rs, self.fs, self.fr = sems
        self.me = lax.axis_index("seq")
        self.chip, self.side = self.me // 2, lax.rem(self.me, 2)
        self.sib = self.me + 1 - 2 * self.side
        order = sorted(range(1, n // 2), key=lambda k: k.bit_count())
        self.early = [k for k in order if k.bit_count() == 1]
        self.late = [k for k in order if k.bit_count() > 1]

    def at(self, device):
        return self.dst.at[rows_of(device, self.T)]

    def partner(self, k):
        return 2 * flipped(self.chip, k, self.n // 2) + self.side

    def direct(self, k):
        peer = self.sib if k == 0 else self.partner(k)
        return remote(self.src, self.at(self.me), self.ss.at[k], self.rs.at[k], "seq", peer)

    def passed(self, k):
        block = self.at(self.partner(k))
        return remote(block, block, self.fs.at[k], self.fr.at[k], "seq", self.sib)

    def relay(self, k):
        top = 1 << (k.bit_length() - 1)
        for side, last in ((0, top), (1, k & -k)):

            @pl.when(self.side == side)
            def _():
                block = self.at(self.partner(k - last))
                remote(block, block, self.ss.at[k], self.rs.at[k], "seq", self.partner(last)).start()

    def start(self):
        for k in (*self.early, 0):
            self.direct(k).start()

    def pass_on(self, k):
        self.direct(k).wait_recv()
        self.passed(k).start()

    def forward(self):
        for k in self.early:
            self.pass_on(k)
        for k in self.late:
            if k.bit_count() == 2:
                self.relay(k)

    def forward_late(self):
        for k in self.late:
            if k.bit_count() > 2:
                self.relay(k)
            self.pass_on(k)

    def arrive(self):
        self.direct(0).wait_recv()
        for k in range(1, self.n // 2):
            self.passed(k).wait_recv()

    def finish(self):
        for k in range(self.n // 2):
            self.direct(k).wait_send()
            if k:
                self.passed(k).wait_send()


def gather_sems(n):
    return [DMA((n // 2,)) for _ in range(4)]


def conv_of(block, taps, docs, T):
    total = block[8:] * taps[CONV - 1 : CONV]
    for lag in range(1, CONV):
        same = (docs[0] == docs[lag]).astype(f32)
        total = total + block[8 - lag : 8 - lag + T] * (taps[CONV - 1 - lag : CONV - lag] * same)
    return total


def chunk_gates(logits, bias, rate, starts, first, T):
    lane = iota((T, HD), 1)
    shifted = logits + bias
    gate = -rate * softplus(shifted)
    place_i, place_j = iota((T, T), 0), iota((T, T), 1)
    lower = place_j <= place_i
    cumul = nn_exact(lower.astype(bf16), jnp.where(lane == NH, gate, 0.0))
    beta = 2.0 * sigmoid(logits)
    b0, b1 = beta[:, 0:1], beta[:, 1:2]
    g = cumul[:, NH : NH + 1]
    g_row = jnp.transpose(cumul)[NH : NH + 1, :]
    g_last = cumul[T - 1 : T, NH : NH + 1]
    position = first + iota((T, 1), 0)
    docs = [doc_at(starts, position - lag) for lag in range(CONV)]
    doc = docs[0]
    doc_row = doc_at(starts, first + iota((1, T), 1))
    doc_before = doc_at(starts, jnp.full((1, 1), first - 1, jnp.int32))
    doc_last = doc_at(starts, jnp.full((1, 1), first + (T - 1), jnp.int32))
    joined = lower & (doc == doc_row)
    decay = jnp.where(joined, jnp.exp(jnp.where(joined, g - g_row, 0.0)), 0.0)
    strict = jnp.where(place_i == place_j, 0.0, decay)
    from_start = jnp.exp(g) * (doc == doc_before).astype(f32)
    to_end = jnp.exp(jnp.minimum(g_last - g, 0.0)) * (doc == doc_last).astype(f32)
    whole = jnp.exp(g_last) * (doc_last == doc_before).astype(f32)
    return dict(
        shifted=shifted, beta=beta, b=stack2(b0, b1), docs=docs, decay=decay,
        decays=quad(strict, strict, decay, strict), hd=from_start, hd2=stack2(from_start, from_start),
        to_end=stack2(to_end, to_end), whole=whole,
    )


def key_scale(raw):
    return lax.rsqrt(jnp.sum(raw * raw, axis=-1, keepdims=True) + EPS)


def chunk_inputs(block, taps, docs, T):
    conv = conv_of(block, taps, docs, T)
    sig = sigmoid(conv)
    active = conv * sig
    cut = [active[:, i * HD : (i + 1) * HD] for i in range(MIXED)]
    scales = (key_scale(cut[1]), key_scale(cut[2]))
    keys = stack2(cut[1] * scales[0], cut[2] * scales[1])
    values = stack2(cut[3], cut[4])
    return conv, sig, cut[0], keys, values, stack2(*scales)


def inverses(lowers, T):
    size = NH * T
    row, col = iota((size, size), 0), iota((size, size), 1)
    differ = (row & (T - 1)) ^ (col & (T - 1))
    eye = (row == col).astype(f32)
    found = [jnp.where(row == col, 1.0, jnp.where(differ == 0, -a, 0.0)) for a in lowers]
    step = 1
    while step < T:
        level = (differ >= step) & (differ < 2 * step)
        parts = [nn(jnp.where(level, a, 0.0), x) for a, x in zip(lowers, found)]
        found = [x - nn(x, part) for x, part in zip(found, parts)]
        step *= 2
    a_cut = [halves(a) for a in lowers]
    x_cut = [halves(x) for x in found]
    errors = [
        eye - x - (nn(a[0], xc[0]) + (nn(a[0], xc[1]) + nn(a[1], xc[0])))
        for a, x, xc in zip(a_cut, found, x_cut)
    ]
    return [x + nn(xc[0], e) for x, xc, e in zip(found, x_cut, errors)]


def head_gate(mixed, raw):
    scale = norm_scale(mixed)
    return mixed * scale, scale, sigmoid(raw)


def head_taps(taps_ref, head):
    cuts = [taps_ref[:, pl.ds(pl.multiple_of(i * D + head * HD, HD), HD)] for i in range(MIXED)]
    return jnp.concatenate(cuts, axis=1)


def intra_turn(T, starts, bias, rate, taps, small, block_of, invs, ubuf, wbuf, qbuf, pbuf, dbuf, gates, chunks, midway):
    held, lowers = [], []
    for c in chunks:
        first = pl.multiple_of(c * T, T)
        gate = chunk_gates(small[pl.ds(first, T), :], bias, rate, starts, first, T)
        conv, sig, query, keys, values, scales = chunk_inputs(block_of(c), taps, gate["docs"], T)
        key_pair = halves(keys)
        lowers.append(gate["b"] * (nt(key_pair, key_pair) * gate["decays"]))
        held.append((c, gate, query, keys, key_pair, values))
    found = inverses(lowers, T)
    midway()
    for (c, gate, query, keys, key_pair, values), inverse in zip(held, found):
        at, two = rows_of(c, T), rows_of(c, NH * T)
        pair = halves(inverse)
        invs[0, c], invs[1, c] = pair
        both = nn(pair, halves(gate["b"] * beside(values, gate["hd2"] * keys)))
        ubuf[two, :] = both[:, :HD]
        keep(wbuf, two, both[:, HD:])
        query_pair = halves(query)
        qbuf[0, at], qbuf[1, at] = query_pair
        keep(pbuf, at, nt(query_pair, key_pair) * beside(gate["decay"], gate["decay"]))
        keep(dbuf, two, gate["to_end"] * keys)
        gates[at, :] = jnp.where(iota((T, HD), 1) == 0, gate["hd"], gate["whole"])


def across_turn(T, gain, proj, mixed_out, states, news, head_rows, ubuf, wbuf, qbuf, pbuf, dbuf, gates, done, c, state):
    at, two = rows_of(c, T), rows_of(c, NH * T)
    state_pair = halves(state)
    states[0, c], states[1, c] = state_pair
    new = ubuf[two, :] - nn(kept(wbuf, two), state_pair)
    new_pair = halves(new)
    news[0, two], news[1, two] = new_pair
    gate = gates[at, :]
    mixed = gate[:, 0:1] * nn(kept(qbuf, at), state_pair) + nn(kept(pbuf, at), new_pair)
    mixed_out[at, :] = mixed
    raw = proj[at, MIXED * HD :].astype(f32)
    normal, _, sig = head_gate(mixed, raw)
    head_rows[at, :] = ((normal * gain[...]) * (raw * sig)).astype(bf16)
    done(c)
    return gate[0:1, 1:2] * state + tn(kept(dbuf, two), new_pair)


def widened(w_wide, parts):
    w_wide[...] = jnp.zeros((HD, D), bf16)
    for i, part in enumerate(parts):
        w_wide[32 * i : 32 * i + SMALL * H, :] = part


def forward_kernel(
    n, rep, T, lengths, bias_ref, rate_ref, tokens, cotangent, gain_in, w_in, w_small, taps_ref, gain,
    gated, normed_out, out_all, proj_out, small_out, mixed_out, states, news, invs_out, head_rows,
    normed, proj, small, invs, own, tails, w_head, w_wide, tail_rows, xbuf, ubuf, wbuf, qbuf, pbuf, dbuf, gates,
    w_sems, own_sems, o_sems, a_ss, a_rs, t_ss, t_rs, *sems,
):
    me = lax.axis_index("seq")
    head = me // rep
    chips = n // 2
    wait_for_all = greet("seq", [lax.rem(me + k, n) for k in range(1, n)])
    width = MIXED * HD
    loads = [
        pltpu.make_async_copy(
            w_in.at[:, pl.ds(pl.multiple_of(i * D + head * HD, HD), HD)], w_head.at[:, i * HD : (i + 1) * HD], w_sems.at[i]
        )
        for i in range(GROUPS)
    ]
    for load in loads:
        load.start()
    values = tokens[...].astype(f32)
    own[...] = (values * norm_scale(values) * gain_in[...]).astype(bf16)
    local = pltpu.make_async_copy(own, normed.at[rows_of(me, T)], own_sems.at[0])
    local.start()
    wait_for_all()
    first_gather = Gather(n, T, own, normed, sems[:4])
    second_gather = Gather(n, T, cotangent, out_all, sems[4:8])
    keep_out = pltpu.make_async_copy(cotangent, out_all.at[rows_of(me, T)], own_sems.at[2])
    keep_out.start()
    chip, side = first_gather.chip, first_gather.side
    last = own.at[T - 16 : T]

    def tail_copy(k):
        return remote(last, tails.at[chip], t_ss.at[k], t_rs.at[chip], "seq", lax.rem(me + k, n))

    mine = pltpu.make_async_copy(last, tails.at[chip], own_sems.at[1])
    early, late = first_gather.early, first_gather.late

    @pl.when(side == 1)
    def _():
        for k in range(1, n):
            tail_copy(k).start()
        mine.start()

    for k in (0, *early):
        first_gather.direct(k).start()

    starts = doc_starts(lengths)
    bias, rate = bias_ref[head], rate_ref[head]
    taps = head_taps(taps_ref, head)
    widened(w_wide, thirds(jnp.where((iota((SMALL * H, D), 0) & (H - 1)) == head, w_small[...], 0.0)))
    group, lane = iota((HD, HD), 0), iota((HD, HD), 1)
    picks = (((group & 31) >> 3) == lane) & (group < 96) & (lane < SMALL)
    picks = picks.astype(bf16)
    for load in loads:
        load.wait()
    local.wait()

    @pl.when(side == 1)
    def _():
        mine.wait()
        for k in range(1, n):
            tail_copy(k).wait_send()

    for j in range(chips):

        @pl.when(me != 2 * j + 1)
        def _():
            remote(last, tails.at[j], t_ss.at[0], t_rs.at[j], "seq", lax.rem(me + 1, n)).wait_recv()

    found = nn(tails[...].reshape(chips * 16, D), w_head[...]).astype(bf16).astype(f32)
    tail_rows[...] = found[:, :width]
    size = T + 8

    def block_of(c):
        return xbuf[pl.ds(pl.multiple_of(c * size, 8), size), :]

    def project(pair):
        at = rows_of(pair, 2 * T)
        block = normed[at, :]
        result = nn(block, w_head[...]).astype(bf16)
        proj[at, :] = result
        raw = thirds(nt(block, w_wide[...]))
        small[at, :] = nn(raw[0], picks) + (nn(raw[1], picks) + nn(raw[2], picks))
        mixing = result[:, :width].astype(f32)
        before = lax.rem(pair + chips - 1, chips)
        halo = tail_rows[pl.ds(pl.multiple_of(before * 16 + 8, 8), 8), :]
        base = pl.multiple_of(pair * (2 * size), 8)
        xbuf[pl.ds(base, 8), :] = jnp.where(pair > 0, halo, 0.0)
        xbuf[pl.ds(pl.multiple_of(base + 8, 8), T), :] = mixing[:T]
        xbuf[pl.ds(pl.multiple_of(base + size, 8), T + 8), :] = mixing[T - 8 :]

    first_gather.direct(0).wait_recv()
    groups = [(0,)] + [(*ks[i : i + 2],) for ks in (early, late) for i in range(0, len(ks), 2)]
    to_late = (len(early) + 1) // 2

    def midway(g):
        if g == 0:
            first_gather.forward()
        if g == to_late:
            first_gather.forward_late()
            second_gather.start()
        if g == len(groups) - 1:
            second_gather.forward()

    for g, group in enumerate(groups):
        for k in group:
            if k:
                first_gather.passed(k).wait_recv()
        pairs = [flipped(chip, k, chips) for k in group]
        for pair in pairs:
            project(pair)
        intra_turn(
            T, starts, bias, rate, taps, small, block_of, invs, ubuf, wbuf, qbuf, pbuf, dbuf, gates,
            [2 * pair + i for pair in pairs for i in range(2)], functools.partial(midway, g),
        )

    first_gather.finish()
    stores = [
        pltpu.make_async_copy(a, b, o_sems.at[i])
        for i, (a, b) in enumerate(((normed, normed_out), (proj, proj_out), (small, small_out), (invs, invs_out)))
    ]
    for store in stores:
        store.start()
    column = pl.ds(pl.multiple_of(head * HD, HD), HD)

    def row_copy(c):
        return remote(head_rows.at[rows_of(c, T)], gated.at[:, column], a_ss.at[c], a_rs.at[head], "seq", c)

    def send_rows(c):
        @pl.when((c != me) & (lax.rem(me, rep) == 0))
        def _():
            row_copy(c).start()

    across = functools.partial(
        across_turn, T, gain, proj, mixed_out, states, news, head_rows, ubuf, wbuf, qbuf, pbuf, dbuf, gates, send_rows
    )
    lax.fori_loop(0, n, across, jnp.zeros((HD, HD), f32))

    @pl.when(lax.rem(me, rep) == 0)
    def _():
        kept_rows = pltpu.make_async_copy(head_rows.at[rows_of(me, T)], gated.at[:, column], own_sems.at[0])
        kept_rows.start()
        kept_rows.wait()

    keep_out.wait()
    second_gather.forward_late()

    def settle(k, _):
        peer = lax.rem(me + k, n)

        @pl.when(lax.rem(me, rep) == 0)
        def _():
            row_copy(peer).wait_send()

        @pl.when(lax.rem(peer, rep) == 0)
        def _():
            source = peer // rep
            remote(
                head_rows.at[rows_of(me, T)], gated.at[:, pl.ds(pl.multiple_of(source * HD, HD), HD)],
                a_ss.at[peer], a_rs.at[source], "seq", peer,
            ).wait_recv()

        return 0

    lax.fori_loop(1, n, settle, 0)
    second_gather.arrive()
    second_gather.finish()
    for store in stores:
        store.wait()


def forward_scratch(n, T):
    rows = n * T
    return [
        pltpu.VMEM((rows + 8 * n, MIXED * HD), f32), pltpu.VMEM((NH * rows, HD), f32),
        pltpu.VMEM((2, NH * rows, HD), bf16), pltpu.VMEM((2, rows, HD), bf16), pltpu.VMEM((2, rows, NH * T), bf16),
        pltpu.VMEM((2, NH * rows, HD), bf16), pltpu.VMEM((rows, HD), f32),
    ]


def run_forward(n, rep, T, lengths, bias, rate, tokens, cotangent, gain_in, w_in, w_small, taps, gain):
    rows = n * T
    return pl.pallas_call(
        functools.partial(forward_kernel, n, rep, T),
        out_shape=(
            shape((T, D), bf16), shape((rows, D), bf16), shape((rows, D), bf16), shape((rows, GROUPS * HD), bf16),
            shape((rows, HD), f32), shape((rows, HD), f32), shape((2, n, HD, HD), bf16), shape((2, NH * rows, HD), bf16),
            shape((2, n, NH * T, NH * T), bf16), shape((rows, HD), bf16),
        ),
        in_specs=[SMEM] * 3 + [VMEM, VMEM, VMEM, ANY, VMEM, VMEM, VMEM],
        out_specs=[VMEM, ANY, ANY, ANY, ANY, VMEM, VMEM, VMEM, ANY, VMEM],
        scratch_shapes=[
            pltpu.VMEM((rows, D), bf16), pltpu.VMEM((rows, GROUPS * HD), bf16), pltpu.VMEM((rows, HD), f32),
            pltpu.VMEM((2, n, NH * T, NH * T), bf16),
            pltpu.VMEM((T, D), bf16), pltpu.VMEM((n // 2, 16, D), bf16), pltpu.VMEM((D, GROUPS * HD), bf16),
            pltpu.VMEM((HD, D), bf16), pltpu.VMEM((n * 8, MIXED * HD), f32),
            *forward_scratch(n, T),
            DMA((GROUPS,)), DMA((3,)), DMA((4,)), DMA((n,)), DMA((H,)), DMA((n,)), DMA((n // 2,)), *gather_sems(n), *gather_sems(n),
        ],
        compiler_params=pltpu.CompilerParams(vmem_limit_bytes=LIMIT, collective_id=1, has_side_effects=True),
        name="mixer_forward",
    )(lengths, bias, rate, tokens, cotangent, gain_in, w_in, w_small, taps, gain)


def feed_kernel(
    n, T, steps, tokens, gated, cotangent, w_out, gain_mid, w_gate, w_up, w_down,
    result, grad_residual, mid_all, gain_grad, residual, middle, total, grad_mid, own_sem, *sems,
):
    step = pl.program_id(0)
    me = lax.axis_index("seq")
    gather = Gather(n, T, middle, mid_all, sems)
    local = pltpu.make_async_copy(middle, mid_all.at[rows_of(me, T)], own_sem)

    @pl.when(step == 0)
    def _():
        peers = [gather.sib] + [gather.partner(k) for k in range(1, n // 2)]
        wait_for_all = greet("seq", peers)
        found = tokens[...].astype(f32) + nn(gated[...], w_out[...])
        residual[...] = found
        middle[...] = (found * norm_scale(found) * gain_mid[...]).astype(bf16)
        total[...] = found
        grad_mid[...] = jnp.zeros((T, D), f32)
        wait_for_all()
        gather.start()
        local.start()

    gate, up = nn(middle[...], w_gate[...]), nn(middle[...], w_up[...])
    sig = sigmoid(gate)
    silu = gate * sig
    hidden = (silu * up).astype(bf16)
    total[...] += nn(hidden, w_down[...])
    grad_hidden = nt(cotangent[...], w_down[...])
    grad_gate = (grad_hidden * up * (sig * (1.0 + gate * (1.0 - sig)))).astype(bf16)
    grad_up = (grad_hidden * silu).astype(bf16)
    grad_mid[...] += nt(grad_gate, w_gate[...]) + nt(grad_up, w_up[...])

    for at, what in ((5, gather.forward), (8, gather.forward_late)):

        @pl.when(step == at)
        def _():
            what()

    @pl.when(step == steps - 1)
    def _():
        result[...] = total[...].astype(bf16)
        values = residual[...]
        back, gain_part = norm_back(values, norm_scale(values), gain_mid[...], grad_mid[...])
        gain_grad[...] = gain_part
        grad_residual[...] = cotangent[...].astype(f32) + back
        gather.arrive()
        gather.finish()
        local.wait()


def run_feed(n, T, tokens, gated, cotangent, w_out, gain_mid, w_gate_up, w_down):
    steps = FF // TILE
    fixed = lambda *dims: pl.BlockSpec(dims, lambda i: (0, 0))
    return pl.pallas_call(
        functools.partial(feed_kernel, n, T, steps),
        grid=(steps,),
        out_shape=(shape((T, D), bf16), shape((T, D), f32), shape((n * T, D), bf16), shape((1, D), f32)),
        in_specs=[
            fixed(T, D), fixed(T, D), fixed(T, D), fixed(D, D), fixed(1, D),
            pl.BlockSpec((D, TILE), lambda i: (0, i)), pl.BlockSpec((D, TILE), lambda i: (0, i + FF // TILE)),
            pl.BlockSpec((TILE, D), lambda i: (i, 0)),
        ],
        out_specs=[fixed(T, D), fixed(T, D), ANY, fixed(1, D)],
        scratch_shapes=[
            pltpu.VMEM((T, D), f32), pltpu.VMEM((T, D), bf16), pltpu.VMEM((T, D), f32), pltpu.VMEM((T, D), f32),
            DMA, *gather_sems(n),
        ],
        compiler_params=pltpu.CompilerParams(vmem_limit_bytes=LIMIT, collective_id=2, has_side_effects=True),
        name="feed_forward",
    )(tokens, gated, cotangent, w_out, gain_mid, w_gate_up, w_gate_up, w_down)


def backward_turn(
    n, T, head, starts, bias, rate, taps, gain, incoming_of, proj, small, states, fetch,
    gp, grad_small, gconv_w, xbuf, halo, gates_sum, grad_state, done, k, _,
):
    width = MIXED * HD
    lane = iota((T, HD), 1)
    place_i, place_j = iota((T, T), 0), iota((T, T), 1)
    upper = (place_j >= place_i).astype(bf16)
    under = place_j < place_i
    c = n - 1 - k
    first = pl.multiple_of(c * T, T)
    at, two = rows_of(c, T), rows_of(c, NH * T)
    gate = chunk_gates(small[at, :], bias, rate, starts, first, T)
    block = xbuf[pl.ds(first, T + 8), :]
    conv, sig, query, keys, values, scales = chunk_inputs(block, taps, gate["docs"], T)
    key_pair, query_pair = halves(keys), halves(query)
    b, hd, hd2, to_end = gate["b"], gate["hd"], gate["hd2"], gate["to_end"]
    decay2 = beside(gate["decay"], gate["decay"])
    pairs = nt(key_pair, key_pair) * gate["decays"]
    scores = nt(query_pair, key_pair) * decay2
    state = (states[0, c], states[1, c])
    state_grad = grad_state[...]
    new, inverse, mixed = fetch(c)
    raw = proj[at, width:].astype(f32)
    normal, scale, zsig = head_gate(mixed, raw)
    incoming = incoming_of(at)
    passed = incoming * (raw * zsig)
    gates_sum[0:1, :] += jnp.sum(passed * normal, axis=0, keepdims=True)
    grad_z = incoming * (normal * gain[...]) * (zsig * (1.0 + raw * (1.0 - zsig)))
    e = passed * gain[...]
    grad_mixed = scale * (e - normal * jnp.mean(e * normal, axis=-1, keepdims=True))
    gm = halves(grad_mixed)
    ended = halves(to_end * keys)
    grad_pair = halves(state_grad)
    grad_new = tn(halves(scores), gm) + nn(ended, grad_pair)
    grad_right = tn(inverse, halves(grad_new))
    moved = b * grad_right
    grad_state[...] = gate["whole"] * state_grad + tn(halves(hd * query), gm) - tn(halves(hd2 * keys), halves(moved))
    grad_ended = nt(new, grad_pair)
    grad_scores = nt(gm, new)
    grad_lower = jnp.where(gate["decays"] != 0.0, -nt(halves(grad_right), new), 0.0)
    from_grad = nt(gm, state)
    scored = grad_scores * decay2
    grad_query = hd * from_grad + nn(scored, key_pair[0])
    paired = (b * grad_lower) * gate["decays"]
    keyed = nn(key_pair, state)
    grad_keys = (
        tn(scored, query_pair[0]) + to_end * grad_ended - hd2 * nt(moved, state[0])
        + nn(paired, key_pair[0]) + tn(paired, key_pair[0])
    )
    lower_pairs = grad_lower * pairs
    grad_b = jnp.sum(grad_right * (values - hd2 * keyed), axis=-1, keepdims=True) + jnp.sum(
        lower_pairs, axis=-1, keepdims=True
    )
    four = b * lower_pairs
    both = grad_scores * scores
    joint = (four[:T, :T] + four[:T, T:]) + (four[T:, :T] + four[T:, T:]) + (both[:, :T] + both[:, T:])
    crossing = jnp.sum(jnp.where(under, nn_exact(upper, joint), 0.0), axis=-1, keepdims=True)
    start_part = -hd2 * jnp.sum(moved * keyed, axis=-1, keepdims=True)
    start_part = start_part[:T] + start_part[T:] + hd * jnp.sum(query * from_grad, axis=-1, keepdims=True)
    end_part = to_end * jnp.sum(grad_ended * keys, axis=-1, keepdims=True)
    end_part = end_part[:T] + end_part[T:]
    sums_in = jnp.where(lane == 0, start_part, jnp.where(lane == 1, end_part, 0.0))
    after = nn_exact(upper, sums_in)
    before = nn_exact(under.astype(bf16), sums_in)
    whole_part = gate["whole"] * jnp.sum(state_grad * (state[0].astype(f32) + state[1].astype(f32)), keepdims=True)
    grad_gate = crossing + after[:, 0:1] + before[:, 1:2] + whole_part
    shifted = gate["shifted"]
    grad_beta = [grad_b[i * T : (i + 1) * T] * (gate["beta"][:, i : i + 1] * (1.0 - 0.5 * gate["beta"][:, i : i + 1])) for i in range(NH)]
    grad_decay = (-grad_gate * rate * sigmoid(shifted))[:, NH : NH + 1]
    which = lane >> 3
    logit = jnp.where(which == 0, grad_beta[0], jnp.where(which == 1, grad_beta[1], grad_decay))
    grad_logits = jnp.where((lane < SMALL * H) & ((lane & (H - 1)) == head), logit, 0.0)
    gates_sum[1:2, :] += jnp.sum(jnp.where(lane == NH, grad_decay, 0.0), axis=0, keepdims=True)
    gates_sum[2:3, :] += jnp.sum(jnp.where(lane == NH, grad_gate * -softplus(shifted), 0.0), axis=0, keepdims=True)
    high = grad_logits.astype(bf16).astype(f32)
    grad_small[at, :] = (
        high + pltpu.roll(grad_logits - high, 32, 1) + pltpu.roll(high, 64, 1)
    ).astype(bf16)
    projected_out = jnp.sum(keys * grad_keys, axis=-1, keepdims=True)
    grad_raw = (grad_keys - keys * projected_out) * scales
    slope = sig * (1.0 + conv * (1.0 - sig))
    grad_active = jnp.concatenate([grad_query, grad_raw[:T], grad_raw[T:], moved[:T], moved[T:]], axis=1)
    grad_conv = grad_active * slope
    after_block = stack2(grad_conv, halo[...])
    halo[...] = grad_conv[:8]
    position = first + iota((T, 1), 0)
    total = grad_conv * taps[CONV - 1 : CONV]
    taps_grads = [None] * CONV
    taps_grads[CONV - 1] = jnp.sum(grad_conv * block[8:], axis=0, keepdims=True)
    for lag in range(1, CONV):
        same = (doc_at(starts, position + lag) == gate["docs"][0]).astype(f32)
        total = total + after_block[lag : lag + T] * (taps[CONV - 1 - lag : CONV - lag] * same)
        same = (gate["docs"][lag] == gate["docs"][0]).astype(f32)
        taps_grads[CONV - 1 - lag] = jnp.sum(
            grad_conv * (block[8 - lag : 8 - lag + T] * same), axis=0, keepdims=True
        )
    everything = beside(total, grad_z).astype(bf16)
    gp[at, :] = everything
    gconv_w[...] += jnp.concatenate(taps_grads, axis=0)
    done(k)
    return 0


class Chain:
    def __init__(self, own, up_in, down_in, sems, my, m):
        self.own, self.up_in, self.down_in = own, up_in, down_in
        self.us, self.ur, self.ds, self.dr = sems
        self.my, self.m = my, m

    def up(self, q):
        slot = q - self.my
        return self.own(self.my + self.m - 1 - q), self.up_in(slot), slot, self.my + 1, self.us, self.ur

    def down(self, q):
        slot = q - (self.m - 1 - self.my)
        return self.own(self.my - (self.m - 1 - q)), self.down_in(slot), slot, self.my - 1, self.ds, self.dr

    def copy(self, hop):
        own, arrived, slot, peer, send, receive = hop
        return remote(own, arrived, send.at[slot], receive.at[slot], "stream", peer)

    def start(self):
        for q in range(self.m - 1):

            @pl.when(self.my == 0)
            def _():
                self.copy(self.up(q)).start()

            @pl.when(self.my == self.m - 1)
            def _():
                self.copy(self.down(q)).start()

    def tick(self, q):
        for inner, way in (
            ((self.my > 0) & (self.my <= q), self.up),
            ((self.my < self.m - 1) & (self.my >= self.m - 1 - q), self.down),
        ):

            @pl.when(inner)
            def _():
                hop = way(q)
                self.copy(hop).wait_recv()
                own, arrived = hop[:2]

                def add(i, _):
                    own[i] = (own[i].astype(f32) + arrived[i].astype(f32)).astype(bf16)
                    return 0

                if len(own.shape) == 3 and own.shape[0] > 2:
                    lax.fori_loop(0, own.shape[0], add, 0)
                else:
                    own[...] = (own[...].astype(f32) + arrived[...].astype(f32)).astype(bf16)
                self.copy(hop).start()

    def finish(self, write):
        last = self.m - 1

        @pl.when(self.my > 0)
        def _():
            slot = last - self.my
            remote(self.own(self.my), self.up_in(slot), self.us.at[slot], self.ur.at[slot], "stream", self.my - 1).wait_recv()

        @pl.when(self.my < last)
        def _():
            slot = self.my
            remote(self.own(self.my), self.down_in(slot), self.ds.at[slot], self.dr.at[slot], "stream", self.my + 1).wait_recv()

        from_below, from_above = self.up_in(lax.rem(last - self.my, last)), self.down_in(lax.rem(self.my, last))
        found = self.own(self.my)[...].astype(f32) + jnp.where(self.my > 0, from_below[...].astype(f32), 0.0)
        write(found + jnp.where(self.my < last, from_above[...].astype(f32), 0.0))

    def settle(self):
        for q in range(self.m - 1):

            @pl.when(self.my <= q)
            def _():
                self.copy(self.up(q)).wait_send()

            @pl.when(self.my >= self.m - 1 - q)
            def _():
                self.copy(self.down(q)).wait_send()


class Sums:
    def __init__(self, own, arrived, every, sems, me, my, n, m):
        self.own, self.arrived, self.every = own, arrived, every
        self.zs, self.zr, self.ss, self.rs = sems
        self.me, self.my, self.n, self.m = me, my, n, m

    def across(self, k):
        peer = lax.rem(self.my + k, self.m)
        return remote(self.own, self.arrived.at[k - 1], self.zs.at[k - 1], self.zr.at[k - 1], "stream", peer)

    def along(self, k):
        block = self.every.at[self.me]
        return remote(block, block, self.ss.at[k - 1], self.rs.at[k - 1], "seq", lax.rem(self.me + k, self.n))

    def start(self):
        for k in range(1, self.m):
            self.across(k).start()

    def add(self):
        total = self.own[...]
        for k in range(1, self.m):
            self.across(k).wait()
            total = total + self.arrived[k - 1]
        self.every[self.me] = total
        for k in range(1, self.n):
            self.along(k).start()

    def settle(self):
        for k in range(1, self.n):
            self.along(k).wait()


def chain_sems(*lead):
    return [DMA(lead) for _ in range(4)]


def scatter_to(own, arrived, k, send, receive, me, size):
    peer = lax.rem(me + k, size)
    return remote(own.at[peer], arrived.at[me], send.at[k - 1], receive.at[k - 1], "seq", peer)


def back_kernel(
    n, m, rep, T, piece, shard, wide,
    lengths, bias_ref, rate_ref, tokens, grad_residual, gain_in, gain_mid_grad, w_small, taps_ref, gain,
    mid_any, out_any, w_gate_up, w_down, w_out, rows_any, proj_any, small_any, mixed_any, states_any, news_any, invs_any,
    normed_any, w_in_any,
    grad_input, q_w_in, g_out, q_gu_in, g_down, q_sum,
    mid, cot, w_gate, w_up, w_hid, w_head, head_rows, proj, small, mixed, states, news, invs, normed, w_in, w_wide,
    low_all, hidden, grad_gate, grad_up, gp, grad_small, gconv_w, xbuf, halo, gates_sum, grad_state,
    z_gu, z_gu_up, z_gu_down, z_down, z_down_up, z_down_down, z_out, z_out_up, z_out_down, z_w, z_w_up, z_w_down,
    z_sum, z_sum_in, gain_sum, q_gu, q_w, part_own, part_out, part_in, chip_out, chip_in,
    l_sems, i_sems, gu_us, gu_ur, gu_ds, gu_dr, dn_us, dn_ur, dn_ds, dn_dr, ou_us, ou_ur, ou_ds, ou_dr, w_us, w_ur, w_ds, w_dr,
    sum_ss, sum_rs, qgu_ss, qgu_rs, qw_ss, qw_rs, qsum_ss, qsum_rs, p_ss, p_rs, c_ss, c_rs, *sems,
):
    me, my = lax.axis_index("seq"), lax.axis_index("stream")
    head, chip, side = me // rep, me // 2, lax.rem(me, 2)
    sib = me + 1 - 2 * side
    barrier = pltpu.get_barrier_semaphore()
    for k in range(1, n):
        pl.semaphore_signal(barrier, inc=1, device_id={"seq": lax.rem(me + k, n)}, device_id_type=MESH)
    for k in range(1, m):
        pl.semaphore_signal(barrier, inc=1, device_id={"stream": lax.rem(my + k, m)}, device_id_type=MESH)
    first_unit = me * shard
    base = (first_unit // HD - me // (n - 1)) * HD
    offset = first_unit - base
    sources = [
        mid_any, out_any, w_gate_up.at[:, pl.ds(pl.multiple_of(base, HD), wide)],
        w_gate_up.at[:, pl.ds(pl.multiple_of(FF + base, HD), wide)], w_down.at[pl.ds(pl.multiple_of(base, HD), wide)],
        w_out.at[rows_of(head, HD)], rows_any, proj_any, small_any, mixed_any, states_any, news_any, invs_any, normed_any,
    ]
    places = [mid, cot, w_gate, w_up, w_hid, w_head, head_rows, proj, small, mixed, states, news, invs, normed]
    roomy = len(normed.shape) == 2
    loads = [pltpu.make_async_copy(a, b, l_sems.at[i]) for i, (a, b) in enumerate(zip(sources, places)) if i not in (9, 11, 12, 13) or roomy]
    for i in range(GROUPS):
        column = pl.ds(pl.multiple_of(i * D + head * HD, HD), HD)
        loads.append(pltpu.make_async_copy(w_in_any.at[:, column], w_in.at[:, i * HD : (i + 1) * HD], i_sems.at[i]))
    for load in loads[:5]:
        load.start()
    low_all[rows_of(me, T), :] = grad_residual[...].astype(bf16)
    pl.semaphore_wait(barrier, n + m - 2)
    gather = Gather(n, T, low_all.at[rows_of(me, T)], low_all, sems)
    gather.start()

    for load in loads[:5]:
        load.wait()
    for load in loads[5:]:
        load.start()

    def feed_turn(i, _):
        at = rows_of(i, TILE)
        block = mid[at, :]
        gate, up = nn(block, w_gate[...]), nn(block, w_up[...])
        sig = sigmoid(gate)
        silu = gate * sig
        grad_hidden = nt(cot[at, :], w_hid[...])
        own = lambda x: pltpu.roll(x, wide - offset, 1)[:, :shard].astype(bf16)
        hidden[at, :] = own(silu * up)
        grad_gate[at, :] = own(grad_hidden * up * (sig * (1.0 + gate * (1.0 - sig))))
        grad_up[at, :] = own(grad_hidden * silu)
        return 0

    lax.fori_loop(0, n * T // TILE, feed_turn, 0)
    downs = Chain(lambda d: z_down.at[d], lambda i: z_down_up.at[i], lambda i: z_down_down.at[i], (dn_us, dn_ur, dn_ds, dn_dr), my, m)
    ups = [
        Chain(
            lambda d, j=j: z_gu.at[j, d], lambda i, j=j: z_gu_up.at[j, i], lambda i, j=j: z_gu_down.at[j, i],
            (gu_us.at[j], gu_ur.at[j], gu_ds.at[j], gu_dr.at[j]), my, m,
        )
        for j in range(2)
    ]
    part = tn(hidden[...], cot[...])
    for d in range(m):
        z_down[d] = part[d * (shard // m) : (d + 1) * (shard // m)].astype(bf16)
    downs.start()
    gather.forward()
    for j, grads in enumerate((grad_gate, grad_up)):
        if j:
            gather.forward_late()

        def strip_turn(t, _, j=j, grads=grads):
            found = tn(mid[:, rows_of(t, TILE)], grads[...])
            for i in range(TILE // piece):
                z_gu[j, i % m, t * (TILE // piece // m) + i // m] = found[i * piece : (i + 1) * piece].astype(bf16)
            return 0

        lax.fori_loop(0, D // TILE, strip_turn, 0)
        ups[j].start()
    w_high, w_low = halves(w_small[...])
    widened(w_wide, (w_high, w_high, w_low))
    gather.arrive()
    gather.finish()
    for load in loads[5:]:
        load.wait()
    rows = tn(head_rows[...], low_all[...])
    for share in range(rep):

        @pl.when(lax.rem(me, rep) == share)
        def _():
            for d in range(m):
                at = share * (HD // rep) + d * piece
                z_out[d] = rows[at : at + piece].astype(bf16)

    outs = Chain(lambda d: z_out.at[d], lambda i: z_out_up.at[i], lambda i: z_out_down.at[i], (ou_us, ou_ur, ou_ds, ou_dr), my, m)
    outs.start()
    if not roomy:
        normed = mid
        late = pltpu.make_async_copy(normed_any, normed, l_sems.at[13])
        late.start()
        late.wait()

    width = MIXED * HD
    starts = doc_starts(lengths)
    bias, rate = bias_ref[head], rate_ref[head]
    taps = head_taps(taps_ref, head)
    xbuf[0:8, :] = jnp.zeros((8, width), f32)
    halo[...] = jnp.zeros((8, width), f32)
    gconv_w[...] = jnp.zeros(gconv_w.shape, f32)
    gates_sum[...] = jnp.zeros((8, HD), f32)
    grad_state[...] = jnp.zeros((HD, HD), f32)

    def fill(c, _):
        xbuf[pl.ds(pl.multiple_of(8 + c * T, 8), T), :] = proj[rows_of(c, T), :width].astype(f32)
        return 0

    lax.fori_loop(0, n, fill, 0)

    def normed_rows(at):
        if roomy:
            return normed[at, :].astype(f32)
        return mid[at, :].astype(f32)

    gain_sum[...] = jnp.zeros((1, D), f32)

    def sibling_copy(j):
        return remote(part_out.at[j], part_in.at[j], p_ss.at[j], p_rs.at[j], "seq", sib)

    def owner_copy(j):
        return remote(chip_out.at[j], chip_in.at[chip], c_ss.at[j], c_rs.at[chip], "seq", 2 * j + side)

    def form(j):
        at = rows_of(j, 2 * T)
        found = nt(gp[at, :], w_in[...]) + nn(grad_small[at, :], w_wide[...])
        if rep > 1:
            found = found * (lax.rem(me, rep) == 0).astype(f32)
        gain_sum[...] += jnp.sum(found * normed_rows(at), axis=0, keepdims=True)
        for i in range(2):

            @pl.when(side == i)
            def _():
                part_own[j] = found[i * T : (i + 1) * T].astype(part_own.dtype)
                part_out[j] = found[(1 - i) * T : (2 - i) * T].astype(bf16)

        sibling_copy(j).start()

    def join(j):
        sibling_copy(j).wait_recv()
        found = part_own[j].astype(f32) + part_in[j].astype(f32)
        part_own[j] = found.astype(part_own.dtype)
        chip_out[j] = found.astype(bf16)

        @pl.when(chip != j)
        def _():
            owner_copy(j).start()

    hops = [(chain, q) for chain in (downs, *ups) for q in range(1, m - 1)]

    def after_turn(k):
        c = n - 1 - k

        @pl.when(lax.rem(k, 2) == 1)
        def _():
            form(c // 2)

        @pl.when((lax.rem(k, 2) == 0) & (k > 0))
        def _():
            join((c + 1) // 2)

        for i, (chain, q) in enumerate(hops):

            @pl.when(k == 4 * i // 3)
            def _():
                chain.tick(q)

    def fetch(c):
        if roomy:
            return kept(news, rows_of(c, NH * T)), (invs[0, c], invs[1, c]), mixed[rows_of(c, T), :]
        late = [
            pltpu.make_async_copy(news_any.at[:, rows_of(c, NH * T)], news, l_sems.at[11]),
            pltpu.make_async_copy(invs_any.at[:, pl.ds(c, 1)], invs, l_sems.at[12]),
            pltpu.make_async_copy(mixed_any.at[rows_of(c, T)], mixed, l_sems.at[9]),
        ]
        for load in late:
            load.start()
        for load in late:
            load.wait()
        return (news[0], news[1]), (invs[0, 0], invs[1, 0]), mixed[...]

    turn = functools.partial(
        backward_turn, n, T, head, starts, bias, rate, taps, gain, lambda at: nt(low_all[at, :], w_head[...]),
        proj, small, states, fetch, gp, grad_small, gconv_w, xbuf, halo, gates_sum, grad_state, after_turn,
    )
    lax.fori_loop(0, n, turn, 0)

    small_t = tn(grad_small[...], normed[...])
    small_t = small_t[: SMALL * H] + small_t[32 : 32 + SMALL * H]
    z_sum[0:1, :] = gain_mid_grad[...]
    for i in range(SMALL):
        z_sum[1 + i : 2 + i, :] = jnp.sum(small_t[i * H : (i + 1) * H], axis=0, keepdims=True)
    z_sum[4:8, :width] = gconv_w[...]
    for i in range(3):
        z_sum[4 + i : 5 + i, width : width + HD] = gates_sum[i : i + 1, :]
    z_sum[7:8, width : width + HD] = jnp.zeros((1, HD), f32)
    gain_part = gain_sum[...] / gain_in[...]
    cut = D - width - HD
    for i in range(4):
        z_sum[4 + i : 5 + i, width + HD :] = gain_part[:, i * cut : (i + 1) * cut]
    first_sums = Sums(z_sum, z_sum_in, q_sum, (sum_ss, sum_rs, qsum_ss, qsum_rs), me, my, n, m)
    first_sums.start()

    lines = D // TILE
    units, strip = n // lines, piece * m

    def line(i):
        return Chain(
            lambda d: z_w.at[i, d], lambda j: z_w_up.at[i, j], lambda j: z_w_down.at[i, j],
            (w_us.at[i], w_ur.at[i], w_ds.at[i], w_dr.at[i]), my, m,
        )

    def line_turn(i, _):
        cuts = []
        for u in range(units):
            first = (i + u * lines) * strip
            if strip % HD == 0:
                first = pl.multiple_of(first, HD)
            cuts.append(normed[:, pl.ds(first, strip)])
        found = tn(jnp.concatenate(cuts, axis=1), gp[...])
        for u in range(units):
            for d in range(m):
                at = u * strip + d * piece
                z_w[i, d, u] = found[at : at + piece].astype(bf16)
        line(i).start()
        return 0

    if strip % HD == 0:
        line_turn(0, 0)
        join(0)
        lax.fori_loop(1, lines, line_turn, 0)
    else:
        for i in range(lines):
            line_turn(i, 0)
        join(0)
    ins = [line(i) for i in range(lines)]
    for i, (chain, q) in enumerate(hops):
        if 4 * i // 3 >= n:
            chain.tick(q)

    def write_down(x):
        g_down[...] = x

    def write_out(x):
        g_out[...] = x

    downs.finish(write_down)
    for j in range(2):

        def write_up(x, j=j):
            q_gu[:, j] = x.astype(bf16)

        ups[j].finish(write_up)
    q_ups = [scatter_to(q_gu, q_gu_in, k, qgu_ss, qgu_rs, me, n) for k in range(1, n)]
    for copy in q_ups:
        copy.start()
    q_gu_in[me] = q_gu[me]
    for q in range(1, m - 1):
        outs.tick(q)

    def input_gradient():
        total = part_own[chip].astype(f32)
        for k in range(1, n // 2):
            other = lax.rem(chip + k, n // 2)
            remote(chip_out.at[other], chip_in.at[other], c_ss.at[other], c_rs.at[other], "seq", 2 * other + side).wait_recv()
            total = total + chip_in[other].astype(f32)
        values = tokens[...].astype(f32)
        part, _ = norm_back(values, norm_scale(values), gain_in[...], total)
        grad_input[...] = grad_residual[...] + part

    def deliver(i):
        def write_in(x):
            for u in range(units):
                q_w[i + u * lines] = x[u].astype(bf16)

        ins[i].finish(write_in)
        for j in range(i, n, lines):

            @pl.when(me != j)
            def _():
                remote(q_w.at[j], q_w_in.at[me], qw_ss.at[j], qw_rs.at[me], "seq", j).start()

    first_sums.add()
    for i, chain in enumerate(ins):
        for q in range(1, m - 1):
            chain.tick(q)
        if i:
            deliver(i - 1)
        if i == 1:
            outs.finish(write_out)
        if i == 2:
            input_gradient()
    deliver(len(ins) - 1)
    q_w_in[me] = q_w[me]
    for chain in (downs, *ups, outs, *ins):
        chain.settle()

    def settle(j, _):
        sibling_copy(j).wait_send()

        @pl.when(chip != j)
        def _():
            owner_copy(j).wait_send()

        return 0

    lax.fori_loop(0, n // 2, settle, 0)
    first_sums.settle()
    for copy in q_ups:
        copy.wait()
    for k in range(1, n):
        peer = lax.rem(me + k, n)
        remote(q_w.at[peer], q_w_in.at[me], qw_ss.at[peer], qw_rs.at[me], "seq", peer).wait_send()
        remote(q_w.at[peer], q_w_in.at[peer], qw_ss.at[peer], qw_rs.at[peer], "seq", peer).wait_recv()


def run_back(n, m, rep, T, lengths, bias, rate, tokens, grad_residual, gain_in, gain_mid_grad, w_small, taps, gain,
             mid, cot, w_gate_up, w_down, w_out, head_rows, proj, small, mixed, states, news, invs, normed, w_in):
    rows, piece, shard = n * T, D // (n * m), FF // n
    wide = -(-(shard + HD - 1) // HD) * HD
    vm, roomy = pltpu.VMEM, rows <= 1024
    band = GROUPS * HD

    def chained(*dims, lead=()):
        return [vm((*lead, m, *dims), bf16), vm((*lead, m - 1, *dims), bf16), vm((*lead, m - 1, *dims), bf16)]

    return pl.pallas_call(
        functools.partial(back_kernel, n, m, rep, T, piece, shard, wide),
        out_shape=(
            shape((T, D), f32), shape((n, piece, band), bf16), shape((piece, D), f32), shape((n, 2, piece, shard), bf16),
            shape((shard // m, D), f32), shape((n, 8, D), f32),
        ),
        in_specs=[SMEM] * 3 + [VMEM] * 7 + [ANY] * 14,
        out_specs=[VMEM] * 6,
        scratch_shapes=[
            vm((rows, D), bf16), vm((rows, D), bf16), vm((D, wide), bf16), vm((D, wide), bf16), vm((wide, D), bf16),
            vm((HD, D), bf16), vm((rows, HD), bf16), vm((rows, band), bf16), vm((rows, HD), f32), vm((rows if roomy else T, HD), f32),
            vm((2, n, HD, HD), bf16), vm((2, NH * (rows if roomy else T), HD), bf16), vm((2, n if roomy else 1, NH * T, NH * T), bf16),
            vm((rows, D) if roomy else (1, 16, HD), bf16), vm((D, band), bf16), vm((HD, D), bf16),
            vm((rows, D), bf16), vm((rows, shard), bf16), vm((rows, shard), bf16), vm((rows, shard), bf16),
            vm((rows, band), bf16), vm((rows, HD), bf16), vm((CONV, MIXED * HD), f32), vm((rows + 8, MIXED * HD), f32),
            vm((8, MIXED * HD), f32), vm((8, HD), f32), vm((HD, HD), f32),
            *chained(n, piece, shard, lead=(2,)), *chained(shard // m, D), *chained(piece, D), *chained(n * TILE // D, piece, band, lead=(D // TILE,)),
            vm((8, D), f32), vm((m - 1, 8, D), f32), vm((1, D), f32), vm((n, 2, piece, shard), bf16), vm((n, piece, band), bf16),
            vm((n // 2, T, D), f32 if roomy else bf16), *[vm((n // 2, T, D), bf16)] * 4,
            DMA((14,)), DMA((GROUPS,)), *chain_sems(2, m - 1), *chain_sems(m - 1), *chain_sems(m - 1),
            *chain_sems(D // TILE, m - 1), DMA((m - 1,)), DMA((m - 1,)), DMA((n - 1,)), DMA((n - 1,)), DMA((n,)), DMA((n,)),
            DMA((n - 1,)), DMA((n - 1,)),
            *[DMA((n // 2,))] * 4, *gather_sems(n),
        ],
        compiler_params=pltpu.CompilerParams(vmem_limit_bytes=(60 if roomy else 63) * 1024 * 1024, collective_id=3, has_side_effects=True),
        name="backward",
    )(lengths, bias, rate, tokens, grad_residual, gain_in, gain_mid_grad, w_small, taps, gain,
      mid, cot, w_gate_up, w_down, w_out, head_rows, proj, small, mixed, states, news, invs, normed, w_in)


def output_kernel(
    n, rep, shard, result_in, grad_input_in, w_parts, out_part, gu_parts, down_part, sums,
    result, grad_input, g_in, g_out, g_gate_up, g_down, g_gain_in, g_gain_mid, g_small, g_bias, g_rate, g_taps, g_gain_head,
):
    result[...] = result_in[...]
    grad_input[...] = grad_input_in[...]
    g_out[...] = out_part[...]
    g_down[...] = down_part[...]
    for i in range(2):
        for source in range(n):
            at = i * FF + source * shard
            g_gate_up[:, at : at + shard] = gu_parts[source, i].astype(f32)
    g_gain_mid[...] = jnp.sum(sums[:, 0:1, :], axis=0)
    width = MIXED * HD
    cut = D - width - HD
    for i in range(4):
        g_gain_in[:, i * cut : (i + 1) * cut] = jnp.sum(sums[:, 4 + i : 5 + i, width + HD :], axis=0)
    gain_total = jnp.zeros((1, HD), f32)
    for h in range(H):
        found = sums[h * rep]
        part = w_parts[h * rep].astype(f32)
        for j in range(SMALL):
            g_small[j * H + h : j * H + h + 1, :] = found[1 + j : 2 + j, :]
        for i in range(MIXED):
            g_taps[:, i * D + h * HD : i * D + (h + 1) * HD] = found[4 : 4 + CONV, i * HD : (i + 1) * HD]
        for i in range(GROUPS):
            g_in[:, i * D + h * HD : i * D + (h + 1) * HD] = part[:, i * HD : (i + 1) * HD]
        gain_total = gain_total + found[4:5, width : width + HD]
        g_bias[h] = found[5, width + NH]
        g_rate[h] = found[6, width + NH]
    g_gain_head[...] = gain_total


def run_output(n, rep, *parts):
    result, grad_input, w_parts, out_part, gu_parts, down_part, sums = parts
    piece, shard = out_part.shape[0], gu_parts.shape[-1]
    return pl.pallas_call(
        functools.partial(output_kernel, n, rep, shard),
        out_shape=(
            shape(result.shape, bf16), shape(grad_input.shape, f32), shape((piece, GROUPS * D), f32), shape((piece, D), f32),
            shape((piece, 2 * FF), f32), shape(down_part.shape, f32), shape((1, D), f32), shape((1, D), f32),
            shape((SMALL * H, D), f32), shape((H,), f32), shape((H,), f32), shape((CONV, MIXED * D), f32), shape((1, HD), f32),
        ),
        in_specs=[VMEM] * 7,
        out_specs=[VMEM] * 9 + [SMEM] * 2 + [VMEM] * 2,
        compiler_params=pltpu.CompilerParams(vmem_limit_bytes=LIMIT),
        name="outputs",
    )(*parts)


def on_device(tokens, grad_out, doc_lengths, gain_in, in_weight, small_weight, gate_bias, decay_rate, conv_weight,
              gain_head, out_weight, gain_mid, gate_up_weight, down_weight):
    seq, stream = lax.axis_size("seq"), lax.axis_size("stream")
    rep = seq // H
    T = tokens.shape[1]
    gain = gain_head.reshape(1, HD)
    gain_in, gain_mid = gain_in.reshape(1, D), gain_mid.reshape(1, D)
    rows, cotangent, small_weight = tokens[0], grad_out[0], small_weight.T
    gated, normed, out_all, proj, small, mixed, states, news, invs, head_rows = run_forward(
        seq, rep, T, doc_lengths, gate_bias, decay_rate, rows, cotangent, gain_in, in_weight, small_weight, conv_weight, gain
    )
    result, grad_residual, mid_all, grad_gain_mid = run_feed(
        seq, T, rows, gated, cotangent, out_weight, gain_mid, gate_up_weight, down_weight
    )
    parts = run_back(
        seq, stream, rep, T, doc_lengths, gate_bias, decay_rate, rows, grad_residual, gain_in, grad_gain_mid, small_weight,
        conv_weight, gain, mid_all, out_all, gate_up_weight, down_weight, out_weight, head_rows, proj, small, mixed, states,
        news, invs, normed, in_weight,
    )
    result, grad_input, g_in, g_out, g_gate_up, g_down, g_gain_in, g_gain_mid, g_small, g_bias, g_rate, g_taps, g_gain_head = (
        run_output(seq, rep, result, *parts)
    )
    return (
        result[None], grad_input[None], g_gain_in.reshape(D), g_in, g_small.T, g_bias, g_rate, g_taps,
        g_gain_head.reshape(HD), g_out, g_gain_mid.reshape(D), g_gate_up, g_down,
    )


def solution(mesh):
    rows, whole, split = P("stream", "seq", None), P(), P(("seq", "stream"), None)
    return jax.shard_map(
        on_device,
        mesh=mesh,
        in_specs=(rows, rows, P("stream", None)) + (whole,) * 11,
        out_specs=(rows, rows, whole, split, whole, whole, whole, whole, whole, split, whole, split, split),
        check_vma=False,
    )
```

```python
import functools

import jax
import jax.numpy as jnp
from jax import lax
from jax.experimental import pallas as pl
from jax.experimental.pallas import tpu as pltpu
from jax.sharding import PartitionSpec as P

D = 1024
H = 8
HD = 128
FF = 2816
NH = 2
CONV = 4
GROUPS = 2 + 2 * NH
MIXED = GROUPS - 1
SMALL = NH + 1
DOCS = 8
TILE = 256
EPS = 1e-06

f32 = jnp.float32
bf16 = jnp.bfloat16
MESH = pl.DeviceIdType.MESH
DMA = pltpu.SemaphoreType.DMA
VMEM = pl.BlockSpec(memory_space=pltpu.VMEM)
SMEM = pl.BlockSpec(memory_space=pltpu.SMEM)
ANY = pl.BlockSpec(memory_space=pl.ANY)
LIMIT = 56 * 1024 * 1024
shape = jax.ShapeDtypeStruct


def dot(a, b, dims):
    if isinstance(a, tuple) and isinstance(b, tuple):
        return dot(a[0], b[0], dims) + (dot(a[0], b[1], dims) + dot(a[1], b[0], dims))
    if isinstance(a, tuple):
        return dot(a[0], b, dims) + dot(a[1], b, dims)
    if isinstance(b, tuple):
        return dot(a, b[0], dims) + dot(a, b[1], dims)
    return lax.dot_general(
        a.astype(bf16), b.astype(bf16), ((dims[:1], dims[1:]), ((), ())), preferred_element_type=f32
    )


def nn(a, b):
    return dot(a, b, (1, 0))


def nt(a, b):
    return dot(a, b, (1, 1))


def tn(a, b):
    return dot(a, b, (0, 0))


def halves(x):
    high = x.astype(bf16)
    return high, (x - high.astype(f32)).astype(bf16)


def thirds(x):
    high, low = halves(x)
    return high, low, (x - high.astype(f32) - low.astype(f32)).astype(bf16)


def keep(ref, at, x):
    ref[0, at], ref[1, at] = halves(x)


def kept(ref, at):
    return ref[0, at], ref[1, at]


def nn_exact(ones, x):
    high, low, lowest = thirds(x)
    return nn(ones, high) + (nn(ones, low) + nn(ones, lowest))


def sigmoid(x):
    return 1.0 / (1.0 + jnp.exp(-x))


def softplus(x):
    return jnp.maximum(x, 0.0) + jnp.log(1.0 + jnp.exp(-jnp.abs(x)))


def norm_scale(values):
    return lax.rsqrt(jnp.mean(values * values, axis=-1, keepdims=True) + EPS)


def norm_back(values, scale, gain, grad):
    normal = values * scale
    e = grad * gain
    back = scale * (e - normal * jnp.mean(e * normal, axis=-1, keepdims=True))
    return back, jnp.sum(grad * normal, axis=0, keepdims=True)


def iota(dims, axis):
    return lax.broadcasted_iota(jnp.int32, dims, axis)


def doc_at(starts, positions):
    total = jnp.full(positions.shape, -1, jnp.int32)
    for start in starts:
        total = total + (start <= positions).astype(jnp.int32)
    return total


def doc_starts(lengths_ref):
    starts, at = [], jnp.int32(0)
    for j in range(DOCS):
        starts.append(at)
        at = at + lengths_ref[0, j]
    return starts


def stack2(a, b):
    return jnp.concatenate([a, b], axis=0)


def beside(a, b):
    return jnp.concatenate([a, b], axis=1)


def quad(a, b, c, d):
    return stack2(beside(a, b), beside(c, d))


def rows_of(i, size):
    return pl.ds(pl.multiple_of(i * size, size), size)


def greet(axis, peers):
    barrier = pltpu.get_barrier_semaphore()
    for peer in peers:
        pl.semaphore_signal(barrier, inc=1, device_id={axis: peer}, device_id_type=MESH)
    return lambda: pl.semaphore_wait(barrier, len(peers))


def remote(src, dst, send, receive, axis, peer):
    return pltpu.make_async_remote_copy(src, dst, send, receive, device_id={axis: peer}, device_id_type=MESH)


def flipped(chip, bits, chips):
    total, place = 0, 1
    while place < chips:
        total = total + place * lax.rem(chip // place + bits // place, 2)
        place *= 2
    return total


class Gather:
    def __init__(self, n, T, src, dst, sems):
        self.n, self.T, self.src, self.dst = n, T, src, dst
        self.ss, self.rs, self.fs, self.fr = sems
        self.me = lax.axis_index("seq")
        self.chip, self.side = self.me // 2, lax.rem(self.me, 2)
        self.sib = self.me + 1 - 2 * self.side
        order = sorted(range(1, n // 2), key=lambda k: k.bit_count())
        self.early = [k for k in order if k.bit_count() == 1]
        self.late = [k for k in order if k.bit_count() > 1]

    def at(self, device):
        return self.dst.at[rows_of(device, self.T)]

    def partner(self, k):
        return 2 * flipped(self.chip, k, self.n // 2) + self.side

    def direct(self, k):
        peer = self.sib if k == 0 else self.partner(k)
        return remote(self.src, self.at(self.me), self.ss.at[k], self.rs.at[k], "seq", peer)

    def passed(self, k):
        block = self.at(self.partner(k))
        return remote(block, block, self.fs.at[k], self.fr.at[k], "seq", self.sib)

    def relay(self, k):
        top = 1 << (k.bit_length() - 1)
        for side, last in ((0, top), (1, k & -k)):

            @pl.when(self.side == side)
            def _():
                block = self.at(self.partner(k - last))
                remote(block, block, self.ss.at[k], self.rs.at[k], "seq", self.partner(last)).start()

    def start(self):
        for k in (*self.early, 0):
            self.direct(k).start()

    def pass_on(self, k):
        self.direct(k).wait_recv()
        self.passed(k).start()

    def forward(self):
        for k in self.early:
            self.pass_on(k)
        for k in self.late:
            if k.bit_count() == 2:
                self.relay(k)

    def forward_late(self):
        for k in self.late:
            if k.bit_count() > 2:
                self.relay(k)
            self.pass_on(k)

    def arrive(self):
        self.direct(0).wait_recv()
        for k in range(1, self.n // 2):
            self.passed(k).wait_recv()

    def finish(self):
        for k in range(self.n // 2):
            self.direct(k).wait_send()
            if k:
                self.passed(k).wait_send()


def gather_sems(n):
    return [DMA((n // 2,)) for _ in range(4)]


def conv_of(block, taps, docs, T):
    total = block[8:] * taps[CONV - 1 : CONV]
    for lag in range(1, CONV):
        same = (docs[0] == docs[lag]).astype(f32)
        total = total + block[8 - lag : 8 - lag + T] * (taps[CONV - 1 - lag : CONV - lag] * same)
    return total


def chunk_gates(logits, bias, rate, starts, first, T):
    lane = iota((T, HD), 1)
    shifted = logits + bias
    gate = -rate * softplus(shifted)
    place_i, place_j = iota((T, T), 0), iota((T, T), 1)
    lower = place_j <= place_i
    cumul = nn_exact(lower.astype(bf16), jnp.where(lane == NH, gate, 0.0))
    beta = 2.0 * sigmoid(logits)
    b0, b1 = beta[:, 0:1], beta[:, 1:2]
    g = cumul[:, NH : NH + 1]
    g_row = jnp.transpose(cumul)[NH : NH + 1, :]
    g_last = cumul[T - 1 : T, NH : NH + 1]
    position = first + iota((T, 1), 0)
    docs = [doc_at(starts, position - lag) for lag in range(CONV)]
    doc = docs[0]
    doc_row = doc_at(starts, first + iota((1, T), 1))
    doc_before = doc_at(starts, jnp.full((1, 1), first - 1, jnp.int32))
    doc_last = doc_at(starts, jnp.full((1, 1), first + (T - 1), jnp.int32))
    joined = lower & (doc == doc_row)
    decay = jnp.where(joined, jnp.exp(jnp.where(joined, g - g_row, 0.0)), 0.0)
    strict = jnp.where(place_i == place_j, 0.0, decay)
    from_start = jnp.exp(g) * (doc == doc_before).astype(f32)
    to_end = jnp.exp(jnp.minimum(g_last - g, 0.0)) * (doc == doc_last).astype(f32)
    whole = jnp.exp(g_last) * (doc_last == doc_before).astype(f32)
    return dict(
        shifted=shifted, beta=beta, b=stack2(b0, b1), docs=docs, decay=decay,
        decays=quad(strict, strict, decay, strict), hd=from_start, hd2=stack2(from_start, from_start),
        to_end=stack2(to_end, to_end), whole=whole,
    )


def key_scale(raw):
    return lax.rsqrt(jnp.sum(raw * raw, axis=-1, keepdims=True) + EPS)


def chunk_inputs(block, taps, docs, T):
    conv = conv_of(block, taps, docs, T)
    sig = sigmoid(conv)
    active = conv * sig
    cut = [active[:, i * HD : (i + 1) * HD] for i in range(MIXED)]
    scales = (key_scale(cut[1]), key_scale(cut[2]))
    keys = stack2(cut[1] * scales[0], cut[2] * scales[1])
    values = stack2(cut[3], cut[4])
    return conv, sig, cut[0], keys, values, stack2(*scales)


def inverses(lowers, T):
    size = NH * T
    row, col = iota((size, size), 0), iota((size, size), 1)
    differ = (row & (T - 1)) ^ (col & (T - 1))
    eye = (row == col).astype(f32)
    found = [jnp.where(row == col, 1.0, jnp.where(differ == 0, -a, 0.0)) for a in lowers]
    step = 1
    while step < T:
        level = (differ >= step) & (differ < 2 * step)
        parts = [nn(jnp.where(level, a, 0.0), x) for a, x in zip(lowers, found)]
        found = [x - nn(x, part) for x, part in zip(found, parts)]
        step *= 2
    a_cut = [halves(a) for a in lowers]
    x_cut = [halves(x) for x in found]
    errors = [
        eye - x - (nn(a[0], xc[0]) + (nn(a[0], xc[1]) + nn(a[1], xc[0])))
        for a, x, xc in zip(a_cut, found, x_cut)
    ]
    return [x + nn(xc[0], e) for x, xc, e in zip(found, x_cut, errors)]


def head_gate(mixed, raw):
    scale = norm_scale(mixed)
    return mixed * scale, scale, sigmoid(raw)


def head_taps(taps_ref, head):
    cuts = [taps_ref[:, pl.ds(pl.multiple_of(i * D + head * HD, HD), HD)] for i in range(MIXED)]
    return jnp.concatenate(cuts, axis=1)


def intra_turn(T, starts, bias, rate, taps, small, block_of, invs, ubuf, wbuf, qbuf, pbuf, dbuf, gates, chunks, midway):
    held, lowers = [], []
    for c in chunks:
        first = pl.multiple_of(c * T, T)
        gate = chunk_gates(small[pl.ds(first, T), :], bias, rate, starts, first, T)
        conv, sig, query, keys, values, scales = chunk_inputs(block_of(c), taps, gate["docs"], T)
        key_pair = halves(keys)
        lowers.append(gate["b"] * (nt(key_pair, key_pair) * gate["decays"]))
        held.append((c, gate, query, keys, key_pair, values))
    found = inverses(lowers, T)
    midway()
    for (c, gate, query, keys, key_pair, values), inverse in zip(held, found):
        at, two = rows_of(c, T), rows_of(c, NH * T)
        pair = halves(inverse)
        invs[0, c], invs[1, c] = pair
        both = nn(pair, halves(gate["b"] * beside(values, gate["hd2"] * keys)))
        ubuf[two, :] = both[:, :HD]
        keep(wbuf, two, both[:, HD:])
        query_pair = halves(query)
        qbuf[0, at], qbuf[1, at] = query_pair
        keep(pbuf, at, nt(query_pair, key_pair) * beside(gate["decay"], gate["decay"]))
        keep(dbuf, two, gate["to_end"] * keys)
        gates[at, :] = jnp.where(iota((T, HD), 1) == 0, gate["hd"], gate["whole"])


def across_turn(T, gain, proj, mixed_out, states, news, head_rows, ubuf, wbuf, qbuf, pbuf, dbuf, gates, done, c, state):
    at, two = rows_of(c, T), rows_of(c, NH * T)
    state_pair = halves(state)
    states[0, c], states[1, c] = state_pair
    new = ubuf[two, :] - nn(kept(wbuf, two), state_pair)
    new_pair = halves(new)
    news[0, two], news[1, two] = new_pair
    gate = gates[at, :]
    mixed = gate[:, 0:1] * nn(kept(qbuf, at), state_pair) + nn(kept(pbuf, at), new_pair)
    mixed_out[at, :] = mixed
    raw = proj[at, MIXED * HD :].astype(f32)
    normal, _, sig = head_gate(mixed, raw)
    head_rows[at, :] = ((normal * gain[...]) * (raw * sig)).astype(bf16)
    done(c)
    return gate[0:1, 1:2] * state + tn(kept(dbuf, two), new_pair)


def widened(w_wide, parts):
    w_wide[...] = jnp.zeros((HD, D), bf16)
    for i, part in enumerate(parts):
        w_wide[32 * i : 32 * i + SMALL * H, :] = part


def forward_kernel(
    n, rep, T, lengths, bias_ref, rate_ref, tokens, cotangent, gain_in, w_in, w_small, taps_ref, gain,
    gated, normed_out, out_all, proj_out, small_out, mixed_out, states, news, invs_out, head_rows,
    normed, proj, small, invs, own, tails, w_head, w_wide, tail_rows, xbuf, ubuf, wbuf, qbuf, pbuf, dbuf, gates,
    w_sems, own_sems, o_sems, a_ss, a_rs, t_ss, t_rs, *sems,
):
    me = lax.axis_index("seq")
    head = me // rep
    chips = n // 2
    wait_for_all = greet("seq", [lax.rem(me + k, n) for k in range(1, n)])
    width = MIXED * HD
    loads = [
        pltpu.make_async_copy(
            w_in.at[:, pl.ds(pl.multiple_of(i * D + head * HD, HD), HD)], w_head.at[:, i * HD : (i + 1) * HD], w_sems.at[i]
        )
        for i in range(GROUPS)
    ]
    for load in loads:
        load.start()
    values = tokens[...].astype(f32)
    own[...] = (values * norm_scale(values) * gain_in[...]).astype(bf16)
    local = pltpu.make_async_copy(own, normed.at[rows_of(me, T)], own_sems.at[0])
    local.start()
    wait_for_all()
    first_gather = Gather(n, T, own, normed, sems[:4])
    second_gather = Gather(n, T, cotangent, out_all, sems[4:8])
    keep_out = pltpu.make_async_copy(cotangent, out_all.at[rows_of(me, T)], own_sems.at[2])
    keep_out.start()
    chip, side = first_gather.chip, first_gather.side
    last = own.at[T - 16 : T]

    def tail_copy(k):
        return remote(last, tails.at[chip], t_ss.at[k], t_rs.at[chip], "seq", lax.rem(me + k, n))

    mine = pltpu.make_async_copy(last, tails.at[chip], own_sems.at[1])
    early, late = first_gather.early, first_gather.late

    @pl.when(side == 1)
    def _():
        for k in range(1, n):
            tail_copy(k).start()
        mine.start()

    for k in (0, *early):
        first_gather.direct(k).start()

    starts = doc_starts(lengths)
    bias, rate = bias_ref[head], rate_ref[head]
    taps = head_taps(taps_ref, head)
    widened(w_wide, thirds(jnp.where((iota((SMALL * H, D), 0) & (H - 1)) == head, w_small[...], 0.0)))
    group, lane = iota((HD, HD), 0), iota((HD, HD), 1)
    picks = (((group & 31) >> 3) == lane) & (group < 96) & (lane < SMALL)
    picks = picks.astype(bf16)
    for load in loads:
        load.wait()
    local.wait()

    @pl.when(side == 1)
    def _():
        mine.wait()
        for k in range(1, n):
            tail_copy(k).wait_send()

    for j in range(chips):

        @pl.when(me != 2 * j + 1)
        def _():
            remote(last, tails.at[j], t_ss.at[0], t_rs.at[j], "seq", lax.rem(me + 1, n)).wait_recv()

    found = nn(tails[...].reshape(chips * 16, D), w_head[...]).astype(bf16).astype(f32)
    tail_rows[...] = found[:, :width]
    size = T + 8

    def block_of(c):
        return xbuf[pl.ds(pl.multiple_of(c * size, 8), size), :]

    def project(pair):
        at = rows_of(pair, 2 * T)
        block = normed[at, :]
        result = nn(block, w_head[...]).astype(bf16)
        proj[at, :] = result
        raw = thirds(nt(block, w_wide[...]))
        small[at, :] = nn(raw[0], picks) + (nn(raw[1], picks) + nn(raw[2], picks))
        mixing = result[:, :width].astype(f32)
        before = lax.rem(pair + chips - 1, chips)
        halo = tail_rows[pl.ds(pl.multiple_of(before * 16 + 8, 8), 8), :]
        base = pl.multiple_of(pair * (2 * size), 8)
        xbuf[pl.ds(base, 8), :] = jnp.where(pair > 0, halo, 0.0)
        xbuf[pl.ds(pl.multiple_of(base + 8, 8), T), :] = mixing[:T]
        xbuf[pl.ds(pl.multiple_of(base + size, 8), T + 8), :] = mixing[T - 8 :]

    first_gather.direct(0).wait_recv()
    groups = [(0,)] + [(*ks[i : i + 2],) for ks in (early, late) for i in range(0, len(ks), 2)]
    to_late = (len(early) + 1) // 2

    def midway(g):
        if g == 0:
            first_gather.forward()
        if g == to_late:
            first_gather.forward_late()
            second_gather.start()
        if g == len(groups) - 1:
            second_gather.forward()

    for g, group in enumerate(groups):
        for k in group:
            if k:
                first_gather.passed(k).wait_recv()
        pairs = [flipped(chip, k, chips) for k in group]
        for pair in pairs:
            project(pair)
        intra_turn(
            T, starts, bias, rate, taps, small, block_of, invs, ubuf, wbuf, qbuf, pbuf, dbuf, gates,
            [2 * pair + i for pair in pairs for i in range(2)], functools.partial(midway, g),
        )

    first_gather.finish()
    stores = [
        pltpu.make_async_copy(a, b, o_sems.at[i])
        for i, (a, b) in enumerate(((normed, normed_out), (proj, proj_out), (small, small_out), (invs, invs_out)))
    ]
    for store in stores:
        store.start()
    column = pl.ds(pl.multiple_of(head * HD, HD), HD)

    def row_copy(c):
        return remote(head_rows.at[rows_of(c, T)], gated.at[:, column], a_ss.at[c], a_rs.at[head], "seq", c)

    def send_rows(c):
        @pl.when((c != me) & (lax.rem(me, rep) == 0))
        def _():
            row_copy(c).start()

    across = functools.partial(
        across_turn, T, gain, proj, mixed_out, states, news, head_rows, ubuf, wbuf, qbuf, pbuf, dbuf, gates, send_rows
    )
    lax.fori_loop(0, n, across, jnp.zeros((HD, HD), f32))

    @pl.when(lax.rem(me, rep) == 0)
    def _():
        kept_rows = pltpu.make_async_copy(head_rows.at[rows_of(me, T)], gated.at[:, column], own_sems.at[0])
        kept_rows.start()
        kept_rows.wait()

    keep_out.wait()
    second_gather.forward_late()

    def settle(k, _):
        peer = lax.rem(me + k, n)

        @pl.when(lax.rem(me, rep) == 0)
        def _():
            row_copy(peer).wait_send()

        @pl.when(lax.rem(peer, rep) == 0)
        def _():
            source = peer // rep
            remote(
                head_rows.at[rows_of(me, T)], gated.at[:, pl.ds(pl.multiple_of(source * HD, HD), HD)],
                a_ss.at[peer], a_rs.at[source], "seq", peer,
            ).wait_recv()

        return 0

    lax.fori_loop(1, n, settle, 0)
    second_gather.arrive()
    second_gather.finish()
    for store in stores:
        store.wait()


def forward_scratch(n, T):
    rows = n * T
    return [
        pltpu.VMEM((rows + 8 * n, MIXED * HD), f32), pltpu.VMEM((NH * rows, HD), f32),
        pltpu.VMEM((2, NH * rows, HD), bf16), pltpu.VMEM((2, rows, HD), bf16), pltpu.VMEM((2, rows, NH * T), bf16),
        pltpu.VMEM((2, NH * rows, HD), bf16), pltpu.VMEM((rows, HD), f32),
    ]


def run_forward(n, rep, T, lengths, bias, rate, tokens, cotangent, gain_in, w_in, w_small, taps, gain):
    rows = n * T
    return pl.pallas_call(
        functools.partial(forward_kernel, n, rep, T),
        out_shape=(
            shape((T, D), bf16), shape((rows, D), bf16), shape((rows, D), bf16), shape((rows, GROUPS * HD), bf16),
            shape((rows, HD), f32), shape((rows, HD), f32), shape((2, n, HD, HD), bf16), shape((2, NH * rows, HD), bf16),
            shape((2, n, NH * T, NH * T), bf16), shape((rows, HD), bf16),
        ),
        in_specs=[SMEM] * 3 + [VMEM, VMEM, VMEM, ANY, VMEM, VMEM, VMEM],
        out_specs=[VMEM, ANY, ANY, ANY, ANY, VMEM, VMEM, VMEM, ANY, VMEM],
        scratch_shapes=[
            pltpu.VMEM((rows, D), bf16), pltpu.VMEM((rows, GROUPS * HD), bf16), pltpu.VMEM((rows, HD), f32),
            pltpu.VMEM((2, n, NH * T, NH * T), bf16),
            pltpu.VMEM((T, D), bf16), pltpu.VMEM((n // 2, 16, D), bf16), pltpu.VMEM((D, GROUPS * HD), bf16),
            pltpu.VMEM((HD, D), bf16), pltpu.VMEM((n * 8, MIXED * HD), f32),
            *forward_scratch(n, T),
            DMA((GROUPS,)), DMA((3,)), DMA((4,)), DMA((n,)), DMA((H,)), DMA((n,)), DMA((n // 2,)), *gather_sems(n), *gather_sems(n),
        ],
        compiler_params=pltpu.CompilerParams(vmem_limit_bytes=LIMIT, collective_id=1, has_side_effects=True),
        name="mixer_forward",
    )(lengths, bias, rate, tokens, cotangent, gain_in, w_in, w_small, taps, gain)


def feed_kernel(
    n, T, steps, tokens, gated, cotangent, w_out, gain_mid, w_gate, w_up, w_down,
    result, grad_residual, mid_all, gain_grad, residual, middle, total, grad_mid, own_sem, *sems,
):
    step = pl.program_id(0)
    me = lax.axis_index("seq")
    gather = Gather(n, T, middle, mid_all, sems)
    local = pltpu.make_async_copy(middle, mid_all.at[rows_of(me, T)], own_sem)

    @pl.when(step == 0)
    def _():
        peers = [gather.sib] + [gather.partner(k) for k in range(1, n // 2)]
        wait_for_all = greet("seq", peers)
        found = tokens[...].astype(f32) + nn(gated[...], w_out[...])
        residual[...] = found
        middle[...] = (found * norm_scale(found) * gain_mid[...]).astype(bf16)
        total[...] = found
        grad_mid[...] = jnp.zeros((T, D), f32)
        wait_for_all()
        gather.start()
        local.start()

    gate, up = nn(middle[...], w_gate[...]), nn(middle[...], w_up[...])
    sig = sigmoid(gate)
    silu = gate * sig
    hidden = (silu * up).astype(bf16)
    total[...] += nn(hidden, w_down[...])
    grad_hidden = nt(cotangent[...], w_down[...])
    grad_gate = (grad_hidden * up * (sig * (1.0 + gate * (1.0 - sig)))).astype(bf16)
    grad_up = (grad_hidden * silu).astype(bf16)
    grad_mid[...] += nt(grad_gate, w_gate[...]) + nt(grad_up, w_up[...])

    for at, what in ((5, gather.forward), (8, gather.forward_late)):

        @pl.when(step == at)
        def _():
            what()

    @pl.when(step == steps - 1)
    def _():
        result[...] = total[...].astype(bf16)
        values = residual[...]
        back, gain_part = norm_back(values, norm_scale(values), gain_mid[...], grad_mid[...])
        gain_grad[...] = gain_part
        grad_residual[...] = cotangent[...].astype(f32) + back
        gather.arrive()
        gather.finish()
        local.wait()


def run_feed(n, T, tokens, gated, cotangent, w_out, gain_mid, w_gate_up, w_down):
    steps = FF // TILE
    fixed = lambda *dims: pl.BlockSpec(dims, lambda i: (0, 0))
    return pl.pallas_call(
        functools.partial(feed_kernel, n, T, steps),
        grid=(steps,),
        out_shape=(shape((T, D), bf16), shape((T, D), f32), shape((n * T, D), bf16), shape((1, D), f32)),
        in_specs=[
            fixed(T, D), fixed(T, D), fixed(T, D), fixed(D, D), fixed(1, D),
            pl.BlockSpec((D, TILE), lambda i: (0, i)), pl.BlockSpec((D, TILE), lambda i: (0, i + FF // TILE)),
            pl.BlockSpec((TILE, D), lambda i: (i, 0)),
        ],
        out_specs=[fixed(T, D), fixed(T, D), ANY, fixed(1, D)],
        scratch_shapes=[
            pltpu.VMEM((T, D), f32), pltpu.VMEM((T, D), bf16), pltpu.VMEM((T, D), f32), pltpu.VMEM((T, D), f32),
            DMA, *gather_sems(n),
        ],
        compiler_params=pltpu.CompilerParams(vmem_limit_bytes=LIMIT, collective_id=2, has_side_effects=True),
        name="feed_forward",
    )(tokens, gated, cotangent, w_out, gain_mid, w_gate_up, w_gate_up, w_down)


def backward_turn(
    n, T, head, starts, bias, rate, taps, gain, incoming_of, proj, small, states, fetch,
    gp, grad_small, gconv_w, xbuf, halo, gates_sum, grad_state, done, k, _,
):
    width = MIXED * HD
    lane = iota((T, HD), 1)
    place_i, place_j = iota((T, T), 0), iota((T, T), 1)
    upper = (place_j >= place_i).astype(bf16)
    under = place_j < place_i
    c = n - 1 - k
    first = pl.multiple_of(c * T, T)
    at, two = rows_of(c, T), rows_of(c, NH * T)
    gate = chunk_gates(small[at, :], bias, rate, starts, first, T)
    block = xbuf[pl.ds(first, T + 8), :]
    conv, sig, query, keys, values, scales = chunk_inputs(block, taps, gate["docs"], T)
    key_pair, query_pair = halves(keys), halves(query)
    b, hd, hd2, to_end = gate["b"], gate["hd"], gate["hd2"], gate["to_end"]
    decay2 = beside(gate["decay"], gate["decay"])
    pairs = nt(key_pair, key_pair) * gate["decays"]
    scores = nt(query_pair, key_pair) * decay2
    state = (states[0, c], states[1, c])
    state_grad = grad_state[...]
    new, inverse, mixed = fetch(c)
    raw = proj[at, width:].astype(f32)
    normal, scale, zsig = head_gate(mixed, raw)
    incoming = incoming_of(at)
    passed = incoming * (raw * zsig)
    gates_sum[0:1, :] += jnp.sum(passed * normal, axis=0, keepdims=True)
    grad_z = incoming * (normal * gain[...]) * (zsig * (1.0 + raw * (1.0 - zsig)))
    e = passed * gain[...]
    grad_mixed = scale * (e - normal * jnp.mean(e * normal, axis=-1, keepdims=True))
    gm = halves(grad_mixed)
    ended = halves(to_end * keys)
    grad_pair = halves(state_grad)
    grad_new = tn(halves(scores), gm) + nn(ended, grad_pair)
    grad_right = tn(inverse, halves(grad_new))
    moved = b * grad_right
    grad_state[...] = gate["whole"] * state_grad + tn(halves(hd * query), gm) - tn(halves(hd2 * keys), halves(moved))
    grad_ended = nt(new, grad_pair)
    grad_scores = nt(gm, new)
    grad_lower = jnp.where(gate["decays"] != 0.0, -nt(halves(grad_right), new), 0.0)
    from_grad = nt(gm, state)
    scored = grad_scores * decay2
    grad_query = hd * from_grad + nn(scored, key_pair[0])
    paired = (b * grad_lower) * gate["decays"]
    keyed = nn(key_pair, state)
    grad_keys = (
        tn(scored, query_pair[0]) + to_end * grad_ended - hd2 * nt(moved, state[0])
        + nn(paired, key_pair[0]) + tn(paired, key_pair[0])
    )
    lower_pairs = grad_lower * pairs
    grad_b = jnp.sum(grad_right * (values - hd2 * keyed), axis=-1, keepdims=True) + jnp.sum(
        lower_pairs, axis=-1, keepdims=True
    )
    four = b * lower_pairs
    both = grad_scores * scores
    joint = (four[:T, :T] + four[:T, T:]) + (four[T:, :T] + four[T:, T:]) + (both[:, :T] + both[:, T:])
    crossing = jnp.sum(jnp.where(under, nn_exact(upper, joint), 0.0), axis=-1, keepdims=True)
    start_part = -hd2 * jnp.sum(moved * keyed, axis=-1, keepdims=True)
    start_part = start_part[:T] + start_part[T:] + hd * jnp.sum(query * from_grad, axis=-1, keepdims=True)
    end_part = to_end * jnp.sum(grad_ended * keys, axis=-1, keepdims=True)
    end_part = end_part[:T] + end_part[T:]
    sums_in = jnp.where(lane == 0, start_part, jnp.where(lane == 1, end_part, 0.0))
    after = nn_exact(upper, sums_in)
    before = nn_exact(under.astype(bf16), sums_in)
    whole_part = gate["whole"] * jnp.sum(state_grad * (state[0].astype(f32) + state[1].astype(f32)), keepdims=True)
    grad_gate = crossing + after[:, 0:1] + before[:, 1:2] + whole_part
    shifted = gate["shifted"]
    grad_beta = [grad_b[i * T : (i + 1) * T] * (gate["beta"][:, i : i + 1] * (1.0 - 0.5 * gate["beta"][:, i : i + 1])) for i in range(NH)]
    grad_decay = (-grad_gate * rate * sigmoid(shifted))[:, NH : NH + 1]
    which = lane >> 3
    logit = jnp.where(which == 0, grad_beta[0], jnp.where(which == 1, grad_beta[1], grad_decay))
    grad_logits = jnp.where((lane < SMALL * H) & ((lane & (H - 1)) == head), logit, 0.0)
    gates_sum[1:2, :] += jnp.sum(jnp.where(lane == NH, grad_decay, 0.0), axis=0, keepdims=True)
    gates_sum[2:3, :] += jnp.sum(jnp.where(lane == NH, grad_gate * -softplus(shifted), 0.0), axis=0, keepdims=True)
    high = grad_logits.astype(bf16).astype(f32)
    grad_small[at, :] = (
        high + pltpu.roll(grad_logits - high, 32, 1) + pltpu.roll(high, 64, 1)
    ).astype(bf16)
    projected_out = jnp.sum(keys * grad_keys, axis=-1, keepdims=True)
    grad_raw = (grad_keys - keys * projected_out) * scales
    slope = sig * (1.0 + conv * (1.0 - sig))
    grad_active = jnp.concatenate([grad_query, grad_raw[:T], grad_raw[T:], moved[:T], moved[T:]], axis=1)
    grad_conv = grad_active * slope
    after_block = stack2(grad_conv, halo[...])
    halo[...] = grad_conv[:8]
    position = first + iota((T, 1), 0)
    total = grad_conv * taps[CONV - 1 : CONV]
    taps_grads = [None] * CONV
    taps_grads[CONV - 1] = jnp.sum(grad_conv * block[8:], axis=0, keepdims=True)
    for lag in range(1, CONV):
        same = (doc_at(starts, position + lag) == gate["docs"][0]).astype(f32)
        total = total + after_block[lag : lag + T] * (taps[CONV - 1 - lag : CONV - lag] * same)
        same = (gate["docs"][lag] == gate["docs"][0]).astype(f32)
        taps_grads[CONV - 1 - lag] = jnp.sum(
            grad_conv * (block[8 - lag : 8 - lag + T] * same), axis=0, keepdims=True
        )
    everything = beside(total, grad_z).astype(bf16)
    gp[at, :] = everything
    gconv_w[...] += jnp.concatenate(taps_grads, axis=0)
    done(k)
    return 0


class Chain:
    def __init__(self, own, up_in, down_in, sems, my, m):
        self.own, self.up_in, self.down_in = own, up_in, down_in
        self.us, self.ur, self.ds, self.dr = sems
        self.my, self.m = my, m

    def up(self, q):
        slot = q - self.my
        return self.own(self.my + self.m - 1 - q), self.up_in(slot), slot, self.my + 1, self.us, self.ur

    def down(self, q):
        slot = q - (self.m - 1 - self.my)
        return self.own(self.my - (self.m - 1 - q)), self.down_in(slot), slot, self.my - 1, self.ds, self.dr

    def copy(self, hop):
        own, arrived, slot, peer, send, receive = hop
        return remote(own, arrived, send.at[slot], receive.at[slot], "stream", peer)

    def start(self):
        for q in range(self.m - 1):

            @pl.when(self.my == 0)
            def _():
                self.copy(self.up(q)).start()

            @pl.when(self.my == self.m - 1)
            def _():
                self.copy(self.down(q)).start()

    def tick(self, q):
        for inner, way in (
            ((self.my > 0) & (self.my <= q), self.up),
            ((self.my < self.m - 1) & (self.my >= self.m - 1 - q), self.down),
        ):

            @pl.when(inner)
            def _():
                hop = way(q)
                self.copy(hop).wait_recv()
                own, arrived = hop[:2]

                def add(i, _):
                    own[i] = (own[i].astype(f32) + arrived[i].astype(f32)).astype(bf16)
                    return 0

                if len(own.shape) == 3 and own.shape[0] > 2:
                    lax.fori_loop(0, own.shape[0], add, 0)
                else:
                    own[...] = (own[...].astype(f32) + arrived[...].astype(f32)).astype(bf16)
                self.copy(hop).start()

    def finish(self, write):
        last = self.m - 1

        @pl.when(self.my > 0)
        def _():
            slot = last - self.my
            remote(self.own(self.my), self.up_in(slot), self.us.at[slot], self.ur.at[slot], "stream", self.my - 1).wait_recv()

        @pl.when(self.my < last)
        def _():
            slot = self.my
            remote(self.own(self.my), self.down_in(slot), self.ds.at[slot], self.dr.at[slot], "stream", self.my + 1).wait_recv()

        from_below, from_above = self.up_in(lax.rem(last - self.my, last)), self.down_in(lax.rem(self.my, last))
        found = self.own(self.my)[...].astype(f32) + jnp.where(self.my > 0, from_below[...].astype(f32), 0.0)
        write(found + jnp.where(self.my < last, from_above[...].astype(f32), 0.0))

    def settle(self):
        for q in range(self.m - 1):

            @pl.when(self.my <= q)
            def _():
                self.copy(self.up(q)).wait_send()

            @pl.when(self.my >= self.m - 1 - q)
            def _():
                self.copy(self.down(q)).wait_send()


class Sums:
    def __init__(self, own, arrived, every, sems, me, my, n, m):
        self.own, self.arrived, self.every = own, arrived, every
        self.zs, self.zr, self.ss, self.rs = sems
        self.me, self.my, self.n, self.m = me, my, n, m

    def across(self, k):
        peer = lax.rem(self.my + k, self.m)
        return remote(self.own, self.arrived.at[k - 1], self.zs.at[k - 1], self.zr.at[k - 1], "stream", peer)

    def along(self, k):
        block = self.every.at[self.me]
        return remote(block, block, self.ss.at[k - 1], self.rs.at[k - 1], "seq", lax.rem(self.me + k, self.n))

    def start(self):
        for k in range(1, self.m):
            self.across(k).start()

    def add(self):
        total = self.own[...]
        for k in range(1, self.m):
            self.across(k).wait()
            total = total + self.arrived[k - 1]
        self.every[self.me] = total
        for k in range(1, self.n):
            self.along(k).start()

    def settle(self):
        for k in range(1, self.n):
            self.along(k).wait()


def chain_sems(*lead):
    return [DMA(lead) for _ in range(4)]


def scatter_to(own, arrived, k, send, receive, me, size):
    peer = lax.rem(me + k, size)
    return remote(own.at[peer], arrived.at[me], send.at[k - 1], receive.at[k - 1], "seq", peer)


def back_kernel(
    n, m, rep, T, piece, shard, wide,
    lengths, bias_ref, rate_ref, tokens, grad_residual, gain_in, gain_mid_grad, w_small, taps_ref, gain,
    mid_any, out_any, w_gate_up, w_down, w_out, rows_any, proj_any, small_any, mixed_any, states_any, news_any, invs_any,
    normed_any, w_in_any,
    grad_input, q_w_in, g_out, q_gu_in, g_down, q_sum,
    mid, cot, w_gate, w_up, w_hid, w_head, head_rows, proj, small, mixed, states, news, invs, normed, w_in, w_wide,
    low_all, hidden, grad_gate, grad_up, gp, grad_small, gconv_w, xbuf, halo, gates_sum, grad_state,
    z_gu, z_gu_up, z_gu_down, z_down, z_down_up, z_down_down, z_out, z_out_up, z_out_down, z_w, z_w_up, z_w_down,
    z_sum, z_sum_in, gain_sum, q_gu, q_w, part_own, part_out, part_in, chip_out, chip_in,
    l_sems, i_sems, gu_us, gu_ur, gu_ds, gu_dr, dn_us, dn_ur, dn_ds, dn_dr, ou_us, ou_ur, ou_ds, ou_dr, w_us, w_ur, w_ds, w_dr,
    sum_ss, sum_rs, qgu_ss, qgu_rs, qw_ss, qw_rs, qsum_ss, qsum_rs, p_ss, p_rs, c_ss, c_rs, *sems,
):
    me, my = lax.axis_index("seq"), lax.axis_index("stream")
    head, chip, side = me // rep, me // 2, lax.rem(me, 2)
    sib = me + 1 - 2 * side
    barrier = pltpu.get_barrier_semaphore()
    for k in range(1, n):
        pl.semaphore_signal(barrier, inc=1, device_id={"seq": lax.rem(me + k, n)}, device_id_type=MESH)
    for k in range(1, m):
        pl.semaphore_signal(barrier, inc=1, device_id={"stream": lax.rem(my + k, m)}, device_id_type=MESH)
    first_unit = me * shard
    base = (first_unit // HD - me // (n - 1)) * HD
    offset = first_unit - base
    sources = [
        mid_any, out_any, w_gate_up.at[:, pl.ds(pl.multiple_of(base, HD), wide)],
        w_gate_up.at[:, pl.ds(pl.multiple_of(FF + base, HD), wide)], w_down.at[pl.ds(pl.multiple_of(base, HD), wide)],
        w_out.at[rows_of(head, HD)], rows_any, proj_any, small_any, mixed_any, states_any, news_any, invs_any, normed_any,
    ]
    places = [mid, cot, w_gate, w_up, w_hid, w_head, head_rows, proj, small, mixed, states, news, invs, normed]
    roomy = len(normed.shape) == 2
    loads = [pltpu.make_async_copy(a, b, l_sems.at[i]) for i, (a, b) in enumerate(zip(sources, places)) if i not in (9, 11, 12, 13) or roomy]
    for i in range(GROUPS):
        column = pl.ds(pl.multiple_of(i * D + head * HD, HD), HD)
        loads.append(pltpu.make_async_copy(w_in_any.at[:, column], w_in.at[:, i * HD : (i + 1) * HD], i_sems.at[i]))
    for load in loads[:5]:
        load.start()
    low_all[rows_of(me, T), :] = grad_residual[...].astype(bf16)
    pl.semaphore_wait(barrier, n + m - 2)
    gather = Gather(n, T, low_all.at[rows_of(me, T)], low_all, sems)
    gather.start()

    for load in loads[:5]:
        load.wait()
    for load in loads[5:]:
        load.start()

    def feed_turn(i, _):
        at = rows_of(i, TILE)
        block = mid[at, :]
        gate, up = nn(block, w_gate[...]), nn(block, w_up[...])
        sig = sigmoid(gate)
        silu = gate * sig
        grad_hidden = nt(cot[at, :], w_hid[...])
        own = lambda x: pltpu.roll(x, wide - offset, 1)[:, :shard].astype(bf16)
        hidden[at, :] = own(silu * up)
        grad_gate[at, :] = own(grad_hidden * up * (sig * (1.0 + gate * (1.0 - sig))))
        grad_up[at, :] = own(grad_hidden * silu)
        return 0

    lax.fori_loop(0, n * T // TILE, feed_turn, 0)
    downs = Chain(lambda d: z_down.at[d], lambda i: z_down_up.at[i], lambda i: z_down_down.at[i], (dn_us, dn_ur, dn_ds, dn_dr), my, m)
    ups = [
        Chain(
            lambda d, j=j: z_gu.at[j, d], lambda i, j=j: z_gu_up.at[j, i], lambda i, j=j: z_gu_down.at[j, i],
            (gu_us.at[j], gu_ur.at[j], gu_ds.at[j], gu_dr.at[j]), my, m,
        )
        for j in range(2)
    ]
    part = tn(hidden[...], cot[...])
    for d in range(m):
        z_down[d] = part[d * (shard // m) : (d + 1) * (shard // m)].astype(bf16)
    downs.start()
    gather.forward()
    for j, grads in enumerate((grad_gate, grad_up)):
        if j:
            gather.forward_late()

        def strip_turn(t, _, j=j, grads=grads):
            found = tn(mid[:, rows_of(t, TILE)], grads[...])
            for i in range(TILE // piece):
                z_gu[j, i % m, t * (TILE // piece // m) + i // m] = found[i * piece : (i + 1) * piece].astype(bf16)
            return 0

        lax.fori_loop(0, D // TILE, strip_turn, 0)
        ups[j].start()
    w_high, w_low = halves(w_small[...])
    widened(w_wide, (w_high, w_high, w_low))
    gather.arrive()
    gather.finish()
    for load in loads[5:]:
        load.wait()
    rows = tn(head_rows[...], low_all[...])
    for share in range(rep):

        @pl.when(lax.rem(me, rep) == share)
        def _():
            for d in range(m):
                at = share * (HD // rep) + d * piece
                z_out[d] = rows[at : at + piece].astype(bf16)

    outs = Chain(lambda d: z_out.at[d], lambda i: z_out_up.at[i], lambda i: z_out_down.at[i], (ou_us, ou_ur, ou_ds, ou_dr), my, m)
    outs.start()
    if not roomy:
        normed = mid
        late = pltpu.make_async_copy(normed_any, normed, l_sems.at[13])
        late.start()
        late.wait()

    width = MIXED * HD
    starts = doc_starts(lengths)
    bias, rate = bias_ref[head], rate_ref[head]
    taps = head_taps(taps_ref, head)
    xbuf[0:8, :] = jnp.zeros((8, width), f32)
    halo[...] = jnp.zeros((8, width), f32)
    gconv_w[...] = jnp.zeros(gconv_w.shape, f32)
    gates_sum[...] = jnp.zeros((8, HD), f32)
    grad_state[...] = jnp.zeros((HD, HD), f32)

    def fill(c, _):
        xbuf[pl.ds(pl.multiple_of(8 + c * T, 8), T), :] = proj[rows_of(c, T), :width].astype(f32)
        return 0

    lax.fori_loop(0, n, fill, 0)

    def normed_rows(at):
        if roomy:
            return normed[at, :].astype(f32)
        return mid[at, :].astype(f32)

    gain_sum[...] = jnp.zeros((1, D), f32)

    def sibling_copy(j):
        return remote(part_out.at[j], part_in.at[j], p_ss.at[j], p_rs.at[j], "seq", sib)

    def owner_copy(j):
        return remote(chip_out.at[j], chip_in.at[chip], c_ss.at[j], c_rs.at[chip], "seq", 2 * j + side)

    def form(j):
        at = rows_of(j, 2 * T)
        found = nt(gp[at, :], w_in[...]) + nn(grad_small[at, :], w_wide[...])
        if rep > 1:
            found = found * (lax.rem(me, rep) == 0).astype(f32)
        gain_sum[...] += jnp.sum(found * normed_rows(at), axis=0, keepdims=True)
        for i in range(2):

            @pl.when(side == i)
            def _():
                part_own[j] = found[i * T : (i + 1) * T].astype(part_own.dtype)
                part_out[j] = found[(1 - i) * T : (2 - i) * T].astype(bf16)

        sibling_copy(j).start()

    def join(j):
        sibling_copy(j).wait_recv()
        found = part_own[j].astype(f32) + part_in[j].astype(f32)
        part_own[j] = found.astype(part_own.dtype)
        chip_out[j] = found.astype(bf16)

        @pl.when(chip != j)
        def _():
            owner_copy(j).start()

    hops = [(chain, q) for chain in (downs, *ups, outs) for q in range(1, m - 1)]

    def after_turn(k):
        c = n - 1 - k

        @pl.when(lax.rem(k, 2) == 1)
        def _():
            form(c // 2)

        @pl.when((lax.rem(k, 2) == 0) & (k > 0))
        def _():
            join((c + 1) // 2)

        for i, (chain, q) in enumerate(hops):

            @pl.when(k == i)
            def _():
                chain.tick(q)

    def fetch(c):
        if roomy:
            return kept(news, rows_of(c, NH * T)), (invs[0, c], invs[1, c]), mixed[rows_of(c, T), :]
        late = [
            pltpu.make_async_copy(news_any.at[:, rows_of(c, NH * T)], news, l_sems.at[11]),
            pltpu.make_async_copy(invs_any.at[:, pl.ds(c, 1)], invs, l_sems.at[12]),
            pltpu.make_async_copy(mixed_any.at[rows_of(c, T)], mixed, l_sems.at[9]),
        ]
        for load in late:
            load.start()
        for load in late:
            load.wait()
        return (news[0], news[1]), (invs[0, 0], invs[1, 0]), mixed[...]

    turn = functools.partial(
        backward_turn, n, T, head, starts, bias, rate, taps, gain, lambda at: nt(low_all[at, :], w_head[...]),
        proj, small, states, fetch, gp, grad_small, gconv_w, xbuf, halo, gates_sum, grad_state, after_turn,
    )
    lax.fori_loop(0, n, turn, 0)

    small_t = tn(grad_small[...], normed[...])
    small_t = small_t[: SMALL * H] + small_t[32 : 32 + SMALL * H]
    z_sum[0:1, :] = gain_mid_grad[...]
    for i in range(SMALL):
        z_sum[1 + i : 2 + i, :] = jnp.sum(small_t[i * H : (i + 1) * H], axis=0, keepdims=True)
    z_sum[4:8, :width] = gconv_w[...]
    for i in range(3):
        z_sum[4 + i : 5 + i, width : width + HD] = gates_sum[i : i + 1, :]
    z_sum[7:8, width : width + HD] = jnp.zeros((1, HD), f32)
    gain_part = gain_sum[...] / gain_in[...]
    cut = D - width - HD
    for i in range(4):
        z_sum[4 + i : 5 + i, width + HD :] = gain_part[:, i * cut : (i + 1) * cut]
    first_sums = Sums(z_sum, z_sum_in, q_sum, (sum_ss, sum_rs, qsum_ss, qsum_rs), me, my, n, m)
    first_sums.start()

    lines = D // TILE
    units, strip = n // lines, piece * m

    def line(i):
        return Chain(
            lambda d: z_w.at[i, d], lambda j: z_w_up.at[i, j], lambda j: z_w_down.at[i, j],
            (w_us.at[i], w_ur.at[i], w_ds.at[i], w_dr.at[i]), my, m,
        )

    def line_turn(i, _):
        cuts = []
        for u in range(units):
            first = (i + u * lines) * strip
            if strip % HD == 0:
                first = pl.multiple_of(first, HD)
            cuts.append(normed[:, pl.ds(first, strip)])
        found = tn(jnp.concatenate(cuts, axis=1), gp[...])
        for u in range(units):
            for d in range(m):
                at = u * strip + d * piece
                z_w[i, d, u] = found[at : at + piece].astype(bf16)
        line(i).start()
        return 0

    if strip % HD == 0:
        line_turn(0, 0)
        join(0)
        lax.fori_loop(1, lines, line_turn, 0)
    else:
        for i in range(lines):
            line_turn(i, 0)
        join(0)
    ins = [line(i) for i in range(lines)]
    for i, (chain, q) in enumerate(hops):
        if i >= n:
            chain.tick(q)

    def write_down(x):
        g_down[...] = x

    def write_out(x):
        g_out[...] = x

    downs.finish(write_down)
    for j in range(2):

        def write_up(x, j=j):
            q_gu[:, j] = x.astype(bf16)

        ups[j].finish(write_up)
    q_ups = [scatter_to(q_gu, q_gu_in, k, qgu_ss, qgu_rs, me, n) for k in range(1, n)]
    for copy in q_ups:
        copy.start()
    q_gu_in[me] = q_gu[me]

    def input_gradient():
        total = part_own[chip].astype(f32)
        for k in range(1, n // 2):
            other = lax.rem(chip + k, n // 2)
            remote(chip_out.at[other], chip_in.at[other], c_ss.at[other], c_rs.at[other], "seq", 2 * other + side).wait_recv()
            total = total + chip_in[other].astype(f32)
        values = tokens[...].astype(f32)
        part, _ = norm_back(values, norm_scale(values), gain_in[...], total)
        grad_input[...] = grad_residual[...] + part

    def deliver(i):
        def write_in(x):
            for u in range(units):
                q_w[i + u * lines] = x[u].astype(bf16)

        ins[i].finish(write_in)
        for j in range(i, n, lines):

            @pl.when(me != j)
            def _():
                remote(q_w.at[j], q_w_in.at[me], qw_ss.at[j], qw_rs.at[me], "seq", j).start()

    first_sums.add()
    for i, chain in enumerate(ins):
        for q in range(1, m - 1):
            chain.tick(q)
        if i:
            deliver(i - 1)
        if i == 1:
            outs.finish(write_out)
        if i == 2:
            input_gradient()
    deliver(len(ins) - 1)
    q_w_in[me] = q_w[me]
    for chain in (downs, *ups, outs, *ins):
        chain.settle()

    def settle(j, _):
        sibling_copy(j).wait_send()

        @pl.when(chip != j)
        def _():
            owner_copy(j).wait_send()

        return 0

    lax.fori_loop(0, n // 2, settle, 0)
    first_sums.settle()
    for copy in q_ups:
        copy.wait()
    for k in range(1, n):
        peer = lax.rem(me + k, n)
        remote(q_w.at[peer], q_w_in.at[me], qw_ss.at[peer], qw_rs.at[me], "seq", peer).wait_send()
        remote(q_w.at[peer], q_w_in.at[peer], qw_ss.at[peer], qw_rs.at[peer], "seq", peer).wait_recv()


def run_back(n, m, rep, T, lengths, bias, rate, tokens, grad_residual, gain_in, gain_mid_grad, w_small, taps, gain,
             mid, cot, w_gate_up, w_down, w_out, head_rows, proj, small, mixed, states, news, invs, normed, w_in):
    rows, piece, shard = n * T, D // (n * m), FF // n
    wide = -(-(shard + HD - 1) // HD) * HD
    vm, roomy = pltpu.VMEM, rows <= 1024
    band = GROUPS * HD

    def chained(*dims, lead=()):
        return [vm((*lead, m, *dims), bf16), vm((*lead, m - 1, *dims), bf16), vm((*lead, m - 1, *dims), bf16)]

    return pl.pallas_call(
        functools.partial(back_kernel, n, m, rep, T, piece, shard, wide),
        out_shape=(
            shape((T, D), f32), shape((n, piece, band), bf16), shape((piece, D), f32), shape((n, 2, piece, shard), bf16),
            shape((shard // m, D), f32), shape((n, 8, D), f32),
        ),
        in_specs=[SMEM] * 3 + [VMEM] * 7 + [ANY] * 14,
        out_specs=[VMEM] * 6,
        scratch_shapes=[
            vm((rows, D), bf16), vm((rows, D), bf16), vm((D, wide), bf16), vm((D, wide), bf16), vm((wide, D), bf16),
            vm((HD, D), bf16), vm((rows, HD), bf16), vm((rows, band), bf16), vm((rows, HD), f32), vm((rows if roomy else T, HD), f32),
            vm((2, n, HD, HD), bf16), vm((2, NH * (rows if roomy else T), HD), bf16), vm((2, n if roomy else 1, NH * T, NH * T), bf16),
            vm((rows, D) if roomy else (1, 16, HD), bf16), vm((D, band), bf16), vm((HD, D), bf16),
            vm((rows, D), bf16), vm((rows, shard), bf16), vm((rows, shard), bf16), vm((rows, shard), bf16),
            vm((rows, band), bf16), vm((rows, HD), bf16), vm((CONV, MIXED * HD), f32), vm((rows + 8, MIXED * HD), f32),
            vm((8, MIXED * HD), f32), vm((8, HD), f32), vm((HD, HD), f32),
            *chained(n, piece, shard, lead=(2,)), *chained(shard // m, D), *chained(piece, D), *chained(n * TILE // D, piece, band, lead=(D // TILE,)),
            vm((8, D), f32), vm((m - 1, 8, D), f32), vm((1, D), f32), vm((n, 2, piece, shard), bf16), vm((n, piece, band), bf16),
            vm((n // 2, T, D), f32 if roomy else bf16), *[vm((n // 2, T, D), bf16)] * 4,
            DMA((14,)), DMA((GROUPS,)), *chain_sems(2, m - 1), *chain_sems(m - 1), *chain_sems(m - 1),
            *chain_sems(D // TILE, m - 1), DMA((m - 1,)), DMA((m - 1,)), DMA((n - 1,)), DMA((n - 1,)), DMA((n,)), DMA((n,)),
            DMA((n - 1,)), DMA((n - 1,)),
            *[DMA((n // 2,))] * 4, *gather_sems(n),
        ],
        compiler_params=pltpu.CompilerParams(vmem_limit_bytes=(60 if roomy else 63) * 1024 * 1024, collective_id=3, has_side_effects=True),
        name="backward",
    )(lengths, bias, rate, tokens, grad_residual, gain_in, gain_mid_grad, w_small, taps, gain,
      mid, cot, w_gate_up, w_down, w_out, head_rows, proj, small, mixed, states, news, invs, normed, w_in)


def output_kernel(
    n, rep, shard, result_in, grad_input_in, w_parts, out_part, gu_parts, down_part, sums,
    result, grad_input, g_in, g_out, g_gate_up, g_down, g_gain_in, g_gain_mid, g_small, g_bias, g_rate, g_taps, g_gain_head,
):
    result[...] = result_in[...]
    grad_input[...] = grad_input_in[...]
    g_out[...] = out_part[...]
    g_down[...] = down_part[...]
    for i in range(2):
        for source in range(n):
            at = i * FF + source * shard
            g_gate_up[:, at : at + shard] = gu_parts[source, i].astype(f32)
    g_gain_mid[...] = jnp.sum(sums[:, 0:1, :], axis=0)
    width = MIXED * HD
    cut = D - width - HD
    for i in range(4):
        g_gain_in[:, i * cut : (i + 1) * cut] = jnp.sum(sums[:, 4 + i : 5 + i, width + HD :], axis=0)
    gain_total = jnp.zeros((1, HD), f32)
    for h in range(H):
        found = sums[h * rep]
        part = w_parts[h * rep].astype(f32)
        for j in range(SMALL):
            g_small[j * H + h : j * H + h + 1, :] = found[1 + j : 2 + j, :]
        for i in range(MIXED):
            g_taps[:, i * D + h * HD : i * D + (h + 1) * HD] = found[4 : 4 + CONV, i * HD : (i + 1) * HD]
        for i in range(GROUPS):
            g_in[:, i * D + h * HD : i * D + (h + 1) * HD] = part[:, i * HD : (i + 1) * HD]
        gain_total = gain_total + found[4:5, width : width + HD]
        g_bias[h] = found[5, width + NH]
        g_rate[h] = found[6, width + NH]
    g_gain_head[...] = gain_total


def run_output(n, rep, *parts):
    result, grad_input, w_parts, out_part, gu_parts, down_part, sums = parts
    piece, shard = out_part.shape[0], gu_parts.shape[-1]
    return pl.pallas_call(
        functools.partial(output_kernel, n, rep, shard),
        out_shape=(
            shape(result.shape, bf16), shape(grad_input.shape, f32), shape((piece, GROUPS * D), f32), shape((piece, D), f32),
            shape((piece, 2 * FF), f32), shape(down_part.shape, f32), shape((1, D), f32), shape((1, D), f32),
            shape((SMALL * H, D), f32), shape((H,), f32), shape((H,), f32), shape((CONV, MIXED * D), f32), shape((1, HD), f32),
        ),
        in_specs=[VMEM] * 7,
        out_specs=[VMEM] * 9 + [SMEM] * 2 + [VMEM] * 2,
        compiler_params=pltpu.CompilerParams(vmem_limit_bytes=LIMIT),
        name="outputs",
    )(*parts)


def on_device(tokens, grad_out, doc_lengths, gain_in, in_weight, small_weight, gate_bias, decay_rate, conv_weight,
              gain_head, out_weight, gain_mid, gate_up_weight, down_weight):
    seq, stream = lax.axis_size("seq"), lax.axis_size("stream")
    rep = seq // H
    T = tokens.shape[1]
    gain = gain_head.reshape(1, HD)
    gain_in, gain_mid = gain_in.reshape(1, D), gain_mid.reshape(1, D)
    rows, cotangent, small_weight = tokens[0], grad_out[0], small_weight.T
    gated, normed, out_all, proj, small, mixed, states, news, invs, head_rows = run_forward(
        seq, rep, T, doc_lengths, gate_bias, decay_rate, rows, cotangent, gain_in, in_weight, small_weight, conv_weight, gain
    )
    result, grad_residual, mid_all, grad_gain_mid = run_feed(
        seq, T, rows, gated, cotangent, out_weight, gain_mid, gate_up_weight, down_weight
    )
    parts = run_back(
        seq, stream, rep, T, doc_lengths, gate_bias, decay_rate, rows, grad_residual, gain_in, grad_gain_mid, small_weight,
        conv_weight, gain, mid_all, out_all, gate_up_weight, down_weight, out_weight, head_rows, proj, small, mixed, states,
        news, invs, normed, in_weight,
    )
    result, grad_input, g_in, g_out, g_gate_up, g_down, g_gain_in, g_gain_mid, g_small, g_bias, g_rate, g_taps, g_gain_head = (
        run_output(seq, rep, result, *parts)
    )
    return (
        result[None], grad_input[None], g_gain_in.reshape(D), g_in, g_small.T, g_bias, g_rate, g_taps,
        g_gain_head.reshape(HD), g_out, g_gain_mid.reshape(D), g_gate_up, g_down,
    )


def solution(mesh):
    rows, whole, split = P("stream", "seq", None), P(), P(("seq", "stream"), None)
    return jax.shard_map(
        on_device,
        mesh=mesh,
        in_specs=(rows, rows, P("stream", None)) + (whole,) * 11,
        out_specs=(rows, rows, whole, split, whole, whole, whole, whole, whole, split, whole, split, split),
        check_vma=False,
    )
```
